32 devices in a mesh: seq: 8 (over z, x), dp: 4 (over y, core).
Axes of the slice: x: 2, y: 2, z: 4, core: 2. Of those that a mesh axis runs over, the one named last changes fastest.
Arguments:
- tokens: bfloat16 [32, 2048, 768], P('dp', 'seq'), may hold values from -6 to 6
- segments: int32 [32, 2048], P('dp', 'seq'), may hold values from 0 to 2097151, as said below
- token_types: int32 [32, 2048], P('dp', 'seq'), may hold values from 0 to 2097151, as said below
- cotangent: bfloat16 [32, 1024, 768], P('dp', 'seq'), may hold values from -6 to 6
- query_weight: float32 [768, 768], P('dp'), may hold values from -0.21875 to 0.21875
- key_weight: float32 [768, 768], P('dp'), may hold values from -0.21875 to 0.21875
- value_weight: float32 [768, 768], P('dp'), may hold values from -0.21875 to 0.21875
- output_weight: float32 [768, 768], P('dp'), may hold values from -1.25 to 1.25
- inner_weight: float32 [768, 3072], P('dp'), may hold values from -0.21875 to 0.21875
- outer_weight: float32 [3072, 768], P('dp'), may hold values from -0.109375 to 0.109375
- value_bias: float32 [768], P('dp'), may hold values from -2 to 2
- output_bias: float32 [768], P('dp'), may hold values from -2 to 2
- inner_bias: float32 [3072], P('dp'), may hold values from -2 to 2
- outer_bias: float32 [768], P('dp'), may hold values from -2 to 2
- attention_norm_gain: float32 [768], P('dp'), may hold values from 0.25 to 1.75
- first_shift: float32 [768], P('dp'), may hold values from -2 to 2
- second_gain: float32 [768], P('dp'), may hold values from 0.25 to 1.75
- second_shift: float32 [768], P('dp'), may hold values from -2 to 2
- content_bias: float32 [12, 64], P('dp'), may hold values from -3 to 3
- position_bias: float32 [12, 64], P('dp'), may hold values from -3 to 3
- type_bias: float32 [12, 64], P('dp'), may hold values from -3 to 3
- relative_kernel: float32 [12, 64, 64], P('dp'), may hold values from -0.75 to 0.75
- type_embed: float32 [12, 2, 64], P('dp'), may hold values from -5 to 5
Outputs:
- output: bfloat16 [32, 1024, 768], P('dp', 'seq')
- grad_tokens: bfloat16 [32, 2048, 768], P('dp', 'seq')
- grad_query_weight: float32 [768, 768], P('dp')
- grad_key_weight: float32 [768, 768], P('dp')
- grad_value_weight: float32 [768, 768], P('dp')
- grad_output_weight: float32 [768, 768], P('dp')
- grad_inner_weight: float32 [768, 3072], P('dp')
- grad_outer_weight: float32 [3072, 768], P('dp')
- grad_value_bias: float32 [768], P('dp')
- grad_output_bias: float32 [768], P('dp')
- grad_inner_bias: float32 [3072], P('dp')
- grad_outer_bias: float32 [768], P('dp')
- grad_first_gain: float32 [768], P('dp')
- grad_first_shift: float32 [768], P('dp')
- grad_second_gain: float32 [768], P('dp')
- grad_second_shift: float32 [768], P('dp')
- grad_content_bias: float32 [12, 64], P('dp')
- grad_position_bias: float32 [12, 64], P('dp')
- grad_type_bias: float32 [12, 64], P('dp')
- grad_relative_kernel: float32 [12, 64, 64], P('dp')
- grad_type_embed: float32 [12, 2, 64], P('dp')
The draws below stay inside these ranges and needn't reach their ends.
Inputs may be any that keep to these rules, and one draw needn't show every extreme that they name: `segments`: each sequence holds two or three documents, each a contiguous run of positions with a label of its own that differs from the labels of the sequence's other documents; every document has at least 204 positions; only equality of labels within a sequence has meaning. `token_types`: each sequence uses up to three type labels; only equality of labels within a sequence has meaning.
All inputs are finite; a program needn't handle non-finite values.
Results may differ from the reference program's by a relative error of at most 0.023.
The reference program's roundings to bfloat16 on the way count: a program that leaves them out, or rounds other values in their place, can miss the bound.
Values may be sent and summed in bfloat16 or wider, within the bound.
A program may use at most 256 MiB of HBM per device.

```python
import math
import jax
import jax.numpy as jnp
from jax import lax

MODEL_WIDTH = 768
HEAD_COUNT = 12
HEAD_SIZE = 64
FF = 3072
LEN = 2048
SEQS = 32
PQ = 1024


def distinct_labels(key):
    label_range = 2 ** 21
    base_label = jax.random.randint(jax.random.fold_in(key, 1), (SEQS, 1), 0, label_range, dtype=jnp.int32)
    near_offset = jax.random.randint(jax.random.fold_in(key, 2), (SEQS, 1), 1, 2 ** 20, dtype=jnp.int32)
    far_offset = jax.random.randint(jax.random.fold_in(key, 3), (SEQS, 1), 2 ** 20, label_range, dtype=jnp.int32)
    labels = jnp.concatenate([base_label, (base_label + near_offset) % label_range, (base_label + far_offset) % label_range], axis=1)
    top_label = jnp.max(labels)
    return (labels + (label_range - 1 - top_label)) % label_range


def draw_segments(key, part):
    shortest = LEN // 10
    first_key = jax.random.fold_in(key, 11)
    second_key = jax.random.fold_in(key, 12)
    first_length = jax.random.randint(first_key, (SEQS, 1), shortest, LEN - shortest + 1, dtype=jnp.int32)
    remaining = LEN - first_length
    upper_second = jnp.maximum(remaining - shortest, shortest)
    second_length = jax.random.randint(second_key, (SEQS, 1), shortest, upper_second + 1, dtype=jnp.int32)
    second_end = jnp.where(remaining >= 2 * shortest, first_length + second_length, LEN)
    places = jnp.arange(LEN, dtype=jnp.int32)[None, :]
    doc_index = (places >= first_length).astype(jnp.int32) + (places >= second_end).astype(jnp.int32)
    labels = distinct_labels(jax.random.fold_in(key, 21))
    return jnp.take_along_axis(labels, doc_index, axis=1)


def draw_token_types(key, part):
    kind_index = jax.random.randint(jax.random.fold_in(key, 34), (SEQS, LEN), 0, 3, dtype=jnp.int32)
    labels = distinct_labels(jax.random.fold_in(key, 31))
    return jnp.take_along_axis(labels, kind_index, axis=1)


def levels(key, shape, split, least, high):
    level = 1.0
    for dim, shards_of in split:
        steps = jax.random.uniform(jax.random.fold_in(jax.random.fold_in(key, 6), dim), (shards_of,), jnp.float32, least / len(split), high / len(split))
        level = level * jnp.repeat(jnp.exp(steps), shape[dim] // shards_of).reshape((-1,) + (1,) * (len(shape) - 1 - dim))
    return level


def noise(key, dims, width, limit, shards=(), kind=jnp.bfloat16):
    loudness = levels(key, dims, shards, -0.22, 0.18) if shards else 1.0
    values = jax.random.normal(key, dims, jnp.float32) * width * loudness
    return jnp.minimum(jnp.maximum(values, -limit), limit).astype(kind)


def setup_inputs(seed: int = 0) -> dict:
    arg_keys = jax.random.split(jax.random.key(seed), 24)
    tokens = noise(arg_keys[0], (SEQS, LEN, MODEL_WIDTH), 1.0, 6.0, ((0, 4), (1, 8)))
    segments = draw_segments(jax.random.fold_in(arg_keys[23], 71), 0)
    token_types = draw_token_types(jax.random.fold_in(arg_keys[23], 71), 0)
    cotangent = noise(arg_keys[3], (SEQS, PQ, MODEL_WIDTH), 1.0, 6.0, ((0, 4), (1, 8)))
    query_weight = noise(arg_keys[4], (MODEL_WIDTH, MODEL_WIDTH), MODEL_WIDTH ** -0.5, 0.21875, ((0, 4),), jnp.float32)
    key_weight = noise(arg_keys[5], (MODEL_WIDTH, MODEL_WIDTH), MODEL_WIDTH ** -0.5, 0.21875, ((0, 4),), jnp.float32)
    value_weight = noise(arg_keys[6], (MODEL_WIDTH, MODEL_WIDTH), MODEL_WIDTH ** -0.5, 0.21875, ((0, 4),), jnp.float32)
    output_weight = noise(arg_keys[7], (MODEL_WIDTH, MODEL_WIDTH), (MODEL_WIDTH // 32) ** -0.5, 1.25, ((0, 4),), jnp.float32)
    inner_weight = noise(arg_keys[8], (MODEL_WIDTH, FF), MODEL_WIDTH ** -0.5, 0.21875, ((0, 4),), jnp.float32)
    outer_weight = noise(arg_keys[9], (FF, MODEL_WIDTH), FF ** -0.5, 0.109375, ((0, 4),), jnp.float32)
    value_bias = noise(arg_keys[10], (MODEL_WIDTH,), 0.3, 2.0, ((0, 4),), jnp.float32)
    output_bias = noise(arg_keys[11], (MODEL_WIDTH,), 0.3, 2.0, ((0, 4),), jnp.float32)
    inner_bias = noise(arg_keys[12], (FF,), 0.3, 2.0, ((0, 4),), jnp.float32)
    outer_bias = noise(arg_keys[13], (MODEL_WIDTH,), 0.3, 2.0, ((0, 4),), jnp.float32)
    attention_norm_gain = jnp.clip(1.0 + 0.15 * jax.random.normal(arg_keys[14], (MODEL_WIDTH,), jnp.float32), 0.25, 1.75)
    first_shift = noise(arg_keys[15], (MODEL_WIDTH,), 0.3, 2.0, ((0, 4),), jnp.float32)
    second_gain = jnp.clip(1.0 + 0.15 * jax.random.normal(arg_keys[16], (MODEL_WIDTH,), jnp.float32), 0.25, 1.75)
    second_shift = noise(arg_keys[17], (MODEL_WIDTH,), 0.3, 2.0, ((0, 4),), jnp.float32)
    content_bias = noise(arg_keys[18], (HEAD_COUNT, HEAD_SIZE), 0.5, 3.0, ((0, 4),), jnp.float32)
    position_bias = noise(arg_keys[19], (HEAD_COUNT, HEAD_SIZE), 0.5, 3.0, ((0, 4),), jnp.float32)
    type_bias = noise(arg_keys[20], (HEAD_COUNT, HEAD_SIZE), 0.5, 3.0, ((0, 4),), jnp.float32)
    relative_kernel = noise(arg_keys[21], (HEAD_COUNT, HEAD_SIZE, HEAD_SIZE), HEAD_SIZE ** -0.5, 0.75, ((0, 4),), jnp.float32)
    type_embed = noise(arg_keys[22], (HEAD_COUNT, 2, HEAD_SIZE), 1.0, 5.0, ((0, 4),), jnp.float32)
    return {"tokens": tokens, "segments": segments, "token_types": token_types, "cotangent": cotangent, "query_weight": query_weight, "key_weight": key_weight, "value_weight": value_weight, "output_weight": output_weight, "inner_weight": inner_weight, "outer_weight": outer_weight, "value_bias": value_bias, "output_bias": output_bias, "inner_bias": inner_bias, "outer_bias": outer_bias, "attention_norm_gain": attention_norm_gain, "first_shift": first_shift, "second_gain": second_gain, "second_shift": second_shift, "content_bias": content_bias, "position_bias": position_bias, "type_bias": type_bias, "relative_kernel": relative_kernel, "type_embed": type_embed}


highest = lax.Precision.HIGHEST
norm_eps = 1e-05
masked_score = -1e+30

@jax.custom_vjp
def low(v):
    return lax.optimization_barrier(v.astype(jnp.bfloat16)).astype(jnp.float32)

@jax.custom_vjp
def low_back(v):
    return v

def low_keep(v):
    return (low(v), None)

def low_pass(kept, grad):
    return (grad,)

def back_keep(v):
    return (v, None)

def back_low(kept, grad):
    return (low(grad),)
low.defvjp(low_keep, low_pass)
low_back.defvjp(back_keep, back_low)

def product(left_side, right_side):
    return jnp.dot(left_side, right_side, precision=highest)

def layer_norm(inputs, gains, shifts):
    row_mean = lax.optimization_barrier(jnp.mean(inputs, axis=-1, keepdims=True))
    centred = inputs - row_mean
    spread = lax.optimization_barrier(jnp.mean(centred * centred, axis=-1, keepdims=True))
    return centred * lax.rsqrt(spread + norm_eps) * gains + shifts

def frequencies():
    half_width = HEAD_SIZE // 2
    return jnp.exp(jnp.arange(half_width, dtype=jnp.float32) * (-math.log(10000.0) / half_width))

def forward_one(masters, tokens, segments, token_types):
    query_weight, key_weight, value_weight, output_weight, inner_weight, outer_weight, value_bias, output_bias, inner_bias, outer_bias, attention_norm_gain, first_shift, second_gain, second_shift, content_bias, position_bias, type_bias, relative_kernel, type_embed = [low(master) for master in masters]
    half_width = HEAD_SIZE // 2
    score_scale = HEAD_SIZE ** (-0.5)
    frequency = frequencies()
    first_rows = tokens[0::2]
    second = tokens[1::2]
    pair_same = segments[0::2] == segments[1::2]
    pooled = jnp.where(pair_same[:, None], (first_rows + second) * 0.5, first_rows)
    queries = low_back(product(low(pooled), query_weight)).reshape(PQ, HEAD_COUNT, HEAD_SIZE)
    key_rows = product(tokens, key_weight).reshape(LEN, HEAD_COUNT, HEAD_SIZE)
    value_rows = (product(tokens, value_weight) + value_bias).reshape(LEN, HEAD_COUNT, HEAD_SIZE)
    pair_rows = low_back(low(jnp.concatenate([key_rows, value_rows], axis=-1)))
    relative = jnp.einsum('phe,hef->phf', queries + position_bias, relative_kernel, precision=highest)
    query_angle = (2.0 * jnp.arange(PQ, dtype=jnp.float32))[:, None] * frequency[None, :]
    query_cos = jnp.cos(query_angle)[:, None, :]
    query_sin = jnp.sin(query_angle)[:, None, :]
    relative_cos = relative[..., :half_width]
    relative_sin = relative[..., half_width:]
    position = jnp.concatenate([relative_cos * query_cos + relative_sin * query_sin, relative_cos * query_sin - relative_sin * query_cos], axis=-1)
    query_join = low_back(low(jnp.concatenate([queries + content_bias, position], axis=-1)))
    type_terms = low_back(low(jnp.einsum('phe,hbe->phb', queries + type_bias, type_embed, precision=highest)))
    key_angle = jnp.arange(LEN, dtype=jnp.float32)[:, None] * frequency[None, :]
    key_phase = low(jnp.concatenate([jnp.cos(key_angle), jnp.sin(key_angle)], axis=-1))
    same_document = segments[0::2][:, None] == segments[None, :]
    same_type = token_types[0::2][:, None] == token_types[None, :]

    def one_head(packed):
        query_head, type_head, pair_head = packed
        key_join = jnp.concatenate([pair_head[:, :HEAD_SIZE], key_phase], axis=-1)
        raw_score = product(query_head, key_join.T) + jnp.where(same_type, type_head[:, 1:2], type_head[:, 0:1])
        scores = jnp.where(same_document, low_back(raw_score * score_scale), masked_score)
        row_max = lax.optimization_barrier(jnp.max(scores, axis=1, keepdims=True))
        exponent = jnp.exp(scores - row_max)
        weights = exponent / lax.optimization_barrier(jnp.sum(exponent, axis=1, keepdims=True))
        return product(low(weights), pair_head[:, HEAD_SIZE:])
    mixture = lax.map(jax.checkpoint(one_head), (jnp.swapaxes(query_join, 0, 1), jnp.swapaxes(type_terms, 0, 1), jnp.swapaxes(pair_rows, 0, 1)))
    mixture = low_back(low(jnp.swapaxes(mixture, 0, 1).reshape(PQ, MODEL_WIDTH)))
    attention = low_back(product(mixture, output_weight) + output_bias)
    hidden = layer_norm(pooled + attention, attention_norm_gain, first_shift)
    expanded = low_back(product(low(hidden), inner_weight) + inner_bias)
    active = low(jax.nn.gelu(expanded, approximate=True))
    branch = low_back(product(active, outer_weight) + outer_bias)
    return layer_norm(hidden + branch, second_gain, second_shift)

def reference(tokens, segments, token_types, cotangent, query_weight, key_weight, value_weight, output_weight, inner_weight, outer_weight, value_bias, output_bias, inner_bias, outer_bias, attention_norm_gain, first_shift, second_gain, second_shift, content_bias, position_bias, type_bias, relative_kernel, type_embed):
    masters = (query_weight, key_weight, value_weight, output_weight, inner_weight, outer_weight, value_bias, output_bias, inner_bias, outer_bias, attention_norm_gain, first_shift, second_gain, second_shift, content_bias, position_bias, type_bias, relative_kernel, type_embed)

    def one_sequence(totals, sample):
        sample_tokens, sample_segments, sample_types, sample_cotangent = sample

        def forward(params, inputs):
            return forward_one(params, inputs, sample_segments, sample_types)
        result, pullback = jax.vjp(forward, masters, sample_tokens.astype(jnp.float32))
        grad_params, grad_inputs = pullback(sample_cotangent.astype(jnp.float32))
        totals = jax.tree.map(jnp.add, totals, grad_params)
        return (totals, (result.astype(jnp.bfloat16), grad_inputs.astype(jnp.bfloat16)))
    zero_grads = jax.tree.map(jnp.zeros_like, masters)
    totals, (output, grad_tokens) = lax.scan(one_sequence, zero_grads, (tokens, segments, token_types, cotangent))
    return (output, grad_tokens, totals[0], totals[1], totals[2], totals[3], totals[4], totals[5], totals[6], totals[7], totals[8], totals[9], totals[10], totals[11], totals[12], totals[13], totals[14], totals[15], totals[16], totals[17], totals[18])
```

```python
from functools import partial
import math

import jax
import jax.numpy as jnp
from jax import lax
from jax.experimental import pallas as pl
from jax.experimental.pallas import tpu as pltpu
from jax.sharding import PartitionSpec as P

MODEL_WIDTH = 768
HEAD_COUNT = 12
HEAD_SIZE = 64
LEN = 2048
SG = 8
PQ = 1024


highest = lax.Precision.HIGHEST
norm_eps = 1e-05
masked_score = -1e30


def frequencies():
    half_width = HEAD_SIZE // 2
    return jnp.exp(jnp.arange(half_width, dtype=jnp.float32) * (-math.log(10000.0) / half_width))


def norm_forward(inputs, gains, shifts):
    row_mean = jnp.mean(inputs, axis=-1, keepdims=True)
    centred = inputs - row_mean
    inverse = lax.rsqrt(jnp.mean(centred * centred, axis=-1, keepdims=True) + norm_eps)
    normed = centred * inverse
    return (normed * gains + shifts, normed, inverse)


def norm_backward(upstream, normed, inverse, gains):
    scaled = upstream * gains
    along = jnp.mean(scaled * normed, axis=-1, keepdims=True)
    centre = jnp.mean(scaled, axis=-1, keepdims=True)
    return inverse * (scaled - centre - normed * along)


def doc_masks(segment_row, type_row):
    same_document = segment_row[0::2][:, None] == segment_row[None, :]
    same_type = type_row[0::2][:, None] == type_row[None, :]
    return (same_document, same_type)


def score_block(query_row, type_row_terms, pair_row, key_phase, same_document, same_type):
    key_join = jnp.concatenate([pair_row[:, :HEAD_SIZE], key_phase], axis=-1)
    raw_score = lax.dot_general(
        query_row, key_join, (((1,), (1,)), ((), ())), preferred_element_type=jnp.float32
    )
    type_float = type_row_terms.astype(jnp.float32)
    raw_score = raw_score + jnp.where(same_type, type_float[:, 1:2], type_float[:, 0:1])
    return (jnp.where(same_document, raw_score * HEAD_SIZE ** (-0.5), masked_score), key_join)


def body(
    tokens,
    segments,
    token_types,
    cotangent,
    query_weight,
    key_weight,
    value_weight,
    output_weight,
    inner_weight,
    outer_weight,
    value_bias,
    output_bias,
    inner_bias,
    outer_bias,
    attention_norm_gain,
    first_shift,
    second_gain,
    second_shift,
    content_bias,
    position_bias,
    type_bias,
    relative_kernel,
    type_embed,
):
    local_tokens = tokens.shape[1]
    local_pooled = local_tokens // 2
    group_size = lax.axis_size("seq")
    shard_rank = lax.axis_index("seq")
    item_count = SG * HEAD_COUNT // group_size
    half_width = HEAD_SIZE // 2
    score_scale = HEAD_SIZE ** (-0.5)
    frequency = frequencies()
    duplicate_params = (
        lax.all_gather(query_weight.astype(jnp.bfloat16), "dp", axis=0, tiled=True),
        lax.all_gather(key_weight.astype(jnp.bfloat16), "dp", axis=0, tiled=True),
        lax.all_gather(value_weight.astype(jnp.bfloat16), "dp", axis=0, tiled=True),
        lax.all_gather(output_weight.astype(jnp.bfloat16), "dp", axis=0, tiled=True),
        lax.all_gather(inner_weight.astype(jnp.bfloat16), "dp", axis=0, tiled=True),
        lax.all_gather(outer_weight.astype(jnp.bfloat16), "dp", axis=0, tiled=True),
        lax.all_gather(value_bias.astype(jnp.bfloat16), "dp", axis=0, tiled=True),
        lax.all_gather(output_bias.astype(jnp.bfloat16), "dp", axis=0, tiled=True),
        lax.all_gather(inner_bias.astype(jnp.bfloat16), "dp", axis=0, tiled=True),
        lax.all_gather(outer_bias.astype(jnp.bfloat16), "dp", axis=0, tiled=True),
        lax.all_gather(attention_norm_gain.astype(jnp.bfloat16), "dp", axis=0, tiled=True),
        lax.all_gather(first_shift.astype(jnp.bfloat16), "dp", axis=0, tiled=True),
        lax.all_gather(second_gain.astype(jnp.bfloat16), "dp", axis=0, tiled=True),
        lax.all_gather(second_shift.astype(jnp.bfloat16), "dp", axis=0, tiled=True),
        lax.all_gather(content_bias.astype(jnp.bfloat16), "dp", axis=0, tiled=True),
        lax.all_gather(position_bias.astype(jnp.bfloat16), "dp", axis=0, tiled=True),
        lax.all_gather(type_bias.astype(jnp.bfloat16), "dp", axis=0, tiled=True),
        lax.all_gather(relative_kernel.astype(jnp.bfloat16), "dp", axis=0, tiled=True),
        lax.all_gather(type_embed.astype(jnp.bfloat16), "dp", axis=0, tiled=True),
    )
    value_add = duplicate_params[6].astype(jnp.float32)
    output_add = duplicate_params[7].astype(jnp.float32)
    inner_add = duplicate_params[8].astype(jnp.float32)
    outer_add = duplicate_params[9].astype(jnp.float32)
    gain_one = duplicate_params[10].astype(jnp.float32)
    shift_one = duplicate_params[11].astype(jnp.float32)
    gain_two = duplicate_params[12].astype(jnp.float32)
    shift_two = duplicate_params[13].astype(jnp.float32)
    content_add = duplicate_params[14].astype(jnp.float32)[None, :, None, :]
    position_add = duplicate_params[15].astype(jnp.float32)[None, :, None, :]
    type_add = duplicate_params[16].astype(jnp.float32)[None, :, None, :]
    relative = duplicate_params[17].astype(jnp.float32)
    type_table = duplicate_params[18].astype(jnp.float32)
    whole_segments, whole_types = (
        lax.all_gather(segments, "seq", axis=1, tiled=True),
        lax.all_gather(token_types, "seq", axis=1, tiled=True),
    )
    first_rows = tokens[:, 0::2].astype(jnp.float32)
    second = tokens[:, 1::2].astype(jnp.float32)
    pair_same = (segments[:, 0::2] == segments[:, 1::2])[..., None]
    pooled = jnp.where(pair_same, (first_rows + second) * 0.5, first_rows)
    pooled_low = pooled.astype(jnp.bfloat16)
    queries = jnp.einsum(
        "spd,dhe->shpe",
        pooled_low,
        duplicate_params[0].reshape(MODEL_WIDTH, HEAD_COUNT, HEAD_SIZE),
        preferred_element_type=jnp.float32,
    )
    key_rows = jnp.einsum(
        "ukf,fra->urka",
        tokens,
        duplicate_params[1].reshape(MODEL_WIDTH, HEAD_COUNT, HEAD_SIZE),
        preferred_element_type=jnp.float32,
    )
    value_rows = (
        jnp.einsum(
            "ukf,fra->urka",
            tokens,
            duplicate_params[2].reshape(MODEL_WIDTH, HEAD_COUNT, HEAD_SIZE),
            preferred_element_type=jnp.float32,
        )
        + value_add.reshape(HEAD_COUNT, HEAD_SIZE)[None, :, None, :]
    )
    pair_rows = (
        jnp.concatenate([key_rows, value_rows], axis=-1)
        .astype(jnp.bfloat16)
        .reshape(SG * HEAD_COUNT, local_tokens, 2 * HEAD_SIZE)
    )
    shifted = queries + position_add
    relative_terms = jnp.einsum("shpe,hef->shpf", shifted, relative, precision=highest)
    pooled_place = 2.0 * (
        shard_rank * local_pooled + jnp.arange(local_pooled, dtype=jnp.int32)
    ).astype(jnp.float32)
    query_angle = pooled_place[:, None] * frequency[None, :]
    query_cos = jnp.cos(query_angle)
    query_sin = jnp.sin(query_angle)
    relative_cos = relative_terms[..., :half_width]
    relative_sin = relative_terms[..., half_width:]
    position = jnp.concatenate(
        [
            relative_cos * query_cos + relative_sin * query_sin,
            relative_cos * query_sin - relative_sin * query_cos,
        ],
        axis=-1,
    )
    query_join = (
        jnp.concatenate([queries + content_add, position], axis=-1)
        .astype(jnp.bfloat16)
        .reshape(SG * HEAD_COUNT, local_pooled, 2 * HEAD_SIZE)
    )
    typed = queries + type_add
    type_terms = (
        jnp.einsum("shpe,hbe->shpb", typed, type_table, precision=highest)
        .astype(jnp.bfloat16)
        .reshape(SG * HEAD_COUNT, local_pooled, 2)
    )
    query_heads, type_heads, pair_heads = (
        lax.all_to_all(query_join, "seq", split_axis=0, concat_axis=1, tiled=True),
        lax.all_to_all(type_terms, "seq", split_axis=0, concat_axis=1, tiled=True),
        lax.all_to_all(pair_rows, "seq", split_axis=0, concat_axis=1, tiled=True),
    )
    item_rows = (shard_rank * item_count + jnp.arange(item_count, dtype=jnp.int32)) // HEAD_COUNT
    item_segments = whole_segments[item_rows]
    item_types = whole_types[item_rows]
    key_angle = jnp.arange(LEN, dtype=jnp.float32)[:, None] * frequency[None, :]
    key_phase = jnp.concatenate([jnp.cos(key_angle), jnp.sin(key_angle)], axis=-1).astype(
        jnp.bfloat16
    )

    def attend(packed):
        query_row, type_row_terms, pair_row, segment_row, type_row = packed
        same_document, same_type = doc_masks(segment_row, type_row)
        scores, key_join = score_block(
            query_row, type_row_terms, pair_row, key_phase, same_document, same_type
        )
        row_max = jnp.max(scores, axis=1, keepdims=True)
        exponent = jnp.exp(scores - row_max)
        row_total = jnp.sum(exponent, axis=1, keepdims=True)
        weights = exponent / row_total
        mixture = jnp.dot(
            weights.astype(jnp.bfloat16),
            pair_row[:, HEAD_SIZE:],
            preferred_element_type=jnp.float32,
        )
        return (mixture.astype(jnp.bfloat16), row_max + jnp.log(row_total))

    mixed_heads, log_totals = lax.map(
        attend, (query_heads, type_heads, pair_heads, item_segments, item_types)
    )
    mixed_tokens = lax.all_to_all(
        mixed_heads.reshape(item_count, PQ // 2, 2 * HEAD_SIZE),
        "seq",
        split_axis=1,
        concat_axis=0,
        tiled=True,
    ).reshape(SG, HEAD_COUNT, local_pooled, HEAD_SIZE)
    attention = (
        jnp.einsum(
            "shpe,hed->spd",
            mixed_tokens,
            duplicate_params[3].reshape(HEAD_COUNT, HEAD_SIZE, MODEL_WIDTH),
            preferred_element_type=jnp.float32,
        )
        + output_add
    )
    hidden, normed_one, inverse_one = norm_forward(pooled + attention, gain_one, shift_one)
    hidden_low = hidden.astype(jnp.bfloat16)
    expanded = (
        jnp.einsum(
            "spd,df->spf", hidden_low, duplicate_params[4], preferred_element_type=jnp.float32
        )
        + inner_add
    )
    active = jax.nn.gelu(expanded, approximate=True).astype(jnp.bfloat16)
    branch = (
        jnp.einsum("spf,fd->spd", active, duplicate_params[5], preferred_element_type=jnp.float32)
        + outer_add
    )
    result, normed_two, inverse_two = norm_forward(hidden + branch, gain_two, shift_two)
    output = result.astype(jnp.bfloat16)
    again = (
        lax.all_gather(query_weight.astype(jnp.bfloat16), "dp", axis=0, tiled=True),
        lax.all_gather(key_weight.astype(jnp.bfloat16), "dp", axis=0, tiled=True),
        lax.all_gather(value_weight.astype(jnp.bfloat16), "dp", axis=0, tiled=True),
        lax.all_gather(output_weight.astype(jnp.bfloat16), "dp", axis=0, tiled=True),
        lax.all_gather(inner_weight.astype(jnp.bfloat16), "dp", axis=0, tiled=True),
        lax.all_gather(outer_weight.astype(jnp.bfloat16), "dp", axis=0, tiled=True),
        lax.all_gather(attention_norm_gain.astype(jnp.bfloat16), "dp", axis=0, tiled=True),
        lax.all_gather(second_gain.astype(jnp.bfloat16), "dp", axis=0, tiled=True),
        lax.all_gather(relative_kernel.astype(jnp.bfloat16), "dp", axis=0, tiled=True),
        lax.all_gather(type_embed.astype(jnp.bfloat16), "dp", axis=0, tiled=True),
    )
    query_back = again[0]
    key_back = again[1]
    value_back = again[2]
    output_back = again[3]
    inner_back = again[4]
    outer_back = again[5]
    gain_one_back = again[6].astype(jnp.float32)
    gain_two_back = again[7].astype(jnp.float32)
    relative_back = again[8].astype(jnp.float32)
    table_back = again[9].astype(jnp.float32)
    grad_result = cotangent.astype(jnp.float32)
    grad_gain_two = jnp.sum(grad_result * normed_two, axis=(0, 1))
    grad_shift_two = jnp.sum(grad_result, axis=(0, 1))
    grad_second = norm_backward(grad_result, normed_two, inverse_two, gain_two_back)
    grad_branch = grad_second.astype(jnp.bfloat16)
    grad_outer_weight = jnp.einsum(
        "spf,spd->fd", active, grad_branch, preferred_element_type=jnp.float32
    )
    grad_outer_bias = jnp.sum(grad_branch.astype(jnp.float32), axis=(0, 1))
    grad_active = jnp.einsum(
        "spd,fd->spf", grad_branch, outer_back, preferred_element_type=jnp.float32
    )
    gelu_value, gelu_pull = jax.vjp(partial(jax.nn.gelu, approximate=True), expanded)
    grad_expanded = gelu_pull(grad_active)[0].astype(jnp.bfloat16)
    grad_inner_weight = jnp.einsum(
        "spd,spf->df", hidden_low, grad_expanded, preferred_element_type=jnp.float32
    )
    grad_inner_bias = jnp.sum(grad_expanded.astype(jnp.float32), axis=(0, 1))
    grad_hidden = grad_second + jnp.einsum(
        "spf,df->spd", grad_expanded, inner_back, preferred_element_type=jnp.float32
    )
    grad_gain_one = jnp.sum(grad_hidden * normed_one, axis=(0, 1))
    grad_shift_one = jnp.sum(grad_hidden, axis=(0, 1))
    grad_first = norm_backward(grad_hidden, normed_one, inverse_one, gain_one_back)
    grad_attention = grad_first.astype(jnp.bfloat16)
    grad_output_weight = jnp.einsum(
        "shpe,spd->hed", mixed_tokens, grad_attention, preferred_element_type=jnp.float32
    ).reshape(MODEL_WIDTH, MODEL_WIDTH)
    grad_output_bias = jnp.sum(grad_attention.astype(jnp.float32), axis=(0, 1))
    grad_mixture = jnp.einsum(
        "spd,hed->shpe",
        grad_attention,
        output_back.reshape(HEAD_COUNT, HEAD_SIZE, MODEL_WIDTH),
        preferred_element_type=jnp.float32,
    ).astype(jnp.bfloat16)
    grad_mixed_heads = lax.all_to_all(
        grad_mixture.reshape(SG * HEAD_COUNT, local_pooled // 2, 2 * HEAD_SIZE),
        "seq",
        split_axis=0,
        concat_axis=1,
        tiled=True,
    ).reshape(item_count, PQ, HEAD_SIZE)

    def attend_back(packed):
        query_row, type_row_terms, pair_row, segment_row, type_row, log_row, grad_row = packed
        same_document, same_type = doc_masks(segment_row, type_row)
        scores, key_join = score_block(
            query_row, type_row_terms, pair_row, key_phase, same_document, same_type
        )
        weights = jnp.exp(scores - log_row)
        grad_weights = lax.dot_general(
            grad_row,
            pair_row[:, HEAD_SIZE:],
            (((1,), (1,)), ((), ())),
            preferred_element_type=jnp.float32,
        )
        row_dot = jnp.sum(grad_weights * weights, axis=1, keepdims=True)
        grad_scores = (weights * (grad_weights - row_dot)).astype(jnp.bfloat16)
        grad_query = (
            jnp.dot(grad_scores, key_join, preferred_element_type=jnp.float32) * score_scale
        ).astype(jnp.bfloat16)
        grad_float = grad_scores.astype(jnp.float32) * score_scale
        grad_same = jnp.sum(jnp.where(same_type, grad_float, 0.0), axis=1)
        grad_other = jnp.sum(jnp.where(same_type, 0.0, grad_float), axis=1)
        grad_kinds = jnp.stack([grad_other, grad_same], axis=-1).astype(jnp.bfloat16)
        grad_keys = (
            lax.dot_general(
                grad_scores,
                query_row[:, :HEAD_SIZE],
                (((0,), (0,)), ((), ())),
                preferred_element_type=jnp.float32,
            )
            * score_scale
        )
        grad_values = lax.dot_general(
            weights.astype(jnp.bfloat16),
            grad_row,
            (((0,), (0,)), ((), ())),
            preferred_element_type=jnp.float32,
        )
        return (
            grad_query,
            grad_kinds,
            jnp.concatenate([grad_keys, grad_values], axis=-1).astype(jnp.bfloat16),
        )

    grad_query_heads, grad_type_heads, grad_pair_heads = lax.map(
        attend_back,
        (
            query_heads,
            type_heads,
            pair_heads,
            item_segments,
            item_types,
            log_totals,
            grad_mixed_heads,
        ),
    )
    grad_query_tok, grad_type_tok, grad_pair_tok = (
        lax.all_to_all(grad_query_heads, "seq", split_axis=1, concat_axis=0, tiled=True),
        lax.all_to_all(grad_type_heads, "seq", split_axis=1, concat_axis=0, tiled=True),
        lax.all_to_all(grad_pair_heads, "seq", split_axis=1, concat_axis=0, tiled=True),
    )
    grad_query_join = grad_query_tok.astype(jnp.float32).reshape(
        SG, HEAD_COUNT, local_pooled, 2 * HEAD_SIZE
    )
    grad_content = grad_query_join[..., :HEAD_SIZE]
    grad_first_half = grad_query_join[..., HEAD_SIZE : HEAD_SIZE + half_width]
    grad_second_half = grad_query_join[..., HEAD_SIZE + half_width :]
    grad_relative_terms = jnp.concatenate(
        [
            grad_first_half * query_cos + grad_second_half * query_sin,
            grad_first_half * query_sin - grad_second_half * query_cos,
        ],
        axis=-1,
    )
    grad_shifted = jnp.einsum(
        "shpf,hef->shpe", grad_relative_terms, relative_back, precision=highest
    )
    grad_relative_kernel = jnp.einsum(
        "shpe,shpf->hef", shifted, grad_relative_terms, precision=highest
    )
    grad_type_terms = grad_type_tok.astype(jnp.float32).reshape(SG, HEAD_COUNT, local_pooled, 2)
    grad_typed = jnp.einsum("shpb,hbe->shpe", grad_type_terms, table_back, precision=highest)
    grad_type_embed = jnp.einsum("shpe,shpb->hbe", typed, grad_type_terms, precision=highest)
    query_rows_gradient = (grad_content + grad_shifted + grad_typed).astype(jnp.bfloat16)
    grad_content_bias = jnp.sum(grad_content, axis=(0, 2))
    grad_position_bias = jnp.sum(grad_shifted, axis=(0, 2))
    grad_type_bias = jnp.sum(grad_typed, axis=(0, 2))
    grad_query_weight = jnp.einsum(
        "spd,shpe->dhe", pooled_low, query_rows_gradient, preferred_element_type=jnp.float32
    ).reshape(MODEL_WIDTH, MODEL_WIDTH)
    grad_pooled = grad_first + jnp.einsum(
        "shpe,dhe->spd",
        query_rows_gradient,
        query_back.reshape(MODEL_WIDTH, HEAD_COUNT, HEAD_SIZE),
        preferred_element_type=jnp.float32,
    )
    grad_pairs = grad_pair_tok.reshape(SG, HEAD_COUNT, local_tokens, 2 * HEAD_SIZE)
    key_rows_gradient = grad_pairs[..., :HEAD_SIZE]
    value_rows_gradient = grad_pairs[..., HEAD_SIZE:]
    grad_key_weight = jnp.einsum(
        "ozb,opzx->bpx", tokens, key_rows_gradient, preferred_element_type=jnp.float32
    ).reshape(MODEL_WIDTH, MODEL_WIDTH)
    grad_value_weight = jnp.einsum(
        "ozb,opzx->bpx", tokens, value_rows_gradient, preferred_element_type=jnp.float32
    ).reshape(MODEL_WIDTH, MODEL_WIDTH)
    grad_value_bias = jnp.sum(value_rows_gradient.astype(jnp.float32), axis=(0, 2)).reshape(
        MODEL_WIDTH
    )
    grad_direct = jnp.einsum(
        "mivt,git->mvg",
        key_rows_gradient,
        key_back.reshape(MODEL_WIDTH, HEAD_COUNT, HEAD_SIZE),
        preferred_element_type=jnp.float32,
    )
    grad_direct = grad_direct + jnp.einsum(
        "mivt,git->mvg",
        value_rows_gradient,
        value_back.reshape(MODEL_WIDTH, HEAD_COUNT, HEAD_SIZE),
        preferred_element_type=jnp.float32,
    )
    pool_first = jnp.where(pair_same, 0.5 * grad_pooled, grad_pooled)
    pool_second = jnp.where(pair_same, 0.5 * grad_pooled, 0.0)
    grad_tokens = (
        grad_direct
        + jnp.stack([pool_first, pool_second], axis=2).reshape(SG, local_tokens, MODEL_WIDTH)
    ).astype(jnp.bfloat16)
    summed = lax.psum(
        (
            grad_query_weight,
            grad_key_weight,
            grad_value_weight,
            grad_output_weight,
            grad_inner_weight,
            grad_outer_weight,
            grad_value_bias,
            grad_output_bias,
            grad_inner_bias,
            grad_outer_bias,
            grad_gain_one,
            grad_shift_one,
            grad_gain_two,
            grad_shift_two,
            grad_content_bias,
            grad_position_bias,
            grad_type_bias,
            grad_relative_kernel,
            grad_type_embed,
        ),
        "seq",
    )
    owned = (
        lax.psum_scatter(
            summed[0].astype(jnp.bfloat16), "dp", scatter_dimension=0, tiled=True
        ).astype(jnp.float32),
        lax.psum_scatter(
            summed[1].astype(jnp.bfloat16), "dp", scatter_dimension=0, tiled=True
        ).astype(jnp.float32),
        lax.psum_scatter(
            summed[2].astype(jnp.bfloat16), "dp", scatter_dimension=0, tiled=True
        ).astype(jnp.float32),
        lax.psum_scatter(
            summed[3].astype(jnp.bfloat16), "dp", scatter_dimension=0, tiled=True
        ).astype(jnp.float32),
        lax.psum_scatter(
            summed[4].astype(jnp.bfloat16), "dp", scatter_dimension=0, tiled=True
        ).astype(jnp.float32),
        lax.psum_scatter(
            summed[5].astype(jnp.bfloat16), "dp", scatter_dimension=0, tiled=True
        ).astype(jnp.float32),
        lax.psum_scatter(
            summed[6].astype(jnp.bfloat16), "dp", scatter_dimension=0, tiled=True
        ).astype(jnp.float32),
        lax.psum_scatter(
            summed[7].astype(jnp.bfloat16), "dp", scatter_dimension=0, tiled=True
        ).astype(jnp.float32),
        lax.psum_scatter(
            summed[8].astype(jnp.bfloat16), "dp", scatter_dimension=0, tiled=True
        ).astype(jnp.float32),
        lax.psum_scatter(
            summed[9].astype(jnp.bfloat16), "dp", scatter_dimension=0, tiled=True
        ).astype(jnp.float32),
        lax.psum_scatter(
            summed[10].astype(jnp.bfloat16), "dp", scatter_dimension=0, tiled=True
        ).astype(jnp.float32),
        lax.psum_scatter(
            summed[11].astype(jnp.bfloat16), "dp", scatter_dimension=0, tiled=True
        ).astype(jnp.float32),
        lax.psum_scatter(
            summed[12].astype(jnp.bfloat16), "dp", scatter_dimension=0, tiled=True
        ).astype(jnp.float32),
        lax.psum_scatter(
            summed[13].astype(jnp.bfloat16), "dp", scatter_dimension=0, tiled=True
        ).astype(jnp.float32),
        lax.psum_scatter(
            summed[14].astype(jnp.bfloat16), "dp", scatter_dimension=0, tiled=True
        ).astype(jnp.float32),
        lax.psum_scatter(
            summed[15].astype(jnp.bfloat16), "dp", scatter_dimension=0, tiled=True
        ).astype(jnp.float32),
        lax.psum_scatter(
            summed[16].astype(jnp.bfloat16), "dp", scatter_dimension=0, tiled=True
        ).astype(jnp.float32),
        lax.psum_scatter(
            summed[17].astype(jnp.bfloat16), "dp", scatter_dimension=0, tiled=True
        ).astype(jnp.float32),
        lax.psum_scatter(
            summed[18].astype(jnp.bfloat16), "dp", scatter_dimension=0, tiled=True
        ).astype(jnp.float32),
    )
    return (
        output,
        grad_tokens,
        owned[0],
        owned[1],
        owned[2],
        owned[3],
        owned[4],
        owned[5],
        owned[6],
        owned[7],
        owned[8],
        owned[9],
        owned[10],
        owned[11],
        owned[12],
        owned[13],
        owned[14],
        owned[15],
        owned[16],
        owned[17],
        owned[18],
    )


BF16 = jnp.bfloat16
F32 = jnp.float32
PAIRS = HEAD_COUNT // 2
LANES = 2 * HEAD_SIZE
ROWS = 256
FAR = -(2.0**100)
FF = 3072
NN = (((1,), (0,)), ((), ()))
NT = (((1,), (1,)), ((), ()))
TN = (((0,), (0,)), ((), ()))


def mm(left, right, dims=NN):
    return lax.dot_general(left, right, dims, preferred_element_type=F32)


def split(value):
    high = value.astype(BF16)
    return high, (value - high.astype(F32)).astype(BF16)


def lane_ids(rows):
    return lax.broadcasted_iota(jnp.int32, (rows, LANES), 1)


def attend_kernel(
    query_ref,
    key_ref,
    value_ref,
    map_ref,
    map_add_ref,
    content_ref,
    query_side_ref,
    key_side_ref,
    phase_ref,
    cos_ref,
    sin_ref,
    mixture_ref,
    join_ref,
    key_join,
    value_join,
):
    query = query_ref[...]
    high, low = split(query)
    terms = mm(jnp.concatenate([high, low], axis=1), map_ref[0]) + map_add_ref[0]
    lane = lane_ids(PQ)
    left = lane < HEAD_SIZE
    content = query + content_ref[...]
    position = terms[:, :LANES] * cos_ref[...] + terms[:, LANES : 2 * LANES] * sin_ref[...]
    side = query_side_ref[...]
    typed = (lane >= 3) & (lane < 6)
    scale = HEAD_SIZE ** (-0.5)
    for h in range(2):
        first, second = (content, position) if h == 0 else (position, content)
        join_ref[h, :, :LANES] = (jnp.where(left, first, second) * scale).astype(BF16)
        base = 2 * LANES * (h + 1)
        same = terms[:, base : base + LANES]
        other = terms[:, base + LANES : base + 2 * LANES]
        kind = jnp.where(side > 0.5, same, other) * scale
        join_ref[h, :, LANES:] = jnp.where(typed, kind, side).astype(BF16)
    key_left = lane_ids(LEN) < HEAD_SIZE
    key_join[:, LANES:] = key_side_ref[...]
    value_join[:, :LANES] = value_ref[...]
    value_join[:, LANES:] = key_side_ref[...]
    tile_lane = lane_ids(ROWS)
    for h in range(2):
        pieces = (key_ref[...], phase_ref[...]) if h == 0 else (phase_ref[...], key_ref[...])
        key_join[:, :LANES] = jnp.where(key_left, *pieces)
        for i in range(PQ // ROWS):
            rows = slice(i * ROWS, (i + 1) * ROWS)
            scores = mm(join_ref[h, rows, :], key_join[...], NT)
            top = jnp.max(scores, axis=1, keepdims=True)
            weights = jnp.exp(scores - top).astype(BF16)
            mixed = mm(weights, value_join[...])
            total = mixed[:, LANES + 6 : LANES + 7]
            result = (mixed[:, :LANES] / total).astype(BF16)
            if h == 0:
                mixture_ref[rows, :] = result
            else:
                mixture_ref[rows, :] = jnp.where(
                    tile_lane < HEAD_SIZE, mixture_ref[rows, :], result
                )
            shift = -(top + jnp.log(total))
            one = shift.astype(BF16).astype(F32)
            two = (shift - one).astype(BF16).astype(F32)
            three = shift - one - two
            extra = jnp.where(tile_lane == 6, one, jnp.where(tile_lane == 7, two, three))
            kept = join_ref[h, rows, LANES:].astype(F32)
            inside = (tile_lane >= 6) & (tile_lane < 9)
            join_ref[h, rows, LANES:] = jnp.where(inside, extra, kept).astype(BF16)


def attend_forward(query, pairs, maps, map_add, content, query_side, key_side, phase, cosm, sinm):
    whole = lambda shape: pl.BlockSpec(shape, lambda i: (0, 0))
    return pl.pallas_call(
        attend_kernel,
        grid=(PAIRS,),
        in_specs=[
            pl.BlockSpec((PQ, LANES), lambda i: (0, i)),
            pl.BlockSpec((LEN, LANES), lambda i: (0, i)),
            pl.BlockSpec((LEN, LANES), lambda i: (0, i + PAIRS)),
            pl.BlockSpec((1, 2 * LANES, 6 * LANES), lambda i: (i, 0, 0)),
            pl.BlockSpec((1, 1, 6 * LANES), lambda i: (i, 0, 0)),
            pl.BlockSpec((1, LANES), lambda i: (0, i)),
            whole((PQ, LANES)),
            whole((LEN, LANES)),
            whole((LEN, LANES)),
            whole((PQ, LANES)),
            whole((PQ, LANES)),
        ],
        out_specs=[
            pl.BlockSpec((PQ, LANES), lambda i: (0, i)),
            pl.BlockSpec((2, PQ, 2 * LANES), lambda i: (i, 0, 0)),
        ],
        out_shape=[
            jax.ShapeDtypeStruct((PQ, MODEL_WIDTH), BF16),
            jax.ShapeDtypeStruct((HEAD_COUNT, PQ, 2 * LANES), BF16),
        ],
        scratch_shapes=[
            pltpu.VMEM((LEN, 2 * LANES), BF16),
            pltpu.VMEM((LEN, 2 * LANES), BF16),
        ],
        cost_estimate=pl.CostEstimate(
            flops=4 * HEAD_COUNT * PQ * LEN * 256,
            bytes_accessed=20_000_000,
            transcendentals=HEAD_COUNT * PQ * LEN,
        ),
        compiler_params=pltpu.CompilerParams(vmem_limit_bytes=56 * 2**20),
        name="attend_forward",
    )(query, pairs, pairs, maps, map_add, content, query_side, key_side, phase, cosm, sinm)


def attend_back_kernel(
    join_ref,
    key_ref,
    value_ref,
    query_ref,
    mixture_ref,
    grad_ref,
    map_back_ref,
    rows_ref,
    query_side_ref,
    key_side_ref,
    phase_ref,
    cos_ref,
    sin_ref,
    grad_query_ref,
    grad_key_ref,
    grad_value_ref,
    sums_ref,
    grad_map_ref,
    key_join,
    value_join,
    key_total,
    value_total,
    join_grads,
):
    scale = HEAD_SIZE ** (-0.5)
    key_left = lane_ids(LEN) < HEAD_SIZE
    tile_lane = lane_ids(ROWS)
    key_join[:, LANES:] = key_side_ref[...]
    value_join[:, :LANES] = value_ref[...]
    value_join[:, LANES:] = key_side_ref[...]
    for h in range(2):
        pieces = (key_ref[...], phase_ref[...]) if h == 0 else (phase_ref[...], key_ref[...])
        key_join[:, :LANES] = jnp.where(key_left, *pieces)
        mine = (tile_lane < HEAD_SIZE) if h == 0 else (tile_lane >= HEAD_SIZE)
        part = slice(h * HEAD_SIZE, (h + 1) * HEAD_SIZE)
        for i in range(PQ // ROWS):
            rows = slice(i * ROWS, (i + 1) * ROWS)
            join = join_ref[h, rows, :]
            grad = jnp.where(mine, grad_ref[rows, :].astype(F32), 0.0)
            dot = -jnp.sum(grad * mixture_ref[rows, :].astype(F32), axis=1, keepdims=True)
            one = dot.astype(BF16).astype(F32)
            two = (dot - one).astype(BF16).astype(F32)
            three = dot - one - two
            extra = jnp.where(tile_lane == 6, one, jnp.where(tile_lane == 7, two, three))
            inside = (tile_lane >= 6) & (tile_lane < 9)
            extra = jnp.where(inside, extra, 0.0)
            grad_low = grad.astype(BF16)
            weights = jnp.exp(mm(join, key_join[...], NT))
            slope = mm(
                jnp.concatenate([grad_low, extra.astype(BF16)], axis=1), value_join[...], NT
            )
            low_slope = (weights * slope).astype(BF16)
            low_weights = weights.astype(BF16)
            join_grads[h, rows, :] = mm(low_slope, key_join[...])
            to_key = mm(join_ref[h, rows, part], low_slope, TN)
            to_value = mm(grad_ref[rows, part], low_weights, TN)
            if i == 0:
                key_total[part, :] = to_key
                value_total[part, :] = to_value
            else:
                key_total[part, :] += to_key
                value_total[part, :] += to_value
    grad_key_ref[...] = key_total[...].T.astype(BF16)
    grad_value_ref[...] = value_total[...].T.astype(BF16)
    lane = lane_ids(PQ)
    left = lane < HEAD_SIZE
    typed = (lane >= 3) & (lane < 6)
    rounded = [(join_grads[h, :, :LANES] * scale).astype(BF16).astype(F32) for h in range(2)]
    content = jnp.where(left, rounded[0], rounded[1])
    position = jnp.where(left, rounded[1], rounded[0])
    turned = jnp.concatenate([position * cos_ref[...], position * sin_ref[...]], axis=1)
    turned_high, turned_low = split(turned)
    shifted_grad = mm(turned_high, map_back_ref[0]) + mm(turned_low, map_back_ref[0])
    side = query_side_ref[...]
    sames, others = [], []
    for h in range(2):
        kinds = jnp.where(typed, join_grads[h, :, LANES:], 0.0)
        same = jnp.sum(jnp.where(side > 0.5, kinds, 0.0), axis=1, keepdims=True)
        other = jnp.sum(jnp.where(side > 0.5, 0.0, kinds), axis=1, keepdims=True)
        sames.append((same * scale).astype(BF16).astype(F32))
        others.append((other * scale).astype(BF16).astype(F32))
    same = jnp.where(left, sames[0], sames[1])
    other = jnp.where(left, others[0], others[1])
    position_add = rows_ref[0, 0:1, :]
    type_add = rows_ref[0, 1:2, :]
    type_other = rows_ref[0, 2:3, :]
    type_same = rows_ref[0, 3:4, :]
    typed_grad = same * type_same + other * type_other
    grad_query_ref[...] = (content + shifted_grad + typed_grad).astype(BF16)
    query = query_ref[...]
    shifted_high, shifted_low = split(query + position_add)
    grad_map_ref[0] = (
        mm(shifted_high, turned_high, TN)
        + mm(shifted_low, turned_high, TN)
        + mm(shifted_high, turned_low, TN)
    )
    kinds = query + type_add
    row = lambda v: jnp.sum(v, axis=0, keepdims=True)
    sums_ref[0, 0:1, :] = row(content)
    sums_ref[0, 1:2, :] = row(shifted_grad)
    sums_ref[0, 2:3, :] = row(typed_grad)
    sums_ref[0, 3:4, :] = row(kinds * other)
    sums_ref[0, 4:5, :] = row(kinds * same)
    sums_ref[0, 5:6, :] = row(grad_value_ref[...].astype(F32))


def attend_backward(
    join, pairs, query, mixture, grad, map_back, rows, query_side, key_side, phase, cosm, sinm
):
    whole = lambda shape: pl.BlockSpec(shape, lambda i: (0, 0))
    return pl.pallas_call(
        attend_back_kernel,
        grid=(PAIRS,),
        in_specs=[
            pl.BlockSpec((2, PQ, 2 * LANES), lambda i: (i, 0, 0)),
            pl.BlockSpec((LEN, LANES), lambda i: (0, i)),
            pl.BlockSpec((LEN, LANES), lambda i: (0, i + PAIRS)),
            pl.BlockSpec((PQ, LANES), lambda i: (0, i)),
            pl.BlockSpec((PQ, LANES), lambda i: (0, i)),
            pl.BlockSpec((PQ, LANES), lambda i: (0, i)),
            pl.BlockSpec((1, 2 * LANES, LANES), lambda i: (i, 0, 0)),
            pl.BlockSpec((1, 8, LANES), lambda i: (i, 0, 0)),
            whole((PQ, LANES)),
            whole((LEN, LANES)),
            whole((LEN, LANES)),
            whole((PQ, LANES)),
            whole((PQ, LANES)),
        ],
        out_specs=[
            pl.BlockSpec((PQ, LANES), lambda i: (0, i)),
            pl.BlockSpec((LEN, LANES), lambda i: (0, i)),
            pl.BlockSpec((LEN, LANES), lambda i: (0, i)),
            pl.BlockSpec((1, 8, LANES), lambda i: (i, 0, 0)),
            pl.BlockSpec((1, LANES, 2 * LANES), lambda i: (i, 0, 0)),
        ],
        out_shape=[
            jax.ShapeDtypeStruct((PQ, MODEL_WIDTH), BF16),
            jax.ShapeDtypeStruct((LEN, MODEL_WIDTH), BF16),
            jax.ShapeDtypeStruct((LEN, MODEL_WIDTH), BF16),
            jax.ShapeDtypeStruct((PAIRS, 8, LANES), F32),
            jax.ShapeDtypeStruct((PAIRS, LANES, 2 * LANES), F32),
        ],
        scratch_shapes=[
            pltpu.VMEM((LEN, 2 * LANES), BF16),
            pltpu.VMEM((LEN, 2 * LANES), BF16),
            pltpu.VMEM((LANES, LEN), F32),
            pltpu.VMEM((LANES, LEN), F32),
            pltpu.VMEM((2, PQ, 2 * LANES), F32),
        ],
        cost_estimate=pl.CostEstimate(
            flops=10 * HEAD_COUNT * PQ * LEN * 256,
            bytes_accessed=32_000_000,
            transcendentals=HEAD_COUNT * PQ * LEN,
        ),
        compiler_params=pltpu.CompilerParams(vmem_limit_bytes=58 * 2**20),
        name="attend_backward",
    )(
        join,
        pairs,
        pairs,
        query,
        mixture,
        grad,
        map_back,
        rows,
        query_side,
        key_side,
        phase,
        cosm,
        sinm,
    )


def swap_halves(value, axis):
    first, second = jnp.split(value, 2, axis=axis)
    return jnp.concatenate([second, first], axis=axis)


def pair_maps(relative, table):
    relative = relative.reshape(PAIRS, 2, HEAD_SIZE, HEAD_SIZE)
    nothing = jnp.zeros((PAIRS, HEAD_SIZE, HEAD_SIZE), F32)
    turned = swap_halves(relative, 3)

    def crossed(value):
        top = jnp.concatenate([nothing, value[:, 0]], axis=2)
        bottom = jnp.concatenate([value[:, 1], nothing], axis=2)
        return jnp.concatenate([top, bottom], axis=1)

    plain, swapped = crossed(relative), crossed(turned)
    table = table.reshape(PAIRS, 2, 2, HEAD_SIZE)
    columns = jnp.arange(LANES)
    wanted = ((columns >= 3) & (columns < 6)).astype(F32)
    kinds = []
    for h in range(2):
        for b in (1, 0):
            vector = table[:, h, b]
            zero = jnp.zeros_like(vector)
            full = jnp.concatenate([vector, zero] if h == 0 else [zero, vector], axis=1)
            kinds.append(full[:, :, None] * wanted[None, None, :])
    return plain, swapped, kinds


def sequence_body(
    tokens,
    segments,
    token_types,
    cotangent,
    query_weight,
    key_weight,
    value_weight,
    output_weight,
    inner_weight,
    outer_weight,
    value_bias,
    output_bias,
    inner_bias,
    outer_bias,
    attention_norm_gain,
    first_shift,
    second_gain,
    second_shift,
    content_bias,
    position_bias,
    type_bias,
    relative_kernel,
    type_embed,
):
    owners = lax.axis_size("dp")
    part = MODEL_WIDTH // owners
    low = lambda value: value.astype(BF16)
    even_segments, odd_segments = segments[:, 0::2], segments[:, 1::2]
    labels = jnp.stack(
        [
            segments[:, :128],
            segments[:, 128:],
            token_types[:, :128],
            token_types[:, 128:],
            even_segments,
            token_types[:, 0::2],
            (even_segments == odd_segments).astype(jnp.int32),
        ],
        axis=1,
    )
    labels = lax.all_to_all(labels, "seq", split_axis=0, concat_axis=0, tiled=True)
    rows = lax.all_to_all(tokens, "seq", split_axis=0, concat_axis=0, tiled=True)
    small = jnp.concatenate(
        [
            low(value).reshape(-1)
            for value in (
                value_bias,
                output_bias,
                outer_bias,
                attention_norm_gain,
                first_shift,
                second_gain,
                second_shift,
                content_bias,
                position_bias,
                type_bias,
                inner_bias,
                relative_kernel,
                type_embed,
            )
        ]
    )
    small = lax.all_gather(small.reshape(1, -1), "dp", axis=0, tiled=True)
    first = jnp.concatenate([low(query_weight), low(key_weight), low(value_weight)], axis=1)
    first = lax.all_gather(first, "dp", axis=0, tiled=True)
    next_weights = jnp.concatenate([low(output_weight), low(inner_weight)], axis=1)
    next_weights = lax.all_gather(next_weights, "dp", axis=0, tiled=True)
    outer_low = lax.all_gather(low(outer_weight), "dp", axis=0, tiled=True)

    def take(start, size):
        return small[:, start : start + size].astype(F32)

    vectors = [take(part * j, part).reshape(1, MODEL_WIDTH) for j in range(10)]
    (
        value_add,
        output_add,
        outer_add,
        gain_one,
        shift_one,
        gain_two,
        shift_two,
        content_add,
        position_add,
        type_add,
    ) = vectors
    place = 10 * part
    inner_add = take(place, FF // owners).reshape(1, FF)
    place += FF // owners
    kernel_size = HEAD_COUNT * HEAD_SIZE * HEAD_SIZE // owners
    relative = take(place, kernel_size).reshape(HEAD_COUNT, HEAD_SIZE, HEAD_SIZE)
    place += kernel_size
    table = take(place, HEAD_COUNT * 2 * HEAD_SIZE // owners).reshape(HEAD_COUNT, 2, HEAD_SIZE)

    segment_row = labels[:, 0:2].reshape(LEN)
    type_row = labels[:, 2:4].reshape(LEN)
    query_segments = labels[:, 4].reshape(PQ)
    query_types = labels[:, 5].reshape(PQ)
    pair_same = labels[:, 6] > 0

    first_doc, last_doc = segment_row[0], segment_row[LEN - 1]
    first_type = type_row[0]
    last_type = jnp.max(jnp.where(type_row == first_type, -1, type_row))

    def classes(values, start, end):
        return jnp.where(values == start, 0, jnp.where(values == end, 2, 1))[:, None]

    columns = jnp.arange(LANES, dtype=jnp.int32)[None, :]
    key_side = (
        (columns == classes(segment_row, first_doc, last_doc))
        | (columns == 3 + classes(type_row, first_type, last_type))
        | ((columns >= 6) & (columns < 9))
    ).astype(BF16)
    query_docs = classes(query_segments, first_doc, last_doc)
    query_side = jnp.where(
        columns < 3,
        jnp.where(columns == query_docs, 0.0, FAR),
        (columns == 3 + classes(query_types, first_type, last_type)).astype(F32),
    )
    frequency = frequencies()
    key_angle = jnp.arange(LEN, dtype=F32)[:, None] * frequency[None, :]
    phase = jnp.concatenate([jnp.cos(key_angle), jnp.sin(key_angle)], axis=1).astype(BF16)
    phase = jnp.concatenate([phase, phase], axis=1)
    query_angle = (2.0 * jnp.arange(PQ, dtype=F32))[:, None] * frequency[None, :]
    cos, sin = jnp.cos(query_angle), jnp.sin(query_angle)
    cosm = jnp.concatenate([cos, -cos, cos, -cos], axis=1)
    sinm = jnp.concatenate([sin, sin, sin, sin], axis=1)

    plain, swapped, kinds = pair_maps(relative, table)
    stacked = jnp.concatenate([plain, swapped, *kinds], axis=2)
    maps = low(jnp.concatenate([stacked, stacked], axis=1))
    pair_vector = lambda vector: vector.reshape(PAIRS, 1, LANES)
    position_pairs, type_pairs = pair_vector(position_add), pair_vector(type_add)
    product = partial(jnp.einsum, "pke,pef->pkf", precision=highest)
    map_add = jnp.concatenate(
        [
            product(position_pairs, stacked[:, :, : 2 * LANES]),
            product(type_pairs, stacked[:, :, 2 * LANES :]),
        ],
        axis=2,
    )
    map_back = low(
        jnp.concatenate([plain.transpose(0, 2, 1), swapped.transpose(0, 2, 1)], axis=1)
    )
    table_pairs = table.reshape(PAIRS, 2, 2, HEAD_SIZE).transpose(0, 2, 1, 3)
    table_pairs = table_pairs.reshape(PAIRS, 2, LANES)
    row_terms = jnp.concatenate(
        [position_pairs, type_pairs, table_pairs, jnp.zeros((PAIRS, 4, LANES), F32)], axis=1
    )

    block = 2 * rows.shape[1] // 2
    pooled_block = block // 2
    at = jnp.arange(block, dtype=jnp.int32)[None, None, :]
    want = 2 * jnp.arange(pooled_block, dtype=jnp.int32)[None, :, None]
    half = jnp.where(pair_same, 0.5, 1.0)[:, :, None]
    pool = jnp.where(at == want, half, jnp.where(at == want + 1, 1.0 - half, 0.0)).astype(BF16)
    pool = jnp.where(at == want + 1, jnp.where(pair_same, 0.5, 0.0)[:, :, None].astype(BF16), pool)

    pooled = jnp.einsum("cpt,ctd->cpd", pool, rows, preferred_element_type=F32)
    pooled = pooled.reshape(PQ, MODEL_WIDTH)
    pooled_low = low(pooled)
    token_rows = rows.reshape(LEN, MODEL_WIDTH)
    query = mm(pooled_low, first[:, :MODEL_WIDTH])
    pair_add = jnp.concatenate([jnp.zeros_like(value_add), value_add], axis=1)
    pairs = low(mm(token_rows, first[:, MODEL_WIDTH:]) + pair_add)
    mixture, join = attend_forward(
        query, pairs, maps, map_add, content_add, query_side, key_side, phase, cosm, sinm
    )

    cotangent, _ = lax.optimization_barrier((cotangent, pairs))
    cotangent = lax.all_to_all(cotangent, "seq", split_axis=0, concat_axis=0, tiled=True)
    upstream = cotangent.reshape(PQ, MODEL_WIDTH).astype(F32)

    output_low, inner_low = next_weights[:, :MODEL_WIDTH], next_weights[:, MODEL_WIDTH:]
    attention = mm(mixture, output_low) + output_add
    hidden, normed_one, inverse_one = norm_forward(pooled + attention, gain_one, shift_one)
    hidden_low = low(hidden)
    expanded = mm(hidden_low, inner_low) + inner_add
    active = low(jax.nn.gelu(expanded, approximate=True))
    branch = mm(active, outer_low) + outer_add
    result, normed_two, inverse_two = norm_forward(hidden + branch, gain_two, shift_two)
    output = low(result).reshape(SG, PQ // SG, MODEL_WIDTH)
    output = lax.all_to_all(output, "seq", split_axis=0, concat_axis=0, tiled=True)

    total = lambda value: jnp.sum(value, axis=0)
    grad_gain_two = total(upstream * normed_two)
    grad_shift_two = total(upstream)
    grad_second = norm_backward(upstream, normed_two, inverse_two, gain_two)
    grad_branch = low(grad_second)
    grad_outer_weight = mm(active, grad_branch, TN)
    grad_outer_bias = total(grad_branch.astype(F32))
    grad_active = mm(grad_branch, outer_low, NT)
    _, gelu_pull = jax.vjp(partial(jax.nn.gelu, approximate=True), expanded)
    grad_expanded = low(gelu_pull(grad_active)[0])
    grad_inner_weight = mm(hidden_low, grad_expanded, TN)
    grad_inner_bias = total(grad_expanded.astype(F32))

    def shared(value):
        value = lax.psum_scatter(low(value), "dp", scatter_dimension=0, tiled=True)
        return lax.psum(value, "seq").astype(F32)

    owned_outer = shared(grad_outer_weight)
    owned_inner = shared(grad_inner_weight)
    grad_hidden = grad_second + mm(grad_expanded, inner_low, NT)
    grad_gain_one = total(grad_hidden * normed_one)
    grad_shift_one = total(grad_hidden)
    grad_first = norm_backward(grad_hidden, normed_one, inverse_one, gain_one)
    grad_attention = low(grad_first)
    grad_output_weight = mm(mixture, grad_attention, TN)
    grad_output_bias = total(grad_attention.astype(F32))
    grad_mixture = low(mm(grad_attention, output_low, NT))

    grad_query, grad_key, grad_value, sums, grad_map = attend_backward(
        join,
        pairs,
        query,
        mixture,
        grad_mixture,
        map_back,
        row_terms,
        query_side,
        key_side,
        phase,
        cosm,
        sinm,
    )
    grad_query_weight = mm(pooled_low, grad_query, TN)
    grad_key_weight = mm(token_rows, grad_key, TN)
    grad_value_weight = mm(token_rows, grad_value, TN)
    grad_pooled = grad_first + mm(grad_query, first[:, :MODEL_WIDTH], NT)
    grad_direct = mm(grad_key, first[:, MODEL_WIDTH : 2 * MODEL_WIDTH], NT)
    grad_direct = grad_direct + mm(grad_value, first[:, 2 * MODEL_WIDTH :], NT)
    high_pooled, low_pooled = split(grad_pooled.reshape(SG, pooled_block, MODEL_WIDTH))
    spread = partial(jnp.einsum, "cpt,cpd->ctd", preferred_element_type=F32)
    spread_sum = spread(pool, high_pooled) + spread(pool, low_pooled)
    grad_tokens = low(grad_direct.reshape(SG, block, MODEL_WIDTH) + spread_sum)
    grad_tokens = lax.all_to_all(grad_tokens, "seq", split_axis=0, concat_axis=0, tiled=True)

    crossed = grad_map.reshape(PAIRS, 2, HEAD_SIZE, 2, 2, HEAD_SIZE)
    grad_relative = jnp.stack(
        [
            crossed[:, h, :, 0, 1 - h] + swap_halves(crossed[:, h, :, 1, 1 - h], 2)
            for h in range(2)
        ],
        axis=1,
    ).reshape(HEAD_COUNT, HEAD_SIZE, HEAD_SIZE)
    grad_table = sums[:, 3:5].reshape(PAIRS, 2, 2, HEAD_SIZE).transpose(0, 2, 1, 3)
    sum_row = lambda j: sums[:, j].reshape(owners, -1)
    small_grads = jnp.concatenate(
        [
            value.reshape(owners, -1)
            for value in (
                sum_row(5),
                grad_output_bias,
                grad_outer_bias,
                grad_gain_one,
                grad_shift_one,
                grad_gain_two,
                grad_shift_two,
                sum_row(0),
                sum_row(1),
                sum_row(2),
                grad_inner_bias,
                grad_relative,
                grad_table,
            )
        ],
        axis=1,
    )
    wide = 4 * MODEL_WIDTH
    small_rows = small_grads.shape[1] // wide
    late = jnp.concatenate(
        [grad_query_weight, grad_key_weight, grad_value_weight, grad_output_weight], axis=1
    ).reshape(owners, part, wide)
    spare = jnp.zeros((owners, -small_rows % 8, wide), F32)
    late = jnp.concatenate(
        [late, small_grads.reshape(owners, small_rows, wide), spare], axis=1
    ).reshape(-1, wide)
    owned_late = shared(late)
    squares = [owned_late[:part, j * MODEL_WIDTH : (j + 1) * MODEL_WIDTH] for j in range(4)]
    small_owned = owned_late[part : part + small_rows].reshape(-1)
    place = 0
    pieces = []
    for size in [part] * 10 + [FF // owners, kernel_size, HEAD_COUNT * 2 * HEAD_SIZE // owners]:
        pieces.append(small_owned[place : place + size])
        place += size
    heads = HEAD_COUNT // owners
    return (
        output.reshape(SG, PQ // SG, MODEL_WIDTH),
        grad_tokens,
        squares[0],
        squares[1],
        squares[2],
        squares[3],
        owned_inner,
        owned_outer,
        pieces[0],
        pieces[1],
        pieces[10],
        pieces[2],
        pieces[3],
        pieces[4],
        pieces[5],
        pieces[6],
        pieces[7].reshape(heads, HEAD_SIZE),
        pieces[8].reshape(heads, HEAD_SIZE),
        pieces[9].reshape(heads, HEAD_SIZE),
        pieces[11].reshape(heads, HEAD_SIZE, HEAD_SIZE),
        pieces[12].reshape(heads, 2, HEAD_SIZE),
    )


def solution(mesh):
    whole = mesh.shape["seq"] == SG and mesh.shape["dp"] == 4
    return jax.shard_map(
        sequence_body if whole else body,
        mesh=mesh,
        in_specs=(
            P("dp", "seq", None),
            P("dp", "seq"),
            P("dp", "seq"),
            P("dp", "seq", None),
            P("dp", None),
            P("dp", None),
            P("dp", None),
            P("dp", None),
            P("dp", None),
            P("dp", None),
            P("dp"),
            P("dp"),
            P("dp"),
            P("dp"),
            P("dp"),
            P("dp"),
            P("dp"),
            P("dp"),
            P("dp", None),
            P("dp", None),
            P("dp", None),
            P("dp", None, None),
            P("dp", None, None),
        ),
        out_specs=(
            P("dp", "seq", None),
            P("dp", "seq", None),
            P("dp", None),
            P("dp", None),
            P("dp", None),
            P("dp", None),
            P("dp", None),
            P("dp", None),
            P("dp"),
            P("dp"),
            P("dp"),
            P("dp"),
            P("dp"),
            P("dp"),
            P("dp"),
            P("dp"),
            P("dp", None),
            P("dp", None),
            P("dp", None),
            P("dp", None, None),
            P("dp", None, None),
        ),
        check_vma=False,
    )
```

```python
from functools import partial
import math

import jax
import jax.numpy as jnp
from jax import lax
from jax.experimental import pallas as pl
from jax.experimental.pallas import tpu as pltpu
from jax.sharding import PartitionSpec as P

MODEL_WIDTH = 768
HEAD_COUNT = 12
HEAD_SIZE = 64
LEN = 2048
SG = 8
PQ = 1024


highest = lax.Precision.HIGHEST
norm_eps = 1e-05
masked_score = -1e30


def frequencies():
    half_width = HEAD_SIZE // 2
    return jnp.exp(jnp.arange(half_width, dtype=jnp.float32) * (-math.log(10000.0) / half_width))


def norm_forward(inputs, gains, shifts):
    row_mean = jnp.mean(inputs, axis=-1, keepdims=True)
    centred = inputs - row_mean
    inverse = lax.rsqrt(jnp.mean(centred * centred, axis=-1, keepdims=True) + norm_eps)
    normed = centred * inverse
    return (normed * gains + shifts, normed, inverse)


def norm_backward(upstream, normed, inverse, gains):
    scaled = upstream * gains
    along = jnp.mean(scaled * normed, axis=-1, keepdims=True)
    centre = jnp.mean(scaled, axis=-1, keepdims=True)
    return inverse * (scaled - centre - normed * along)


def doc_masks(segment_row, type_row):
    same_document = segment_row[0::2][:, None] == segment_row[None, :]
    same_type = type_row[0::2][:, None] == type_row[None, :]
    return (same_document, same_type)


def score_block(query_row, type_row_terms, pair_row, key_phase, same_document, same_type):
    key_join = jnp.concatenate([pair_row[:, :HEAD_SIZE], key_phase], axis=-1)
    raw_score = lax.dot_general(
        query_row, key_join, (((1,), (1,)), ((), ())), preferred_element_type=jnp.float32
    )
    type_float = type_row_terms.astype(jnp.float32)
    raw_score = raw_score + jnp.where(same_type, type_float[:, 1:2], type_float[:, 0:1])
    return (jnp.where(same_document, raw_score * HEAD_SIZE ** (-0.5), masked_score), key_join)


def body(
    tokens,
    segments,
    token_types,
    cotangent,
    query_weight,
    key_weight,
    value_weight,
    output_weight,
    inner_weight,
    outer_weight,
    value_bias,
    output_bias,
    inner_bias,
    outer_bias,
    attention_norm_gain,
    first_shift,
    second_gain,
    second_shift,
    content_bias,
    position_bias,
    type_bias,
    relative_kernel,
    type_embed,
):
    local_tokens = tokens.shape[1]
    local_pooled = local_tokens // 2
    group_size = lax.axis_size("seq")
    shard_rank = lax.axis_index("seq")
    item_count = SG * HEAD_COUNT // group_size
    half_width = HEAD_SIZE // 2
    score_scale = HEAD_SIZE ** (-0.5)
    frequency = frequencies()
    duplicate_params = (
        lax.all_gather(query_weight.astype(jnp.bfloat16), "dp", axis=0, tiled=True),
        lax.all_gather(key_weight.astype(jnp.bfloat16), "dp", axis=0, tiled=True),
        lax.all_gather(value_weight.astype(jnp.bfloat16), "dp", axis=0, tiled=True),
        lax.all_gather(output_weight.astype(jnp.bfloat16), "dp", axis=0, tiled=True),
        lax.all_gather(inner_weight.astype(jnp.bfloat16), "dp", axis=0, tiled=True),
        lax.all_gather(outer_weight.astype(jnp.bfloat16), "dp", axis=0, tiled=True),
        lax.all_gather(value_bias.astype(jnp.bfloat16), "dp", axis=0, tiled=True),
        lax.all_gather(output_bias.astype(jnp.bfloat16), "dp", axis=0, tiled=True),
        lax.all_gather(inner_bias.astype(jnp.bfloat16), "dp", axis=0, tiled=True),
        lax.all_gather(outer_bias.astype(jnp.bfloat16), "dp", axis=0, tiled=True),
        lax.all_gather(attention_norm_gain.astype(jnp.bfloat16), "dp", axis=0, tiled=True),
        lax.all_gather(first_shift.astype(jnp.bfloat16), "dp", axis=0, tiled=True),
        lax.all_gather(second_gain.astype(jnp.bfloat16), "dp", axis=0, tiled=True),
        lax.all_gather(second_shift.astype(jnp.bfloat16), "dp", axis=0, tiled=True),
        lax.all_gather(content_bias.astype(jnp.bfloat16), "dp", axis=0, tiled=True),
        lax.all_gather(position_bias.astype(jnp.bfloat16), "dp", axis=0, tiled=True),
        lax.all_gather(type_bias.astype(jnp.bfloat16), "dp", axis=0, tiled=True),
        lax.all_gather(relative_kernel.astype(jnp.bfloat16), "dp", axis=0, tiled=True),
        lax.all_gather(type_embed.astype(jnp.bfloat16), "dp", axis=0, tiled=True),
    )
    value_add = duplicate_params[6].astype(jnp.float32)
    output_add = duplicate_params[7].astype(jnp.float32)
    inner_add = duplicate_params[8].astype(jnp.float32)
    outer_add = duplicate_params[9].astype(jnp.float32)
    gain_one = duplicate_params[10].astype(jnp.float32)
    shift_one = duplicate_params[11].astype(jnp.float32)
    gain_two = duplicate_params[12].astype(jnp.float32)
    shift_two = duplicate_params[13].astype(jnp.float32)
    content_add = duplicate_params[14].astype(jnp.float32)[None, :, None, :]
    position_add = duplicate_params[15].astype(jnp.float32)[None, :, None, :]
    type_add = duplicate_params[16].astype(jnp.float32)[None, :, None, :]
    relative = duplicate_params[17].astype(jnp.float32)
    type_table = duplicate_params[18].astype(jnp.float32)
    whole_segments, whole_types = (
        lax.all_gather(segments, "seq", axis=1, tiled=True),
        lax.all_gather(token_types, "seq", axis=1, tiled=True),
    )
    first_rows = tokens[:, 0::2].astype(jnp.float32)
    second = tokens[:, 1::2].astype(jnp.float32)
    pair_same = (segments[:, 0::2] == segments[:, 1::2])[..., None]
    pooled = jnp.where(pair_same, (first_rows + second) * 0.5, first_rows)
    pooled_low = pooled.astype(jnp.bfloat16)
    queries = jnp.einsum(
        "spd,dhe->shpe",
        pooled_low,
        duplicate_params[0].reshape(MODEL_WIDTH, HEAD_COUNT, HEAD_SIZE),
        preferred_element_type=jnp.float32,
    )
    key_rows = jnp.einsum(
        "ukf,fra->urka",
        tokens,
        duplicate_params[1].reshape(MODEL_WIDTH, HEAD_COUNT, HEAD_SIZE),
        preferred_element_type=jnp.float32,
    )
    value_rows = (
        jnp.einsum(
            "ukf,fra->urka",
            tokens,
            duplicate_params[2].reshape(MODEL_WIDTH, HEAD_COUNT, HEAD_SIZE),
            preferred_element_type=jnp.float32,
        )
        + value_add.reshape(HEAD_COUNT, HEAD_SIZE)[None, :, None, :]
    )
    pair_rows = (
        jnp.concatenate([key_rows, value_rows], axis=-1)
        .astype(jnp.bfloat16)
        .reshape(SG * HEAD_COUNT, local_tokens, 2 * HEAD_SIZE)
    )
    shifted = queries + position_add
    relative_terms = jnp.einsum("shpe,hef->shpf", shifted, relative, precision=highest)
    pooled_place = 2.0 * (
        shard_rank * local_pooled + jnp.arange(local_pooled, dtype=jnp.int32)
    ).astype(jnp.float32)
    query_angle = pooled_place[:, None] * frequency[None, :]
    query_cos = jnp.cos(query_angle)
    query_sin = jnp.sin(query_angle)
    relative_cos = relative_terms[..., :half_width]
    relative_sin = relative_terms[..., half_width:]
    position = jnp.concatenate(
        [
            relative_cos * query_cos + relative_sin * query_sin,
            relative_cos * query_sin - relative_sin * query_cos,
        ],
        axis=-1,
    )
    query_join = (
        jnp.concatenate([queries + content_add, position], axis=-1)
        .astype(jnp.bfloat16)
        .reshape(SG * HEAD_COUNT, local_pooled, 2 * HEAD_SIZE)
    )
    typed = queries + type_add
    type_terms = (
        jnp.einsum("shpe,hbe->shpb", typed, type_table, precision=highest)
        .astype(jnp.bfloat16)
        .reshape(SG * HEAD_COUNT, local_pooled, 2)
    )
    query_heads, type_heads, pair_heads = (
        lax.all_to_all(query_join, "seq", split_axis=0, concat_axis=1, tiled=True),
        lax.all_to_all(type_terms, "seq", split_axis=0, concat_axis=1, tiled=True),
        lax.all_to_all(pair_rows, "seq", split_axis=0, concat_axis=1, tiled=True),
    )
    item_rows = (shard_rank * item_count + jnp.arange(item_count, dtype=jnp.int32)) // HEAD_COUNT
    item_segments = whole_segments[item_rows]
    item_types = whole_types[item_rows]
    key_angle = jnp.arange(LEN, dtype=jnp.float32)[:, None] * frequency[None, :]
    key_phase = jnp.concatenate([jnp.cos(key_angle), jnp.sin(key_angle)], axis=-1).astype(
        jnp.bfloat16
    )

    def attend(packed):
        query_row, type_row_terms, pair_row, segment_row, type_row = packed
        same_document, same_type = doc_masks(segment_row, type_row)
        scores, key_join = score_block(
            query_row, type_row_terms, pair_row, key_phase, same_document, same_type
        )
        row_max = jnp.max(scores, axis=1, keepdims=True)
        exponent = jnp.exp(scores - row_max)
        row_total = jnp.sum(exponent, axis=1, keepdims=True)
        weights = exponent / row_total
        mixture = jnp.dot(
            weights.astype(jnp.bfloat16),
            pair_row[:, HEAD_SIZE:],
            preferred_element_type=jnp.float32,
        )
        return (mixture.astype(jnp.bfloat16), row_max + jnp.log(row_total))

    mixed_heads, log_totals = lax.map(
        attend, (query_heads, type_heads, pair_heads, item_segments, item_types)
    )
    mixed_tokens = lax.all_to_all(
        mixed_heads.reshape(item_count, PQ // 2, 2 * HEAD_SIZE),
        "seq",
        split_axis=1,
        concat_axis=0,
        tiled=True,
    ).reshape(SG, HEAD_COUNT, local_pooled, HEAD_SIZE)
    attention = (
        jnp.einsum(
            "shpe,hed->spd",
            mixed_tokens,
            duplicate_params[3].reshape(HEAD_COUNT, HEAD_SIZE, MODEL_WIDTH),
            preferred_element_type=jnp.float32,
        )
        + output_add
    )
    hidden, normed_one, inverse_one = norm_forward(pooled + attention, gain_one, shift_one)
    hidden_low = hidden.astype(jnp.bfloat16)
    expanded = (
        jnp.einsum(
            "spd,df->spf", hidden_low, duplicate_params[4], preferred_element_type=jnp.float32
        )
        + inner_add
    )
    active = jax.nn.gelu(expanded, approximate=True).astype(jnp.bfloat16)
    branch = (
        jnp.einsum("spf,fd->spd", active, duplicate_params[5], preferred_element_type=jnp.float32)
        + outer_add
    )
    result, normed_two, inverse_two = norm_forward(hidden + branch, gain_two, shift_two)
    output = result.astype(jnp.bfloat16)
    again = (
        lax.all_gather(query_weight.astype(jnp.bfloat16), "dp", axis=0, tiled=True),
        lax.all_gather(key_weight.astype(jnp.bfloat16), "dp", axis=0, tiled=True),
        lax.all_gather(value_weight.astype(jnp.bfloat16), "dp", axis=0, tiled=True),
        lax.all_gather(output_weight.astype(jnp.bfloat16), "dp", axis=0, tiled=True),
        lax.all_gather(inner_weight.astype(jnp.bfloat16), "dp", axis=0, tiled=True),
        lax.all_gather(outer_weight.astype(jnp.bfloat16), "dp", axis=0, tiled=True),
        lax.all_gather(attention_norm_gain.astype(jnp.bfloat16), "dp", axis=0, tiled=True),
        lax.all_gather(second_gain.astype(jnp.bfloat16), "dp", axis=0, tiled=True),
        lax.all_gather(relative_kernel.astype(jnp.bfloat16), "dp", axis=0, tiled=True),
        lax.all_gather(type_embed.astype(jnp.bfloat16), "dp", axis=0, tiled=True),
    )
    query_back = again[0]
    key_back = again[1]
    value_back = again[2]
    output_back = again[3]
    inner_back = again[4]
    outer_back = again[5]
    gain_one_back = again[6].astype(jnp.float32)
    gain_two_back = again[7].astype(jnp.float32)
    relative_back = again[8].astype(jnp.float32)
    table_back = again[9].astype(jnp.float32)
    grad_result = cotangent.astype(jnp.float32)
    grad_gain_two = jnp.sum(grad_result * normed_two, axis=(0, 1))
    grad_shift_two = jnp.sum(grad_result, axis=(0, 1))
    grad_second = norm_backward(grad_result, normed_two, inverse_two, gain_two_back)
    grad_branch = grad_second.astype(jnp.bfloat16)
    grad_outer_weight = jnp.einsum(
        "spf,spd->fd", active, grad_branch, preferred_element_type=jnp.float32
    )
    grad_outer_bias = jnp.sum(grad_branch.astype(jnp.float32), axis=(0, 1))
    grad_active = jnp.einsum(
        "spd,fd->spf", grad_branch, outer_back, preferred_element_type=jnp.float32
    )
    gelu_value, gelu_pull = jax.vjp(partial(jax.nn.gelu, approximate=True), expanded)
    grad_expanded = gelu_pull(grad_active)[0].astype(jnp.bfloat16)
    grad_inner_weight = jnp.einsum(
        "spd,spf->df", hidden_low, grad_expanded, preferred_element_type=jnp.float32
    )
    grad_inner_bias = jnp.sum(grad_expanded.astype(jnp.float32), axis=(0, 1))
    grad_hidden = grad_second + jnp.einsum(
        "spf,df->spd", grad_expanded, inner_back, preferred_element_type=jnp.float32
    )
    grad_gain_one = jnp.sum(grad_hidden * normed_one, axis=(0, 1))
    grad_shift_one = jnp.sum(grad_hidden, axis=(0, 1))
    grad_first = norm_backward(grad_hidden, normed_one, inverse_one, gain_one_back)
    grad_attention = grad_first.astype(jnp.bfloat16)
    grad_output_weight = jnp.einsum(
        "shpe,spd->hed", mixed_tokens, grad_attention, preferred_element_type=jnp.float32
    ).reshape(MODEL_WIDTH, MODEL_WIDTH)
    grad_output_bias = jnp.sum(grad_attention.astype(jnp.float32), axis=(0, 1))
    grad_mixture = jnp.einsum(
        "spd,hed->shpe",
        grad_attention,
        output_back.reshape(HEAD_COUNT, HEAD_SIZE, MODEL_WIDTH),
        preferred_element_type=jnp.float32,
    ).astype(jnp.bfloat16)
    grad_mixed_heads = lax.all_to_all(
        grad_mixture.reshape(SG * HEAD_COUNT, local_pooled // 2, 2 * HEAD_SIZE),
        "seq",
        split_axis=0,
        concat_axis=1,
        tiled=True,
    ).reshape(item_count, PQ, HEAD_SIZE)

    def attend_back(packed):
        query_row, type_row_terms, pair_row, segment_row, type_row, log_row, grad_row = packed
        same_document, same_type = doc_masks(segment_row, type_row)
        scores, key_join = score_block(
            query_row, type_row_terms, pair_row, key_phase, same_document, same_type
        )
        weights = jnp.exp(scores - log_row)
        grad_weights = lax.dot_general(
            grad_row,
            pair_row[:, HEAD_SIZE:],
            (((1,), (1,)), ((), ())),
            preferred_element_type=jnp.float32,
        )
        row_dot = jnp.sum(grad_weights * weights, axis=1, keepdims=True)
        grad_scores = (weights * (grad_weights - row_dot)).astype(jnp.bfloat16)
        grad_query = (
            jnp.dot(grad_scores, key_join, preferred_element_type=jnp.float32) * score_scale
        ).astype(jnp.bfloat16)
        grad_float = grad_scores.astype(jnp.float32) * score_scale
        grad_same = jnp.sum(jnp.where(same_type, grad_float, 0.0), axis=1)
        grad_other = jnp.sum(jnp.where(same_type, 0.0, grad_float), axis=1)
        grad_kinds = jnp.stack([grad_other, grad_same], axis=-1).astype(jnp.bfloat16)
        grad_keys = (
            lax.dot_general(
                grad_scores,
                query_row[:, :HEAD_SIZE],
                (((0,), (0,)), ((), ())),
                preferred_element_type=jnp.float32,
            )
            * score_scale
        )
        grad_values = lax.dot_general(
            weights.astype(jnp.bfloat16),
            grad_row,
            (((0,), (0,)), ((), ())),
            preferred_element_type=jnp.float32,
        )
        return (
            grad_query,
            grad_kinds,
            jnp.concatenate([grad_keys, grad_values], axis=-1).astype(jnp.bfloat16),
        )

    grad_query_heads, grad_type_heads, grad_pair_heads = lax.map(
        attend_back,
        (
            query_heads,
            type_heads,
            pair_heads,
            item_segments,
            item_types,
            log_totals,
            grad_mixed_heads,
        ),
    )
    grad_query_tok, grad_type_tok, grad_pair_tok = (
        lax.all_to_all(grad_query_heads, "seq", split_axis=1, concat_axis=0, tiled=True),
        lax.all_to_all(grad_type_heads, "seq", split_axis=1, concat_axis=0, tiled=True),
        lax.all_to_all(grad_pair_heads, "seq", split_axis=1, concat_axis=0, tiled=True),
    )
    grad_query_join = grad_query_tok.astype(jnp.float32).reshape(
        SG, HEAD_COUNT, local_pooled, 2 * HEAD_SIZE
    )
    grad_content = grad_query_join[..., :HEAD_SIZE]
    grad_first_half = grad_query_join[..., HEAD_SIZE : HEAD_SIZE + half_width]
    grad_second_half = grad_query_join[..., HEAD_SIZE + half_width :]
    grad_relative_terms = jnp.concatenate(
        [
            grad_first_half * query_cos + grad_second_half * query_sin,
            grad_first_half * query_sin - grad_second_half * query_cos,
        ],
        axis=-1,
    )
    grad_shifted = jnp.einsum(
        "shpf,hef->shpe", grad_relative_terms, relative_back, precision=highest
    )
    grad_relative_kernel = jnp.einsum(
        "shpe,shpf->hef", shifted, grad_relative_terms, precision=highest
    )
    grad_type_terms = grad_type_tok.astype(jnp.float32).reshape(SG, HEAD_COUNT, local_pooled, 2)
    grad_typed = jnp.einsum("shpb,hbe->shpe", grad_type_terms, table_back, precision=highest)
    grad_type_embed = jnp.einsum("shpe,shpb->hbe", typed, grad_type_terms, precision=highest)
    query_rows_gradient = (grad_content + grad_shifted + grad_typed).astype(jnp.bfloat16)
    grad_content_bias = jnp.sum(grad_content, axis=(0, 2))
    grad_position_bias = jnp.sum(grad_shifted, axis=(0, 2))
    grad_type_bias = jnp.sum(grad_typed, axis=(0, 2))
    grad_query_weight = jnp.einsum(
        "spd,shpe->dhe", pooled_low, query_rows_gradient, preferred_element_type=jnp.float32
    ).reshape(MODEL_WIDTH, MODEL_WIDTH)
    grad_pooled = grad_first + jnp.einsum(
        "shpe,dhe->spd",
        query_rows_gradient,
        query_back.reshape(MODEL_WIDTH, HEAD_COUNT, HEAD_SIZE),
        preferred_element_type=jnp.float32,
    )
    grad_pairs = grad_pair_tok.reshape(SG, HEAD_COUNT, local_tokens, 2 * HEAD_SIZE)
    key_rows_gradient = grad_pairs[..., :HEAD_SIZE]
    value_rows_gradient = grad_pairs[..., HEAD_SIZE:]
    grad_key_weight = jnp.einsum(
        "ozb,opzx->bpx", tokens, key_rows_gradient, preferred_element_type=jnp.float32
    ).reshape(MODEL_WIDTH, MODEL_WIDTH)
    grad_value_weight = jnp.einsum(
        "ozb,opzx->bpx", tokens, value_rows_gradient, preferred_element_type=jnp.float32
    ).reshape(MODEL_WIDTH, MODEL_WIDTH)
    grad_value_bias = jnp.sum(value_rows_gradient.astype(jnp.float32), axis=(0, 2)).reshape(
        MODEL_WIDTH
    )
    grad_direct = jnp.einsum(
        "mivt,git->mvg",
        key_rows_gradient,
        key_back.reshape(MODEL_WIDTH, HEAD_COUNT, HEAD_SIZE),
        preferred_element_type=jnp.float32,
    )
    grad_direct = grad_direct + jnp.einsum(
        "mivt,git->mvg",
        value_rows_gradient,
        value_back.reshape(MODEL_WIDTH, HEAD_COUNT, HEAD_SIZE),
        preferred_element_type=jnp.float32,
    )
    pool_first = jnp.where(pair_same, 0.5 * grad_pooled, grad_pooled)
    pool_second = jnp.where(pair_same, 0.5 * grad_pooled, 0.0)
    grad_tokens = (
        grad_direct
        + jnp.stack([pool_first, pool_second], axis=2).reshape(SG, local_tokens, MODEL_WIDTH)
    ).astype(jnp.bfloat16)
    summed = lax.psum(
        (
            grad_query_weight,
            grad_key_weight,
            grad_value_weight,
            grad_output_weight,
            grad_inner_weight,
            grad_outer_weight,
            grad_value_bias,
            grad_output_bias,
            grad_inner_bias,
            grad_outer_bias,
            grad_gain_one,
            grad_shift_one,
            grad_gain_two,
            grad_shift_two,
            grad_content_bias,
            grad_position_bias,
            grad_type_bias,
            grad_relative_kernel,
            grad_type_embed,
        ),
        "seq",
    )
    owned = (
        lax.psum_scatter(
            summed[0].astype(jnp.bfloat16), "dp", scatter_dimension=0, tiled=True
        ).astype(jnp.float32),
        lax.psum_scatter(
            summed[1].astype(jnp.bfloat16), "dp", scatter_dimension=0, tiled=True
        ).astype(jnp.float32),
        lax.psum_scatter(
            summed[2].astype(jnp.bfloat16), "dp", scatter_dimension=0, tiled=True
        ).astype(jnp.float32),
        lax.psum_scatter(
            summed[3].astype(jnp.bfloat16), "dp", scatter_dimension=0, tiled=True
        ).astype(jnp.float32),
        lax.psum_scatter(
            summed[4].astype(jnp.bfloat16), "dp", scatter_dimension=0, tiled=True
        ).astype(jnp.float32),
        lax.psum_scatter(
            summed[5].astype(jnp.bfloat16), "dp", scatter_dimension=0, tiled=True
        ).astype(jnp.float32),
        lax.psum_scatter(
            summed[6].astype(jnp.bfloat16), "dp", scatter_dimension=0, tiled=True
        ).astype(jnp.float32),
        lax.psum_scatter(
            summed[7].astype(jnp.bfloat16), "dp", scatter_dimension=0, tiled=True
        ).astype(jnp.float32),
        lax.psum_scatter(
            summed[8].astype(jnp.bfloat16), "dp", scatter_dimension=0, tiled=True
        ).astype(jnp.float32),
        lax.psum_scatter(
            summed[9].astype(jnp.bfloat16), "dp", scatter_dimension=0, tiled=True
        ).astype(jnp.float32),
        lax.psum_scatter(
            summed[10].astype(jnp.bfloat16), "dp", scatter_dimension=0, tiled=True
        ).astype(jnp.float32),
        lax.psum_scatter(
            summed[11].astype(jnp.bfloat16), "dp", scatter_dimension=0, tiled=True
        ).astype(jnp.float32),
        lax.psum_scatter(
            summed[12].astype(jnp.bfloat16), "dp", scatter_dimension=0, tiled=True
        ).astype(jnp.float32),
        lax.psum_scatter(
            summed[13].astype(jnp.bfloat16), "dp", scatter_dimension=0, tiled=True
        ).astype(jnp.float32),
        lax.psum_scatter(
            summed[14].astype(jnp.bfloat16), "dp", scatter_dimension=0, tiled=True
        ).astype(jnp.float32),
        lax.psum_scatter(
            summed[15].astype(jnp.bfloat16), "dp", scatter_dimension=0, tiled=True
        ).astype(jnp.float32),
        lax.psum_scatter(
            summed[16].astype(jnp.bfloat16), "dp", scatter_dimension=0, tiled=True
        ).astype(jnp.float32),
        lax.psum_scatter(
            summed[17].astype(jnp.bfloat16), "dp", scatter_dimension=0, tiled=True
        ).astype(jnp.float32),
        lax.psum_scatter(
            summed[18].astype(jnp.bfloat16), "dp", scatter_dimension=0, tiled=True
        ).astype(jnp.float32),
    )
    return (
        output,
        grad_tokens,
        owned[0],
        owned[1],
        owned[2],
        owned[3],
        owned[4],
        owned[5],
        owned[6],
        owned[7],
        owned[8],
        owned[9],
        owned[10],
        owned[11],
        owned[12],
        owned[13],
        owned[14],
        owned[15],
        owned[16],
        owned[17],
        owned[18],
    )


BF16 = jnp.bfloat16
F32 = jnp.float32
PAIRS = HEAD_COUNT // 2
LANES = 2 * HEAD_SIZE
ROWS = 256
FAR = -(2.0**100)
FF = 3072
NN = (((1,), (0,)), ((), ()))
NT = (((1,), (1,)), ((), ()))
TN = (((0,), (0,)), ((), ()))


def mm(left, right, dims=NN):
    return lax.dot_general(left, right, dims, preferred_element_type=F32)


def split(value):
    high = value.astype(BF16)
    return high, (value - high.astype(F32)).astype(BF16)


def lane_ids(rows):
    return lax.broadcasted_iota(jnp.int32, (rows, LANES), 1)


def attend_kernel(
    query_ref,
    key_ref,
    value_ref,
    map_ref,
    map_add_ref,
    content_ref,
    query_side_ref,
    key_side_ref,
    phase_ref,
    cos_ref,
    sin_ref,
    mixture_ref,
    join_ref,
    key_join,
    value_join,
):
    query = query_ref[...]
    high, low = split(query)
    terms = mm(jnp.concatenate([high, low], axis=1), map_ref[0]) + map_add_ref[0]
    lane = lane_ids(PQ)
    left = lane < HEAD_SIZE
    content = query + content_ref[...]
    position = terms[:, :LANES] * cos_ref[...] + terms[:, LANES : 2 * LANES] * sin_ref[...]
    side = query_side_ref[...]
    typed = (lane >= 3) & (lane < 6)
    scale = HEAD_SIZE ** (-0.5)
    for h in range(2):
        first, second = (content, position) if h == 0 else (position, content)
        join_ref[h, :, :LANES] = (jnp.where(left, first, second) * scale).astype(BF16)
        base = 2 * LANES * (h + 1)
        same = terms[:, base : base + LANES]
        other = terms[:, base + LANES : base + 2 * LANES]
        kind = jnp.where(side > 0.5, same, other) * scale
        join_ref[h, :, LANES:] = jnp.where(typed, kind, side).astype(BF16)
    key_left = lane_ids(LEN) < HEAD_SIZE
    key_join[:, LANES:] = key_side_ref[...]
    value_join[:, :LANES] = value_ref[...]
    value_join[:, LANES:] = key_side_ref[...]
    tile_lane = lane_ids(ROWS)
    for h in range(2):
        pieces = (key_ref[...], phase_ref[...]) if h == 0 else (phase_ref[...], key_ref[...])
        key_join[:, :LANES] = jnp.where(key_left, *pieces)
        for i in range(PQ // ROWS):
            rows = slice(i * ROWS, (i + 1) * ROWS)
            scores = mm(join_ref[h, rows, :], key_join[...], NT)
            top = jnp.max(scores, axis=1, keepdims=True)
            weights = jnp.exp(scores - top).astype(BF16)
            mixed = mm(weights, value_join[...])
            total = mixed[:, LANES + 6 : LANES + 7]
            result = (mixed[:, :LANES] / total).astype(BF16)
            if h == 0:
                mixture_ref[rows, :] = result
            else:
                mixture_ref[rows, :] = jnp.where(
                    tile_lane < HEAD_SIZE, mixture_ref[rows, :], result
                )
            shift = -(top + jnp.log(total))
            one = shift.astype(BF16).astype(F32)
            two = (shift - one).astype(BF16).astype(F32)
            three = shift - one - two
            extra = jnp.where(tile_lane == 6, one, jnp.where(tile_lane == 7, two, three))
            kept = join_ref[h, rows, LANES:].astype(F32)
            inside = (tile_lane >= 6) & (tile_lane < 9)
            join_ref[h, rows, LANES:] = jnp.where(inside, extra, kept).astype(BF16)


def attend_forward(query, pairs, maps, map_add, content, query_side, key_side, phase, cosm, sinm):
    whole = lambda shape: pl.BlockSpec(shape, lambda i: (0, 0))
    return pl.pallas_call(
        attend_kernel,
        grid=(PAIRS,),
        in_specs=[
            pl.BlockSpec((PQ, LANES), lambda i: (0, i)),
            pl.BlockSpec((LEN, LANES), lambda i: (0, i)),
            pl.BlockSpec((LEN, LANES), lambda i: (0, i + PAIRS)),
            pl.BlockSpec((1, 2 * LANES, 6 * LANES), lambda i: (i, 0, 0)),
            pl.BlockSpec((1, 1, 6 * LANES), lambda i: (i, 0, 0)),
            pl.BlockSpec((1, LANES), lambda i: (0, i)),
            whole((PQ, LANES)),
            whole((LEN, LANES)),
            whole((LEN, LANES)),
            whole((PQ, LANES)),
            whole((PQ, LANES)),
        ],
        out_specs=[
            pl.BlockSpec((PQ, LANES), lambda i: (0, i)),
            pl.BlockSpec((2, PQ, 2 * LANES), lambda i: (i, 0, 0)),
        ],
        out_shape=[
            jax.ShapeDtypeStruct((PQ, MODEL_WIDTH), BF16),
            jax.ShapeDtypeStruct((HEAD_COUNT, PQ, 2 * LANES), BF16),
        ],
        scratch_shapes=[
            pltpu.VMEM((LEN, 2 * LANES), BF16),
            pltpu.VMEM((LEN, 2 * LANES), BF16),
        ],
        cost_estimate=pl.CostEstimate(
            flops=4 * HEAD_COUNT * PQ * LEN * 256,
            bytes_accessed=20_000_000,
            transcendentals=HEAD_COUNT * PQ * LEN,
        ),
        compiler_params=pltpu.CompilerParams(vmem_limit_bytes=56 * 2**20),
        name="attend_forward",
    )(query, pairs, pairs, maps, map_add, content, query_side, key_side, phase, cosm, sinm)


def attend_back_kernel(
    join_ref,
    key_ref,
    value_ref,
    query_ref,
    mixture_ref,
    grad_ref,
    map_back_ref,
    rows_ref,
    query_side_ref,
    key_side_ref,
    phase_ref,
    cos_ref,
    sin_ref,
    grad_query_ref,
    grad_key_ref,
    grad_value_ref,
    sums_ref,
    grad_map_ref,
    key_join,
    value_join,
    key_total,
    value_total,
    join_grads,
):
    scale = HEAD_SIZE ** (-0.5)
    key_left = lane_ids(LEN) < HEAD_SIZE
    tile_lane = lane_ids(ROWS)
    key_join[:, LANES:] = key_side_ref[...]
    value_join[:, :LANES] = value_ref[...]
    value_join[:, LANES:] = key_side_ref[...]
    for h in range(2):
        pieces = (key_ref[...], phase_ref[...]) if h == 0 else (phase_ref[...], key_ref[...])
        key_join[:, :LANES] = jnp.where(key_left, *pieces)
        mine = (tile_lane < HEAD_SIZE) if h == 0 else (tile_lane >= HEAD_SIZE)
        part = slice(h * HEAD_SIZE, (h + 1) * HEAD_SIZE)
        for i in range(PQ // ROWS):
            rows = slice(i * ROWS, (i + 1) * ROWS)
            join = join_ref[h, rows, :]
            grad = jnp.where(mine, grad_ref[rows, :].astype(F32), 0.0)
            dot = -jnp.sum(grad * mixture_ref[rows, :].astype(F32), axis=1, keepdims=True)
            one = dot.astype(BF16).astype(F32)
            two = (dot - one).astype(BF16).astype(F32)
            three = dot - one - two
            extra = jnp.where(tile_lane == 6, one, jnp.where(tile_lane == 7, two, three))
            inside = (tile_lane >= 6) & (tile_lane < 9)
            extra = jnp.where(inside, extra, 0.0)
            grad_low = grad.astype(BF16)
            weights = jnp.exp(mm(join, key_join[...], NT))
            slope = mm(
                jnp.concatenate([grad_low, extra.astype(BF16)], axis=1), value_join[...], NT
            )
            low_slope = (weights * slope).astype(BF16)
            low_weights = weights.astype(BF16)
            join_grads[h, rows, :] = mm(low_slope, key_join[...])
            to_key = mm(join_ref[h, rows, part], low_slope, TN)
            to_value = mm(grad_ref[rows, part], low_weights, TN)
            if i == 0:
                key_total[part, :] = to_key
                value_total[part, :] = to_value
            else:
                key_total[part, :] += to_key
                value_total[part, :] += to_value
    grad_key_ref[...] = key_total[...].T.astype(BF16)
    grad_value_ref[...] = value_total[...].T.astype(BF16)
    lane = lane_ids(PQ)
    left = lane < HEAD_SIZE
    typed = (lane >= 3) & (lane < 6)
    rounded = [(join_grads[h, :, :LANES] * scale).astype(BF16).astype(F32) for h in range(2)]
    content = jnp.where(left, rounded[0], rounded[1])
    position = jnp.where(left, rounded[1], rounded[0])
    turned = jnp.concatenate([position * cos_ref[...], position * sin_ref[...]], axis=1)
    turned_high, turned_low = split(turned)
    shifted_grad = mm(turned_high, map_back_ref[0]) + mm(turned_low, map_back_ref[0])
    side = query_side_ref[...]
    sames, others = [], []
    for h in range(2):
        kinds = jnp.where(typed, join_grads[h, :, LANES:], 0.0)
        same = jnp.sum(jnp.where(side > 0.5, kinds, 0.0), axis=1, keepdims=True)
        other = jnp.sum(jnp.where(side > 0.5, 0.0, kinds), axis=1, keepdims=True)
        sames.append((same * scale).astype(BF16).astype(F32))
        others.append((other * scale).astype(BF16).astype(F32))
    same = jnp.where(left, sames[0], sames[1])
    other = jnp.where(left, others[0], others[1])
    position_add = rows_ref[0, 0:1, :]
    type_add = rows_ref[0, 1:2, :]
    type_other = rows_ref[0, 2:3, :]
    type_same = rows_ref[0, 3:4, :]
    typed_grad = same * type_same + other * type_other
    grad_query_ref[...] = (content + shifted_grad + typed_grad).astype(BF16)
    query = query_ref[...]
    shifted_high, shifted_low = split(query + position_add)
    grad_map_ref[0] = (
        mm(shifted_high, turned_high, TN)
        + mm(shifted_low, turned_high, TN)
        + mm(shifted_high, turned_low, TN)
    )
    kinds = query + type_add
    row = lambda v: jnp.sum(v, axis=0, keepdims=True)
    sums_ref[0, 0:1, :] = row(content)
    sums_ref[0, 1:2, :] = row(shifted_grad)
    sums_ref[0, 2:3, :] = row(typed_grad)
    sums_ref[0, 3:4, :] = row(kinds * other)
    sums_ref[0, 4:5, :] = row(kinds * same)
    sums_ref[0, 5:6, :] = row(grad_value_ref[...].astype(F32))


def attend_backward(
    join, pairs, query, mixture, grad, map_back, rows, query_side, key_side, phase, cosm, sinm
):
    whole = lambda shape: pl.BlockSpec(shape, lambda i: (0, 0))
    return pl.pallas_call(
        attend_back_kernel,
        grid=(PAIRS,),
        in_specs=[
            pl.BlockSpec((2, PQ, 2 * LANES), lambda i: (i, 0, 0)),
            pl.BlockSpec((LEN, LANES), lambda i: (0, i)),
            pl.BlockSpec((LEN, LANES), lambda i: (0, i + PAIRS)),
            pl.BlockSpec((PQ, LANES), lambda i: (0, i)),
            pl.BlockSpec((PQ, LANES), lambda i: (0, i)),
            pl.BlockSpec((PQ, LANES), lambda i: (0, i)),
            pl.BlockSpec((1, 2 * LANES, LANES), lambda i: (i, 0, 0)),
            pl.BlockSpec((1, 8, LANES), lambda i: (i, 0, 0)),
            whole((PQ, LANES)),
            whole((LEN, LANES)),
            whole((LEN, LANES)),
            whole((PQ, LANES)),
            whole((PQ, LANES)),
        ],
        out_specs=[
            pl.BlockSpec((PQ, LANES), lambda i: (0, i)),
            pl.BlockSpec((LEN, LANES), lambda i: (0, i)),
            pl.BlockSpec((LEN, LANES), lambda i: (0, i)),
            pl.BlockSpec((1, 8, LANES), lambda i: (i, 0, 0)),
            pl.BlockSpec((1, LANES, 2 * LANES), lambda i: (i, 0, 0)),
        ],
        out_shape=[
            jax.ShapeDtypeStruct((PQ, MODEL_WIDTH), BF16),
            jax.ShapeDtypeStruct((LEN, MODEL_WIDTH), BF16),
            jax.ShapeDtypeStruct((LEN, MODEL_WIDTH), BF16),
            jax.ShapeDtypeStruct((PAIRS, 8, LANES), F32),
            jax.ShapeDtypeStruct((PAIRS, LANES, 2 * LANES), F32),
        ],
        scratch_shapes=[
            pltpu.VMEM((LEN, 2 * LANES), BF16),
            pltpu.VMEM((LEN, 2 * LANES), BF16),
            pltpu.VMEM((LANES, LEN), F32),
            pltpu.VMEM((LANES, LEN), F32),
            pltpu.VMEM((2, PQ, 2 * LANES), F32),
        ],
        cost_estimate=pl.CostEstimate(
            flops=10 * HEAD_COUNT * PQ * LEN * 256,
            bytes_accessed=32_000_000,
            transcendentals=HEAD_COUNT * PQ * LEN,
        ),
        compiler_params=pltpu.CompilerParams(vmem_limit_bytes=58 * 2**20),
        name="attend_backward",
    )(
        join,
        pairs,
        pairs,
        query,
        mixture,
        grad,
        map_back,
        rows,
        query_side,
        key_side,
        phase,
        cosm,
        sinm,
    )


FF_STEP = 512
FF_TILES = FF // FF_STEP
ROW_TILES = PQ // ROWS


def row_norm(value):
    centred = value - jnp.mean(value, axis=1, keepdims=True)
    inverse = lax.rsqrt(jnp.mean(centred * centred, axis=1, keepdims=True) + norm_eps)
    return centred * inverse, inverse


def row_norm_back(scaled, normed, inverse):
    along = jnp.mean(scaled * normed, axis=1, keepdims=True)
    return inverse * (scaled - jnp.mean(scaled, axis=1, keepdims=True) - normed * along)


def gelu_pieces(value):
    rate = math.sqrt(2.0 / math.pi)
    square = value * value
    bend = jnp.tanh(rate * value * (1.0 + 0.044715 * square))
    half = 0.5 * (1.0 + bend)
    slope = half + (0.5 * rate) * value * (1.0 - bend * bend) * (1.0 + 0.134145 * square)
    return value * half, slope


def mlp_kernel(
    mixture_ref,
    pooled_ref,
    upstream_ref,
    output_weight_ref,
    inner_weight_ref,
    outer_weight_ref,
    vectors_ref,
    inner_add_ref,
    output_ref,
    grad_mixture_ref,
    grad_first_ref,
    grad_outer_ref,
    grad_inner_ref,
    grad_output_ref,
    sums_ref,
    inner_sums_ref,
    active,
    slopes,
    grad_expanded,
    hidden_low,
    grad_branch,
    grad_attention,
):
    step = pl.program_id(0)

    @pl.when(step < ROW_TILES)
    def _():
        rows = pl.ds(pl.multiple_of(step * ROWS, ROWS), ROWS)
        vector = lambda j: vectors_ref[j : j + 1, :]
        output_add, outer_add, gain_one, shift_one, gain_two, shift_two = map(vector, range(6))
        attention = mm(mixture_ref[rows, :], output_weight_ref[...]) + output_add
        normed_one, inverse_one = row_norm(pooled_ref[...] + attention)
        hidden = normed_one * gain_one + shift_one
        low_hidden = hidden.astype(BF16)
        hidden_low[rows, :] = low_hidden
        branch = jnp.zeros((ROWS, MODEL_WIDTH), F32)
        for j in range(FF_TILES):
            part = slice(j * FF_STEP, (j + 1) * FF_STEP)
            expanded = mm(low_hidden, inner_weight_ref[:, part]) + inner_add_ref[:, part]
            value, slope = gelu_pieces(expanded)
            low_value = value.astype(BF16)
            active[rows, part] = low_value
            slopes[:, part] = slope
            branch += mm(low_value, outer_weight_ref[part, :])
        normed_two, inverse_two = row_norm(hidden + (branch + outer_add))
        output_ref[...] = (normed_two * gain_two + shift_two).astype(BF16)
        upstream = upstream_ref[...].astype(F32)
        grad_second = row_norm_back(upstream * gain_two, normed_two, inverse_two)
        low_branch = grad_second.astype(BF16)
        grad_branch[rows, :] = low_branch
        grad_hidden = grad_second
        inner_sums = []
        for j in range(FF_TILES):
            part = slice(j * FF_STEP, (j + 1) * FF_STEP)
            grad_active = mm(low_branch, outer_weight_ref[part, :], NT)
            low_grad = (slopes[:, part] * grad_active).astype(BF16)
            grad_expanded[rows, part] = low_grad
            inner_sums.append(jnp.sum(low_grad.astype(F32), axis=0, keepdims=True))
            grad_hidden += mm(low_grad, inner_weight_ref[:, part], NT)
        grad_first = row_norm_back(grad_hidden * gain_one, normed_one, inverse_one)
        grad_first_ref[...] = grad_first
        low_attention = grad_first.astype(BF16)
        grad_attention[rows, :] = low_attention
        grad_mixture_ref[...] = mm(low_attention, output_weight_ref[...], NT).astype(BF16)
        row = lambda v: jnp.sum(v, axis=0, keepdims=True)
        sums = jnp.concatenate(
            [
                row(low_attention.astype(F32)),
                row(low_branch.astype(F32)),
                row(grad_hidden * normed_one),
                row(grad_hidden),
                row(upstream * normed_two),
                row(upstream),
                jnp.zeros((2, MODEL_WIDTH), F32),
            ],
            axis=0,
        )
        inner_sum = jnp.concatenate(inner_sums, axis=1)

        @pl.when(step == 0)
        def _():
            sums_ref[...] = sums
            inner_sums_ref[...] = inner_sum

        @pl.when(step > 0)
        def _():
            sums_ref[...] += sums
            inner_sums_ref[...] += inner_sum

    for j in range(FF_TILES):

        @pl.when(step == ROW_TILES + j)
        def _():
            part = slice(j * FF_STEP, (j + 1) * FF_STEP)
            grad_outer_ref[...] = mm(active[:, part], grad_branch[...], TN).astype(BF16)
            grad_inner_ref[...] = mm(hidden_low[...], grad_expanded[:, part], TN).astype(BF16)
            if j == 0:
                grad_output_ref[...] = mm(mixture_ref[...], grad_attention[...], TN).astype(BF16)


def mlp(mixture, pooled, upstream, output_weight, inner_weight, outer_weight, vectors, inner_add):
    fixed = lambda shape: pl.BlockSpec(shape, lambda i: (0, 0), pipeline_mode=pl.Buffered(1))
    still = lambda shape: pl.BlockSpec(shape, lambda i: (0, 0))
    tile = pl.BlockSpec((ROWS, MODEL_WIDTH), lambda i: (jnp.minimum(i, ROW_TILES - 1), 0))
    late = lambda i: jnp.maximum(i - ROW_TILES, 0)
    whole = (PQ, MODEL_WIDTH)
    square = (MODEL_WIDTH, MODEL_WIDTH)
    return pl.pallas_call(
        mlp_kernel,
        grid=(ROW_TILES + FF_TILES,),
        in_specs=[
            fixed(whole),
            tile,
            tile,
            fixed(square),
            fixed((MODEL_WIDTH, FF)),
            fixed((FF, MODEL_WIDTH)),
            fixed((8, MODEL_WIDTH)),
            fixed((1, FF)),
        ],
        out_specs=[
            tile,
            tile,
            tile,
            pl.BlockSpec((FF_STEP, MODEL_WIDTH), lambda i: (late(i), 0)),
            pl.BlockSpec((MODEL_WIDTH, FF_STEP), lambda i: (0, late(i))),
            still(square),
            still((8, MODEL_WIDTH)),
            still((1, FF)),
        ],
        out_shape=[
            jax.ShapeDtypeStruct(whole, BF16),
            jax.ShapeDtypeStruct(whole, BF16),
            jax.ShapeDtypeStruct(whole, F32),
            jax.ShapeDtypeStruct((FF, MODEL_WIDTH), BF16),
            jax.ShapeDtypeStruct((MODEL_WIDTH, FF), BF16),
            jax.ShapeDtypeStruct(square, BF16),
            jax.ShapeDtypeStruct((8, MODEL_WIDTH), F32),
            jax.ShapeDtypeStruct((1, FF), F32),
        ],
        scratch_shapes=[
            pltpu.VMEM((PQ, FF), BF16),
            pltpu.VMEM((ROWS, FF), F32),
            pltpu.VMEM((PQ, FF), BF16),
            pltpu.VMEM(whole, BF16),
            pltpu.VMEM(whole, BF16),
            pltpu.VMEM(whole, BF16),
        ],
        cost_estimate=pl.CostEstimate(
            flops=2 * PQ * MODEL_WIDTH * (3 * MODEL_WIDTH + 6 * FF),
            bytes_accessed=40_000_000,
            transcendentals=PQ * FF,
        ),
        compiler_params=pltpu.CompilerParams(vmem_limit_bytes=58 * 2**20),
        name="mlp",
    )(mixture, pooled, upstream, output_weight, inner_weight, outer_weight, vectors, inner_add)


MESH = pl.DeviceIdType.MESH
SUM_ROWS = 48
STAGES = ("core", "y", "x", "near", "far", "far_back", "near_back", "x_back")
SMALL_ROWS = 16
SMALL_COLUMNS = 1024


class Place:
    def __init__(self):
        self.seq, self.dp = lax.axis_index("seq"), lax.axis_index("dp")
        self.core, self.y = self.dp % 2, self.dp // 2
        self.x, self.near, self.far = self.seq % 2, (self.seq // 2) % 2, self.seq // 4
        self.partner = {
            "core": (self.seq, self.dp + 1 - 2 * self.core),
            "y": (self.seq, self.dp + 2 - 4 * self.y),
            "x": (self.seq + 1 - 2 * self.x, self.dp),
            "near": (self.seq + 2 - 4 * self.near, self.dp),
            "far": (self.seq + 4 - 8 * self.far, self.dp),
        }

    def peers(self):
        return [((self.seq + k) % SG, self.dp) for k in range(1, SG)]

    def greet(self):
        barrier = pltpu.get_barrier_semaphore()
        others = [self.partner["core"], self.partner["y"], *self.peers()]
        for device in others:
            pl.semaphore_signal(barrier, inc=1, device_id=device, device_id_type=MESH)
        pl.semaphore_wait(barrier, len(others))


def add_rows(target, addend, rows):
    def step(i, carry):
        at = pl.ds(pl.multiple_of(i * SUM_ROWS, 16), SUM_ROWS)
        left, right = target(at), addend(at)
        left[...] = (left[...].astype(F32) + right[...].astype(F32)).astype(BF16)
        return carry

    lax.fori_loop(0, rows // SUM_ROWS, step, 0)


class Chunk:
    def __init__(self, place, index, source, rows, columns, buffers, send, receive, local):
        self.place, self.source, self.rows, self.columns = place, source, rows, columns
        self.own, self.from_core, self.from_y, self.from_x, self.from_near, self.from_far, self.full = buffers
        self.send_at = lambda stage, k=0: send.at[index, STAGES.index(stage) + (8 if k else 0)]
        self.receive_at = lambda stage, k=0: receive.at[index, STAGES.index(stage) + (8 if k else 0)]
        self.local = lambda k: local.at[index, k]
        half, quarter = rows // 2, rows // 4
        self.my_columns = pl.ds(pl.multiple_of(place.x * (columns // 2), 128), columns // 2)
        self.other_columns = pl.ds(
            pl.multiple_of((1 - place.x) * (columns // 2), 128), columns // 2
        )
        self.my_half = pl.multiple_of(place.near * half, 16)
        self.my_quarter = pl.multiple_of(place.near * half + place.far * quarter, 16)

    def remote(self, stage, source, target, k=0):
        return pltpu.make_async_remote_copy(
            src_ref=source,
            dst_ref=target,
            send_sem=self.send_at(stage, k),
            recv_sem=self.receive_at(stage, k),
            device_id=self.place.partner[stage.split("_")[0]],
            device_id_type=MESH,
        )

    def locals(self):
        return [
            pltpu.make_async_copy(
                self.source(2 * k + self.place.core), self.own.at[k], self.local(k)
            )
            for k in range(2)
        ]

    def copies(self, stage):
        place, rows = self.place, self.rows
        half, quarter = rows // 2, rows // 4
        if stage == "core":
            return [
                self.remote(
                    stage, self.source(2 * k + 1 - place.core), self.from_core.at[k], k
                )
                for k in range(2)
            ]
        if stage == "y":
            return [self.remote(stage, self.from_core.at[1 - place.y], self.from_y)]
        if stage == "x":
            return [self.remote(stage, self.from_y.at[:, self.other_columns], self.from_x)]
        if stage == "near":
            other = pl.ds(pl.multiple_of((1 - place.near) * half, 16), half)
            return [self.remote(stage, self.from_x.at[other, :], self.from_near)]
        if stage == "far":
            other = pl.ds(pl.multiple_of((1 - place.far) * quarter, 16), quarter)
            return [self.remote(stage, self.from_near.at[other, :], self.from_far)]
        if stage == "far_back":
            mine = self.full.at[pl.ds(self.my_quarter, quarter), self.my_columns]
            return [self.remote(stage, self.from_far, mine)]
        if stage == "near_back":
            mine = self.full.at[pl.ds(self.my_half, half), self.my_columns]
            return [self.remote(stage, mine, mine)]
        mine = self.full.at[:, self.my_columns]
        return [self.remote(stage, mine, mine)]

    def start(self, stage):
        if stage == "core":
            for copy in self.locals():
                copy.start()
        for copy in self.copies(stage):
            copy.start()

    def finish(self, stage):
        place, rows = self.place, self.rows
        half, quarter = rows // 2, rows // 4
        for copy in self.copies(stage):
            copy.wait_recv()
        if stage == "core":
            for copy in self.locals():
                copy.wait()
            for k in range(2):
                add_rows(
                    lambda at: self.from_core.at[k, at, :], lambda at: self.own.at[k, at, :], rows
                )
        elif stage == "y":
            add_rows(
                lambda at: self.from_y.at[at, :],
                lambda at: self.from_core.at[place.y, at, :],
                rows,
            )
        elif stage == "x":
            add_rows(
                lambda at: self.from_x.at[at, :],
                lambda at: self.from_y.at[at, self.my_columns],
                rows,
            )
        elif stage == "near":
            add_rows(
                lambda at: self.from_near.at[at, :],
                lambda at: self.from_x.at[
                    pl.ds(pl.multiple_of(at.start + self.my_half, 16), SUM_ROWS), :
                ],
                half,
            )
        elif stage == "far":
            begin = place.far * quarter
            add_rows(
                lambda at: self.from_far.at[at, :],
                lambda at: self.from_near.at[
                    pl.ds(pl.multiple_of(at.start + begin, 16), SUM_ROWS), :
                ],
                quarter,
            )

            def step(i, carry):
                at = pl.ds(pl.multiple_of(i * SUM_ROWS, 16), SUM_ROWS)
                to = pl.ds(pl.multiple_of(i * SUM_ROWS + self.my_quarter, 16), SUM_ROWS)
                self.full[to, self.my_columns] = self.from_far[at, :]
                return carry

            lax.fori_loop(0, quarter // SUM_ROWS, step, 0)

    def close(self, stages):
        for stage in stages:
            for copy in self.copies(stage):
                copy.wait_send()


def chunk_buffers(rows, columns):
    buffer = lambda *shape: pltpu.VMEM(shape, BF16)
    return [
        buffer(2, rows, columns),
        buffer(2, rows, columns),
        buffer(rows, columns),
        buffer(rows, columns // 2),
        buffer(rows // 2, columns // 2),
        buffer(rows // 4, columns // 2),
        buffer(rows, columns),
    ]


def grad_chunks():
    quarter = MODEL_WIDTH // 4
    return [
        (0, MODEL_WIDTH, 0, 0, MODEL_WIDTH // 2, MODEL_WIDTH),
        (0, MODEL_WIDTH, MODEL_WIDTH // 2, 0, MODEL_WIDTH // 2, MODEL_WIDTH),
        (1, quarter, 0, 0, quarter, FF // 2),
        (1, quarter, 0, FF // 2, quarter, FF // 2),
        (2, quarter, 0, 0, quarter, MODEL_WIDTH),
        (3, quarter, 0, 0, quarter, MODEL_WIDTH),
        (4, quarter, 0, 0, quarter, MODEL_WIDTH),
        (5, quarter, 0, 0, quarter, MODEL_WIDTH),
    ]


def finish_kernel(tokens_ref, small_ref, *refs):
    chunks = grad_chunks()
    grads, refs = refs[:6], refs[6:]
    tokens_out, small_out, refs = refs[0], refs[1], refs[2:]
    outs, refs = refs[:6], refs[6:]
    buffers, refs = refs[: 7 * len(chunks)], refs[7 * len(chunks) :]
    (
        send,
        receive,
        local,
        token_send,
        token_receive,
        token_local,
        small_core,
        small_y,
        small_all,
        small_send,
        small_receive,
    ) = refs
    place = Place()
    place.greet()
    kept = pltpu.make_async_copy(
        tokens_ref.at[place.seq], tokens_out.at[place.seq], token_local
    )
    kept.start()
    moved = []
    for k in range(1, SG):
        to = (place.seq + k) % SG
        copy = pltpu.make_async_remote_copy(
            src_ref=tokens_ref.at[to],
            dst_ref=tokens_out.at[place.seq],
            send_sem=token_send.at[k - 1],
            recv_sem=token_receive.at[k - 1],
            device_id=(to, place.dp),
            device_id_type=MESH,
        )
        copy.start()
        moved.append(copy)

    def small_copy(source, target, slot, device):
        return pltpu.make_async_remote_copy(
            src_ref=source,
            dst_ref=target,
            send_sem=small_send.at[slot],
            recv_sem=small_receive.at[slot],
            device_id=device,
            device_id_type=MESH,
        )

    core_copies = [
        small_copy(
            small_ref.at[2 * k + 1 - place.core], small_core.at[k], k, place.partner["core"]
        )
        for k in range(2)
    ]
    for copy in core_copies:
        copy.start()

    def chunk_of(index):
        which, owner_rows, row, column, rows, columns = chunks[index]

        def source(owner):
            begin = pl.multiple_of(owner * owner_rows + row, 16)
            return grads[which].at[pl.ds(begin, rows), pl.ds(column, columns)]

        return Chunk(
            place,
            index,
            source,
            rows,
            columns,
            buffers[7 * index : 7 * index + 7],
            send,
            receive,
            local,
        )

    work = [chunk_of(i) for i in range(len(chunks))]
    small_copies = []
    for tick in range(len(work) + len(STAGES)):
        for s in reversed(range(len(STAGES) + 1)):
            i = tick - s
            if 0 <= i < len(work):
                if s > 0:
                    work[i].finish(STAGES[s - 1])
                if s < len(STAGES):
                    work[i].start(STAGES[s])
        if tick == 0:
            for k, copy in enumerate(core_copies):
                copy.wait_recv()
                small_core[k] += small_ref[2 * k + place.core]
            y_copy = small_copy(
                small_core.at[1 - place.y], small_y, 2, place.partner["y"]
            )
            y_copy.start()
        if tick == 1:
            y_copy.wait_recv()
            small_all[place.seq] = small_core[place.y] + small_y[...]
            for k, device in enumerate(place.peers()):
                copy = small_copy(
                    small_all.at[place.seq], small_all.at[place.seq], 3 + k, device
                )
                copy.start()
                small_copies.append(copy)
    for copy in small_copies:
        copy.wait_recv()
    total = small_all[0]
    for k in range(1, SG):
        total = total + small_all[k]
    small_out[...] = total
    for i, item in enumerate(work):
        which, _, row, column, rows, columns = chunks[i]
        outs[which][row : row + rows, column : column + columns] = item.full[...]
        item.close(STAGES)
    for copy in [*core_copies, y_copy, *small_copies]:
        copy.wait_send()
    for copy in moved:
        copy.wait()
    kept.wait()


def finish(tokens, small, grads):
    anywhere = pl.BlockSpec(memory_space=pl.ANY)
    chunks = grad_chunks()
    quarter = MODEL_WIDTH // 4
    shapes = [
        (MODEL_WIDTH, MODEL_WIDTH),
        (quarter, FF),
        *[(quarter, MODEL_WIDTH)] * 4,
    ]
    count = len(chunks)
    small_shape = (SMALL_ROWS, SMALL_COLUMNS)
    inside = pl.BlockSpec(memory_space=pltpu.VMEM)
    return pl.pallas_call(
        finish_kernel,
        in_specs=[anywhere, inside, *[anywhere] * 6],
        out_specs=[anywhere, inside, *[inside] * 6],
        out_shape=[
            jax.ShapeDtypeStruct(tokens.shape, BF16),
            jax.ShapeDtypeStruct(small_shape, F32),
            *[jax.ShapeDtypeStruct(shape, BF16) for shape in shapes],
        ],
        scratch_shapes=[
            *[buffer for chunk in chunks for buffer in chunk_buffers(*chunk[4:])],
            pltpu.SemaphoreType.DMA((count, 16)),
            pltpu.SemaphoreType.DMA((count, 16)),
            pltpu.SemaphoreType.DMA((count, 2)),
            pltpu.SemaphoreType.DMA((SG - 1,)),
            pltpu.SemaphoreType.DMA((SG - 1,)),
            pltpu.SemaphoreType.DMA,
            pltpu.VMEM((2, *small_shape), F32),
            pltpu.VMEM(small_shape, F32),
            pltpu.VMEM((SG, *small_shape), F32),
            pltpu.SemaphoreType.DMA((SG + 2,)),
            pltpu.SemaphoreType.DMA((SG + 2,)),
        ],
        compiler_params=pltpu.CompilerParams(
            collective_id=3, has_side_effects=True, vmem_limit_bytes=56 * 2**20
        ),
        name="finish",
    )(tokens, small, *grads)


def swap_halves(value, axis):
    first, second = jnp.split(value, 2, axis=axis)
    return jnp.concatenate([second, first], axis=axis)


def pair_maps(relative, table):
    relative = relative.reshape(PAIRS, 2, HEAD_SIZE, HEAD_SIZE)
    nothing = jnp.zeros((PAIRS, HEAD_SIZE, HEAD_SIZE), F32)
    turned = swap_halves(relative, 3)

    def crossed(value):
        top = jnp.concatenate([nothing, value[:, 0]], axis=2)
        bottom = jnp.concatenate([value[:, 1], nothing], axis=2)
        return jnp.concatenate([top, bottom], axis=1)

    plain, swapped = crossed(relative), crossed(turned)
    table = table.reshape(PAIRS, 2, 2, HEAD_SIZE)
    columns = jnp.arange(LANES)
    wanted = ((columns >= 3) & (columns < 6)).astype(F32)
    kinds = []
    for h in range(2):
        for b in (1, 0):
            vector = table[:, h, b]
            zero = jnp.zeros_like(vector)
            full = jnp.concatenate([vector, zero] if h == 0 else [zero, vector], axis=1)
            kinds.append(full[:, :, None] * wanted[None, None, :])
    return plain, swapped, kinds


def sequence_body(
    tokens,
    segments,
    token_types,
    cotangent,
    query_weight,
    key_weight,
    value_weight,
    output_weight,
    inner_weight,
    outer_weight,
    value_bias,
    output_bias,
    inner_bias,
    outer_bias,
    attention_norm_gain,
    first_shift,
    second_gain,
    second_shift,
    content_bias,
    position_bias,
    type_bias,
    relative_kernel,
    type_embed,
):
    owners = lax.axis_size("dp")
    part = MODEL_WIDTH // owners
    low = lambda value: value.astype(BF16)
    even_segments, odd_segments = segments[:, 0::2], segments[:, 1::2]
    labels = jnp.stack(
        [
            segments[:, :128],
            segments[:, 128:],
            token_types[:, :128],
            token_types[:, 128:],
            even_segments,
            token_types[:, 0::2],
            (even_segments == odd_segments).astype(jnp.int32),
        ],
        axis=1,
    )
    rows = lax.all_to_all(tokens, "seq", split_axis=0, concat_axis=0, tiled=True)
    labels, _ = lax.optimization_barrier((labels, rows))
    labels = lax.all_to_all(labels, "seq", split_axis=0, concat_axis=0, tiled=True)
    small = jnp.concatenate(
        [
            low(value).reshape(-1)
            for value in (
                value_bias,
                output_bias,
                outer_bias,
                attention_norm_gain,
                first_shift,
                second_gain,
                second_shift,
                content_bias,
                position_bias,
                type_bias,
                inner_bias,
                relative_kernel,
                type_embed,
            )
        ]
    )
    small = lax.all_gather(small.reshape(1, -1), "dp", axis=0, tiled=True)
    first = jnp.concatenate([low(query_weight), low(key_weight), low(value_weight)], axis=1)
    first = lax.all_gather(first, "dp", axis=0, tiled=True)
    next_weights = jnp.concatenate([low(output_weight), low(inner_weight)], axis=1)
    next_weights = lax.all_gather(next_weights, "dp", axis=0, tiled=True)
    outer_low = lax.all_gather(low(outer_weight), "dp", axis=0, tiled=True)

    def take(start, size):
        return small[:, start : start + size].astype(F32)

    vectors = [take(part * j, part).reshape(1, MODEL_WIDTH) for j in range(10)]
    (
        value_add,
        output_add,
        outer_add,
        gain_one,
        shift_one,
        gain_two,
        shift_two,
        content_add,
        position_add,
        type_add,
    ) = vectors
    place = 10 * part
    inner_add = take(place, FF // owners).reshape(1, FF)
    place += FF // owners
    kernel_size = HEAD_COUNT * HEAD_SIZE * HEAD_SIZE // owners
    relative = take(place, kernel_size).reshape(HEAD_COUNT, HEAD_SIZE, HEAD_SIZE)
    place += kernel_size
    table = take(place, HEAD_COUNT * 2 * HEAD_SIZE // owners).reshape(HEAD_COUNT, 2, HEAD_SIZE)

    segment_row = labels[:, 0:2].reshape(LEN)
    type_row = labels[:, 2:4].reshape(LEN)
    query_segments = labels[:, 4].reshape(PQ)
    query_types = labels[:, 5].reshape(PQ)
    pair_same = labels[:, 6] > 0

    first_doc, last_doc = segment_row[0], segment_row[LEN - 1]
    first_type = type_row[0]
    last_type = jnp.max(jnp.where(type_row == first_type, -1, type_row))

    def classes(values, start, end):
        return jnp.where(values == start, 0, jnp.where(values == end, 2, 1))[:, None]

    columns = jnp.arange(LANES, dtype=jnp.int32)[None, :]
    key_side = (
        (columns == classes(segment_row, first_doc, last_doc))
        | (columns == 3 + classes(type_row, first_type, last_type))
        | ((columns >= 6) & (columns < 9))
    ).astype(BF16)
    query_docs = classes(query_segments, first_doc, last_doc)
    query_side = jnp.where(
        columns < 3,
        jnp.where(columns == query_docs, 0.0, FAR),
        (columns == 3 + classes(query_types, first_type, last_type)).astype(F32),
    )
    frequency = frequencies()
    key_angle = jnp.arange(LEN, dtype=F32)[:, None] * frequency[None, :]
    phase = jnp.concatenate([jnp.cos(key_angle), jnp.sin(key_angle)], axis=1).astype(BF16)
    phase = jnp.concatenate([phase, phase], axis=1)
    query_angle = (2.0 * jnp.arange(PQ, dtype=F32))[:, None] * frequency[None, :]
    cos, sin = jnp.cos(query_angle), jnp.sin(query_angle)
    cosm = jnp.concatenate([cos, -cos, cos, -cos], axis=1)
    sinm = jnp.concatenate([sin, sin, sin, sin], axis=1)

    plain, swapped, kinds = pair_maps(relative, table)
    stacked = jnp.concatenate([plain, swapped, *kinds], axis=2)
    maps = low(jnp.concatenate([stacked, stacked], axis=1))
    pair_vector = lambda vector: vector.reshape(PAIRS, 1, LANES)
    position_pairs, type_pairs = pair_vector(position_add), pair_vector(type_add)
    product = partial(jnp.einsum, "pke,pef->pkf", precision=highest)
    map_add = jnp.concatenate(
        [
            product(position_pairs, stacked[:, :, : 2 * LANES]),
            product(type_pairs, stacked[:, :, 2 * LANES :]),
        ],
        axis=2,
    )
    map_back = low(
        jnp.concatenate([plain.transpose(0, 2, 1), swapped.transpose(0, 2, 1)], axis=1)
    )
    table_pairs = table.reshape(PAIRS, 2, 2, HEAD_SIZE).transpose(0, 2, 1, 3)
    table_pairs = table_pairs.reshape(PAIRS, 2, LANES)
    row_terms = jnp.concatenate(
        [position_pairs, type_pairs, table_pairs, jnp.zeros((PAIRS, 4, LANES), F32)], axis=1
    )

    block = rows.shape[1]
    pooled_block = block // 2
    at = jnp.arange(block, dtype=jnp.int32)[None, None, :]
    want = 2 * jnp.arange(pooled_block, dtype=jnp.int32)[None, :, None]
    half = jnp.where(pair_same, 0.5, 1.0)[:, :, None]
    other_half = jnp.where(pair_same, 0.5, 0.0)[:, :, None]
    pool = jnp.where(at == want, half, jnp.where(at == want + 1, other_half, 0.0)).astype(BF16)

    pooled = jnp.einsum("cpt,ctd->cpd", pool, rows, preferred_element_type=F32)
    pooled = pooled.reshape(PQ, MODEL_WIDTH)
    pooled_low = low(pooled)
    token_rows = rows.reshape(LEN, MODEL_WIDTH)
    query = mm(pooled_low, first[:, :MODEL_WIDTH])
    pair_add = jnp.concatenate([jnp.zeros_like(value_add), value_add], axis=1)
    pairs = low(mm(token_rows, first[:, MODEL_WIDTH:]) + pair_add)
    mixture, join = attend_forward(
        query, pairs, maps, map_add, content_add, query_side, key_side, phase, cosm, sinm
    )

    cotangent, _ = lax.optimization_barrier((cotangent, labels))
    cotangent = lax.all_to_all(cotangent, "seq", split_axis=0, concat_axis=0, tiled=True)
    upstream = cotangent.reshape(PQ, MODEL_WIDTH)

    output_low, inner_low = next_weights[:, :MODEL_WIDTH], next_weights[:, MODEL_WIDTH:]
    vectors = jnp.concatenate(
        [
            output_add,
            outer_add,
            gain_one,
            shift_one,
            gain_two,
            shift_two,
            jnp.zeros((2, MODEL_WIDTH), F32),
        ],
        axis=0,
    )
    (
        output,
        grad_mixture,
        grad_first,
        grad_outer_weight,
        grad_inner_weight,
        grad_output_weight,
        row_sums,
        grad_inner_bias,
    ) = mlp(
        mixture, pooled, upstream, output_low, inner_low, outer_low, vectors, inner_add
    )
    (
        grad_output_bias,
        grad_outer_bias,
        grad_gain_one,
        grad_shift_one,
        grad_gain_two,
        grad_shift_two,
    ) = [row_sums[j] for j in range(6)]
    output = output.reshape(SG, PQ // SG, MODEL_WIDTH)
    output = lax.all_to_all(output, "seq", split_axis=0, concat_axis=0, tiled=True)

    grad_query, grad_key, grad_value, sums, grad_map = attend_backward(
        join,
        pairs,
        query,
        mixture,
        grad_mixture,
        map_back,
        row_terms,
        query_side,
        key_side,
        phase,
        cosm,
        sinm,
    )
    grad_pooled = grad_first + mm(grad_query, first[:, :MODEL_WIDTH], NT)
    grad_direct = mm(grad_key, first[:, MODEL_WIDTH : 2 * MODEL_WIDTH], NT)
    grad_direct = grad_direct + mm(grad_value, first[:, 2 * MODEL_WIDTH :], NT)
    high_pooled, low_pooled = split(grad_pooled.reshape(SG, pooled_block, MODEL_WIDTH))
    spread = partial(jnp.einsum, "cpt,cpd->ctd", preferred_element_type=F32)
    spread_sum = spread(pool, high_pooled) + spread(pool, low_pooled)
    grad_tokens = low(grad_direct.reshape(SG, block, MODEL_WIDTH) + spread_sum)
    grad_query_weight = low(mm(pooled_low, grad_query, TN))
    grad_key_weight = low(mm(token_rows, grad_key, TN))
    grad_value_weight = low(mm(token_rows, grad_value, TN))

    crossed = grad_map.reshape(PAIRS, 2, HEAD_SIZE, 2, 2, HEAD_SIZE)
    grad_relative = jnp.stack(
        [
            crossed[:, h, :, 0, 1 - h] + swap_halves(crossed[:, h, :, 1, 1 - h], 2)
            for h in range(2)
        ],
        axis=1,
    ).reshape(HEAD_COUNT, HEAD_SIZE, HEAD_SIZE)
    grad_table = sums[:, 3:5].reshape(PAIRS, 2, 2, HEAD_SIZE).transpose(0, 2, 1, 3)
    sum_row = lambda j: sums[:, j].reshape(owners, -1)
    small_grads = jnp.concatenate(
        [
            value.reshape(owners, -1)
            for value in (
                sum_row(5),
                grad_output_bias,
                grad_outer_bias,
                grad_gain_one,
                grad_shift_one,
                grad_gain_two,
                grad_shift_two,
                sum_row(0),
                sum_row(1),
                sum_row(2),
                grad_inner_bias,
                grad_relative,
                grad_table,
            )
        ],
        axis=1,
    )
    count = small_grads.shape[1]
    room = SMALL_ROWS * SMALL_COLUMNS
    small_grads = jnp.pad(small_grads, ((0, 0), (0, room - count)))
    grad_tokens, small_owned, *owned = finish(
        grad_tokens,
        small_grads.reshape(owners, SMALL_ROWS, SMALL_COLUMNS),
        [
            grad_outer_weight,
            grad_inner_weight,
            grad_output_weight,
            grad_query_weight,
            grad_key_weight,
            grad_value_weight,
        ],
    )
    owned_outer, owned_inner, owned_output, *squares = [value.astype(F32) for value in owned]
    squares.append(owned_output)
    small_owned = small_owned.reshape(-1)
    place = 0
    pieces = []
    for size in [part] * 10 + [FF // owners, kernel_size, HEAD_COUNT * 2 * HEAD_SIZE // owners]:
        pieces.append(small_owned[place : place + size])
        place += size
    heads = HEAD_COUNT // owners
    return (
        output.reshape(SG, PQ // SG, MODEL_WIDTH),
        grad_tokens,
        squares[0],
        squares[1],
        squares[2],
        squares[3],
        owned_inner,
        owned_outer,
        pieces[0],
        pieces[1],
        pieces[10],
        pieces[2],
        pieces[3],
        pieces[4],
        pieces[5],
        pieces[6],
        pieces[7].reshape(heads, HEAD_SIZE),
        pieces[8].reshape(heads, HEAD_SIZE),
        pieces[9].reshape(heads, HEAD_SIZE),
        pieces[11].reshape(heads, HEAD_SIZE, HEAD_SIZE),
        pieces[12].reshape(heads, 2, HEAD_SIZE),
    )


def solution(mesh):
    whole = mesh.shape["seq"] == SG and mesh.shape["dp"] == 4
    return jax.shard_map(
        sequence_body if whole else body,
        mesh=mesh,
        in_specs=(
            P("dp", "seq", None),
            P("dp", "seq"),
            P("dp", "seq"),
            P("dp", "seq", None),
            P("dp", None),
            P("dp", None),
            P("dp", None),
            P("dp", None),
            P("dp", None),
            P("dp", None),
            P("dp"),
            P("dp"),
            P("dp"),
            P("dp"),
            P("dp"),
            P("dp"),
            P("dp"),
            P("dp"),
            P("dp", None),
            P("dp", None),
            P("dp", None),
            P("dp", None, None),
            P("dp", None, None),
        ),
        out_specs=(
            P("dp", "seq", None),
            P("dp", "seq", None),
            P("dp", None),
            P("dp", None),
            P("dp", None),
            P("dp", None),
            P("dp", None),
            P("dp", None),
            P("dp"),
            P("dp"),
            P("dp"),
            P("dp"),
            P("dp"),
            P("dp"),
            P("dp"),
            P("dp"),
            P("dp", None),
            P("dp", None),
            P("dp", None),
            P("dp", None, None),
            P("dp", None, None),
        ),
        check_vma=False,
    )
```

```python
from functools import partial
import math

import jax
import jax.numpy as jnp
import numpy as np
from jax import lax
from jax.experimental import pallas as pl
from jax.experimental.pallas import tpu as pltpu
from jax.sharding import PartitionSpec as P

MODEL_WIDTH = 768
HEAD_COUNT = 12
HEAD_SIZE = 64
LEN = 2048
SG = 8
PQ = 1024


highest = lax.Precision.HIGHEST
norm_eps = 1e-05
masked_score = -1e30


def frequencies():
    half_width = HEAD_SIZE // 2
    return jnp.exp(jnp.arange(half_width, dtype=jnp.float32) * (-math.log(10000.0) / half_width))


def norm_forward(inputs, gains, shifts):
    row_mean = jnp.mean(inputs, axis=-1, keepdims=True)
    centred = inputs - row_mean
    inverse = lax.rsqrt(jnp.mean(centred * centred, axis=-1, keepdims=True) + norm_eps)
    normed = centred * inverse
    return (normed * gains + shifts, normed, inverse)


def norm_backward(upstream, normed, inverse, gains):
    scaled = upstream * gains
    along = jnp.mean(scaled * normed, axis=-1, keepdims=True)
    centre = jnp.mean(scaled, axis=-1, keepdims=True)
    return inverse * (scaled - centre - normed * along)


def doc_masks(segment_row, type_row):
    same_document = segment_row[0::2][:, None] == segment_row[None, :]
    same_type = type_row[0::2][:, None] == type_row[None, :]
    return (same_document, same_type)


def score_block(query_row, type_row_terms, pair_row, key_phase, same_document, same_type):
    key_join = jnp.concatenate([pair_row[:, :HEAD_SIZE], key_phase], axis=-1)
    raw_score = lax.dot_general(
        query_row, key_join, (((1,), (1,)), ((), ())), preferred_element_type=jnp.float32
    )
    type_float = type_row_terms.astype(jnp.float32)
    raw_score = raw_score + jnp.where(same_type, type_float[:, 1:2], type_float[:, 0:1])
    return (jnp.where(same_document, raw_score * HEAD_SIZE ** (-0.5), masked_score), key_join)


def body(
    tokens,
    segments,
    token_types,
    cotangent,
    query_weight,
    key_weight,
    value_weight,
    output_weight,
    inner_weight,
    outer_weight,
    value_bias,
    output_bias,
    inner_bias,
    outer_bias,
    attention_norm_gain,
    first_shift,
    second_gain,
    second_shift,
    content_bias,
    position_bias,
    type_bias,
    relative_kernel,
    type_embed,
):
    local_tokens = tokens.shape[1]
    local_pooled = local_tokens // 2
    group_size = lax.axis_size("seq")
    shard_rank = lax.axis_index("seq")
    item_count = SG * HEAD_COUNT // group_size
    half_width = HEAD_SIZE // 2
    score_scale = HEAD_SIZE ** (-0.5)
    frequency = frequencies()
    duplicate_params = (
        lax.all_gather(query_weight.astype(jnp.bfloat16), "dp", axis=0, tiled=True),
        lax.all_gather(key_weight.astype(jnp.bfloat16), "dp", axis=0, tiled=True),
        lax.all_gather(value_weight.astype(jnp.bfloat16), "dp", axis=0, tiled=True),
        lax.all_gather(output_weight.astype(jnp.bfloat16), "dp", axis=0, tiled=True),
        lax.all_gather(inner_weight.astype(jnp.bfloat16), "dp", axis=0, tiled=True),
        lax.all_gather(outer_weight.astype(jnp.bfloat16), "dp", axis=0, tiled=True),
        lax.all_gather(value_bias.astype(jnp.bfloat16), "dp", axis=0, tiled=True),
        lax.all_gather(output_bias.astype(jnp.bfloat16), "dp", axis=0, tiled=True),
        lax.all_gather(inner_bias.astype(jnp.bfloat16), "dp", axis=0, tiled=True),
        lax.all_gather(outer_bias.astype(jnp.bfloat16), "dp", axis=0, tiled=True),
        lax.all_gather(attention_norm_gain.astype(jnp.bfloat16), "dp", axis=0, tiled=True),
        lax.all_gather(first_shift.astype(jnp.bfloat16), "dp", axis=0, tiled=True),
        lax.all_gather(second_gain.astype(jnp.bfloat16), "dp", axis=0, tiled=True),
        lax.all_gather(second_shift.astype(jnp.bfloat16), "dp", axis=0, tiled=True),
        lax.all_gather(content_bias.astype(jnp.bfloat16), "dp", axis=0, tiled=True),
        lax.all_gather(position_bias.astype(jnp.bfloat16), "dp", axis=0, tiled=True),
        lax.all_gather(type_bias.astype(jnp.bfloat16), "dp", axis=0, tiled=True),
        lax.all_gather(relative_kernel.astype(jnp.bfloat16), "dp", axis=0, tiled=True),
        lax.all_gather(type_embed.astype(jnp.bfloat16), "dp", axis=0, tiled=True),
    )
    value_add = duplicate_params[6].astype(jnp.float32)
    output_add = duplicate_params[7].astype(jnp.float32)
    inner_add = duplicate_params[8].astype(jnp.float32)
    outer_add = duplicate_params[9].astype(jnp.float32)
    gain_one = duplicate_params[10].astype(jnp.float32)
    shift_one = duplicate_params[11].astype(jnp.float32)
    gain_two = duplicate_params[12].astype(jnp.float32)
    shift_two = duplicate_params[13].astype(jnp.float32)
    content_add = duplicate_params[14].astype(jnp.float32)[None, :, None, :]
    position_add = duplicate_params[15].astype(jnp.float32)[None, :, None, :]
    type_add = duplicate_params[16].astype(jnp.float32)[None, :, None, :]
    relative = duplicate_params[17].astype(jnp.float32)
    type_table = duplicate_params[18].astype(jnp.float32)
    whole_segments, whole_types = (
        lax.all_gather(segments, "seq", axis=1, tiled=True),
        lax.all_gather(token_types, "seq", axis=1, tiled=True),
    )
    first_rows = tokens[:, 0::2].astype(jnp.float32)
    second = tokens[:, 1::2].astype(jnp.float32)
    pair_same = (segments[:, 0::2] == segments[:, 1::2])[..., None]
    pooled = jnp.where(pair_same, (first_rows + second) * 0.5, first_rows)
    pooled_low = pooled.astype(jnp.bfloat16)
    queries = jnp.einsum(
        "spd,dhe->shpe",
        pooled_low,
        duplicate_params[0].reshape(MODEL_WIDTH, HEAD_COUNT, HEAD_SIZE),
        preferred_element_type=jnp.float32,
    )
    key_rows = jnp.einsum(
        "ukf,fra->urka",
        tokens,
        duplicate_params[1].reshape(MODEL_WIDTH, HEAD_COUNT, HEAD_SIZE),
        preferred_element_type=jnp.float32,
    )
    value_rows = (
        jnp.einsum(
            "ukf,fra->urka",
            tokens,
            duplicate_params[2].reshape(MODEL_WIDTH, HEAD_COUNT, HEAD_SIZE),
            preferred_element_type=jnp.float32,
        )
        + value_add.reshape(HEAD_COUNT, HEAD_SIZE)[None, :, None, :]
    )
    pair_rows = (
        jnp.concatenate([key_rows, value_rows], axis=-1)
        .astype(jnp.bfloat16)
        .reshape(SG * HEAD_COUNT, local_tokens, 2 * HEAD_SIZE)
    )
    shifted = queries + position_add
    relative_terms = jnp.einsum("shpe,hef->shpf", shifted, relative, precision=highest)
    pooled_place = 2.0 * (
        shard_rank * local_pooled + jnp.arange(local_pooled, dtype=jnp.int32)
    ).astype(jnp.float32)
    query_angle = pooled_place[:, None] * frequency[None, :]
    query_cos = jnp.cos(query_angle)
    query_sin = jnp.sin(query_angle)
    relative_cos = relative_terms[..., :half_width]
    relative_sin = relative_terms[..., half_width:]
    position = jnp.concatenate(
        [
            relative_cos * query_cos + relative_sin * query_sin,
            relative_cos * query_sin - relative_sin * query_cos,
        ],
        axis=-1,
    )
    query_join = (
        jnp.concatenate([queries + content_add, position], axis=-1)
        .astype(jnp.bfloat16)
        .reshape(SG * HEAD_COUNT, local_pooled, 2 * HEAD_SIZE)
    )
    typed = queries + type_add
    type_terms = (
        jnp.einsum("shpe,hbe->shpb", typed, type_table, precision=highest)
        .astype(jnp.bfloat16)
        .reshape(SG * HEAD_COUNT, local_pooled, 2)
    )
    query_heads, type_heads, pair_heads = (
        lax.all_to_all(query_join, "seq", split_axis=0, concat_axis=1, tiled=True),
        lax.all_to_all(type_terms, "seq", split_axis=0, concat_axis=1, tiled=True),
        lax.all_to_all(pair_rows, "seq", split_axis=0, concat_axis=1, tiled=True),
    )
    item_rows = (shard_rank * item_count + jnp.arange(item_count, dtype=jnp.int32)) // HEAD_COUNT
    item_segments = whole_segments[item_rows]
    item_types = whole_types[item_rows]
    key_angle = jnp.arange(LEN, dtype=jnp.float32)[:, None] * frequency[None, :]
    key_phase = jnp.concatenate([jnp.cos(key_angle), jnp.sin(key_angle)], axis=-1).astype(
        jnp.bfloat16
    )

    def attend(packed):
        query_row, type_row_terms, pair_row, segment_row, type_row = packed
        same_document, same_type = doc_masks(segment_row, type_row)
        scores, key_join = score_block(
            query_row, type_row_terms, pair_row, key_phase, same_document, same_type
        )
        row_max = jnp.max(scores, axis=1, keepdims=True)
        exponent = jnp.exp(scores - row_max)
        row_total = jnp.sum(exponent, axis=1, keepdims=True)
        weights = exponent / row_total
        mixture = jnp.dot(
            weights.astype(jnp.bfloat16),
            pair_row[:, HEAD_SIZE:],
            preferred_element_type=jnp.float32,
        )
        return (mixture.astype(jnp.bfloat16), row_max + jnp.log(row_total))

    mixed_heads, log_totals = lax.map(
        attend, (query_heads, type_heads, pair_heads, item_segments, item_types)
    )
    mixed_tokens = lax.all_to_all(
        mixed_heads.reshape(item_count, PQ // 2, 2 * HEAD_SIZE),
        "seq",
        split_axis=1,
        concat_axis=0,
        tiled=True,
    ).reshape(SG, HEAD_COUNT, local_pooled, HEAD_SIZE)
    attention = (
        jnp.einsum(
            "shpe,hed->spd",
            mixed_tokens,
            duplicate_params[3].reshape(HEAD_COUNT, HEAD_SIZE, MODEL_WIDTH),
            preferred_element_type=jnp.float32,
        )
        + output_add
    )
    hidden, normed_one, inverse_one = norm_forward(pooled + attention, gain_one, shift_one)
    hidden_low = hidden.astype(jnp.bfloat16)
    expanded = (
        jnp.einsum(
            "spd,df->spf", hidden_low, duplicate_params[4], preferred_element_type=jnp.float32
        )
        + inner_add
    )
    active = jax.nn.gelu(expanded, approximate=True).astype(jnp.bfloat16)
    branch = (
        jnp.einsum("spf,fd->spd", active, duplicate_params[5], preferred_element_type=jnp.float32)
        + outer_add
    )
    result, normed_two, inverse_two = norm_forward(hidden + branch, gain_two, shift_two)
    output = result.astype(jnp.bfloat16)
    again = (
        lax.all_gather(query_weight.astype(jnp.bfloat16), "dp", axis=0, tiled=True),
        lax.all_gather(key_weight.astype(jnp.bfloat16), "dp", axis=0, tiled=True),
        lax.all_gather(value_weight.astype(jnp.bfloat16), "dp", axis=0, tiled=True),
        lax.all_gather(output_weight.astype(jnp.bfloat16), "dp", axis=0, tiled=True),
        lax.all_gather(inner_weight.astype(jnp.bfloat16), "dp", axis=0, tiled=True),
        lax.all_gather(outer_weight.astype(jnp.bfloat16), "dp", axis=0, tiled=True),
        lax.all_gather(attention_norm_gain.astype(jnp.bfloat16), "dp", axis=0, tiled=True),
        lax.all_gather(second_gain.astype(jnp.bfloat16), "dp", axis=0, tiled=True),
        lax.all_gather(relative_kernel.astype(jnp.bfloat16), "dp", axis=0, tiled=True),
        lax.all_gather(type_embed.astype(jnp.bfloat16), "dp", axis=0, tiled=True),
    )
    query_back = again[0]
    key_back = again[1]
    value_back = again[2]
    output_back = again[3]
    inner_back = again[4]
    outer_back = again[5]
    gain_one_back = again[6].astype(jnp.float32)
    gain_two_back = again[7].astype(jnp.float32)
    relative_back = again[8].astype(jnp.float32)
    table_back = again[9].astype(jnp.float32)
    grad_result = cotangent.astype(jnp.float32)
    grad_gain_two = jnp.sum(grad_result * normed_two, axis=(0, 1))
    grad_shift_two = jnp.sum(grad_result, axis=(0, 1))
    grad_second = norm_backward(grad_result, normed_two, inverse_two, gain_two_back)
    grad_branch = grad_second.astype(jnp.bfloat16)
    grad_outer_weight = jnp.einsum(
        "spf,spd->fd", active, grad_branch, preferred_element_type=jnp.float32
    )
    grad_outer_bias = jnp.sum(grad_branch.astype(jnp.float32), axis=(0, 1))
    grad_active = jnp.einsum(
        "spd,fd->spf", grad_branch, outer_back, preferred_element_type=jnp.float32
    )
    gelu_value, gelu_pull = jax.vjp(partial(jax.nn.gelu, approximate=True), expanded)
    grad_expanded = gelu_pull(grad_active)[0].astype(jnp.bfloat16)
    grad_inner_weight = jnp.einsum(
        "spd,spf->df", hidden_low, grad_expanded, preferred_element_type=jnp.float32
    )
    grad_inner_bias = jnp.sum(grad_expanded.astype(jnp.float32), axis=(0, 1))
    grad_hidden = grad_second + jnp.einsum(
        "spf,df->spd", grad_expanded, inner_back, preferred_element_type=jnp.float32
    )
    grad_gain_one = jnp.sum(grad_hidden * normed_one, axis=(0, 1))
    grad_shift_one = jnp.sum(grad_hidden, axis=(0, 1))
    grad_first = norm_backward(grad_hidden, normed_one, inverse_one, gain_one_back)
    grad_attention = grad_first.astype(jnp.bfloat16)
    grad_output_weight = jnp.einsum(
        "shpe,spd->hed", mixed_tokens, grad_attention, preferred_element_type=jnp.float32
    ).reshape(MODEL_WIDTH, MODEL_WIDTH)
    grad_output_bias = jnp.sum(grad_attention.astype(jnp.float32), axis=(0, 1))
    grad_mixture = jnp.einsum(
        "spd,hed->shpe",
        grad_attention,
        output_back.reshape(HEAD_COUNT, HEAD_SIZE, MODEL_WIDTH),
        preferred_element_type=jnp.float32,
    ).astype(jnp.bfloat16)
    grad_mixed_heads = lax.all_to_all(
        grad_mixture.reshape(SG * HEAD_COUNT, local_pooled // 2, 2 * HEAD_SIZE),
        "seq",
        split_axis=0,
        concat_axis=1,
        tiled=True,
    ).reshape(item_count, PQ, HEAD_SIZE)

    def attend_back(packed):
        query_row, type_row_terms, pair_row, segment_row, type_row, log_row, grad_row = packed
        same_document, same_type = doc_masks(segment_row, type_row)
        scores, key_join = score_block(
            query_row, type_row_terms, pair_row, key_phase, same_document, same_type
        )
        weights = jnp.exp(scores - log_row)
        grad_weights = lax.dot_general(
            grad_row,
            pair_row[:, HEAD_SIZE:],
            (((1,), (1,)), ((), ())),
            preferred_element_type=jnp.float32,
        )
        row_dot = jnp.sum(grad_weights * weights, axis=1, keepdims=True)
        grad_scores = (weights * (grad_weights - row_dot)).astype(jnp.bfloat16)
        grad_query = (
            jnp.dot(grad_scores, key_join, preferred_element_type=jnp.float32) * score_scale
        ).astype(jnp.bfloat16)
        grad_float = grad_scores.astype(jnp.float32) * score_scale
        grad_same = jnp.sum(jnp.where(same_type, grad_float, 0.0), axis=1)
        grad_other = jnp.sum(jnp.where(same_type, 0.0, grad_float), axis=1)
        grad_kinds = jnp.stack([grad_other, grad_same], axis=-1).astype(jnp.bfloat16)
        grad_keys = (
            lax.dot_general(
                grad_scores,
                query_row[:, :HEAD_SIZE],
                (((0,), (0,)), ((), ())),
                preferred_element_type=jnp.float32,
            )
            * score_scale
        )
        grad_values = lax.dot_general(
            weights.astype(jnp.bfloat16),
            grad_row,
            (((0,), (0,)), ((), ())),
            preferred_element_type=jnp.float32,
        )
        return (
            grad_query,
            grad_kinds,
            jnp.concatenate([grad_keys, grad_values], axis=-1).astype(jnp.bfloat16),
        )

    grad_query_heads, grad_type_heads, grad_pair_heads = lax.map(
        attend_back,
        (
            query_heads,
            type_heads,
            pair_heads,
            item_segments,
            item_types,
            log_totals,
            grad_mixed_heads,
        ),
    )
    grad_query_tok, grad_type_tok, grad_pair_tok = (
        lax.all_to_all(grad_query_heads, "seq", split_axis=1, concat_axis=0, tiled=True),
        lax.all_to_all(grad_type_heads, "seq", split_axis=1, concat_axis=0, tiled=True),
        lax.all_to_all(grad_pair_heads, "seq", split_axis=1, concat_axis=0, tiled=True),
    )
    grad_query_join = grad_query_tok.astype(jnp.float32).reshape(
        SG, HEAD_COUNT, local_pooled, 2 * HEAD_SIZE
    )
    grad_content = grad_query_join[..., :HEAD_SIZE]
    grad_first_half = grad_query_join[..., HEAD_SIZE : HEAD_SIZE + half_width]
    grad_second_half = grad_query_join[..., HEAD_SIZE + half_width :]
    grad_relative_terms = jnp.concatenate(
        [
            grad_first_half * query_cos + grad_second_half * query_sin,
            grad_first_half * query_sin - grad_second_half * query_cos,
        ],
        axis=-1,
    )
    grad_shifted = jnp.einsum(
        "shpf,hef->shpe", grad_relative_terms, relative_back, precision=highest
    )
    grad_relative_kernel = jnp.einsum(
        "shpe,shpf->hef", shifted, grad_relative_terms, precision=highest
    )
    grad_type_terms = grad_type_tok.astype(jnp.float32).reshape(SG, HEAD_COUNT, local_pooled, 2)
    grad_typed = jnp.einsum("shpb,hbe->shpe", grad_type_terms, table_back, precision=highest)
    grad_type_embed = jnp.einsum("shpe,shpb->hbe", typed, grad_type_terms, precision=highest)
    query_rows_gradient = (grad_content + grad_shifted + grad_typed).astype(jnp.bfloat16)
    grad_content_bias = jnp.sum(grad_content, axis=(0, 2))
    grad_position_bias = jnp.sum(grad_shifted, axis=(0, 2))
    grad_type_bias = jnp.sum(grad_typed, axis=(0, 2))
    grad_query_weight = jnp.einsum(
        "spd,shpe->dhe", pooled_low, query_rows_gradient, preferred_element_type=jnp.float32
    ).reshape(MODEL_WIDTH, MODEL_WIDTH)
    grad_pooled = grad_first + jnp.einsum(
        "shpe,dhe->spd",
        query_rows_gradient,
        query_back.reshape(MODEL_WIDTH, HEAD_COUNT, HEAD_SIZE),
        preferred_element_type=jnp.float32,
    )
    grad_pairs = grad_pair_tok.reshape(SG, HEAD_COUNT, local_tokens, 2 * HEAD_SIZE)
    key_rows_gradient = grad_pairs[..., :HEAD_SIZE]
    value_rows_gradient = grad_pairs[..., HEAD_SIZE:]
    grad_key_weight = jnp.einsum(
        "ozb,opzx->bpx", tokens, key_rows_gradient, preferred_element_type=jnp.float32
    ).reshape(MODEL_WIDTH, MODEL_WIDTH)
    grad_value_weight = jnp.einsum(
        "ozb,opzx->bpx", tokens, value_rows_gradient, preferred_element_type=jnp.float32
    ).reshape(MODEL_WIDTH, MODEL_WIDTH)
    grad_value_bias = jnp.sum(value_rows_gradient.astype(jnp.float32), axis=(0, 2)).reshape(
        MODEL_WIDTH
    )
    grad_direct = jnp.einsum(
        "mivt,git->mvg",
        key_rows_gradient,
        key_back.reshape(MODEL_WIDTH, HEAD_COUNT, HEAD_SIZE),
        preferred_element_type=jnp.float32,
    )
    grad_direct = grad_direct + jnp.einsum(
        "mivt,git->mvg",
        value_rows_gradient,
        value_back.reshape(MODEL_WIDTH, HEAD_COUNT, HEAD_SIZE),
        preferred_element_type=jnp.float32,
    )
    pool_first = jnp.where(pair_same, 0.5 * grad_pooled, grad_pooled)
    pool_second = jnp.where(pair_same, 0.5 * grad_pooled, 0.0)
    grad_tokens = (
        grad_direct
        + jnp.stack([pool_first, pool_second], axis=2).reshape(SG, local_tokens, MODEL_WIDTH)
    ).astype(jnp.bfloat16)
    summed = lax.psum(
        (
            grad_query_weight,
            grad_key_weight,
            grad_value_weight,
            grad_output_weight,
            grad_inner_weight,
            grad_outer_weight,
            grad_value_bias,
            grad_output_bias,
            grad_inner_bias,
            grad_outer_bias,
            grad_gain_one,
            grad_shift_one,
            grad_gain_two,
            grad_shift_two,
            grad_content_bias,
            grad_position_bias,
            grad_type_bias,
            grad_relative_kernel,
            grad_type_embed,
        ),
        "seq",
    )
    owned = (
        lax.psum_scatter(
            summed[0].astype(jnp.bfloat16), "dp", scatter_dimension=0, tiled=True
        ).astype(jnp.float32),
        lax.psum_scatter(
            summed[1].astype(jnp.bfloat16), "dp", scatter_dimension=0, tiled=True
        ).astype(jnp.float32),
        lax.psum_scatter(
            summed[2].astype(jnp.bfloat16), "dp", scatter_dimension=0, tiled=True
        ).astype(jnp.float32),
        lax.psum_scatter(
            summed[3].astype(jnp.bfloat16), "dp", scatter_dimension=0, tiled=True
        ).astype(jnp.float32),
        lax.psum_scatter(
            summed[4].astype(jnp.bfloat16), "dp", scatter_dimension=0, tiled=True
        ).astype(jnp.float32),
        lax.psum_scatter(
            summed[5].astype(jnp.bfloat16), "dp", scatter_dimension=0, tiled=True
        ).astype(jnp.float32),
        lax.psum_scatter(
            summed[6].astype(jnp.bfloat16), "dp", scatter_dimension=0, tiled=True
        ).astype(jnp.float32),
        lax.psum_scatter(
            summed[7].astype(jnp.bfloat16), "dp", scatter_dimension=0, tiled=True
        ).astype(jnp.float32),
        lax.psum_scatter(
            summed[8].astype(jnp.bfloat16), "dp", scatter_dimension=0, tiled=True
        ).astype(jnp.float32),
        lax.psum_scatter(
            summed[9].astype(jnp.bfloat16), "dp", scatter_dimension=0, tiled=True
        ).astype(jnp.float32),
        lax.psum_scatter(
            summed[10].astype(jnp.bfloat16), "dp", scatter_dimension=0, tiled=True
        ).astype(jnp.float32),
        lax.psum_scatter(
            summed[11].astype(jnp.bfloat16), "dp", scatter_dimension=0, tiled=True
        ).astype(jnp.float32),
        lax.psum_scatter(
            summed[12].astype(jnp.bfloat16), "dp", scatter_dimension=0, tiled=True
        ).astype(jnp.float32),
        lax.psum_scatter(
            summed[13].astype(jnp.bfloat16), "dp", scatter_dimension=0, tiled=True
        ).astype(jnp.float32),
        lax.psum_scatter(
            summed[14].astype(jnp.bfloat16), "dp", scatter_dimension=0, tiled=True
        ).astype(jnp.float32),
        lax.psum_scatter(
            summed[15].astype(jnp.bfloat16), "dp", scatter_dimension=0, tiled=True
        ).astype(jnp.float32),
        lax.psum_scatter(
            summed[16].astype(jnp.bfloat16), "dp", scatter_dimension=0, tiled=True
        ).astype(jnp.float32),
        lax.psum_scatter(
            summed[17].astype(jnp.bfloat16), "dp", scatter_dimension=0, tiled=True
        ).astype(jnp.float32),
        lax.psum_scatter(
            summed[18].astype(jnp.bfloat16), "dp", scatter_dimension=0, tiled=True
        ).astype(jnp.float32),
    )
    return (
        output,
        grad_tokens,
        owned[0],
        owned[1],
        owned[2],
        owned[3],
        owned[4],
        owned[5],
        owned[6],
        owned[7],
        owned[8],
        owned[9],
        owned[10],
        owned[11],
        owned[12],
        owned[13],
        owned[14],
        owned[15],
        owned[16],
        owned[17],
        owned[18],
    )


BF16 = jnp.bfloat16
F32 = jnp.float32
PAIRS = HEAD_COUNT // 2
LANES = 2 * HEAD_SIZE
ROWS = 256
FAR = -(2.0**100)
FF = 3072
NN = (((1,), (0,)), ((), ()))
NT = (((1,), (1,)), ((), ()))
TN = (((0,), (0,)), ((), ()))


def mm(left, right, dims=NN):
    return lax.dot_general(left, right, dims, preferred_element_type=F32)


def split(value):
    high = value.astype(BF16)
    return high, (value - high.astype(F32)).astype(BF16)


def lane_ids(rows):
    return lax.broadcasted_iota(jnp.int32, (rows, LANES), 1)


VECTORS = 16


def pair_maps(relative):
    row = lax.broadcasted_iota(jnp.int32, (HEAD_SIZE, LANES), 0)
    twice = (lane_ids(HEAD_SIZE) % HEAD_SIZE == row).astype(BF16)
    lane = lane_ids(LANES)
    row = lax.broadcasted_iota(jnp.int32, (LANES, LANES), 0)
    crossed = (row < HEAD_SIZE) != (lane < HEAD_SIZE)
    plain = jnp.where(crossed, mm(relative, twice), 0.0).astype(BF16)
    half = HEAD_SIZE // 2
    partner = jnp.where(lane % HEAD_SIZE < half, lane + half, lane - half)
    swapped = mm(plain, (row == partner).astype(BF16)).astype(BF16)
    return plain, swapped


def kind_maps(vectors):
    row = lax.broadcasted_iota(jnp.int32, (VECTORS, 4 * LANES), 0)
    column = lax.broadcasted_iota(jnp.int32, (VECTORS, 4 * LANES), 1)
    lane = column % LANES
    wanted = (lane >= 3) & (lane < 6) & (row == 11 - (column // LANES) % 2)
    both = mm(vectors.astype(BF16), wanted.astype(BF16), TN)
    row = lax.broadcasted_iota(jnp.int32, (LANES, 4 * LANES), 0)
    column = lax.broadcasted_iota(jnp.int32, (LANES, 4 * LANES), 1)
    return jnp.where((row < HEAD_SIZE) == (column < 2 * LANES), both, 0.0).astype(BF16)


def attend_kernel(
    query_ref,
    key_ref,
    value_ref,
    relative_ref,
    vectors_ref,
    query_side_ref,
    key_side_ref,
    phase_ref,
    cos_ref,
    sin_ref,
    mixture_ref,
    join_ref,
    key_join,
    value_join,
):
    query = query_ref[...]
    high, low = split(query)
    plain, swapped = pair_maps(relative_ref[...])
    kinds = kind_maps(vectors_ref[...])
    maps = jnp.concatenate([plain, swapped, kinds], axis=1)
    position_add, type_add = vectors_ref[8:9, :].astype(BF16), vectors_ref[9:10, :].astype(BF16)
    map_add = jnp.concatenate(
        [mm(position_add, plain), mm(position_add, swapped), mm(type_add, kinds)], axis=1
    )
    terms = mm(jnp.concatenate([high, low], axis=1), jnp.concatenate([maps, maps], axis=0))
    terms = terms + map_add
    lane = lane_ids(PQ)
    left = lane < HEAD_SIZE
    content = query + vectors_ref[7:8, :]
    position = terms[:, :LANES] * cos_ref[...] + terms[:, LANES : 2 * LANES] * sin_ref[...]
    side = query_side_ref[...]
    typed = (lane >= 3) & (lane < 6)
    scale = HEAD_SIZE ** (-0.5)
    for h in range(2):
        first, second = (content, position) if h == 0 else (position, content)
        join_ref[h, :, :LANES] = (jnp.where(left, first, second) * scale).astype(BF16)
        base = 2 * LANES * (h + 1)
        same = terms[:, base : base + LANES]
        other = terms[:, base + LANES : base + 2 * LANES]
        kind = jnp.where(side > 0.5, same, other) * scale
        join_ref[h, :, LANES:] = jnp.where(typed, kind, side).astype(BF16)
    key_left = lane_ids(LEN) < HEAD_SIZE
    key_join[:, LANES:] = key_side_ref[...]
    value_join[:, :LANES] = value_ref[...]
    value_join[:, LANES:] = key_side_ref[...]
    tile_lane = lane_ids(ROWS)
    for h in range(2):
        pieces = (key_ref[...], phase_ref[...]) if h == 0 else (phase_ref[...], key_ref[...])
        key_join[:, :LANES] = jnp.where(key_left, *pieces)
        for i in range(PQ // ROWS):
            rows = slice(i * ROWS, (i + 1) * ROWS)
            scores = mm(join_ref[h, rows, :], key_join[...], NT)
            top = jnp.max(scores, axis=1, keepdims=True)
            weights = jnp.exp(scores - top).astype(BF16)
            mixed = mm(weights, value_join[...])
            total = mixed[:, LANES + 6 : LANES + 7]
            result = (mixed[:, :LANES] / total).astype(BF16)
            if h == 0:
                mixture_ref[rows, :] = result
            else:
                mixture_ref[rows, :] = jnp.where(
                    tile_lane < HEAD_SIZE, mixture_ref[rows, :], result
                )
            shift = -(top + jnp.log(total))
            one = shift.astype(BF16).astype(F32)
            two = (shift - one).astype(BF16).astype(F32)
            three = shift - one - two
            extra = jnp.where(tile_lane == 6, one, jnp.where(tile_lane == 7, two, three))
            kept = join_ref[h, rows, LANES:].astype(F32)
            inside = (tile_lane >= 6) & (tile_lane < 9)
            join_ref[h, rows, LANES:] = jnp.where(inside, extra, kept).astype(BF16)


def attend_forward(query, pairs, relative, vectors, query_side, key_side, phase, cosm, sinm):
    whole = lambda shape: pl.BlockSpec(shape, lambda i: (0, 0))
    return pl.pallas_call(
        attend_kernel,
        grid=(PAIRS,),
        in_specs=[
            pl.BlockSpec((PQ, LANES), lambda i: (0, i)),
            pl.BlockSpec((LEN, LANES), lambda i: (0, i)),
            pl.BlockSpec((LEN, LANES), lambda i: (0, i + PAIRS)),
            pl.BlockSpec((LANES, HEAD_SIZE), lambda i: (i, 0)),
            pl.BlockSpec((VECTORS, LANES), lambda i: (0, i)),
            whole((PQ, LANES)),
            whole((LEN, LANES)),
            whole((LEN, LANES)),
            whole((PQ, LANES)),
            whole((PQ, LANES)),
        ],
        out_specs=[
            pl.BlockSpec((PQ, LANES), lambda i: (0, i)),
            pl.BlockSpec((2, PQ, 2 * LANES), lambda i: (i, 0, 0)),
        ],
        out_shape=[
            jax.ShapeDtypeStruct((PQ, MODEL_WIDTH), BF16),
            jax.ShapeDtypeStruct((HEAD_COUNT, PQ, 2 * LANES), BF16),
        ],
        scratch_shapes=[
            pltpu.VMEM((LEN, 2 * LANES), BF16),
            pltpu.VMEM((LEN, 2 * LANES), BF16),
        ],
        cost_estimate=pl.CostEstimate(
            flops=4 * HEAD_COUNT * PQ * LEN * 256,
            bytes_accessed=20_000_000,
            transcendentals=HEAD_COUNT * PQ * LEN,
        ),
        compiler_params=pltpu.CompilerParams(vmem_limit_bytes=56 * 2**20),
        name="attend_forward",
    )(query, pairs, pairs, relative, vectors, query_side, key_side, phase, cosm, sinm)


MESH = pl.DeviceIdType.MESH
SUM_ROWS = 48
STAGES = ("core", "y", "x", "near", "far", "far_back", "near_back", "x_back")
SMALL_ROWS = 16
SMALL_COLUMNS = 1024


class Place:
    def __init__(self):
        self.seq, self.dp = lax.axis_index("seq"), lax.axis_index("dp")
        self.core, self.y = self.dp % 2, self.dp // 2
        self.x, self.near, self.far = self.seq % 2, (self.seq // 2) % 2, self.seq // 4
        self.partner = {
            "core": (self.seq, self.dp + 1 - 2 * self.core),
            "y": (self.seq, self.dp + 2 - 4 * self.y),
            "x": (self.seq + 1 - 2 * self.x, self.dp),
            "near": (self.seq + 2 - 4 * self.near, self.dp),
            "far": (self.seq + 4 - 8 * self.far, self.dp),
        }

    def peers(self):
        return [((self.seq + k) % SG, self.dp) for k in range(1, SG)]

    def greet(self):
        barrier = pltpu.get_barrier_semaphore()
        others = [self.partner["core"], self.partner["y"], *self.peers()]
        for device in others:
            pl.semaphore_signal(barrier, inc=1, device_id=device, device_id_type=MESH)
        pl.semaphore_wait(barrier, len(others))


def add_rows(target, addend, rows):
    def step(i, carry):
        at = pl.ds(pl.multiple_of(i * SUM_ROWS, 16), SUM_ROWS)
        left, right = target(at), addend(at)
        left[...] = left[...] + right[...]
        return carry

    lax.fori_loop(0, rows // SUM_ROWS, step, 0)


class Chunk:
    def __init__(self, place, index, source, rows, columns, buffers, send, receive, local):
        self.place, self.source, self.rows, self.columns = place, source, rows, columns
        self.own, self.from_core, self.from_y, self.from_x, self.from_near, self.from_far, self.full = buffers
        self.send_at = lambda stage, k=0: send.at[index, STAGES.index(stage) + (8 if k else 0)]
        self.receive_at = lambda stage, k=0: receive.at[index, STAGES.index(stage) + (8 if k else 0)]
        self.local = lambda k: local.at[index, k]
        half, quarter = rows // 2, rows // 4
        self.my_columns = pl.ds(pl.multiple_of(place.x * (columns // 2), 128), columns // 2)
        self.other_columns = pl.ds(
            pl.multiple_of((1 - place.x) * (columns // 2), 128), columns // 2
        )
        self.my_half = pl.multiple_of(place.near * half, 16)
        self.my_quarter = pl.multiple_of(place.near * half + place.far * quarter, 16)

    def remote(self, stage, source, target, k=0):
        return pltpu.make_async_remote_copy(
            src_ref=source,
            dst_ref=target,
            send_sem=self.send_at(stage, k),
            recv_sem=self.receive_at(stage, k),
            device_id=self.place.partner[stage.split("_")[0]],
            device_id_type=MESH,
        )

    def locals(self):
        if self.own is None:
            return []
        return [
            pltpu.make_async_copy(
                self.source(2 * k + self.place.core), self.own.at[k], self.local(k)
            )
            for k in range(2)
        ]

    def copies(self, stage):
        place, rows = self.place, self.rows
        half, quarter = rows // 2, rows // 4
        if stage == "core":
            return [
                self.remote(
                    stage, self.source(2 * k + 1 - place.core), self.from_core.at[k], k
                )
                for k in range(2)
            ]
        if stage == "y":
            return [self.remote(stage, self.from_core.at[1 - place.y], self.from_y)]
        if stage == "x":
            return [self.remote(stage, self.from_y.at[:, self.other_columns], self.from_x)]
        if stage == "near":
            other = pl.ds(pl.multiple_of((1 - place.near) * half, 16), half)
            return [self.remote(stage, self.from_x.at[other, :], self.from_near)]
        if stage == "far":
            other = pl.ds(pl.multiple_of((1 - place.far) * quarter, 16), quarter)
            return [self.remote(stage, self.from_near.at[other, :], self.from_far)]
        if stage == "far_back":
            mine = self.full.at[pl.ds(self.my_quarter, quarter), self.my_columns]
            return [self.remote(stage, self.from_far, mine)]
        if stage == "near_back":
            mine = self.full.at[pl.ds(self.my_half, half), self.my_columns]
            return [self.remote(stage, mine, mine)]
        mine = self.full.at[:, self.my_columns]
        return [self.remote(stage, mine, mine)]

    def start(self, stage):
        if stage == "core":
            for copy in self.locals():
                copy.start()
        for copy in self.copies(stage):
            copy.start()

    def finish(self, stage):
        place, rows = self.place, self.rows
        half, quarter = rows // 2, rows // 4
        for copy in self.copies(stage):
            copy.wait_recv()
        if stage == "core":
            for copy in self.locals():
                copy.wait()
            for k in range(2):
                kept = (
                    self.source(2 * k + place.core) if self.own is None else self.own.at[k]
                )
                add_rows(
                    lambda at: self.from_core.at[k, at, :], lambda at: kept.at[at, :], rows
                )
        elif stage == "y":
            add_rows(
                lambda at: self.from_y.at[at, :],
                lambda at: self.from_core.at[place.y, at, :],
                rows,
            )
        elif stage == "x":
            add_rows(
                lambda at: self.from_x.at[at, :],
                lambda at: self.from_y.at[at, self.my_columns],
                rows,
            )
        elif stage == "near":
            add_rows(
                lambda at: self.from_near.at[at, :],
                lambda at: self.from_x.at[
                    pl.ds(pl.multiple_of(at.start + self.my_half, 16), SUM_ROWS), :
                ],
                half,
            )
        elif stage == "far":
            begin = place.far * quarter
            add_rows(
                lambda at: self.from_far.at[at, :],
                lambda at: self.from_near.at[
                    pl.ds(pl.multiple_of(at.start + begin, 16), SUM_ROWS), :
                ],
                quarter,
            )

    def place_piece(self):
        def step(i, carry):
            at = pl.ds(pl.multiple_of(i * SUM_ROWS, 16), SUM_ROWS)
            to = pl.ds(pl.multiple_of(i * SUM_ROWS + self.my_quarter, 16), SUM_ROWS)
            self.full[to, self.my_columns] = self.from_far[at, :]
            return carry

        lax.fori_loop(0, self.rows // 4 // SUM_ROWS, step, 0)

    def step(self, stage):
        at = STAGES.index(stage)
        if at > 0:
            self.finish(STAGES[at - 1])
        if stage == "far_back":
            self.place_piece()
        self.start(stage)

    def close(self, stages):
        for stage in stages:
            for copy in self.copies(stage):
                copy.wait_send()


DOWN, UP = STAGES[:5], STAGES[5:]
WHOLE = 3


def down_buffers(rows, columns, own):
    buffer = lambda *shape: pltpu.VMEM(shape, BF16)
    return [
        *([buffer(2, rows, columns)] if own else []),
        buffer(2, rows, columns),
        buffer(rows, columns),
        buffer(rows, columns // 2),
        buffer(rows // 2, columns // 2),
        buffer(rows // 4, columns // 2),
    ]


def grad_chunks():
    quarter = MODEL_WIDTH // 4
    half = MODEL_WIDTH // 2
    early = [
        (0, MODEL_WIDTH, 0, 0, half, MODEL_WIDTH),
        (0, MODEL_WIDTH, half, 0, half, MODEL_WIDTH),
        (1, quarter, 0, 0, quarter, FF // 2),
        (1, quarter, 0, FF // 2, quarter, FF // 2),
        (2, quarter, 0, 0, quarter, MODEL_WIDTH),
    ]
    late = [(j, quarter, 0, 0, quarter, MODEL_WIDTH) for j in (3, 4, 5)]
    return early, late


def chunk_source(grad, chunk):
    _, owner_rows, row, column, rows, columns = chunk

    def source(owner):
        begin = pl.multiple_of(owner * owner_rows + row, 16)
        return grad.at[pl.ds(begin, rows), pl.ds(column, columns)]

    return source


SEND_ORDER = (4, 3, 5, 2, 6, 1, 7, 0)


def finish_kernel(
    grad_query_ref,
    grad_key_ref,
    grad_value_ref,
    tokens_ref,
    pooled_ref,
    grad_first_ref,
    pool_ref,
    weights_ref,
    small_ref,
    *refs,
):
    early, late = grad_chunks()
    early = early[WHOLE:]
    pieces, refs = refs[: len(early)], refs[len(early) :]
    tokens_out, small_out, refs = refs[0], refs[1], refs[2:]
    count = len(early) + len(late)
    outs, refs = refs[:count], refs[count:]
    fulls, refs = refs[:count], refs[count:]
    buffers, refs = refs[: 5 * len(late)], refs[5 * len(late) :]
    (
        tokens_stage,
        late_grads,
        send,
        receive,
        token_send,
        token_receive,
        token_local,
        small_core,
        small_y,
        small_all,
        small_send,
        small_receive,
    ) = refs
    place = Place()
    place.greet()
    first = []
    for i, chunk in enumerate(early):
        kept = [None, None, None, None, None, pieces[i], fulls[i]]
        first.append(Chunk(place, i, None, *chunk[4:], kept, send, receive, None))
    second = []
    for j, chunk in enumerate(late):
        i = len(early) + j
        kept = [None, *buffers[5 * j : 5 * j + 5], fulls[i]]
        source = chunk_source(late_grads.at[j], chunk)
        second.append(Chunk(place, i, source, *chunk[4:], kept, send, receive, None))
    for item in first:
        item.place_piece()
        item.start("far_back")

    moved = []

    def send_tokens(k):
        to = (place.seq + k) % SG
        block = LEN // SG
        rows = pl.ds(pl.multiple_of(to * block, block), block)
        pooled_rows = pl.ds(pl.multiple_of(to * (block // 2), block // 2), block // 2)
        weight = lambda j: weights_ref[:, j * MODEL_WIDTH : (j + 1) * MODEL_WIDTH]
        grad_pooled = grad_first_ref[pooled_rows, :] + mm(
            grad_query_ref[pooled_rows, :], weight(0), NT
        )
        high, low = split(grad_pooled)
        total = mm(grad_key_ref[rows, :], weight(1), NT)
        total += mm(grad_value_ref[rows, :], weight(2), NT)
        total += mm(pool_ref[to], high, TN) + mm(pool_ref[to], low, TN)
        tokens_stage[to] = total.astype(BF16)
        if k == 0:
            copy = pltpu.make_async_copy(
                tokens_stage.at[to], tokens_out.at[place.seq], token_local
            )
        else:
            copy = pltpu.make_async_remote_copy(
                src_ref=tokens_stage.at[to],
                dst_ref=tokens_out.at[place.seq],
                send_sem=token_send.at[k - 1],
                recv_sem=token_receive.at[k - 1],
                device_id=(to, place.dp),
                device_id_type=MESH,
            )
        copy.start()
        moved.append(copy)

    for k in SEND_ORDER[:3]:
        send_tokens(k)
    for item in first:
        item.step("near_back")
    for k in SEND_ORDER[3:6]:
        send_tokens(k)
    for item in first:
        item.step("x_back")
    for k in SEND_ORDER[6:]:
        send_tokens(k)

    def small_copy(source, target, slot, device):
        return pltpu.make_async_remote_copy(
            src_ref=source,
            dst_ref=target,
            send_sem=small_send.at[slot],
            recv_sem=small_receive.at[slot],
            device_id=device,
            device_id_type=MESH,
        )

    core_copies = [
        small_copy(
            small_ref.at[2 * k + 1 - place.core], small_core.at[k], k, place.partner["core"]
        )
        for k in range(2)
    ]
    for copy in core_copies:
        copy.start()
    operands = [
        (pooled_ref, grad_query_ref),
        (tokens_ref, grad_key_ref),
        (tokens_ref, grad_value_ref),
    ]
    for j, (left, right) in enumerate(operands):
        for r in range(0, MODEL_WIDTH, 256):
            late_grads[j, r : r + 256, :] = mm(left[:, r : r + 256], right[...], TN).astype(BF16)
        second[j].start("core")
    for k, copy in enumerate(core_copies):
        copy.wait_recv()
        small_core[k] += small_ref[2 * k + place.core]
    y_copy = small_copy(small_core.at[1 - place.y], small_y, 2, place.partner["y"])
    y_copy.start()
    for item in second:
        item.step("y")
    y_copy.wait_recv()
    small_all[place.seq] = small_core[place.y] + small_y[...]
    small_copies = []
    for k, device in enumerate(place.peers()):
        copy = small_copy(small_all.at[place.seq], small_all.at[place.seq], 3 + k, device)
        copy.start()
        small_copies.append(copy)
    for stage in STAGES[2:]:
        for item in second:
            item.step(stage)

    for item, out in zip(first, outs):
        item.finish(STAGES[-1])
        out[...] = item.full[...]
        item.close(UP)
    for copy in small_copies:
        copy.wait_recv()
    total = small_all[0]
    for k in range(1, SG):
        total = total + small_all[k]
    small_out[...] = total
    for item, out in zip(second, outs[len(first) :]):
        item.finish(STAGES[-1])
        out[...] = item.full[...]
        item.close(STAGES)
    for copy in [*core_copies, y_copy, *small_copies]:
        copy.wait_send()
    for copy in moved:
        copy.wait()


def finish(
    grad_query, grad_key, grad_value, tokens, pooled, grad_first, pool, weights, small, pieces
):
    anywhere = pl.BlockSpec(memory_space=pl.ANY)
    early, late = grad_chunks()
    early = early[WHOLE:]
    chunks = early + late
    count = len(chunks)
    small_shape = (SMALL_ROWS, SMALL_COLUMNS)
    inside = pl.BlockSpec(memory_space=pltpu.VMEM)
    out_tokens = (SG, LEN // SG, MODEL_WIDTH)
    return pl.pallas_call(
        finish_kernel,
        in_specs=[inside] * (9 + len(early)),
        out_specs=[anywhere, inside, *[inside] * count],
        out_shape=[
            jax.ShapeDtypeStruct(out_tokens, BF16),
            jax.ShapeDtypeStruct(small_shape, F32),
            *[jax.ShapeDtypeStruct(chunk[4:], BF16) for chunk in chunks],
        ],
        scratch_shapes=[
            *[pltpu.VMEM(chunk[4:], BF16) for chunk in chunks],
            *[buffer for chunk in late for buffer in down_buffers(*chunk[4:], False)],
            pltpu.VMEM(out_tokens, BF16),
            pltpu.VMEM((3, MODEL_WIDTH, MODEL_WIDTH), BF16),
            pltpu.SemaphoreType.DMA((count, 16)),
            pltpu.SemaphoreType.DMA((count, 16)),
            pltpu.SemaphoreType.DMA((SG - 1,)),
            pltpu.SemaphoreType.DMA((SG - 1,)),
            pltpu.SemaphoreType.DMA,
            pltpu.VMEM((2, *small_shape), F32),
            pltpu.VMEM(small_shape, F32),
            pltpu.VMEM((SG, *small_shape), F32),
            pltpu.SemaphoreType.DMA((SG + 2,)),
            pltpu.SemaphoreType.DMA((SG + 2,)),
        ],
        compiler_params=pltpu.CompilerParams(
            collective_id=3, has_side_effects=True, vmem_limit_bytes=58 * 2**20
        ),
        name="finish",
    )(
        grad_query,
        grad_key,
        grad_value,
        tokens,
        pooled,
        grad_first,
        pool,
        weights,
        small,
        *pieces,
    )


FF_STEP = 512
FF_TILES = FF // FF_STEP
ROW_TILES = PQ // ROWS


def row_norm(value):
    centred = value - jnp.mean(value, axis=1, keepdims=True)
    inverse = lax.rsqrt(jnp.mean(centred * centred, axis=1, keepdims=True) + norm_eps)
    return centred * inverse, inverse


def row_norm_back(scaled, normed, inverse):
    along = jnp.mean(scaled * normed, axis=1, keepdims=True)
    return inverse * (scaled - jnp.mean(scaled, axis=1, keepdims=True) - normed * along)


def gelu_pieces(value):
    rate = math.sqrt(2.0 / math.pi)
    square = value * value
    bend = jnp.tanh(rate * value * (1.0 + 0.044715 * square))
    half = 0.5 * (1.0 + bend)
    slope = half + (0.5 * rate) * value * (1.0 - bend * bend) * (1.0 + 0.134145 * square)
    return value * half, slope


def mlp_kernel(
    mixture_ref,
    pooled_ref,
    upstream_ref,
    output_weight_ref,
    inner_weight_ref,
    outer_weight_ref,
    vectors_ref,
    inner_add_ref,
    output_ref,
    grad_mixture_ref,
    grad_first_ref,
    grad_outer_ref,
    grad_inner_ref,
    grad_output_ref,
    sums_ref,
    inner_sums_ref,
    active,
    slopes,
    grad_expanded,
    hidden_low,
    grad_branch,
    grad_attention,
    output_stage,
    mixture_stage,
    first_stage,
    send,
    receive,
    local,
):
    step = pl.program_id(0)
    place = Place()
    block = PQ // SG
    tile = (step + place.seq // 2 + 1) % ROW_TILES
    begin = pl.multiple_of(tile * ROWS, ROWS)

    def output_copy(to):
        return pltpu.make_async_remote_copy(
            src_ref=output_stage.at[to],
            dst_ref=output_ref.at[place.seq],
            send_sem=send.at[to],
            recv_sem=receive.at[place.seq],
            device_id=(to, place.dp),
            device_id_type=MESH,
        )

    def kept_copy():
        return pltpu.make_async_copy(
            output_stage.at[place.seq], output_ref.at[place.seq], local.at[0]
        )

    def row_copies():
        rows = pl.ds(begin, ROWS)
        return [
            pltpu.make_async_copy(
                mixture_stage.at[rows, :], grad_mixture_ref.at[rows, :], local.at[1 + 2 * tile]
            ),
            pltpu.make_async_copy(
                first_stage.at[rows, :], grad_first_ref.at[rows, :], local.at[2 + 2 * tile]
            ),
        ]

    @pl.when(step == 0)
    def _():
        place.greet()

    @pl.when(step < ROW_TILES)
    def _():
        rows = pl.ds(begin, ROWS)
        vector = lambda j: vectors_ref[j : j + 1, :]
        output_add, outer_add, gain_one, shift_one, gain_two, shift_two = map(vector, range(1, 7))
        attention = mm(mixture_ref[rows, :], output_weight_ref[...]) + output_add
        normed_one, inverse_one = row_norm(pooled_ref[rows, :] + attention)
        hidden = normed_one * gain_one + shift_one
        low_hidden = hidden.astype(BF16)
        hidden_low[rows, :] = low_hidden
        branch = jnp.zeros((ROWS, MODEL_WIDTH), F32)
        for j in range(FF_TILES):
            part = slice(j * FF_STEP, (j + 1) * FF_STEP)
            expanded = mm(low_hidden, inner_weight_ref[:, part]) + inner_add_ref[:, part]
            value, slope = gelu_pieces(expanded)
            low_value = value.astype(BF16)
            active[rows, part] = low_value
            slopes[:, part] = slope
            branch += mm(low_value, outer_weight_ref[part, :])
        normed_two, inverse_two = row_norm(hidden + (branch + outer_add))
        result = (normed_two * gain_two + shift_two).astype(BF16)
        for k in range(ROWS // block):
            to = tile * (ROWS // block) + k
            output_stage[to] = result[k * block : (k + 1) * block]

            @pl.when(to == place.seq)
            def _():
                kept_copy().start()

            @pl.when(to != place.seq)
            def _():
                output_copy(to).start()

        upstream = upstream_ref[rows, :].astype(F32)
        grad_second = row_norm_back(upstream * gain_two, normed_two, inverse_two)
        low_branch = grad_second.astype(BF16)
        grad_branch[rows, :] = low_branch
        grad_hidden = grad_second
        inner_sums = []
        for j in range(FF_TILES):
            part = slice(j * FF_STEP, (j + 1) * FF_STEP)
            grad_active = mm(low_branch, outer_weight_ref[part, :], NT)
            low_grad = (slopes[:, part] * grad_active).astype(BF16)
            grad_expanded[rows, part] = low_grad
            inner_sums.append(jnp.sum(low_grad.astype(F32), axis=0, keepdims=True))
            grad_hidden += mm(low_grad, inner_weight_ref[:, part], NT)
        grad_first = row_norm_back(grad_hidden * gain_one, normed_one, inverse_one)
        first_stage[rows, :] = grad_first
        low_attention = grad_first.astype(BF16)
        grad_attention[rows, :] = low_attention
        mixture_stage[rows, :] = mm(low_attention, output_weight_ref[...], NT).astype(BF16)
        for copy in row_copies():
            copy.start()
        row = lambda v: jnp.sum(v, axis=0, keepdims=True)
        sums = jnp.concatenate(
            [
                row(low_attention.astype(F32)),
                row(low_branch.astype(F32)),
                row(grad_hidden * normed_one),
                row(grad_hidden),
                row(upstream * normed_two),
                row(upstream),
                jnp.zeros((2, MODEL_WIDTH), F32),
            ],
            axis=0,
        )
        inner_sum = jnp.concatenate(inner_sums, axis=1)

        @pl.when(step == 0)
        def _():
            sums_ref[...] = sums
            inner_sums_ref[...] = inner_sum

        @pl.when(step > 0)
        def _():
            sums_ref[...] += sums
            inner_sums_ref[...] += inner_sum

    for j in range(FF_TILES):

        @pl.when(step == ROW_TILES + j)
        def _():
            part = slice(j * FF_STEP, (j + 1) * FF_STEP)
            grad_outer_ref[...] = mm(active[:, part], grad_branch[...], TN).astype(BF16)
            grad_inner_ref[...] = mm(hidden_low[...], grad_expanded[:, part], TN).astype(BF16)
            if j == 0:
                grad_output_ref[...] = mm(mixture_ref[...], grad_attention[...], TN).astype(BF16)

    @pl.when(step == ROW_TILES + FF_TILES - 1)
    def _():
        for t in range(ROW_TILES):
            rows = pl.ds(t * ROWS, ROWS)
            pltpu.make_async_copy(
                mixture_stage.at[rows, :], grad_mixture_ref.at[rows, :], local.at[1 + 2 * t]
            ).wait()
            pltpu.make_async_copy(
                first_stage.at[rows, :], grad_first_ref.at[rows, :], local.at[2 + 2 * t]
            ).wait()
        kept_copy().wait()
        for k in range(1, SG):
            other = (place.seq + k) % SG
            output_copy(other).wait_send()
            pltpu.make_async_remote_copy(
                src_ref=output_stage.at[other],
                dst_ref=output_ref.at[other],
                send_sem=send.at[other],
                recv_sem=receive.at[other],
                device_id=(other, place.dp),
                device_id_type=MESH,
            ).wait_recv()


def mlp(mixture, pooled, upstream, output_weight, inner_weight, outer_weight, vectors, inner_add):
    fixed = lambda shape: pl.BlockSpec(shape, lambda i: (0, 0), pipeline_mode=pl.Buffered(1))
    still = lambda shape: pl.BlockSpec(shape, lambda i: (0, 0))
    anywhere = pl.BlockSpec(memory_space=pl.ANY)
    out_shape = (SG, PQ // SG, MODEL_WIDTH)
    late = lambda i: jnp.maximum(i - ROW_TILES, 0)
    whole = (PQ, MODEL_WIDTH)
    square = (MODEL_WIDTH, MODEL_WIDTH)
    return pl.pallas_call(
        mlp_kernel,
        grid=(ROW_TILES + FF_TILES,),
        in_specs=[
            fixed(whole),
            fixed(whole),
            fixed(whole),
            fixed(square),
            fixed((MODEL_WIDTH, FF)),
            fixed((FF, MODEL_WIDTH)),
            fixed((VECTORS, MODEL_WIDTH)),
            fixed((1, FF)),
        ],
        out_specs=[
            anywhere,
            anywhere,
            anywhere,
            pl.BlockSpec((FF_STEP, MODEL_WIDTH), lambda i: (late(i), 0)),
            pl.BlockSpec((MODEL_WIDTH, FF_STEP), lambda i: (0, late(i))),
            still(square),
            still((8, MODEL_WIDTH)),
            still((1, FF)),
        ],
        out_shape=[
            jax.ShapeDtypeStruct(out_shape, BF16),
            jax.ShapeDtypeStruct(whole, BF16),
            jax.ShapeDtypeStruct(whole, F32),
            jax.ShapeDtypeStruct((FF, MODEL_WIDTH), BF16),
            jax.ShapeDtypeStruct((MODEL_WIDTH, FF), BF16),
            jax.ShapeDtypeStruct(square, BF16),
            jax.ShapeDtypeStruct((8, MODEL_WIDTH), F32),
            jax.ShapeDtypeStruct((1, FF), F32),
        ],
        scratch_shapes=[
            pltpu.VMEM((PQ, FF), BF16),
            pltpu.VMEM((ROWS, FF), F32),
            pltpu.VMEM((PQ, FF), BF16),
            pltpu.VMEM(whole, BF16),
            pltpu.VMEM(whole, BF16),
            pltpu.VMEM(whole, BF16),
            pltpu.VMEM(out_shape, BF16),
            pltpu.VMEM(whole, BF16),
            pltpu.VMEM(whole, F32),
            pltpu.SemaphoreType.DMA((SG,)),
            pltpu.SemaphoreType.DMA((SG,)),
            pltpu.SemaphoreType.DMA((1 + 2 * ROW_TILES,)),
        ],
        cost_estimate=pl.CostEstimate(
            flops=2 * PQ * MODEL_WIDTH * (3 * MODEL_WIDTH + 6 * FF),
            bytes_accessed=40_000_000,
            transcendentals=PQ * FF,
        ),
        compiler_params=pltpu.CompilerParams(
            collective_id=1, has_side_effects=True, vmem_limit_bytes=60 * 2**20
        ),
        name="mlp",
    )(mixture, pooled, upstream, output_weight, inner_weight, outer_weight, vectors, inner_add)


SLOTS = 2 * (PQ // ROWS)
EARLY_SLOTS = {}
for _i, _steps in enumerate(
    (
        (3, 12, 17, 20, 23, 26, 29, 34),
        (6, 20, 25, 28, 31, 34, 37, 42),
        (9, 28, 33, 36, 39, 42, 45, 48),
        (12, 36, 41, 44, 48),
        (14, 41, 45, 47, 48),
    )
):
    for _stage, _slot in zip((*STAGES[1 : len(_steps)], None), _steps):
        EARLY_SLOTS.setdefault(_slot, []).append((_i, _stage))


def attend_back_kernel(
    join_ref,
    key_ref,
    value_ref,
    query_ref,
    mixture_ref,
    grad_ref,
    relative_ref,
    vectors_ref,
    query_side_ref,
    key_side_ref,
    phase_ref,
    cos_ref,
    sin_ref,
    grad_outer_ref,
    grad_inner_ref,
    grad_output_ref,
    grad_query_ref,
    grad_key_ref,
    grad_value_ref,
    sums_ref,
    grad_map_ref,
    *refs,
):
    early, _ = grad_chunks()
    sent, refs = refs[: len(early)], refs[len(early) :]
    key_join, value_join, key_total, value_total, join_grads, *refs = refs
    fulls, refs = refs[:WHOLE], refs[WHOLE:]
    buffers, (send, receive, local) = refs[: 6 * len(early)], refs[6 * len(early) :]
    pair = pl.program_id(0)
    place = Place()
    grads = (grad_outer_ref, grad_inner_ref, grad_output_ref)
    work = []
    for i, chunk in enumerate(early):
        kept = [*buffers[6 * i : 6 * i + 6], fulls[i] if i < WHOLE else None]
        source = chunk_source(grads[chunk[0]], chunk)
        work.append(Chunk(place, i, source, *chunk[4:], kept, send, receive, local))

    def exchange(slot):
        for i, stage in EARLY_SLOTS.get(slot, ()):
            if stage is not None:
                work[i].step(stage)
            elif i < WHOLE:
                work[i].finish(STAGES[-1])
                sent[i][...] = work[i].full[...]
                work[i].close(STAGES)
            else:
                work[i].finish(DOWN[-1])
                sent[i][...] = work[i].from_far[...]
                work[i].close(DOWN)

    @pl.when(pair == 0)
    def _():
        place.greet()
        for item in work:
            item.start("core")

    scale = HEAD_SIZE ** (-0.5)
    key_left = lane_ids(LEN) < HEAD_SIZE
    tile_lane = lane_ids(ROWS)
    key_join[:, LANES:] = key_side_ref[...]
    value_join[:, :LANES] = value_ref[...]
    value_join[:, LANES:] = key_side_ref[...]
    for h in range(2):
        pieces = (key_ref[...], phase_ref[...]) if h == 0 else (phase_ref[...], key_ref[...])
        key_join[:, :LANES] = jnp.where(key_left, *pieces)
        mine = (tile_lane < HEAD_SIZE) if h == 0 else (tile_lane >= HEAD_SIZE)
        part = slice(h * HEAD_SIZE, (h + 1) * HEAD_SIZE)
        for i in range(PQ // ROWS):
            rows = slice(i * ROWS, (i + 1) * ROWS)
            for slot in EARLY_SLOTS:
                if slot % SLOTS == h * (PQ // ROWS) + i:

                    @pl.when(pair == slot // SLOTS)
                    def _():
                        exchange(slot)

            join = join_ref[h, rows, :]
            grad = jnp.where(mine, grad_ref[rows, :].astype(F32), 0.0)
            dot = -jnp.sum(grad * mixture_ref[rows, :].astype(F32), axis=1, keepdims=True)
            one = dot.astype(BF16).astype(F32)
            two = (dot - one).astype(BF16).astype(F32)
            three = dot - one - two
            extra = jnp.where(tile_lane == 6, one, jnp.where(tile_lane == 7, two, three))
            inside = (tile_lane >= 6) & (tile_lane < 9)
            extra = jnp.where(inside, extra, 0.0)
            grad_low = grad.astype(BF16)
            weights = jnp.exp(mm(join, key_join[...], NT))
            slope = mm(
                jnp.concatenate([grad_low, extra.astype(BF16)], axis=1), value_join[...], NT
            )
            low_slope = (weights * slope).astype(BF16)
            low_weights = weights.astype(BF16)
            join_grads[h, rows, :] = mm(low_slope, key_join[...])
            to_key = mm(join_ref[h, rows, part], low_slope, TN)
            to_value = mm(grad_ref[rows, part], low_weights, TN)
            if i == 0:
                key_total[part, :] = to_key
                value_total[part, :] = to_value
            else:
                key_total[part, :] += to_key
                value_total[part, :] += to_value
    grad_key_ref[...] = key_total[...].T.astype(BF16)
    grad_value_ref[...] = value_total[...].T.astype(BF16)
    lane = lane_ids(PQ)
    left = lane < HEAD_SIZE
    typed = (lane >= 3) & (lane < 6)
    rounded = [(join_grads[h, :, :LANES] * scale).astype(BF16).astype(F32) for h in range(2)]
    content = jnp.where(left, rounded[0], rounded[1])
    position = jnp.where(left, rounded[1], rounded[0])
    turned = jnp.concatenate([position * cos_ref[...], position * sin_ref[...]], axis=1)
    turned_high, turned_low = split(turned)
    plain, swapped = pair_maps(relative_ref[...])
    maps = jnp.concatenate([plain, swapped], axis=1)
    shifted_grad = mm(turned_high, maps, NT) + mm(turned_low, maps, NT)
    side = query_side_ref[...]
    sames, others = [], []
    for h in range(2):
        kinds = jnp.where(typed, join_grads[h, :, LANES:], 0.0)
        same = jnp.sum(jnp.where(side > 0.5, kinds, 0.0), axis=1, keepdims=True)
        other = jnp.sum(jnp.where(side > 0.5, 0.0, kinds), axis=1, keepdims=True)
        sames.append((same * scale).astype(BF16).astype(F32))
        others.append((other * scale).astype(BF16).astype(F32))
    same = jnp.where(left, sames[0], sames[1])
    other = jnp.where(left, others[0], others[1])
    position_add = vectors_ref[8:9, :]
    type_add = vectors_ref[9:10, :]
    type_other = vectors_ref[10:11, :]
    type_same = vectors_ref[11:12, :]
    typed_grad = same * type_same + other * type_other
    grad_query_ref[...] = (content + shifted_grad + typed_grad).astype(BF16)
    query = query_ref[...]
    shifted_high, shifted_low = split(query + position_add)
    grad_map_ref[0] = (
        mm(shifted_high, turned_high, TN)
        + mm(shifted_low, turned_high, TN)
        + mm(shifted_high, turned_low, TN)
    )
    kinds = query + type_add
    row = lambda v: jnp.sum(v, axis=0, keepdims=True)
    sums_ref[0, 0:1, :] = row(content)
    sums_ref[0, 1:2, :] = row(shifted_grad)
    sums_ref[0, 2:3, :] = row(typed_grad)
    sums_ref[0, 3:4, :] = row(kinds * other)
    sums_ref[0, 4:5, :] = row(kinds * same)
    sums_ref[0, 5:6, :] = row(grad_value_ref[...].astype(F32))

    @pl.when(pair == PAIRS - 1)
    def _():
        exchange(PAIRS * SLOTS)


def attend_backward(
    join,
    pairs,
    query,
    mixture,
    grad,
    relative,
    vectors,
    query_side,
    key_side,
    phase,
    cosm,
    sinm,
    grads,
):
    early, _ = grad_chunks()
    anywhere = pl.BlockSpec(memory_space=pl.ANY)
    shapes = [
        chunk[4:] if i < WHOLE else (chunk[4] // 4, chunk[5] // 2)
        for i, chunk in enumerate(early)
    ]
    whole = lambda shape: pl.BlockSpec(shape, lambda i: (0, 0))
    return pl.pallas_call(
        attend_back_kernel,
        grid=(PAIRS,),
        in_specs=[
            pl.BlockSpec((2, PQ, 2 * LANES), lambda i: (i, 0, 0)),
            pl.BlockSpec((LEN, LANES), lambda i: (0, i)),
            pl.BlockSpec((LEN, LANES), lambda i: (0, i + PAIRS)),
            pl.BlockSpec((PQ, LANES), lambda i: (0, i)),
            pl.BlockSpec((PQ, LANES), lambda i: (0, i)),
            pl.BlockSpec((PQ, LANES), lambda i: (0, i)),
            pl.BlockSpec((LANES, HEAD_SIZE), lambda i: (i, 0)),
            pl.BlockSpec((VECTORS, LANES), lambda i: (0, i)),
            whole((PQ, LANES)),
            whole((LEN, LANES)),
            whole((LEN, LANES)),
            whole((PQ, LANES)),
            whole((PQ, LANES)),
            *[anywhere] * 3,
        ],
        out_specs=[
            pl.BlockSpec((PQ, LANES), lambda i: (0, i)),
            pl.BlockSpec((LEN, LANES), lambda i: (0, i)),
            pl.BlockSpec((LEN, LANES), lambda i: (0, i)),
            pl.BlockSpec((1, 8, LANES), lambda i: (i, 0, 0)),
            pl.BlockSpec((1, LANES, 2 * LANES), lambda i: (i, 0, 0)),
            *[whole(shape) for shape in shapes],
        ],
        out_shape=[
            jax.ShapeDtypeStruct((PQ, MODEL_WIDTH), BF16),
            jax.ShapeDtypeStruct((LEN, MODEL_WIDTH), BF16),
            jax.ShapeDtypeStruct((LEN, MODEL_WIDTH), BF16),
            jax.ShapeDtypeStruct((PAIRS, 8, LANES), F32),
            jax.ShapeDtypeStruct((PAIRS, LANES, 2 * LANES), F32),
            *[jax.ShapeDtypeStruct(shape, BF16) for shape in shapes],
        ],
        scratch_shapes=[
            pltpu.VMEM((LEN, 2 * LANES), BF16),
            pltpu.VMEM((LEN, 2 * LANES), BF16),
            pltpu.VMEM((LANES, LEN), F32),
            pltpu.VMEM((LANES, LEN), F32),
            pltpu.VMEM((2, PQ, 2 * LANES), F32),
            *[pltpu.VMEM(chunk[4:], BF16) for chunk in early[:WHOLE]],
            *[buffer for chunk in early for buffer in down_buffers(*chunk[4:], True)],
            pltpu.SemaphoreType.DMA((len(early), 16)),
            pltpu.SemaphoreType.DMA((len(early), 16)),
            pltpu.SemaphoreType.DMA((len(early), 2)),
        ],
        cost_estimate=pl.CostEstimate(
            flops=10 * HEAD_COUNT * PQ * LEN * 256,
            bytes_accessed=32_000_000,
            transcendentals=HEAD_COUNT * PQ * LEN,
        ),
        compiler_params=pltpu.CompilerParams(
            collective_id=2, has_side_effects=True, vmem_limit_bytes=58 * 2**20
        ),
        name="attend_backward",
    )(
        join,
        pairs,
        pairs,
        query,
        mixture,
        grad,
        relative,
        vectors,
        query_side,
        key_side,
        phase,
        cosm,
        sinm,
        *grads,
    )


def swap_halves(value, axis):
    first, second = jnp.split(value, 2, axis=axis)
    return jnp.concatenate([second, first], axis=axis)


def labels_kernel(labels_ref, out_ref, stage, send, receive):
    place = Place()
    place.greet()
    copies = []
    for k in range(1, SG):
        to = (place.seq + k) % SG
        copy = pltpu.make_async_remote_copy(
            src_ref=labels_ref.at[to],
            dst_ref=stage.at[place.seq],
            send_sem=send.at[k - 1],
            recv_sem=receive.at[k - 1],
            device_id=(to, place.dp),
            device_id_type=MESH,
        )
        copy.start()
        copies.append(copy)
    stage[place.seq] = labels_ref[place.seq]
    for copy in copies:
        copy.wait()
    out_ref[...] = stage[...]


def move_labels(labels):
    inside = pl.BlockSpec(memory_space=pltpu.VMEM)
    return pl.pallas_call(
        labels_kernel,
        in_specs=[inside],
        out_specs=inside,
        out_shape=jax.ShapeDtypeStruct(labels.shape, jnp.int32),
        scratch_shapes=[
            pltpu.VMEM(labels.shape, jnp.int32),
            pltpu.SemaphoreType.DMA((SG - 1,)),
            pltpu.SemaphoreType.DMA((SG - 1,)),
        ],
        compiler_params=pltpu.CompilerParams(collective_id=4, has_side_effects=True),
        name="labels",
    )(labels)


def angle_tables():
    half = HEAD_SIZE // 2
    rate = np.float32(-math.log(10000.0) / half)
    frequency = np.exp(np.arange(half, dtype=np.float32) * rate)
    angle = np.arange(LEN, dtype=np.float32)[:, None] * frequency[None, :]
    cos, sin = np.cos(angle), np.sin(angle)
    phase = np.concatenate([cos, sin, cos, sin], axis=1)
    cos, sin = cos[0::2], sin[0::2]
    return (
        jnp.asarray(phase).astype(BF16),
        np.concatenate([cos, -cos, cos, -cos], axis=1),
        np.concatenate([sin, sin, sin, sin], axis=1),
    )


def sequence_body(
    tokens,
    segments,
    token_types,
    cotangent,
    query_weight,
    key_weight,
    value_weight,
    output_weight,
    inner_weight,
    outer_weight,
    value_bias,
    output_bias,
    inner_bias,
    outer_bias,
    attention_norm_gain,
    first_shift,
    second_gain,
    second_shift,
    content_bias,
    position_bias,
    type_bias,
    relative_kernel,
    type_embed,
):
    owners = lax.axis_size("dp")
    part = MODEL_WIDTH // owners
    low = lambda value: value.astype(BF16)
    even_segments, odd_segments = segments[:, 0::2], segments[:, 1::2]
    labels = jnp.stack(
        [
            segments[:, :128],
            segments[:, 128:],
            token_types[:, :128],
            token_types[:, 128:],
            even_segments,
            token_types[:, 0::2],
            (even_segments == odd_segments).astype(jnp.int32),
        ],
        axis=1,
    )
    labels = move_labels(labels)
    tokens, labels = lax.optimization_barrier((tokens, labels))
    rows = lax.all_to_all(tokens, "seq", split_axis=0, concat_axis=0, tiled=True)
    flat = lambda value: low(value).reshape(1, part)
    vectors = [
        flat(value)
        for value in (
            value_bias,
            output_bias,
            outer_bias,
            attention_norm_gain,
            first_shift,
            second_gain,
            second_shift,
            content_bias,
            position_bias,
            type_bias,
            type_embed[:, 0],
            type_embed[:, 1],
        )
    ]
    vectors.append(jnp.zeros((VECTORS - len(vectors), part), BF16))
    vectors = lax.all_gather(jnp.concatenate(vectors, axis=0), "dp", axis=1, tiled=True)
    vectors = vectors.astype(F32)
    inner_add = lax.all_gather(low(inner_bias).reshape(1, -1), "dp", axis=1, tiled=True)
    inner_add = inner_add.astype(F32)
    relative = low(relative_kernel).reshape(part, HEAD_SIZE)
    relative = lax.all_gather(relative, "dp", axis=0, tiled=True)
    first = jnp.concatenate([low(query_weight), low(key_weight), low(value_weight)], axis=1)
    first = lax.all_gather(first, "dp", axis=0, tiled=True)
    inner_low = lax.all_gather(low(inner_weight), "dp", axis=0, tiled=True)
    output_low = lax.all_gather(low(output_weight), "dp", axis=0, tiled=True)
    outer_low = lax.all_gather(low(outer_weight), "dp", axis=0, tiled=True)

    kernel_size = HEAD_COUNT * HEAD_SIZE * HEAD_SIZE // owners

    segment_row = labels[:, 0:2].reshape(LEN)
    type_row = labels[:, 2:4].reshape(LEN)
    query_segments = labels[:, 4].reshape(PQ)
    query_types = labels[:, 5].reshape(PQ)
    pair_same = labels[:, 6] > 0

    first_doc, last_doc = segment_row[0], segment_row[LEN - 1]
    first_type = type_row[0]
    last_type = jnp.max(jnp.where(type_row == first_type, -1, type_row))

    def classes(values, start, end):
        return jnp.where(values == start, 0, jnp.where(values == end, 2, 1))[:, None]

    columns = jnp.arange(LANES, dtype=jnp.int32)[None, :]
    key_side = (
        (columns == classes(segment_row, first_doc, last_doc))
        | (columns == 3 + classes(type_row, first_type, last_type))
        | ((columns >= 6) & (columns < 9))
    ).astype(BF16)
    query_docs = classes(query_segments, first_doc, last_doc)
    query_side = jnp.where(
        columns < 3,
        jnp.where(columns == query_docs, 0.0, FAR),
        (columns == 3 + classes(query_types, first_type, last_type)).astype(F32),
    )
    phase, cosm, sinm = angle_tables()

    block = rows.shape[1]
    pooled_block = block // 2
    at = jnp.arange(block, dtype=jnp.int32)[None, None, :]
    want = 2 * jnp.arange(pooled_block, dtype=jnp.int32)[None, :, None]
    half = jnp.where(pair_same, 0.5, 1.0)[:, :, None]
    other_half = jnp.where(pair_same, 0.5, 0.0)[:, :, None]
    pool = jnp.where(at == want, half, jnp.where(at == want + 1, other_half, 0.0)).astype(BF16)

    pooled = jnp.einsum("cpt,ctd->cpd", pool, rows, preferred_element_type=F32)
    pooled = pooled.reshape(PQ, MODEL_WIDTH)
    pooled_low = low(pooled)
    token_rows = rows.reshape(LEN, MODEL_WIDTH)
    query = mm(pooled_low, first[:, :MODEL_WIDTH])
    value_add = vectors[0:1]
    pair_add = jnp.concatenate([jnp.zeros_like(value_add), value_add], axis=1)
    pairs = low(mm(token_rows, first[:, MODEL_WIDTH:]) + pair_add)
    mixture, join = attend_forward(
        query, pairs, relative, vectors, query_side, key_side, phase, cosm, sinm
    )

    cotangent, _ = lax.optimization_barrier((cotangent, labels))
    cotangent = lax.all_to_all(cotangent, "seq", split_axis=0, concat_axis=0, tiled=True)
    upstream = cotangent.reshape(PQ, MODEL_WIDTH)

    (
        output,
        grad_mixture,
        grad_first,
        grad_outer_weight,
        grad_inner_weight,
        grad_output_weight,
        row_sums,
        grad_inner_bias,
    ) = mlp(
        mixture, pooled, upstream, output_low, inner_low, outer_low, vectors, inner_add
    )
    (
        grad_output_bias,
        grad_outer_bias,
        grad_gain_one,
        grad_shift_one,
        grad_gain_two,
        grad_shift_two,
    ) = [row_sums[j] for j in range(6)]
    grad_query, grad_key, grad_value, sums, grad_map, *pieces = attend_backward(
        join,
        pairs,
        query,
        mixture,
        grad_mixture,
        relative,
        vectors,
        query_side,
        key_side,
        phase,
        cosm,
        sinm,
        (grad_outer_weight, grad_inner_weight, grad_output_weight),
    )
    crossed = grad_map.reshape(PAIRS, 2, HEAD_SIZE, 2, 2, HEAD_SIZE)
    grad_relative = jnp.stack(
        [
            crossed[:, h, :, 0, 1 - h] + swap_halves(crossed[:, h, :, 1, 1 - h], 2)
            for h in range(2)
        ],
        axis=1,
    ).reshape(HEAD_COUNT, HEAD_SIZE, HEAD_SIZE)
    grad_table = sums[:, 3:5].reshape(PAIRS, 2, 2, HEAD_SIZE).transpose(0, 2, 1, 3)
    sum_row = lambda j: sums[:, j].reshape(owners, -1)
    small_grads = jnp.concatenate(
        [
            value.reshape(owners, -1)
            for value in (
                sum_row(5),
                grad_output_bias,
                grad_outer_bias,
                grad_gain_one,
                grad_shift_one,
                grad_gain_two,
                grad_shift_two,
                sum_row(0),
                sum_row(1),
                sum_row(2),
                grad_inner_bias,
                grad_relative,
                grad_table,
            )
        ],
        axis=1,
    )
    count = small_grads.shape[1]
    room = SMALL_ROWS * SMALL_COLUMNS
    small_grads = jnp.pad(small_grads, ((0, 0), (0, room - count)))
    grad_tokens, small_owned, *owned = finish(
        grad_query,
        grad_key,
        grad_value,
        token_rows,
        pooled_low,
        grad_first,
        pool,
        first,
        small_grads.reshape(owners, SMALL_ROWS, SMALL_COLUMNS),
        pieces[WHOLE:],
    )
    owned = [*pieces[:WHOLE], *owned]
    owned_outer = jnp.concatenate(owned[0:2], axis=0).astype(F32)
    owned_inner = jnp.concatenate(owned[2:4], axis=1).astype(F32)
    owned_output, *squares = [value.astype(F32) for value in owned[4:]]
    squares.append(owned_output)
    small_owned = small_owned.reshape(-1)
    place = 0
    pieces = []
    for size in [part] * 10 + [FF // owners, kernel_size, HEAD_COUNT * 2 * HEAD_SIZE // owners]:
        pieces.append(small_owned[place : place + size])
        place += size
    heads = HEAD_COUNT // owners
    return (
        output,
        grad_tokens,
        squares[0],
        squares[1],
        squares[2],
        squares[3],
        owned_inner,
        owned_outer,
        pieces[0],
        pieces[1],
        pieces[10],
        pieces[2],
        pieces[3],
        pieces[4],
        pieces[5],
        pieces[6],
        pieces[7].reshape(heads, HEAD_SIZE),
        pieces[8].reshape(heads, HEAD_SIZE),
        pieces[9].reshape(heads, HEAD_SIZE),
        pieces[11].reshape(heads, HEAD_SIZE, HEAD_SIZE),
        pieces[12].reshape(heads, 2, HEAD_SIZE),
    )


def solution(mesh):
    whole = mesh.shape["seq"] == SG and mesh.shape["dp"] == 4
    return jax.shard_map(
        sequence_body if whole else body,
        mesh=mesh,
        in_specs=(
            P("dp", "seq", None),
            P("dp", "seq"),
            P("dp", "seq"),
            P("dp", "seq", None),
            P("dp", None),
            P("dp", None),
            P("dp", None),
            P("dp", None),
            P("dp", None),
            P("dp", None),
            P("dp"),
            P("dp"),
            P("dp"),
            P("dp"),
            P("dp"),
            P("dp"),
            P("dp"),
            P("dp"),
            P("dp", None),
            P("dp", None),
            P("dp", None),
            P("dp", None, None),
            P("dp", None, None),
        ),
        out_specs=(
            P("dp", "seq", None),
            P("dp", "seq", None),
            P("dp", None),
            P("dp", None),
            P("dp", None),
            P("dp", None),
            P("dp", None),
            P("dp", None),
            P("dp"),
            P("dp"),
            P("dp"),
            P("dp"),
            P("dp"),
            P("dp"),
            P("dp"),
            P("dp"),
            P("dp", None),
            P("dp", None),
            P("dp", None),
            P("dp", None, None),
            P("dp", None, None),
        ),
        check_vma=False,
    )
```

```python
from functools import partial
import math

import jax
import jax.numpy as jnp
import numpy as np
from jax import lax
from jax.experimental import pallas as pl
from jax.experimental.pallas import tpu as pltpu
from jax.sharding import PartitionSpec as P

MODEL_WIDTH = 768
HEAD_COUNT = 12
HEAD_SIZE = 64
LEN = 2048
SG = 8
PQ = 1024


highest = lax.Precision.HIGHEST
norm_eps = 1e-05
masked_score = -1e30


def frequencies():
    half_width = HEAD_SIZE // 2
    return jnp.exp(jnp.arange(half_width, dtype=jnp.float32) * (-math.log(10000.0) / half_width))


def norm_forward(inputs, gains, shifts):
    row_mean = jnp.mean(inputs, axis=-1, keepdims=True)
    centred = inputs - row_mean
    inverse = lax.rsqrt(jnp.mean(centred * centred, axis=-1, keepdims=True) + norm_eps)
    normed = centred * inverse
    return (normed * gains + shifts, normed, inverse)


def norm_backward(upstream, normed, inverse, gains):
    scaled = upstream * gains
    along = jnp.mean(scaled * normed, axis=-1, keepdims=True)
    centre = jnp.mean(scaled, axis=-1, keepdims=True)
    return inverse * (scaled - centre - normed * along)


def doc_masks(segment_row, type_row):
    same_document = segment_row[0::2][:, None] == segment_row[None, :]
    same_type = type_row[0::2][:, None] == type_row[None, :]
    return (same_document, same_type)


def score_block(query_row, type_row_terms, pair_row, key_phase, same_document, same_type):
    key_join = jnp.concatenate([pair_row[:, :HEAD_SIZE], key_phase], axis=-1)
    raw_score = lax.dot_general(
        query_row, key_join, (((1,), (1,)), ((), ())), preferred_element_type=jnp.float32
    )
    type_float = type_row_terms.astype(jnp.float32)
    raw_score = raw_score + jnp.where(same_type, type_float[:, 1:2], type_float[:, 0:1])
    return (jnp.where(same_document, raw_score * HEAD_SIZE ** (-0.5), masked_score), key_join)


def body(
    tokens,
    segments,
    token_types,
    cotangent,
    query_weight,
    key_weight,
    value_weight,
    output_weight,
    inner_weight,
    outer_weight,
    value_bias,
    output_bias,
    inner_bias,
    outer_bias,
    attention_norm_gain,
    first_shift,
    second_gain,
    second_shift,
    content_bias,
    position_bias,
    type_bias,
    relative_kernel,
    type_embed,
):
    local_tokens = tokens.shape[1]
    local_pooled = local_tokens // 2
    group_size = lax.axis_size("seq")
    shard_rank = lax.axis_index("seq")
    item_count = SG * HEAD_COUNT // group_size
    half_width = HEAD_SIZE // 2
    score_scale = HEAD_SIZE ** (-0.5)
    frequency = frequencies()
    duplicate_params = (
        lax.all_gather(query_weight.astype(jnp.bfloat16), "dp", axis=0, tiled=True),
        lax.all_gather(key_weight.astype(jnp.bfloat16), "dp", axis=0, tiled=True),
        lax.all_gather(value_weight.astype(jnp.bfloat16), "dp", axis=0, tiled=True),
        lax.all_gather(output_weight.astype(jnp.bfloat16), "dp", axis=0, tiled=True),
        lax.all_gather(inner_weight.astype(jnp.bfloat16), "dp", axis=0, tiled=True),
        lax.all_gather(outer_weight.astype(jnp.bfloat16), "dp", axis=0, tiled=True),
        lax.all_gather(value_bias.astype(jnp.bfloat16), "dp", axis=0, tiled=True),
        lax.all_gather(output_bias.astype(jnp.bfloat16), "dp", axis=0, tiled=True),
        lax.all_gather(inner_bias.astype(jnp.bfloat16), "dp", axis=0, tiled=True),
        lax.all_gather(outer_bias.astype(jnp.bfloat16), "dp", axis=0, tiled=True),
        lax.all_gather(attention_norm_gain.astype(jnp.bfloat16), "dp", axis=0, tiled=True),
        lax.all_gather(first_shift.astype(jnp.bfloat16), "dp", axis=0, tiled=True),
        lax.all_gather(second_gain.astype(jnp.bfloat16), "dp", axis=0, tiled=True),
        lax.all_gather(second_shift.astype(jnp.bfloat16), "dp", axis=0, tiled=True),
        lax.all_gather(content_bias.astype(jnp.bfloat16), "dp", axis=0, tiled=True),
        lax.all_gather(position_bias.astype(jnp.bfloat16), "dp", axis=0, tiled=True),
        lax.all_gather(type_bias.astype(jnp.bfloat16), "dp", axis=0, tiled=True),
        lax.all_gather(relative_kernel.astype(jnp.bfloat16), "dp", axis=0, tiled=True),
        lax.all_gather(type_embed.astype(jnp.bfloat16), "dp", axis=0, tiled=True),
    )
    value_add = duplicate_params[6].astype(jnp.float32)
    output_add = duplicate_params[7].astype(jnp.float32)
    inner_add = duplicate_params[8].astype(jnp.float32)
    outer_add = duplicate_params[9].astype(jnp.float32)
    gain_one = duplicate_params[10].astype(jnp.float32)
    shift_one = duplicate_params[11].astype(jnp.float32)
    gain_two = duplicate_params[12].astype(jnp.float32)
    shift_two = duplicate_params[13].astype(jnp.float32)
    content_add = duplicate_params[14].astype(jnp.float32)[None, :, None, :]
    position_add = duplicate_params[15].astype(jnp.float32)[None, :, None, :]
    type_add = duplicate_params[16].astype(jnp.float32)[None, :, None, :]
    relative = duplicate_params[17].astype(jnp.float32)
    type_table = duplicate_params[18].astype(jnp.float32)
    whole_segments, whole_types = (
        lax.all_gather(segments, "seq", axis=1, tiled=True),
        lax.all_gather(token_types, "seq", axis=1, tiled=True),
    )
    first_rows = tokens[:, 0::2].astype(jnp.float32)
    second = tokens[:, 1::2].astype(jnp.float32)
    pair_same = (segments[:, 0::2] == segments[:, 1::2])[..., None]
    pooled = jnp.where(pair_same, (first_rows + second) * 0.5, first_rows)
    pooled_low = pooled.astype(jnp.bfloat16)
    queries = jnp.einsum(
        "spd,dhe->shpe",
        pooled_low,
        duplicate_params[0].reshape(MODEL_WIDTH, HEAD_COUNT, HEAD_SIZE),
        preferred_element_type=jnp.float32,
    )
    key_rows = jnp.einsum(
        "ukf,fra->urka",
        tokens,
        duplicate_params[1].reshape(MODEL_WIDTH, HEAD_COUNT, HEAD_SIZE),
        preferred_element_type=jnp.float32,
    )
    value_rows = (
        jnp.einsum(
            "ukf,fra->urka",
            tokens,
            duplicate_params[2].reshape(MODEL_WIDTH, HEAD_COUNT, HEAD_SIZE),
            preferred_element_type=jnp.float32,
        )
        + value_add.reshape(HEAD_COUNT, HEAD_SIZE)[None, :, None, :]
    )
    pair_rows = (
        jnp.concatenate([key_rows, value_rows], axis=-1)
        .astype(jnp.bfloat16)
        .reshape(SG * HEAD_COUNT, local_tokens, 2 * HEAD_SIZE)
    )
    shifted = queries + position_add
    relative_terms = jnp.einsum("shpe,hef->shpf", shifted, relative, precision=highest)
    pooled_place = 2.0 * (
        shard_rank * local_pooled + jnp.arange(local_pooled, dtype=jnp.int32)
    ).astype(jnp.float32)
    query_angle = pooled_place[:, None] * frequency[None, :]
    query_cos = jnp.cos(query_angle)
    query_sin = jnp.sin(query_angle)
    relative_cos = relative_terms[..., :half_width]
    relative_sin = relative_terms[..., half_width:]
    position = jnp.concatenate(
        [
            relative_cos * query_cos + relative_sin * query_sin,
            relative_cos * query_sin - relative_sin * query_cos,
        ],
        axis=-1,
    )
    query_join = (
        jnp.concatenate([queries + content_add, position], axis=-1)
        .astype(jnp.bfloat16)
        .reshape(SG * HEAD_COUNT, local_pooled, 2 * HEAD_SIZE)
    )
    typed = queries + type_add
    type_terms = (
        jnp.einsum("shpe,hbe->shpb", typed, type_table, precision=highest)
        .astype(jnp.bfloat16)
        .reshape(SG * HEAD_COUNT, local_pooled, 2)
    )
    query_heads, type_heads, pair_heads = (
        lax.all_to_all(query_join, "seq", split_axis=0, concat_axis=1, tiled=True),
        lax.all_to_all(type_terms, "seq", split_axis=0, concat_axis=1, tiled=True),
        lax.all_to_all(pair_rows, "seq", split_axis=0, concat_axis=1, tiled=True),
    )
    item_rows = (shard_rank * item_count + jnp.arange(item_count, dtype=jnp.int32)) // HEAD_COUNT
    item_segments = whole_segments[item_rows]
    item_types = whole_types[item_rows]
    key_angle = jnp.arange(LEN, dtype=jnp.float32)[:, None] * frequency[None, :]
    key_phase = jnp.concatenate([jnp.cos(key_angle), jnp.sin(key_angle)], axis=-1).astype(
        jnp.bfloat16
    )

    def attend(packed):
        query_row, type_row_terms, pair_row, segment_row, type_row = packed
        same_document, same_type = doc_masks(segment_row, type_row)
        scores, key_join = score_block(
            query_row, type_row_terms, pair_row, key_phase, same_document, same_type
        )
        row_max = jnp.max(scores, axis=1, keepdims=True)
        exponent = jnp.exp(scores - row_max)
        row_total = jnp.sum(exponent, axis=1, keepdims=True)
        weights = exponent / row_total
        mixture = jnp.dot(
            weights.astype(jnp.bfloat16),
            pair_row[:, HEAD_SIZE:],
            preferred_element_type=jnp.float32,
        )
        return (mixture.astype(jnp.bfloat16), row_max + jnp.log(row_total))

    mixed_heads, log_totals = lax.map(
        attend, (query_heads, type_heads, pair_heads, item_segments, item_types)
    )
    mixed_tokens = lax.all_to_all(
        mixed_heads.reshape(item_count, PQ // 2, 2 * HEAD_SIZE),
        "seq",
        split_axis=1,
        concat_axis=0,
        tiled=True,
    ).reshape(SG, HEAD_COUNT, local_pooled, HEAD_SIZE)
    attention = (
        jnp.einsum(
            "shpe,hed->spd",
            mixed_tokens,
            duplicate_params[3].reshape(HEAD_COUNT, HEAD_SIZE, MODEL_WIDTH),
            preferred_element_type=jnp.float32,
        )
        + output_add
    )
    hidden, normed_one, inverse_one = norm_forward(pooled + attention, gain_one, shift_one)
    hidden_low = hidden.astype(jnp.bfloat16)
    expanded = (
        jnp.einsum(
            "spd,df->spf", hidden_low, duplicate_params[4], preferred_element_type=jnp.float32
        )
        + inner_add
    )
    active = jax.nn.gelu(expanded, approximate=True).astype(jnp.bfloat16)
    branch = (
        jnp.einsum("spf,fd->spd", active, duplicate_params[5], preferred_element_type=jnp.float32)
        + outer_add
    )
    result, normed_two, inverse_two = norm_forward(hidden + branch, gain_two, shift_two)
    output = result.astype(jnp.bfloat16)
    again = (
        lax.all_gather(query_weight.astype(jnp.bfloat16), "dp", axis=0, tiled=True),
        lax.all_gather(key_weight.astype(jnp.bfloat16), "dp", axis=0, tiled=True),
        lax.all_gather(value_weight.astype(jnp.bfloat16), "dp", axis=0, tiled=True),
        lax.all_gather(output_weight.astype(jnp.bfloat16), "dp", axis=0, tiled=True),
        lax.all_gather(inner_weight.astype(jnp.bfloat16), "dp", axis=0, tiled=True),
        lax.all_gather(outer_weight.astype(jnp.bfloat16), "dp", axis=0, tiled=True),
        lax.all_gather(attention_norm_gain.astype(jnp.bfloat16), "dp", axis=0, tiled=True),
        lax.all_gather(second_gain.astype(jnp.bfloat16), "dp", axis=0, tiled=True),
        lax.all_gather(relative_kernel.astype(jnp.bfloat16), "dp", axis=0, tiled=True),
        lax.all_gather(type_embed.astype(jnp.bfloat16), "dp", axis=0, tiled=True),
    )
    query_back = again[0]
    key_back = again[1]
    value_back = again[2]
    output_back = again[3]
    inner_back = again[4]
    outer_back = again[5]
    gain_one_back = again[6].astype(jnp.float32)
    gain_two_back = again[7].astype(jnp.float32)
    relative_back = again[8].astype(jnp.float32)
    table_back = again[9].astype(jnp.float32)
    grad_result = cotangent.astype(jnp.float32)
    grad_gain_two = jnp.sum(grad_result * normed_two, axis=(0, 1))
    grad_shift_two = jnp.sum(grad_result, axis=(0, 1))
    grad_second = norm_backward(grad_result, normed_two, inverse_two, gain_two_back)
    grad_branch = grad_second.astype(jnp.bfloat16)
    grad_outer_weight = jnp.einsum(
        "spf,spd->fd", active, grad_branch, preferred_element_type=jnp.float32
    )
    grad_outer_bias = jnp.sum(grad_branch.astype(jnp.float32), axis=(0, 1))
    grad_active = jnp.einsum(
        "spd,fd->spf", grad_branch, outer_back, preferred_element_type=jnp.float32
    )
    gelu_value, gelu_pull = jax.vjp(partial(jax.nn.gelu, approximate=True), expanded)
    grad_expanded = gelu_pull(grad_active)[0].astype(jnp.bfloat16)
    grad_inner_weight = jnp.einsum(
        "spd,spf->df", hidden_low, grad_expanded, preferred_element_type=jnp.float32
    )
    grad_inner_bias = jnp.sum(grad_expanded.astype(jnp.float32), axis=(0, 1))
    grad_hidden = grad_second + jnp.einsum(
        "spf,df->spd", grad_expanded, inner_back, preferred_element_type=jnp.float32
    )
    grad_gain_one = jnp.sum(grad_hidden * normed_one, axis=(0, 1))
    grad_shift_one = jnp.sum(grad_hidden, axis=(0, 1))
    grad_first = norm_backward(grad_hidden, normed_one, inverse_one, gain_one_back)
    grad_attention = grad_first.astype(jnp.bfloat16)
    grad_output_weight = jnp.einsum(
        "shpe,spd->hed", mixed_tokens, grad_attention, preferred_element_type=jnp.float32
    ).reshape(MODEL_WIDTH, MODEL_WIDTH)
    grad_output_bias = jnp.sum(grad_attention.astype(jnp.float32), axis=(0, 1))
    grad_mixture = jnp.einsum(
        "spd,hed->shpe",
        grad_attention,
        output_back.reshape(HEAD_COUNT, HEAD_SIZE, MODEL_WIDTH),
        preferred_element_type=jnp.float32,
    ).astype(jnp.bfloat16)
    grad_mixed_heads = lax.all_to_all(
        grad_mixture.reshape(SG * HEAD_COUNT, local_pooled // 2, 2 * HEAD_SIZE),
        "seq",
        split_axis=0,
        concat_axis=1,
        tiled=True,
    ).reshape(item_count, PQ, HEAD_SIZE)

    def attend_back(packed):
        query_row, type_row_terms, pair_row, segment_row, type_row, log_row, grad_row = packed
        same_document, same_type = doc_masks(segment_row, type_row)
        scores, key_join = score_block(
            query_row, type_row_terms, pair_row, key_phase, same_document, same_type
        )
        weights = jnp.exp(scores - log_row)
        grad_weights = lax.dot_general(
            grad_row,
            pair_row[:, HEAD_SIZE:],
            (((1,), (1,)), ((), ())),
            preferred_element_type=jnp.float32,
        )
        row_dot = jnp.sum(grad_weights * weights, axis=1, keepdims=True)
        grad_scores = (weights * (grad_weights - row_dot)).astype(jnp.bfloat16)
        grad_query = (
            jnp.dot(grad_scores, key_join, preferred_element_type=jnp.float32) * score_scale
        ).astype(jnp.bfloat16)
        grad_float = grad_scores.astype(jnp.float32) * score_scale
        grad_same = jnp.sum(jnp.where(same_type, grad_float, 0.0), axis=1)
        grad_other = jnp.sum(jnp.where(same_type, 0.0, grad_float), axis=1)
        grad_kinds = jnp.stack([grad_other, grad_same], axis=-1).astype(jnp.bfloat16)
        grad_keys = (
            lax.dot_general(
                grad_scores,
                query_row[:, :HEAD_SIZE],
                (((0,), (0,)), ((), ())),
                preferred_element_type=jnp.float32,
            )
            * score_scale
        )
        grad_values = lax.dot_general(
            weights.astype(jnp.bfloat16),
            grad_row,
            (((0,), (0,)), ((), ())),
            preferred_element_type=jnp.float32,
        )
        return (
            grad_query,
            grad_kinds,
            jnp.concatenate([grad_keys, grad_values], axis=-1).astype(jnp.bfloat16),
        )

    grad_query_heads, grad_type_heads, grad_pair_heads = lax.map(
        attend_back,
        (
            query_heads,
            type_heads,
            pair_heads,
            item_segments,
            item_types,
            log_totals,
            grad_mixed_heads,
        ),
    )
    grad_query_tok, grad_type_tok, grad_pair_tok = (
        lax.all_to_all(grad_query_heads, "seq", split_axis=1, concat_axis=0, tiled=True),
        lax.all_to_all(grad_type_heads, "seq", split_axis=1, concat_axis=0, tiled=True),
        lax.all_to_all(grad_pair_heads, "seq", split_axis=1, concat_axis=0, tiled=True),
    )
    grad_query_join = grad_query_tok.astype(jnp.float32).reshape(
        SG, HEAD_COUNT, local_pooled, 2 * HEAD_SIZE
    )
    grad_content = grad_query_join[..., :HEAD_SIZE]
    grad_first_half = grad_query_join[..., HEAD_SIZE : HEAD_SIZE + half_width]
    grad_second_half = grad_query_join[..., HEAD_SIZE + half_width :]
    grad_relative_terms = jnp.concatenate(
        [
            grad_first_half * query_cos + grad_second_half * query_sin,
            grad_first_half * query_sin - grad_second_half * query_cos,
        ],
        axis=-1,
    )
    grad_shifted = jnp.einsum(
        "shpf,hef->shpe", grad_relative_terms, relative_back, precision=highest
    )
    grad_relative_kernel = jnp.einsum(
        "shpe,shpf->hef", shifted, grad_relative_terms, precision=highest
    )
    grad_type_terms = grad_type_tok.astype(jnp.float32).reshape(SG, HEAD_COUNT, local_pooled, 2)
    grad_typed = jnp.einsum("shpb,hbe->shpe", grad_type_terms, table_back, precision=highest)
    grad_type_embed = jnp.einsum("shpe,shpb->hbe", typed, grad_type_terms, precision=highest)
    query_rows_gradient = (grad_content + grad_shifted + grad_typed).astype(jnp.bfloat16)
    grad_content_bias = jnp.sum(grad_content, axis=(0, 2))
    grad_position_bias = jnp.sum(grad_shifted, axis=(0, 2))
    grad_type_bias = jnp.sum(grad_typed, axis=(0, 2))
    grad_query_weight = jnp.einsum(
        "spd,shpe->dhe", pooled_low, query_rows_gradient, preferred_element_type=jnp.float32
    ).reshape(MODEL_WIDTH, MODEL_WIDTH)
    grad_pooled = grad_first + jnp.einsum(
        "shpe,dhe->spd",
        query_rows_gradient,
        query_back.reshape(MODEL_WIDTH, HEAD_COUNT, HEAD_SIZE),
        preferred_element_type=jnp.float32,
    )
    grad_pairs = grad_pair_tok.reshape(SG, HEAD_COUNT, local_tokens, 2 * HEAD_SIZE)
    key_rows_gradient = grad_pairs[..., :HEAD_SIZE]
    value_rows_gradient = grad_pairs[..., HEAD_SIZE:]
    grad_key_weight = jnp.einsum(
        "ozb,opzx->bpx", tokens, key_rows_gradient, preferred_element_type=jnp.float32
    ).reshape(MODEL_WIDTH, MODEL_WIDTH)
    grad_value_weight = jnp.einsum(
        "ozb,opzx->bpx", tokens, value_rows_gradient, preferred_element_type=jnp.float32
    ).reshape(MODEL_WIDTH, MODEL_WIDTH)
    grad_value_bias = jnp.sum(value_rows_gradient.astype(jnp.float32), axis=(0, 2)).reshape(
        MODEL_WIDTH
    )
    grad_direct = jnp.einsum(
        "mivt,git->mvg",
        key_rows_gradient,
        key_back.reshape(MODEL_WIDTH, HEAD_COUNT, HEAD_SIZE),
        preferred_element_type=jnp.float32,
    )
    grad_direct = grad_direct + jnp.einsum(
        "mivt,git->mvg",
        value_rows_gradient,
        value_back.reshape(MODEL_WIDTH, HEAD_COUNT, HEAD_SIZE),
        preferred_element_type=jnp.float32,
    )
    pool_first = jnp.where(pair_same, 0.5 * grad_pooled, grad_pooled)
    pool_second = jnp.where(pair_same, 0.5 * grad_pooled, 0.0)
    grad_tokens = (
        grad_direct
        + jnp.stack([pool_first, pool_second], axis=2).reshape(SG, local_tokens, MODEL_WIDTH)
    ).astype(jnp.bfloat16)
    summed = lax.psum(
        (
            grad_query_weight,
            grad_key_weight,
            grad_value_weight,
            grad_output_weight,
            grad_inner_weight,
            grad_outer_weight,
            grad_value_bias,
            grad_output_bias,
            grad_inner_bias,
            grad_outer_bias,
            grad_gain_one,
            grad_shift_one,
            grad_gain_two,
            grad_shift_two,
            grad_content_bias,
            grad_position_bias,
            grad_type_bias,
            grad_relative_kernel,
            grad_type_embed,
        ),
        "seq",
    )
    owned = (
        lax.psum_scatter(
            summed[0].astype(jnp.bfloat16), "dp", scatter_dimension=0, tiled=True
        ).astype(jnp.float32),
        lax.psum_scatter(
            summed[1].astype(jnp.bfloat16), "dp", scatter_dimension=0, tiled=True
        ).astype(jnp.float32),
        lax.psum_scatter(
            summed[2].astype(jnp.bfloat16), "dp", scatter_dimension=0, tiled=True
        ).astype(jnp.float32),
        lax.psum_scatter(
            summed[3].astype(jnp.bfloat16), "dp", scatter_dimension=0, tiled=True
        ).astype(jnp.float32),
        lax.psum_scatter(
            summed[4].astype(jnp.bfloat16), "dp", scatter_dimension=0, tiled=True
        ).astype(jnp.float32),
        lax.psum_scatter(
            summed[5].astype(jnp.bfloat16), "dp", scatter_dimension=0, tiled=True
        ).astype(jnp.float32),
        lax.psum_scatter(
            summed[6].astype(jnp.bfloat16), "dp", scatter_dimension=0, tiled=True
        ).astype(jnp.float32),
        lax.psum_scatter(
            summed[7].astype(jnp.bfloat16), "dp", scatter_dimension=0, tiled=True
        ).astype(jnp.float32),
        lax.psum_scatter(
            summed[8].astype(jnp.bfloat16), "dp", scatter_dimension=0, tiled=True
        ).astype(jnp.float32),
        lax.psum_scatter(
            summed[9].astype(jnp.bfloat16), "dp", scatter_dimension=0, tiled=True
        ).astype(jnp.float32),
        lax.psum_scatter(
            summed[10].astype(jnp.bfloat16), "dp", scatter_dimension=0, tiled=True
        ).astype(jnp.float32),
        lax.psum_scatter(
            summed[11].astype(jnp.bfloat16), "dp", scatter_dimension=0, tiled=True
        ).astype(jnp.float32),
        lax.psum_scatter(
            summed[12].astype(jnp.bfloat16), "dp", scatter_dimension=0, tiled=True
        ).astype(jnp.float32),
        lax.psum_scatter(
            summed[13].astype(jnp.bfloat16), "dp", scatter_dimension=0, tiled=True
        ).astype(jnp.float32),
        lax.psum_scatter(
            summed[14].astype(jnp.bfloat16), "dp", scatter_dimension=0, tiled=True
        ).astype(jnp.float32),
        lax.psum_scatter(
            summed[15].astype(jnp.bfloat16), "dp", scatter_dimension=0, tiled=True
        ).astype(jnp.float32),
        lax.psum_scatter(
            summed[16].astype(jnp.bfloat16), "dp", scatter_dimension=0, tiled=True
        ).astype(jnp.float32),
        lax.psum_scatter(
            summed[17].astype(jnp.bfloat16), "dp", scatter_dimension=0, tiled=True
        ).astype(jnp.float32),
        lax.psum_scatter(
            summed[18].astype(jnp.bfloat16), "dp", scatter_dimension=0, tiled=True
        ).astype(jnp.float32),
    )
    return (
        output,
        grad_tokens,
        owned[0],
        owned[1],
        owned[2],
        owned[3],
        owned[4],
        owned[5],
        owned[6],
        owned[7],
        owned[8],
        owned[9],
        owned[10],
        owned[11],
        owned[12],
        owned[13],
        owned[14],
        owned[15],
        owned[16],
        owned[17],
        owned[18],
    )


BF16 = jnp.bfloat16
F32 = jnp.float32
PAIRS = HEAD_COUNT // 2
LANES = 2 * HEAD_SIZE
ROWS = 256
FAR = -(2.0**100)
FF = 3072
NN = (((1,), (0,)), ((), ()))
NT = (((1,), (1,)), ((), ()))
TN = (((0,), (0,)), ((), ()))


def mm(left, right, dims=NN):
    return lax.dot_general(left, right, dims, preferred_element_type=F32)


def split(value):
    high = value.astype(BF16)
    return high, (value - high.astype(F32)).astype(BF16)


def lane_ids(rows):
    return lax.broadcasted_iota(jnp.int32, (rows, LANES), 1)


VECTORS = 16


def pair_maps(relative):
    row = lax.broadcasted_iota(jnp.int32, (HEAD_SIZE, LANES), 0)
    twice = (lane_ids(HEAD_SIZE) % HEAD_SIZE == row).astype(BF16)
    lane = lane_ids(LANES)
    row = lax.broadcasted_iota(jnp.int32, (LANES, LANES), 0)
    crossed = (row < HEAD_SIZE) != (lane < HEAD_SIZE)
    plain = jnp.where(crossed, mm(relative, twice), 0.0).astype(BF16)
    half = HEAD_SIZE // 2
    partner = jnp.where(lane % HEAD_SIZE < half, lane + half, lane - half)
    swapped = mm(plain, (row == partner).astype(BF16)).astype(BF16)
    return plain, swapped


def fold_maps(grads):
    row = lax.broadcasted_iota(jnp.int32, (LANES, 2 * LANES), 0)
    lane = lax.broadcasted_iota(jnp.int32, (LANES, 2 * LANES), 1)
    crossed = (row < HEAD_SIZE) != (lane % LANES < HEAD_SIZE)
    high, low = split(jnp.where(crossed, grads, 0.0))
    row = lax.broadcasted_iota(jnp.int32, (2 * LANES, LANES), 0)
    lane = lax.broadcasted_iota(jnp.int32, (2 * LANES, LANES), 1)
    half = HEAD_SIZE // 2
    at = row % HEAD_SIZE
    partner = jnp.where(at < half, at + half, at - half)
    fold = (jnp.where(row < LANES, at, partner) == lane).astype(BF16)
    return mm(high, fold) + mm(low, fold)


def kind_maps(vectors):
    row = lax.broadcasted_iota(jnp.int32, (VECTORS, 4 * LANES), 0)
    column = lax.broadcasted_iota(jnp.int32, (VECTORS, 4 * LANES), 1)
    lane = column % LANES
    wanted = (lane >= 3) & (lane < 6) & (row == 11 - (column // LANES) % 2)
    both = mm(vectors.astype(BF16), wanted.astype(BF16), TN)
    row = lax.broadcasted_iota(jnp.int32, (LANES, 4 * LANES), 0)
    column = lax.broadcasted_iota(jnp.int32, (LANES, 4 * LANES), 1)
    return jnp.where((row < HEAD_SIZE) == (column < 2 * LANES), both, 0.0).astype(BF16)


MESH = pl.DeviceIdType.MESH
SUM_ROWS = 48
STAGES = ("core", "y", "x", "near", "far", "far_back", "near_back", "x_back")


class Place:
    def __init__(self):
        self.seq, self.dp = lax.axis_index("seq"), lax.axis_index("dp")
        self.core, self.y = self.dp % 2, self.dp // 2
        self.x, self.near, self.far = self.seq % 2, (self.seq // 2) % 2, self.seq // 4
        self.partner = {
            "core": (self.seq, self.dp + 1 - 2 * self.core),
            "y": (self.seq, self.dp + 2 - 4 * self.y),
            "x": (self.seq + 1 - 2 * self.x, self.dp),
            "near": (self.seq + 2 - 4 * self.near, self.dp),
            "far": (self.seq + 4 - 8 * self.far, self.dp),
        }

    def peers(self):
        return [((self.seq + k) % SG, self.dp) for k in range(1, SG)]

    def greet(self):
        barrier = pltpu.get_barrier_semaphore()
        others = [self.partner["core"], self.partner["y"], *self.peers()]
        for device in others:
            pl.semaphore_signal(barrier, inc=1, device_id=device, device_id_type=MESH)
        pl.semaphore_wait(barrier, len(others))


def add_rows(target, addend, rows):
    def step(i, carry):
        at = pl.ds(pl.multiple_of(i * SUM_ROWS, 16), SUM_ROWS)
        left, right = target(at), addend(at)
        left[...] = left[...] + right[...]
        return carry

    lax.fori_loop(0, rows // SUM_ROWS, step, 0)


class Chunk:
    def __init__(self, place, index, source, rows, columns, buffers, send, receive, local):
        self.place, self.source, self.rows, self.columns = place, source, rows, columns
        self.own, self.from_core, self.from_y, self.from_x, self.from_near, self.from_far, self.full = buffers
        self.send_at = lambda stage, k=0: send.at[index, STAGES.index(stage) + (8 if k else 0)]
        self.receive_at = lambda stage, k=0: receive.at[index, STAGES.index(stage) + (8 if k else 0)]
        self.local = lambda k: local.at[index, k]
        half, quarter = rows // 2, rows // 4
        self.my_columns = pl.ds(pl.multiple_of(place.x * (columns // 2), 128), columns // 2)
        self.other_columns = pl.ds(
            pl.multiple_of((1 - place.x) * (columns // 2), 128), columns // 2
        )
        self.my_half = pl.multiple_of(place.near * half, 16)
        self.my_quarter = pl.multiple_of(place.near * half + place.far * quarter, 16)

    def remote(self, stage, source, target, k=0):
        return pltpu.make_async_remote_copy(
            src_ref=source,
            dst_ref=target,
            send_sem=self.send_at(stage, k),
            recv_sem=self.receive_at(stage, k),
            device_id=self.place.partner[stage.split("_")[0]],
            device_id_type=MESH,
        )

    def locals(self):
        if self.own is None:
            return []
        return [
            pltpu.make_async_copy(
                self.source(2 * k + self.place.core), self.own.at[k], self.local(k)
            )
            for k in range(2)
        ]

    def copies(self, stage):
        place, rows = self.place, self.rows
        half, quarter = rows // 2, rows // 4
        if stage == "core":
            return [
                self.remote(
                    stage, self.source(2 * k + 1 - place.core), self.from_core.at[k], k
                )
                for k in range(2)
            ]
        if stage == "y":
            return [self.remote(stage, self.from_core.at[1 - place.y], self.from_y)]
        if stage == "x":
            return [self.remote(stage, self.from_y.at[:, self.other_columns], self.from_x)]
        if stage == "near":
            other = pl.ds(pl.multiple_of((1 - place.near) * half, 16), half)
            return [self.remote(stage, self.from_x.at[other, :], self.from_near)]
        if stage == "far":
            other = pl.ds(pl.multiple_of((1 - place.far) * quarter, 16), quarter)
            return [self.remote(stage, self.from_near.at[other, :], self.from_far)]
        if stage == "far_back":
            mine = self.full.at[pl.ds(self.my_quarter, quarter), self.my_columns]
            return [self.remote(stage, self.from_far, mine)]
        if stage == "near_back":
            mine = self.full.at[pl.ds(self.my_half, half), self.my_columns]
            return [self.remote(stage, mine, mine)]
        mine = self.full.at[:, self.my_columns]
        return [self.remote(stage, mine, mine)]

    def start(self, stage):
        if stage == "core":
            for copy in self.locals():
                copy.start()
        for copy in self.copies(stage):
            copy.start()

    def finish(self, stage):
        place, rows = self.place, self.rows
        half, quarter = rows // 2, rows // 4
        for copy in self.copies(stage):
            copy.wait_recv()
        if stage == "core":
            for copy in self.locals():
                copy.wait()
            for k in range(2):
                kept = (
                    self.source(2 * k + place.core) if self.own is None else self.own.at[k]
                )
                add_rows(
                    lambda at: self.from_core.at[k, at, :], lambda at: kept.at[at, :], rows
                )
        elif stage == "y":
            add_rows(
                lambda at: self.from_y.at[at, :],
                lambda at: self.from_core.at[place.y, at, :],
                rows,
            )
        elif stage == "x":
            add_rows(
                lambda at: self.from_x.at[at, :],
                lambda at: self.from_y.at[at, self.my_columns],
                rows,
            )
        elif stage == "near":
            add_rows(
                lambda at: self.from_near.at[at, :],
                lambda at: self.from_x.at[
                    pl.ds(pl.multiple_of(at.start + self.my_half, 16), SUM_ROWS), :
                ],
                half,
            )
        elif stage == "far":
            begin = place.far * quarter
            add_rows(
                lambda at: self.from_far.at[at, :],
                lambda at: self.from_near.at[
                    pl.ds(pl.multiple_of(at.start + begin, 16), SUM_ROWS), :
                ],
                quarter,
            )

    def place_piece(self):
        def step(i, carry):
            at = pl.ds(pl.multiple_of(i * SUM_ROWS, 16), SUM_ROWS)
            to = pl.ds(pl.multiple_of(i * SUM_ROWS + self.my_quarter, 16), SUM_ROWS)
            self.full[to, self.my_columns] = self.from_far[at, :]
            return carry

        lax.fori_loop(0, self.rows // 4 // SUM_ROWS, step, 0)

    def step(self, stage):
        at = STAGES.index(stage)
        if at > 0:
            self.finish(STAGES[at - 1])
        if stage == "far_back":
            self.place_piece()
        self.start(stage)

    def close(self, stages):
        for stage in stages:
            for copy in self.copies(stage):
                copy.wait_send()


DOWN, UP = STAGES[:5], STAGES[5:]
WHOLE = 3


def down_buffers(rows, columns, own):
    buffer = lambda *shape: pltpu.VMEM(shape, BF16)
    return [
        *([buffer(2, rows, columns)] if own else []),
        buffer(2, rows, columns),
        buffer(rows, columns),
        buffer(rows, columns // 2),
        buffer(rows // 2, columns // 2),
        buffer(rows // 4, columns // 2),
    ]


def grad_chunks():
    quarter = MODEL_WIDTH // 4
    half = MODEL_WIDTH // 2
    early = [
        (0, MODEL_WIDTH, 0, 0, half, MODEL_WIDTH),
        (0, MODEL_WIDTH, half, 0, half, MODEL_WIDTH),
        (1, quarter, 0, 0, quarter, FF // 2),
        (1, quarter, 0, FF // 2, quarter, FF // 2),
        (2, quarter, 0, 0, quarter, MODEL_WIDTH),
    ]
    late = [(j, quarter, 0, 0, quarter, MODEL_WIDTH) for j in (3, 4, 5)]
    late.insert(0, (6, quarter, 0, 0, quarter, 2 * LANES))
    return early, late


def chunk_source(grad, chunk):
    _, owner_rows, row, column, rows, columns = chunk

    def source(owner):
        begin = pl.multiple_of(owner * owner_rows + row, 16)
        return grad.at[pl.ds(begin, rows), pl.ds(column, columns)]

    return source


SEND_ORDER = (4, 3, 5, 2, 6, 1, 7, 0)


def finish_kernel(
    grad_query_ref,
    grad_key_ref,
    grad_value_ref,
    tokens_ref,
    pooled_ref,
    grad_first_ref,
    pool_ref,
    weights_ref,
    small_ref,
    *refs,
):
    early, late = grad_chunks()
    early = early[WHOLE:]
    pieces, refs = refs[: len(early)], refs[len(early) :]
    tokens_out, refs = refs[0], refs[1:]
    count = len(early) + len(late)
    outs, refs = refs[:count], refs[count:]
    fulls, refs = refs[:count], refs[count:]
    buffers, refs = refs[: 5 * len(late)], refs[5 * len(late) :]
    (
        tokens_stage,
        late_grads,
        send,
        receive,
        token_send,
        token_receive,
        token_local,
    ) = refs
    place = Place()
    place.greet()
    first = []
    for i, chunk in enumerate(early):
        kept = [None, None, None, None, None, pieces[i], fulls[i]]
        first.append(Chunk(place, i, None, *chunk[4:], kept, send, receive, None))
    second = []
    for j, chunk in enumerate(late):
        i = len(early) + j
        kept = [None, *buffers[5 * j : 5 * j + 5], fulls[i]]
        source = chunk_source(late_grads.at[j - 1] if j else small_ref, chunk)
        second.append(Chunk(place, i, source, *chunk[4:], kept, send, receive, None))
    for item in first:
        item.place_piece()
        item.start("far_back")
    second[0].start("core")

    moved = []

    def send_tokens(k):
        to = (place.seq + k) % SG
        block = LEN // SG
        rows = pl.ds(pl.multiple_of(to * block, block), block)
        pooled_rows = pl.ds(pl.multiple_of(to * (block // 2), block // 2), block // 2)
        weight = lambda j: weights_ref[:, j * MODEL_WIDTH : (j + 1) * MODEL_WIDTH]
        grad_pooled = grad_first_ref[pooled_rows, :] + mm(
            grad_query_ref[pooled_rows, :], weight(0), NT
        )
        high, low = split(grad_pooled)
        total = mm(grad_key_ref[rows, :], weight(1), NT)
        total += mm(grad_value_ref[rows, :], weight(2), NT)
        total += mm(pool_ref[to], high, TN) + mm(pool_ref[to], low, TN)
        tokens_stage[to] = total.astype(BF16)
        if k == 0:
            copy = pltpu.make_async_copy(
                tokens_stage.at[to], tokens_out.at[place.seq], token_local
            )
        else:
            copy = pltpu.make_async_remote_copy(
                src_ref=tokens_stage.at[to],
                dst_ref=tokens_out.at[place.seq],
                send_sem=token_send.at[k - 1],
                recv_sem=token_receive.at[k - 1],
                device_id=(to, place.dp),
                device_id_type=MESH,
            )
        copy.start()
        moved.append(copy)

    for k in SEND_ORDER[:3]:
        send_tokens(k)
    for item in first:
        item.step("near_back")
    for k in SEND_ORDER[3:6]:
        send_tokens(k)
    for item in first:
        item.step("x_back")
    for k in SEND_ORDER[6:]:
        send_tokens(k)

    operands = [
        (pooled_ref, grad_query_ref),
        (tokens_ref, grad_key_ref),
        (tokens_ref, grad_value_ref),
    ]
    for j, (left, right) in enumerate(operands):
        for r in range(0, MODEL_WIDTH, 256):
            late_grads[j, r : r + 256, :] = mm(left[:, r : r + 256], right[...], TN).astype(BF16)
        second[j + 1].start("core")
        second[j].step("y")
    second[len(late) - 1].step("y")
    for stage in STAGES[2:]:
        for item in second:
            item.step(stage)

    for item, out in zip(first, outs):
        item.finish(STAGES[-1])
        out[...] = item.full[...]
        item.close(UP)
    for item, out in zip(second, outs[len(first) :]):
        item.finish(STAGES[-1])
        out[...] = item.full[...]
        item.close(STAGES)
    for copy in moved:
        copy.wait()


def finish(
    grad_query, grad_key, grad_value, tokens, pooled, grad_first, pool, weights, small, pieces
):
    anywhere = pl.BlockSpec(memory_space=pl.ANY)
    early, late = grad_chunks()
    early = early[WHOLE:]
    chunks = early + late
    count = len(chunks)
    inside = pl.BlockSpec(memory_space=pltpu.VMEM)
    out_tokens = (SG, LEN // SG, MODEL_WIDTH)
    return pl.pallas_call(
        finish_kernel,
        in_specs=[inside] * (9 + len(early)),
        out_specs=[anywhere, *[inside] * count],
        out_shape=[
            jax.ShapeDtypeStruct(out_tokens, BF16),
            *[jax.ShapeDtypeStruct(chunk[4:], BF16) for chunk in chunks],
        ],
        scratch_shapes=[
            *[pltpu.VMEM(chunk[4:], BF16) for chunk in chunks],
            *[buffer for chunk in late for buffer in down_buffers(*chunk[4:], False)],
            pltpu.VMEM(out_tokens, BF16),
            pltpu.VMEM((3, MODEL_WIDTH, MODEL_WIDTH), BF16),
            pltpu.SemaphoreType.DMA((count, 16)),
            pltpu.SemaphoreType.DMA((count, 16)),
            pltpu.SemaphoreType.DMA((SG - 1,)),
            pltpu.SemaphoreType.DMA((SG - 1,)),
            pltpu.SemaphoreType.DMA,
        ],
        compiler_params=pltpu.CompilerParams(
            collective_id=3, has_side_effects=True, vmem_limit_bytes=58 * 2**20
        ),
        name="finish",
    )(
        grad_query,
        grad_key,
        grad_value,
        tokens,
        pooled,
        grad_first,
        pool,
        weights,
        small,
        *pieces,
    )


def attend_kernel(
    query_ref,
    key_ref,
    value_ref,
    relative_ref,
    vectors_ref,
    query_side_ref,
    key_side_ref,
    phase_ref,
    cos_ref,
    sin_ref,
    cotangent_ref,
    mixture_ref,
    join_ref,
    upstream_ref,
    key_join,
    value_join,
    send,
    receive,
    local,
):
    place = Place()

    def upstream_copies():
        copies = [
            pltpu.make_async_copy(
                cotangent_ref.at[place.seq], upstream_ref.at[place.seq], local
            )
        ]
        for k in range(1, SG):
            to = (place.seq + k) % SG
            copies.append(
                pltpu.make_async_remote_copy(
                    src_ref=cotangent_ref.at[to],
                    dst_ref=upstream_ref.at[place.seq],
                    send_sem=send.at[k - 1],
                    recv_sem=receive.at[k - 1],
                    device_id=(to, place.dp),
                    device_id_type=MESH,
                )
            )
        return copies

    @pl.when(pl.program_id(0) == 0)
    def _():
        place.greet()
        for copy in upstream_copies():
            copy.start()

    query = query_ref[...]
    high, low = split(query)
    plain, swapped = pair_maps(relative_ref[...])
    kinds = kind_maps(vectors_ref[...])
    maps = jnp.concatenate([plain, swapped, kinds], axis=1)
    position_add, type_add = vectors_ref[8:9, :].astype(BF16), vectors_ref[9:10, :].astype(BF16)
    map_add = jnp.concatenate(
        [mm(position_add, plain), mm(position_add, swapped), mm(type_add, kinds)], axis=1
    )
    terms = mm(jnp.concatenate([high, low], axis=1), jnp.concatenate([maps, maps], axis=0))
    terms = terms + map_add
    lane = lane_ids(PQ)
    left = lane < HEAD_SIZE
    content = query + vectors_ref[7:8, :]
    position = terms[:, :LANES] * cos_ref[...] + terms[:, LANES : 2 * LANES] * sin_ref[...]
    side = query_side_ref[...]
    typed = (lane >= 3) & (lane < 6)
    scale = HEAD_SIZE ** (-0.5)
    for h in range(2):
        first, second = (content, position) if h == 0 else (position, content)
        join_ref[h, :, :LANES] = (jnp.where(left, first, second) * scale).astype(BF16)
        base = 2 * LANES * (h + 1)
        same = terms[:, base : base + LANES]
        other = terms[:, base + LANES : base + 2 * LANES]
        kind = jnp.where(side > 0.5, same, other) * scale
        join_ref[h, :, LANES:] = jnp.where(typed, kind, side).astype(BF16)
    key_left = lane_ids(LEN) < HEAD_SIZE
    key_join[:, LANES:] = key_side_ref[...]
    value_join[:, :LANES] = value_ref[...]
    value_join[:, LANES:] = key_side_ref[...]
    tile_lane = lane_ids(ROWS)
    for h in range(2):
        pieces = (key_ref[...], phase_ref[...]) if h == 0 else (phase_ref[...], key_ref[...])
        key_join[:, :LANES] = jnp.where(key_left, *pieces)
        for i in range(PQ // ROWS):
            rows = slice(i * ROWS, (i + 1) * ROWS)
            scores = mm(join_ref[h, rows, :], key_join[...], NT)
            top = jnp.max(scores, axis=1, keepdims=True)
            weights = jnp.exp(scores - top).astype(BF16)
            mixed = mm(weights, value_join[...])
            total = mixed[:, LANES + 6 : LANES + 7]
            result = (mixed[:, :LANES] / total).astype(BF16)
            if h == 0:
                mixture_ref[rows, :] = result
            else:
                mixture_ref[rows, :] = jnp.where(
                    tile_lane < HEAD_SIZE, mixture_ref[rows, :], result
                )
            shift = -(top + jnp.log(total))
            one = shift.astype(BF16).astype(F32)
            two = (shift - one).astype(BF16).astype(F32)
            three = shift - one - two
            extra = jnp.where(tile_lane == 6, one, jnp.where(tile_lane == 7, two, three))
            kept = join_ref[h, rows, LANES:].astype(F32)
            inside = (tile_lane >= 6) & (tile_lane < 9)
            join_ref[h, rows, LANES:] = jnp.where(inside, extra, kept).astype(BF16)

    @pl.when(pl.program_id(0) == PAIRS - 1)
    def _():
        for copy in upstream_copies():
            copy.wait()


def attend_forward(
    query, pairs, relative, vectors, query_side, key_side, phase, cosm, sinm, cotangent
):
    whole = lambda shape: pl.BlockSpec(shape, lambda i: (0, 0))
    return pl.pallas_call(
        attend_kernel,
        grid=(PAIRS,),
        in_specs=[
            pl.BlockSpec((PQ, LANES), lambda i: (0, i)),
            pl.BlockSpec((LEN, LANES), lambda i: (0, i)),
            pl.BlockSpec((LEN, LANES), lambda i: (0, i + PAIRS)),
            pl.BlockSpec((LANES, HEAD_SIZE), lambda i: (i, 0)),
            pl.BlockSpec((VECTORS, LANES), lambda i: (0, i)),
            whole((PQ, LANES)),
            whole((LEN, LANES)),
            whole((LEN, LANES)),
            whole((PQ, LANES)),
            whole((PQ, LANES)),
            pl.BlockSpec(memory_space=pl.ANY),
        ],
        out_specs=[
            pl.BlockSpec((PQ, LANES), lambda i: (0, i)),
            pl.BlockSpec((2, PQ, 2 * LANES), lambda i: (i, 0, 0)),
            pl.BlockSpec(memory_space=pl.ANY),
        ],
        out_shape=[
            jax.ShapeDtypeStruct((PQ, MODEL_WIDTH), BF16),
            jax.ShapeDtypeStruct((HEAD_COUNT, PQ, 2 * LANES), BF16),
            jax.ShapeDtypeStruct(cotangent.shape, BF16),
        ],
        scratch_shapes=[
            pltpu.VMEM((LEN, 2 * LANES), BF16),
            pltpu.VMEM((LEN, 2 * LANES), BF16),
            pltpu.SemaphoreType.DMA((SG - 1,)),
            pltpu.SemaphoreType.DMA((SG - 1,)),
            pltpu.SemaphoreType.DMA,
        ],
        cost_estimate=pl.CostEstimate(
            flops=4 * HEAD_COUNT * PQ * LEN * 256,
            bytes_accessed=20_000_000,
            transcendentals=HEAD_COUNT * PQ * LEN,
        ),
        compiler_params=pltpu.CompilerParams(
            collective_id=5, has_side_effects=True, vmem_limit_bytes=56 * 2**20
        ),
        name="attend_forward",
    )(query, pairs, pairs, relative, vectors, query_side, key_side, phase, cosm, sinm, cotangent)


FF_STEP = 768
FF_TILES = FF // FF_STEP
ROW_TILES = PQ // ROWS


def row_norm(value):
    centred = value - jnp.mean(value, axis=1, keepdims=True)
    inverse = lax.rsqrt(jnp.mean(centred * centred, axis=1, keepdims=True) + norm_eps)
    return centred * inverse, inverse


def row_norm_back(scaled, normed, inverse):
    along = jnp.mean(scaled * normed, axis=1, keepdims=True)
    return inverse * (scaled - jnp.mean(scaled, axis=1, keepdims=True) - normed * along)


def gelu_pieces(value):
    rate = math.sqrt(2.0 / math.pi)
    square = value * value
    bend = jnp.tanh(rate * value * (1.0 + 0.044715 * square))
    half = 0.5 * (1.0 + bend)
    slope = half + (0.5 * rate) * value * (1.0 - bend * bend) * (1.0 + 0.134145 * square)
    return value * half, slope


def mlp_kernel(
    mixture_ref,
    pooled_ref,
    upstream_ref,
    output_weight_ref,
    inner_weight_ref,
    outer_weight_ref,
    vectors_ref,
    inner_add_ref,
    output_ref,
    grad_mixture_ref,
    grad_first_ref,
    grad_outer_ref,
    grad_inner_ref,
    grad_output_ref,
    sums_ref,
    inner_sums_ref,
    active,
    slopes,
    grad_expanded,
    hidden_low,
    grad_branch,
    grad_attention,
    output_stage,
    mixture_stage,
    first_stage,
    send,
    receive,
    local,
):
    step = pl.program_id(0)
    place = Place()
    block = PQ // SG
    tile = (step + place.seq // 2 + 1) % ROW_TILES
    begin = pl.multiple_of(tile * ROWS, ROWS)

    def output_copy(to):
        return pltpu.make_async_remote_copy(
            src_ref=output_stage.at[to],
            dst_ref=output_ref.at[place.seq],
            send_sem=send.at[to],
            recv_sem=receive.at[place.seq],
            device_id=(to, place.dp),
            device_id_type=MESH,
        )

    def kept_copy():
        return pltpu.make_async_copy(
            output_stage.at[place.seq], output_ref.at[place.seq], local.at[0]
        )

    def row_copies():
        rows = pl.ds(begin, ROWS)
        return [
            pltpu.make_async_copy(
                mixture_stage.at[rows, :], grad_mixture_ref.at[rows, :], local.at[1 + 2 * tile]
            ),
            pltpu.make_async_copy(
                first_stage.at[rows, :], grad_first_ref.at[rows, :], local.at[2 + 2 * tile]
            ),
        ]

    @pl.when(step == 0)
    def _():
        place.greet()

    @pl.when(step < ROW_TILES)
    def _():
        rows = pl.ds(begin, ROWS)
        vector = lambda j: vectors_ref[j : j + 1, :]
        output_add, outer_add, gain_one, shift_one, gain_two, shift_two = map(vector, range(1, 7))
        attention = mm(mixture_ref[rows, :], output_weight_ref[...]) + output_add
        normed_one, inverse_one = row_norm(pooled_ref[rows, :] + attention)
        hidden = normed_one * gain_one + shift_one
        low_hidden = hidden.astype(BF16)
        hidden_low[rows, :] = low_hidden
        branch = jnp.zeros((ROWS, MODEL_WIDTH), F32)
        for j in range(FF_TILES):
            part = slice(j * FF_STEP, (j + 1) * FF_STEP)
            expanded = mm(low_hidden, inner_weight_ref[:, part]) + inner_add_ref[:, part]
            value, slope = gelu_pieces(expanded)
            low_value = value.astype(BF16)
            active[rows, part] = low_value
            slopes[:, part] = slope
            branch += mm(low_value, outer_weight_ref[part, :])
        normed_two, inverse_two = row_norm(hidden + (branch + outer_add))
        result = (normed_two * gain_two + shift_two).astype(BF16)
        for k in range(ROWS // block):
            to = tile * (ROWS // block) + k
            output_stage[to] = result[k * block : (k + 1) * block]

            @pl.when(to == place.seq)
            def _():
                kept_copy().start()

            @pl.when(to != place.seq)
            def _():
                output_copy(to).start()

        upstream = upstream_ref[rows, :].astype(F32)
        grad_second = row_norm_back(upstream * gain_two, normed_two, inverse_two)
        low_branch = grad_second.astype(BF16)
        grad_branch[rows, :] = low_branch
        grad_hidden = grad_second
        inner_sums = []
        for j in range(FF_TILES):
            part = slice(j * FF_STEP, (j + 1) * FF_STEP)
            grad_active = mm(low_branch, outer_weight_ref[part, :], NT)
            low_grad = (slopes[:, part] * grad_active).astype(BF16)
            grad_expanded[rows, part] = low_grad
            inner_sums.append(jnp.sum(low_grad.astype(F32), axis=0, keepdims=True))
            grad_hidden += mm(low_grad, inner_weight_ref[:, part], NT)
        grad_first = row_norm_back(grad_hidden * gain_one, normed_one, inverse_one)
        first_stage[rows, :] = grad_first
        low_attention = grad_first.astype(BF16)
        grad_attention[rows, :] = low_attention
        mixture_stage[rows, :] = mm(low_attention, output_weight_ref[...], NT).astype(BF16)
        for copy in row_copies():
            copy.start()
        row = lambda v: jnp.sum(v, axis=0, keepdims=True)
        sums = jnp.concatenate(
            [
                row(low_attention.astype(F32)),
                row(low_branch.astype(F32)),
                row(grad_hidden * normed_one),
                row(grad_hidden),
                row(upstream * normed_two),
                row(upstream),
                jnp.zeros((2, MODEL_WIDTH), F32),
            ],
            axis=0,
        )
        inner_sum = jnp.concatenate(inner_sums, axis=1)

        @pl.when(step == 0)
        def _():
            sums_ref[...] = sums
            inner_sums_ref[...] = inner_sum

        @pl.when(step > 0)
        def _():
            sums_ref[...] += sums
            inner_sums_ref[...] += inner_sum

    for j in range(FF_TILES):

        @pl.when(step == ROW_TILES + j)
        def _():
            part = slice(j * FF_STEP, (j + 1) * FF_STEP)
            grad_outer_ref[...] = mm(active[:, part], grad_branch[...], TN).astype(BF16)
            grad_inner_ref[...] = mm(hidden_low[...], grad_expanded[:, part], TN).astype(BF16)
            if j == 0:
                grad_output_ref[...] = mm(mixture_ref[...], grad_attention[...], TN).astype(BF16)

    @pl.when(step == ROW_TILES + FF_TILES - 1)
    def _():
        for t in range(ROW_TILES):
            rows = pl.ds(t * ROWS, ROWS)
            pltpu.make_async_copy(
                mixture_stage.at[rows, :], grad_mixture_ref.at[rows, :], local.at[1 + 2 * t]
            ).wait()
            pltpu.make_async_copy(
                first_stage.at[rows, :], grad_first_ref.at[rows, :], local.at[2 + 2 * t]
            ).wait()
        kept_copy().wait()
        for k in range(1, SG):
            other = (place.seq + k) % SG
            output_copy(other).wait_send()
            pltpu.make_async_remote_copy(
                src_ref=output_stage.at[other],
                dst_ref=output_ref.at[other],
                send_sem=send.at[other],
                recv_sem=receive.at[other],
                device_id=(other, place.dp),
                device_id_type=MESH,
            ).wait_recv()


def mlp(mixture, pooled, upstream, output_weight, inner_weight, outer_weight, vectors, inner_add):
    fixed = lambda shape: pl.BlockSpec(shape, lambda i: (0, 0), pipeline_mode=pl.Buffered(1))
    still = lambda shape: pl.BlockSpec(shape, lambda i: (0, 0))
    anywhere = pl.BlockSpec(memory_space=pl.ANY)
    out_shape = (SG, PQ // SG, MODEL_WIDTH)
    late = lambda i: jnp.maximum(i - ROW_TILES, 0)
    whole = (PQ, MODEL_WIDTH)
    square = (MODEL_WIDTH, MODEL_WIDTH)
    return pl.pallas_call(
        mlp_kernel,
        grid=(ROW_TILES + FF_TILES,),
        in_specs=[
            fixed(whole),
            fixed(whole),
            fixed(whole),
            fixed(square),
            fixed((MODEL_WIDTH, FF)),
            fixed((FF, MODEL_WIDTH)),
            fixed((VECTORS, MODEL_WIDTH)),
            fixed((1, FF)),
        ],
        out_specs=[
            anywhere,
            anywhere,
            anywhere,
            pl.BlockSpec((FF_STEP, MODEL_WIDTH), lambda i: (late(i), 0)),
            pl.BlockSpec((MODEL_WIDTH, FF_STEP), lambda i: (0, late(i))),
            still(square),
            still((8, MODEL_WIDTH)),
            still((1, FF)),
        ],
        out_shape=[
            jax.ShapeDtypeStruct(out_shape, BF16),
            jax.ShapeDtypeStruct(whole, BF16),
            jax.ShapeDtypeStruct(whole, F32),
            jax.ShapeDtypeStruct((FF, MODEL_WIDTH), BF16),
            jax.ShapeDtypeStruct((MODEL_WIDTH, FF), BF16),
            jax.ShapeDtypeStruct(square, BF16),
            jax.ShapeDtypeStruct((8, MODEL_WIDTH), F32),
            jax.ShapeDtypeStruct((1, FF), F32),
        ],
        scratch_shapes=[
            pltpu.VMEM((PQ, FF), BF16),
            pltpu.VMEM((ROWS, FF), F32),
            pltpu.VMEM((PQ, FF), BF16),
            pltpu.VMEM(whole, BF16),
            pltpu.VMEM(whole, BF16),
            pltpu.VMEM(whole, BF16),
            pltpu.VMEM(out_shape, BF16),
            pltpu.VMEM(whole, BF16),
            pltpu.VMEM(whole, F32),
            pltpu.SemaphoreType.DMA((SG,)),
            pltpu.SemaphoreType.DMA((SG,)),
            pltpu.SemaphoreType.DMA((1 + 2 * ROW_TILES,)),
        ],
        cost_estimate=pl.CostEstimate(
            flops=2 * PQ * MODEL_WIDTH * (3 * MODEL_WIDTH + 6 * FF),
            bytes_accessed=40_000_000,
            transcendentals=PQ * FF,
        ),
        compiler_params=pltpu.CompilerParams(
            collective_id=1, has_side_effects=True, vmem_limit_bytes=60 * 2**20
        ),
        name="mlp",
    )(mixture, pooled, upstream, output_weight, inner_weight, outer_weight, vectors, inner_add)


SLOTS = 2 * (PQ // ROWS)
EARLY_SLOTS = {}
for _i, _steps in enumerate(
    (
        (3, 12, 17, 20, 23, 26, 29, 34),
        (6, 20, 25, 28, 31, 34, 37, 42),
        (9, 28, 33, 36, 39, 42, 45, 48),
        (12, 36, 41, 44, 48),
        (14, 41, 45, 47, 48),
    )
):
    for _stage, _slot in zip((*STAGES[1 : len(_steps)], None), _steps):
        EARLY_SLOTS.setdefault(_slot, []).append((_i, _stage))


def attend_back_kernel(
    join_ref,
    key_ref,
    value_ref,
    query_ref,
    mixture_ref,
    grad_ref,
    relative_ref,
    vectors_ref,
    query_side_ref,
    key_side_ref,
    phase_ref,
    cos_ref,
    sin_ref,
    mlp_sums_ref,
    grad_outer_ref,
    grad_inner_ref,
    grad_output_ref,
    grad_query_ref,
    grad_key_ref,
    grad_value_ref,
    small_ref,
    *refs,
):
    early, _ = grad_chunks()
    sent, refs = refs[: len(early)], refs[len(early) :]
    key_join, value_join, key_total, value_total, join_grads, *refs = refs
    fulls, refs = refs[:WHOLE], refs[WHOLE:]
    buffers, (send, receive, local) = refs[: 6 * len(early)], refs[6 * len(early) :]
    pair = pl.program_id(0)
    place = Place()
    grads = (grad_outer_ref, grad_inner_ref, grad_output_ref)
    work = []
    for i, chunk in enumerate(early):
        kept = [*buffers[6 * i : 6 * i + 6], fulls[i] if i < WHOLE else None]
        source = chunk_source(grads[chunk[0]], chunk)
        work.append(Chunk(place, i, source, *chunk[4:], kept, send, receive, local))

    def exchange(slot):
        for i, stage in EARLY_SLOTS.get(slot, ()):
            if stage is not None:
                work[i].step(stage)
            elif i < WHOLE:
                work[i].finish(STAGES[-1])
                sent[i][...] = work[i].full[...]
                work[i].close(STAGES)
            else:
                work[i].finish(DOWN[-1])
                sent[i][...] = work[i].from_far[...]
                work[i].close(DOWN)

    @pl.when(pair == 0)
    def _():
        place.greet()
        for item in work:
            item.start("core")

    scale = HEAD_SIZE ** (-0.5)
    key_left = lane_ids(LEN) < HEAD_SIZE
    tile_lane = lane_ids(ROWS)
    key_join[:, LANES:] = key_side_ref[...]
    value_join[:, :LANES] = value_ref[...]
    value_join[:, LANES:] = key_side_ref[...]
    for h in range(2):
        pieces = (key_ref[...], phase_ref[...]) if h == 0 else (phase_ref[...], key_ref[...])
        key_join[:, :LANES] = jnp.where(key_left, *pieces)
        mine = (tile_lane < HEAD_SIZE) if h == 0 else (tile_lane >= HEAD_SIZE)
        part = slice(h * HEAD_SIZE, (h + 1) * HEAD_SIZE)
        for i in range(PQ // ROWS):
            rows = slice(i * ROWS, (i + 1) * ROWS)
            for slot in EARLY_SLOTS:
                if slot % SLOTS == h * (PQ // ROWS) + i:

                    @pl.when(pair == slot // SLOTS)
                    def _():
                        exchange(slot)

            join = join_ref[h, rows, :]
            grad = jnp.where(mine, grad_ref[rows, :].astype(F32), 0.0)
            dot = -jnp.sum(grad * mixture_ref[rows, :].astype(F32), axis=1, keepdims=True)
            one = dot.astype(BF16).astype(F32)
            two = (dot - one).astype(BF16).astype(F32)
            three = dot - one - two
            extra = jnp.where(tile_lane == 6, one, jnp.where(tile_lane == 7, two, three))
            inside = (tile_lane >= 6) & (tile_lane < 9)
            extra = jnp.where(inside, extra, 0.0)
            grad_low = grad.astype(BF16)
            weights = jnp.exp(mm(join, key_join[...], NT))
            slope = mm(
                jnp.concatenate([grad_low, extra.astype(BF16)], axis=1), value_join[...], NT
            )
            low_slope = (weights * slope).astype(BF16)
            low_weights = weights.astype(BF16)
            join_grads[h, rows, :] = mm(low_slope, key_join[...])
            to_key = mm(join_ref[h, rows, part], low_slope, TN)
            to_value = mm(grad_ref[rows, part], low_weights, TN)
            if i == 0:
                key_total[part, :] = to_key
                value_total[part, :] = to_value
            else:
                key_total[part, :] += to_key
                value_total[part, :] += to_value
    grad_key_ref[...] = key_total[...].T.astype(BF16)
    grad_value_ref[...] = value_total[...].T.astype(BF16)
    lane = lane_ids(PQ)
    left = lane < HEAD_SIZE
    typed = (lane >= 3) & (lane < 6)
    rounded = [(join_grads[h, :, :LANES] * scale).astype(BF16).astype(F32) for h in range(2)]
    content = jnp.where(left, rounded[0], rounded[1])
    position = jnp.where(left, rounded[1], rounded[0])
    turned = jnp.concatenate([position * cos_ref[...], position * sin_ref[...]], axis=1)
    turned_high, turned_low = split(turned)
    plain, swapped = pair_maps(relative_ref[...])
    maps = jnp.concatenate([plain, swapped], axis=1)
    shifted_grad = mm(turned_high, maps, NT) + mm(turned_low, maps, NT)
    side = query_side_ref[...]
    sames, others = [], []
    for h in range(2):
        kinds = jnp.where(typed, join_grads[h, :, LANES:], 0.0)
        same = jnp.sum(jnp.where(side > 0.5, kinds, 0.0), axis=1, keepdims=True)
        other = jnp.sum(jnp.where(side > 0.5, 0.0, kinds), axis=1, keepdims=True)
        sames.append((same * scale).astype(BF16).astype(F32))
        others.append((other * scale).astype(BF16).astype(F32))
    same = jnp.where(left, sames[0], sames[1])
    other = jnp.where(left, others[0], others[1])
    position_add = vectors_ref[8:9, :]
    type_add = vectors_ref[9:10, :]
    type_other = vectors_ref[10:11, :]
    type_same = vectors_ref[11:12, :]
    typed_grad = same * type_same + other * type_other
    grad_query_ref[...] = (content + shifted_grad + typed_grad).astype(BF16)
    query = query_ref[...]
    shifted_high, shifted_low = split(query + position_add)
    grad_map = (
        mm(shifted_high, turned_high, TN)
        + mm(shifted_low, turned_high, TN)
        + mm(shifted_high, turned_low, TN)
    )
    kinds = query + type_add
    row = lambda v: jnp.sum(v, axis=0, keepdims=True)
    below = mlp_sums_ref[...]
    columns = jnp.concatenate(
        [
            jnp.zeros((HEAD_SIZE, LANES), F32),
            row(grad_value_ref[...].astype(F32)),
            row(content),
            row(shifted_grad),
            row(typed_grad),
            row(kinds * other),
            row(kinds * same),
            jnp.zeros((2, LANES), F32),
            below,
            jnp.zeros((LANES - HEAD_SIZE - 24, LANES), F32),
        ],
        axis=0,
    )
    small_ref[:, :LANES] = (fold_maps(grad_map) + columns.T).astype(BF16)
    small_ref[:, LANES:] = jnp.zeros((LANES, LANES), BF16)

    @pl.when(pair == PAIRS - 1)
    def _():
        exchange(PAIRS * SLOTS)


def attend_backward(
    join,
    pairs,
    query,
    mixture,
    grad,
    relative,
    vectors,
    query_side,
    key_side,
    phase,
    cosm,
    sinm,
    mlp_sums,
    grads,
):
    early, _ = grad_chunks()
    anywhere = pl.BlockSpec(memory_space=pl.ANY)
    shapes = [
        chunk[4:] if i < WHOLE else (chunk[4] // 4, chunk[5] // 2)
        for i, chunk in enumerate(early)
    ]
    whole = lambda shape: pl.BlockSpec(shape, lambda i: (0, 0))
    return pl.pallas_call(
        attend_back_kernel,
        grid=(PAIRS,),
        in_specs=[
            pl.BlockSpec((2, PQ, 2 * LANES), lambda i: (i, 0, 0)),
            pl.BlockSpec((LEN, LANES), lambda i: (0, i)),
            pl.BlockSpec((LEN, LANES), lambda i: (0, i + PAIRS)),
            pl.BlockSpec((PQ, LANES), lambda i: (0, i)),
            pl.BlockSpec((PQ, LANES), lambda i: (0, i)),
            pl.BlockSpec((PQ, LANES), lambda i: (0, i)),
            pl.BlockSpec((LANES, HEAD_SIZE), lambda i: (i, 0)),
            pl.BlockSpec((VECTORS, LANES), lambda i: (0, i)),
            whole((PQ, LANES)),
            whole((LEN, LANES)),
            whole((LEN, LANES)),
            whole((PQ, LANES)),
            whole((PQ, LANES)),
            pl.BlockSpec((16, LANES), lambda i: (0, i)),
            *[anywhere] * 3,
        ],
        out_specs=[
            pl.BlockSpec((PQ, LANES), lambda i: (0, i)),
            pl.BlockSpec((LEN, LANES), lambda i: (0, i)),
            pl.BlockSpec((LEN, LANES), lambda i: (0, i)),
            pl.BlockSpec((LANES, 2 * LANES), lambda i: (i, 0)),
            *[whole(shape) for shape in shapes],
        ],
        out_shape=[
            jax.ShapeDtypeStruct((PQ, MODEL_WIDTH), BF16),
            jax.ShapeDtypeStruct((LEN, MODEL_WIDTH), BF16),
            jax.ShapeDtypeStruct((LEN, MODEL_WIDTH), BF16),
            jax.ShapeDtypeStruct((MODEL_WIDTH, 2 * LANES), BF16),
            *[jax.ShapeDtypeStruct(shape, BF16) for shape in shapes],
        ],
        scratch_shapes=[
            pltpu.VMEM((LEN, 2 * LANES), BF16),
            pltpu.VMEM((LEN, 2 * LANES), BF16),
            pltpu.VMEM((LANES, LEN), F32),
            pltpu.VMEM((LANES, LEN), F32),
            pltpu.VMEM((2, PQ, 2 * LANES), F32),
            *[pltpu.VMEM(chunk[4:], BF16) for chunk in early[:WHOLE]],
            *[buffer for chunk in early for buffer in down_buffers(*chunk[4:], True)],
            pltpu.SemaphoreType.DMA((len(early), 16)),
            pltpu.SemaphoreType.DMA((len(early), 16)),
            pltpu.SemaphoreType.DMA((len(early), 2)),
        ],
        cost_estimate=pl.CostEstimate(
            flops=10 * HEAD_COUNT * PQ * LEN * 256,
            bytes_accessed=32_000_000,
            transcendentals=HEAD_COUNT * PQ * LEN,
        ),
        compiler_params=pltpu.CompilerParams(
            collective_id=2, has_side_effects=True, vmem_limit_bytes=58 * 2**20
        ),
        name="attend_backward",
    )(
        join,
        pairs,
        pairs,
        query,
        mixture,
        grad,
        relative,
        vectors,
        query_side,
        key_side,
        phase,
        cosm,
        sinm,
        mlp_sums,
        *grads,
    )


def labels_kernel(labels_ref, out_ref, stage, send, receive):
    place = Place()
    place.greet()
    copies = []
    for k in range(1, SG):
        to = (place.seq + k) % SG
        copy = pltpu.make_async_remote_copy(
            src_ref=labels_ref.at[to],
            dst_ref=stage.at[place.seq],
            send_sem=send.at[k - 1],
            recv_sem=receive.at[k - 1],
            device_id=(to, place.dp),
            device_id_type=MESH,
        )
        copy.start()
        copies.append(copy)
    stage[place.seq] = labels_ref[place.seq]
    for copy in copies:
        copy.wait()
    out_ref[...] = stage[...]


def move_labels(labels):
    inside = pl.BlockSpec(memory_space=pltpu.VMEM)
    return pl.pallas_call(
        labels_kernel,
        in_specs=[inside],
        out_specs=inside,
        out_shape=jax.ShapeDtypeStruct(labels.shape, jnp.int32),
        scratch_shapes=[
            pltpu.VMEM(labels.shape, jnp.int32),
            pltpu.SemaphoreType.DMA((SG - 1,)),
            pltpu.SemaphoreType.DMA((SG - 1,)),
        ],
        compiler_params=pltpu.CompilerParams(collective_id=4, has_side_effects=True),
        name="labels",
    )(labels)


def angle_tables():
    half = HEAD_SIZE // 2
    rate = np.float32(-math.log(10000.0) / half)
    frequency = np.exp(np.arange(half, dtype=np.float32) * rate)
    angle = np.arange(LEN, dtype=np.float32)[:, None] * frequency[None, :]
    cos, sin = np.cos(angle), np.sin(angle)
    phase = np.concatenate([cos, sin, cos, sin], axis=1)
    cos, sin = cos[0::2], sin[0::2]
    return (
        jnp.asarray(phase).astype(BF16),
        np.concatenate([cos, -cos, cos, -cos], axis=1),
        np.concatenate([sin, sin, sin, sin], axis=1),
    )


def sequence_body(
    tokens,
    segments,
    token_types,
    cotangent,
    query_weight,
    key_weight,
    value_weight,
    output_weight,
    inner_weight,
    outer_weight,
    value_bias,
    output_bias,
    inner_bias,
    outer_bias,
    attention_norm_gain,
    first_shift,
    second_gain,
    second_shift,
    content_bias,
    position_bias,
    type_bias,
    relative_kernel,
    type_embed,
):
    owners = lax.axis_size("dp")
    part = MODEL_WIDTH // owners
    low = lambda value: value.astype(BF16)
    even_segments, odd_segments = segments[:, 0::2], segments[:, 1::2]
    labels = jnp.stack(
        [
            segments[:, :128],
            segments[:, 128:],
            token_types[:, :128],
            token_types[:, 128:],
            even_segments,
            token_types[:, 0::2],
            (even_segments == odd_segments).astype(jnp.int32),
        ],
        axis=1,
    )
    labels = move_labels(labels)
    tokens, labels = lax.optimization_barrier((tokens, labels))
    rows = lax.all_to_all(tokens, "seq", split_axis=0, concat_axis=0, tiled=True)
    flat = lambda value: low(value).reshape(1, part)
    vectors = [
        flat(value)
        for value in (
            value_bias,
            output_bias,
            outer_bias,
            attention_norm_gain,
            first_shift,
            second_gain,
            second_shift,
            content_bias,
            position_bias,
            type_bias,
            type_embed[:, 0],
            type_embed[:, 1],
        )
    ]
    vectors.append(jnp.zeros((VECTORS - len(vectors), part), BF16))
    vectors = lax.all_gather(jnp.concatenate(vectors, axis=0), "dp", axis=1, tiled=True)
    vectors = vectors.astype(F32)
    inner_add = lax.all_gather(low(inner_bias).reshape(1, -1), "dp", axis=1, tiled=True)
    inner_add = inner_add.astype(F32)
    relative = low(relative_kernel).reshape(part, HEAD_SIZE)
    relative = lax.all_gather(relative, "dp", axis=0, tiled=True)
    first = jnp.concatenate([low(query_weight), low(key_weight), low(value_weight)], axis=1)
    first = lax.all_gather(first, "dp", axis=0, tiled=True)
    inner_low = lax.all_gather(low(inner_weight), "dp", axis=0, tiled=True)
    output_low = lax.all_gather(low(output_weight), "dp", axis=0, tiled=True)
    outer_low = lax.all_gather(low(outer_weight), "dp", axis=0, tiled=True)


    segment_row = labels[:, 0:2].reshape(LEN)
    type_row = labels[:, 2:4].reshape(LEN)
    query_segments = labels[:, 4].reshape(PQ)
    query_types = labels[:, 5].reshape(PQ)
    pair_same = labels[:, 6] > 0

    first_doc, last_doc = segment_row[0], segment_row[LEN - 1]
    first_type = type_row[0]
    last_type = jnp.max(jnp.where(type_row == first_type, -1, type_row))

    def classes(values, start, end):
        return jnp.where(values == start, 0, jnp.where(values == end, 2, 1))[:, None]

    columns = jnp.arange(LANES, dtype=jnp.int32)[None, :]
    key_side = (
        (columns == classes(segment_row, first_doc, last_doc))
        | (columns == 3 + classes(type_row, first_type, last_type))
        | ((columns >= 6) & (columns < 9))
    ).astype(BF16)
    query_docs = classes(query_segments, first_doc, last_doc)
    query_side = jnp.where(
        columns < 3,
        jnp.where(columns == query_docs, 0.0, FAR),
        (columns == 3 + classes(query_types, first_type, last_type)).astype(F32),
    )
    phase, cosm, sinm = angle_tables()

    block = rows.shape[1]
    pooled_block = block // 2
    at = jnp.arange(block, dtype=jnp.int32)[None, None, :]
    want = 2 * jnp.arange(pooled_block, dtype=jnp.int32)[None, :, None]
    half = jnp.where(pair_same, 0.5, 1.0)[:, :, None]
    other_half = jnp.where(pair_same, 0.5, 0.0)[:, :, None]
    pool = jnp.where(at == want, half, jnp.where(at == want + 1, other_half, 0.0)).astype(BF16)

    pooled = jnp.einsum("cpt,ctd->cpd", pool, rows, preferred_element_type=F32)
    pooled = pooled.reshape(PQ, MODEL_WIDTH)
    pooled_low = low(pooled)
    token_rows = rows.reshape(LEN, MODEL_WIDTH)
    query = mm(pooled_low, first[:, :MODEL_WIDTH])
    value_add = vectors[0:1]
    pair_add = jnp.concatenate([jnp.zeros_like(value_add), value_add], axis=1)
    pairs = low(mm(token_rows, first[:, MODEL_WIDTH:]) + pair_add)
    mixture, join, upstream = attend_forward(
        query, pairs, relative, vectors, query_side, key_side, phase, cosm, sinm, cotangent
    )
    upstream = upstream.reshape(PQ, MODEL_WIDTH)

    (
        output,
        grad_mixture,
        grad_first,
        grad_outer_weight,
        grad_inner_weight,
        grad_output_weight,
        row_sums,
        grad_inner_bias,
    ) = mlp(
        mixture, pooled, upstream, output_low, inner_low, outer_low, vectors, inner_add
    )
    inner_rows = grad_inner_bias.reshape(owners, owners, part).transpose(1, 0, 2)
    mlp_sums = jnp.concatenate(
        [row_sums, inner_rows.reshape(owners, MODEL_WIDTH), jnp.zeros((4, MODEL_WIDTH), F32)],
        axis=0,
    )

    grad_query, grad_key, grad_value, small_grads, *pieces = attend_backward(
        join,
        pairs,
        query,
        mixture,
        grad_mixture,
        relative,
        vectors,
        query_side,
        key_side,
        phase,
        cosm,
        sinm,
        mlp_sums,
        (grad_outer_weight, grad_inner_weight, grad_output_weight),
    )
    grad_tokens, *owned = finish(
        grad_query,
        grad_key,
        grad_value,
        token_rows,
        pooled_low,
        grad_first,
        pool,
        first,
        small_grads,
        pieces[WHOLE:],
    )
    owned = [*pieces[:WHOLE], *owned]
    owned_outer = jnp.concatenate(owned[0:2], axis=0).astype(F32)
    owned_inner = jnp.concatenate(owned[2:4], axis=1).astype(F32)
    owned_output, small_owned, *squares = [value.astype(F32) for value in owned[4:]]
    squares.append(owned_output)
    columns = small_owned[:, HEAD_SIZE : HEAD_SIZE + 24].T
    vector = lambda j: columns[j]
    heads = HEAD_COUNT // owners
    return (
        output,
        grad_tokens,
        squares[0],
        squares[1],
        squares[2],
        squares[3],
        owned_inner,
        owned_outer,
        vector(0),
        vector(8),
        columns[16:20].reshape(FF // owners),
        vector(9),
        vector(10),
        vector(11),
        vector(12),
        vector(13),
        vector(1).reshape(heads, HEAD_SIZE),
        vector(2).reshape(heads, HEAD_SIZE),
        vector(3).reshape(heads, HEAD_SIZE),
        small_owned[:, :HEAD_SIZE].reshape(heads, HEAD_SIZE, HEAD_SIZE),
        columns[4:6].reshape(2, heads, HEAD_SIZE).transpose(1, 0, 2),
    )


def solution(mesh):
    whole = mesh.shape["seq"] == SG and mesh.shape["dp"] == 4
    return jax.shard_map(
        sequence_body if whole else body,
        mesh=mesh,
        in_specs=(
            P("dp", "seq", None),
            P("dp", "seq"),
            P("dp", "seq"),
            P("dp", "seq", None),
            P("dp", None),
            P("dp", None),
            P("dp", None),
            P("dp", None),
            P("dp", None),
            P("dp", None),
            P("dp"),
            P("dp"),
            P("dp"),
            P("dp"),
            P("dp"),
            P("dp"),
            P("dp"),
            P("dp"),
            P("dp", None),
            P("dp", None),
            P("dp", None),
            P("dp", None, None),
            P("dp", None, None),
        ),
        out_specs=(
            P("dp", "seq", None),
            P("dp", "seq", None),
            P("dp", None),
            P("dp", None),
            P("dp", None),
            P("dp", None),
            P("dp", None),
            P("dp", None),
            P("dp"),
            P("dp"),
            P("dp"),
            P("dp"),
            P("dp"),
            P("dp"),
            P("dp"),
            P("dp"),
            P("dp", None),
            P("dp", None),
            P("dp", None),
            P("dp", None, None),
            P("dp", None, None),
        ),
        check_vma=False,
    )
```

```python
from functools import partial
import math

import jax
import jax.numpy as jnp
import numpy as np
from jax import lax
from jax.experimental import pallas as pl
from jax.experimental.pallas import tpu as pltpu
from jax.sharding import PartitionSpec as P

MODEL_WIDTH = 768
HEAD_COUNT = 12
HEAD_SIZE = 64
LEN = 2048
SG = 8
PQ = 1024


highest = lax.Precision.HIGHEST
norm_eps = 1e-05
masked_score = -1e30


def frequencies():
    half_width = HEAD_SIZE // 2
    return jnp.exp(jnp.arange(half_width, dtype=jnp.float32) * (-math.log(10000.0) / half_width))


def norm_forward(inputs, gains, shifts):
    row_mean = jnp.mean(inputs, axis=-1, keepdims=True)
    centred = inputs - row_mean
    inverse = lax.rsqrt(jnp.mean(centred * centred, axis=-1, keepdims=True) + norm_eps)
    normed = centred * inverse
    return (normed * gains + shifts, normed, inverse)


def norm_backward(upstream, normed, inverse, gains):
    scaled = upstream * gains
    along = jnp.mean(scaled * normed, axis=-1, keepdims=True)
    centre = jnp.mean(scaled, axis=-1, keepdims=True)
    return inverse * (scaled - centre - normed * along)


def doc_masks(segment_row, type_row):
    same_document = segment_row[0::2][:, None] == segment_row[None, :]
    same_type = type_row[0::2][:, None] == type_row[None, :]
    return (same_document, same_type)


def score_block(query_row, type_row_terms, pair_row, key_phase, same_document, same_type):
    key_join = jnp.concatenate([pair_row[:, :HEAD_SIZE], key_phase], axis=-1)
    raw_score = lax.dot_general(
        query_row, key_join, (((1,), (1,)), ((), ())), preferred_element_type=jnp.float32
    )
    type_float = type_row_terms.astype(jnp.float32)
    raw_score = raw_score + jnp.where(same_type, type_float[:, 1:2], type_float[:, 0:1])
    return (jnp.where(same_document, raw_score * HEAD_SIZE ** (-0.5), masked_score), key_join)


def body(
    tokens,
    segments,
    token_types,
    cotangent,
    query_weight,
    key_weight,
    value_weight,
    output_weight,
    inner_weight,
    outer_weight,
    value_bias,
    output_bias,
    inner_bias,
    outer_bias,
    attention_norm_gain,
    first_shift,
    second_gain,
    second_shift,
    content_bias,
    position_bias,
    type_bias,
    relative_kernel,
    type_embed,
):
    local_tokens = tokens.shape[1]
    local_pooled = local_tokens // 2
    group_size = lax.axis_size("seq")
    shard_rank = lax.axis_index("seq")
    item_count = SG * HEAD_COUNT // group_size
    half_width = HEAD_SIZE // 2
    score_scale = HEAD_SIZE ** (-0.5)
    frequency = frequencies()
    duplicate_params = (
        lax.all_gather(query_weight.astype(jnp.bfloat16), "dp", axis=0, tiled=True),
        lax.all_gather(key_weight.astype(jnp.bfloat16), "dp", axis=0, tiled=True),
        lax.all_gather(value_weight.astype(jnp.bfloat16), "dp", axis=0, tiled=True),
        lax.all_gather(output_weight.astype(jnp.bfloat16), "dp", axis=0, tiled=True),
        lax.all_gather(inner_weight.astype(jnp.bfloat16), "dp", axis=0, tiled=True),
        lax.all_gather(outer_weight.astype(jnp.bfloat16), "dp", axis=0, tiled=True),
        lax.all_gather(value_bias.astype(jnp.bfloat16), "dp", axis=0, tiled=True),
        lax.all_gather(output_bias.astype(jnp.bfloat16), "dp", axis=0, tiled=True),
        lax.all_gather(inner_bias.astype(jnp.bfloat16), "dp", axis=0, tiled=True),
        lax.all_gather(outer_bias.astype(jnp.bfloat16), "dp", axis=0, tiled=True),
        lax.all_gather(attention_norm_gain.astype(jnp.bfloat16), "dp", axis=0, tiled=True),
        lax.all_gather(first_shift.astype(jnp.bfloat16), "dp", axis=0, tiled=True),
        lax.all_gather(second_gain.astype(jnp.bfloat16), "dp", axis=0, tiled=True),
        lax.all_gather(second_shift.astype(jnp.bfloat16), "dp", axis=0, tiled=True),
        lax.all_gather(content_bias.astype(jnp.bfloat16), "dp", axis=0, tiled=True),
        lax.all_gather(position_bias.astype(jnp.bfloat16), "dp", axis=0, tiled=True),
        lax.all_gather(type_bias.astype(jnp.bfloat16), "dp", axis=0, tiled=True),
        lax.all_gather(relative_kernel.astype(jnp.bfloat16), "dp", axis=0, tiled=True),
        lax.all_gather(type_embed.astype(jnp.bfloat16), "dp", axis=0, tiled=True),
    )
    value_add = duplicate_params[6].astype(jnp.float32)
    output_add = duplicate_params[7].astype(jnp.float32)
    inner_add = duplicate_params[8].astype(jnp.float32)
    outer_add = duplicate_params[9].astype(jnp.float32)
    gain_one = duplicate_params[10].astype(jnp.float32)
    shift_one = duplicate_params[11].astype(jnp.float32)
    gain_two = duplicate_params[12].astype(jnp.float32)
    shift_two = duplicate_params[13].astype(jnp.float32)
    content_add = duplicate_params[14].astype(jnp.float32)[None, :, None, :]
    position_add = duplicate_params[15].astype(jnp.float32)[None, :, None, :]
    type_add = duplicate_params[16].astype(jnp.float32)[None, :, None, :]
    relative = duplicate_params[17].astype(jnp.float32)
    type_table = duplicate_params[18].astype(jnp.float32)
    whole_segments, whole_types = (
        lax.all_gather(segments, "seq", axis=1, tiled=True),
        lax.all_gather(token_types, "seq", axis=1, tiled=True),
    )
    first_rows = tokens[:, 0::2].astype(jnp.float32)
    second = tokens[:, 1::2].astype(jnp.float32)
    pair_same = (segments[:, 0::2] == segments[:, 1::2])[..., None]
    pooled = jnp.where(pair_same, (first_rows + second) * 0.5, first_rows)
    pooled_low = pooled.astype(jnp.bfloat16)
    queries = jnp.einsum(
        "spd,dhe->shpe",
        pooled_low,
        duplicate_params[0].reshape(MODEL_WIDTH, HEAD_COUNT, HEAD_SIZE),
        preferred_element_type=jnp.float32,
    )
    key_rows = jnp.einsum(
        "ukf,fra->urka",
        tokens,
        duplicate_params[1].reshape(MODEL_WIDTH, HEAD_COUNT, HEAD_SIZE),
        preferred_element_type=jnp.float32,
    )
    value_rows = (
        jnp.einsum(
            "ukf,fra->urka",
            tokens,
            duplicate_params[2].reshape(MODEL_WIDTH, HEAD_COUNT, HEAD_SIZE),
            preferred_element_type=jnp.float32,
        )
        + value_add.reshape(HEAD_COUNT, HEAD_SIZE)[None, :, None, :]
    )
    pair_rows = (
        jnp.concatenate([key_rows, value_rows], axis=-1)
        .astype(jnp.bfloat16)
        .reshape(SG * HEAD_COUNT, local_tokens, 2 * HEAD_SIZE)
    )
    shifted = queries + position_add
    relative_terms = jnp.einsum("shpe,hef->shpf", shifted, relative, precision=highest)
    pooled_place = 2.0 * (
        shard_rank * local_pooled + jnp.arange(local_pooled, dtype=jnp.int32)
    ).astype(jnp.float32)
    query_angle = pooled_place[:, None] * frequency[None, :]
    query_cos = jnp.cos(query_angle)
    query_sin = jnp.sin(query_angle)
    relative_cos = relative_terms[..., :half_width]
    relative_sin = relative_terms[..., half_width:]
    position = jnp.concatenate(
        [
            relative_cos * query_cos + relative_sin * query_sin,
            relative_cos * query_sin - relative_sin * query_cos,
        ],
        axis=-1,
    )
    query_join = (
        jnp.concatenate([queries + content_add, position], axis=-1)
        .astype(jnp.bfloat16)
        .reshape(SG * HEAD_COUNT, local_pooled, 2 * HEAD_SIZE)
    )
    typed = queries + type_add
    type_terms = (
        jnp.einsum("shpe,hbe->shpb", typed, type_table, precision=highest)
        .astype(jnp.bfloat16)
        .reshape(SG * HEAD_COUNT, local_pooled, 2)
    )
    query_heads, type_heads, pair_heads = (
        lax.all_to_all(query_join, "seq", split_axis=0, concat_axis=1, tiled=True),
        lax.all_to_all(type_terms, "seq", split_axis=0, concat_axis=1, tiled=True),
        lax.all_to_all(pair_rows, "seq", split_axis=0, concat_axis=1, tiled=True),
    )
    item_rows = (shard_rank * item_count + jnp.arange(item_count, dtype=jnp.int32)) // HEAD_COUNT
    item_segments = whole_segments[item_rows]
    item_types = whole_types[item_rows]
    key_angle = jnp.arange(LEN, dtype=jnp.float32)[:, None] * frequency[None, :]
    key_phase = jnp.concatenate([jnp.cos(key_angle), jnp.sin(key_angle)], axis=-1).astype(
        jnp.bfloat16
    )

    def attend(packed):
        query_row, type_row_terms, pair_row, segment_row, type_row = packed
        same_document, same_type = doc_masks(segment_row, type_row)
        scores, key_join = score_block(
            query_row, type_row_terms, pair_row, key_phase, same_document, same_type
        )
        row_max = jnp.max(scores, axis=1, keepdims=True)
        exponent = jnp.exp(scores - row_max)
        row_total = jnp.sum(exponent, axis=1, keepdims=True)
        weights = exponent / row_total
        mixture = jnp.dot(
            weights.astype(jnp.bfloat16),
            pair_row[:, HEAD_SIZE:],
            preferred_element_type=jnp.float32,
        )
        return (mixture.astype(jnp.bfloat16), row_max + jnp.log(row_total))

    mixed_heads, log_totals = lax.map(
        attend, (query_heads, type_heads, pair_heads, item_segments, item_types)
    )
    mixed_tokens = lax.all_to_all(
        mixed_heads.reshape(item_count, PQ // 2, 2 * HEAD_SIZE),
        "seq",
        split_axis=1,
        concat_axis=0,
        tiled=True,
    ).reshape(SG, HEAD_COUNT, local_pooled, HEAD_SIZE)
    attention = (
        jnp.einsum(
            "shpe,hed->spd",
            mixed_tokens,
            duplicate_params[3].reshape(HEAD_COUNT, HEAD_SIZE, MODEL_WIDTH),
            preferred_element_type=jnp.float32,
        )
        + output_add
    )
    hidden, normed_one, inverse_one = norm_forward(pooled + attention, gain_one, shift_one)
    hidden_low = hidden.astype(jnp.bfloat16)
    expanded = (
        jnp.einsum(
            "spd,df->spf", hidden_low, duplicate_params[4], preferred_element_type=jnp.float32
        )
        + inner_add
    )
    active = jax.nn.gelu(expanded, approximate=True).astype(jnp.bfloat16)
    branch = (
        jnp.einsum("spf,fd->spd", active, duplicate_params[5], preferred_element_type=jnp.float32)
        + outer_add
    )
    result, normed_two, inverse_two = norm_forward(hidden + branch, gain_two, shift_two)
    output = result.astype(jnp.bfloat16)
    again = (
        lax.all_gather(query_weight.astype(jnp.bfloat16), "dp", axis=0, tiled=True),
        lax.all_gather(key_weight.astype(jnp.bfloat16), "dp", axis=0, tiled=True),
        lax.all_gather(value_weight.astype(jnp.bfloat16), "dp", axis=0, tiled=True),
        lax.all_gather(output_weight.astype(jnp.bfloat16), "dp", axis=0, tiled=True),
        lax.all_gather(inner_weight.astype(jnp.bfloat16), "dp", axis=0, tiled=True),
        lax.all_gather(outer_weight.astype(jnp.bfloat16), "dp", axis=0, tiled=True),
        lax.all_gather(attention_norm_gain.astype(jnp.bfloat16), "dp", axis=0, tiled=True),
        lax.all_gather(second_gain.astype(jnp.bfloat16), "dp", axis=0, tiled=True),
        lax.all_gather(relative_kernel.astype(jnp.bfloat16), "dp", axis=0, tiled=True),
        lax.all_gather(type_embed.astype(jnp.bfloat16), "dp", axis=0, tiled=True),
    )
    query_back = again[0]
    key_back = again[1]
    value_back = again[2]
    output_back = again[3]
    inner_back = again[4]
    outer_back = again[5]
    gain_one_back = again[6].astype(jnp.float32)
    gain_two_back = again[7].astype(jnp.float32)
    relative_back = again[8].astype(jnp.float32)
    table_back = again[9].astype(jnp.float32)
    grad_result = cotangent.astype(jnp.float32)
    grad_gain_two = jnp.sum(grad_result * normed_two, axis=(0, 1))
    grad_shift_two = jnp.sum(grad_result, axis=(0, 1))
    grad_second = norm_backward(grad_result, normed_two, inverse_two, gain_two_back)
    grad_branch = grad_second.astype(jnp.bfloat16)
    grad_outer_weight = jnp.einsum(
        "spf,spd->fd", active, grad_branch, preferred_element_type=jnp.float32
    )
    grad_outer_bias = jnp.sum(grad_branch.astype(jnp.float32), axis=(0, 1))
    grad_active = jnp.einsum(
        "spd,fd->spf", grad_branch, outer_back, preferred_element_type=jnp.float32
    )
    gelu_value, gelu_pull = jax.vjp(partial(jax.nn.gelu, approximate=True), expanded)
    grad_expanded = gelu_pull(grad_active)[0].astype(jnp.bfloat16)
    grad_inner_weight = jnp.einsum(
        "spd,spf->df", hidden_low, grad_expanded, preferred_element_type=jnp.float32
    )
    grad_inner_bias = jnp.sum(grad_expanded.astype(jnp.float32), axis=(0, 1))
    grad_hidden = grad_second + jnp.einsum(
        "spf,df->spd", grad_expanded, inner_back, preferred_element_type=jnp.float32
    )
    grad_gain_one = jnp.sum(grad_hidden * normed_one, axis=(0, 1))
    grad_shift_one = jnp.sum(grad_hidden, axis=(0, 1))
    grad_first = norm_backward(grad_hidden, normed_one, inverse_one, gain_one_back)
    grad_attention = grad_first.astype(jnp.bfloat16)
    grad_output_weight = jnp.einsum(
        "shpe,spd->hed", mixed_tokens, grad_attention, preferred_element_type=jnp.float32
    ).reshape(MODEL_WIDTH, MODEL_WIDTH)
    grad_output_bias = jnp.sum(grad_attention.astype(jnp.float32), axis=(0, 1))
    grad_mixture = jnp.einsum(
        "spd,hed->shpe",
        grad_attention,
        output_back.reshape(HEAD_COUNT, HEAD_SIZE, MODEL_WIDTH),
        preferred_element_type=jnp.float32,
    ).astype(jnp.bfloat16)
    grad_mixed_heads = lax.all_to_all(
        grad_mixture.reshape(SG * HEAD_COUNT, local_pooled // 2, 2 * HEAD_SIZE),
        "seq",
        split_axis=0,
        concat_axis=1,
        tiled=True,
    ).reshape(item_count, PQ, HEAD_SIZE)

    def attend_back(packed):
        query_row, type_row_terms, pair_row, segment_row, type_row, log_row, grad_row = packed
        same_document, same_type = doc_masks(segment_row, type_row)
        scores, key_join = score_block(
            query_row, type_row_terms, pair_row, key_phase, same_document, same_type
        )
        weights = jnp.exp(scores - log_row)
        grad_weights = lax.dot_general(
            grad_row,
            pair_row[:, HEAD_SIZE:],
            (((1,), (1,)), ((), ())),
            preferred_element_type=jnp.float32,
        )
        row_dot = jnp.sum(grad_weights * weights, axis=1, keepdims=True)
        grad_scores = (weights * (grad_weights - row_dot)).astype(jnp.bfloat16)
        grad_query = (
            jnp.dot(grad_scores, key_join, preferred_element_type=jnp.float32) * score_scale
        ).astype(jnp.bfloat16)
        grad_float = grad_scores.astype(jnp.float32) * score_scale
        grad_same = jnp.sum(jnp.where(same_type, grad_float, 0.0), axis=1)
        grad_other = jnp.sum(jnp.where(same_type, 0.0, grad_float), axis=1)
        grad_kinds = jnp.stack([grad_other, grad_same], axis=-1).astype(jnp.bfloat16)
        grad_keys = (
            lax.dot_general(
                grad_scores,
                query_row[:, :HEAD_SIZE],
                (((0,), (0,)), ((), ())),
                preferred_element_type=jnp.float32,
            )
            * score_scale
        )
        grad_values = lax.dot_general(
            weights.astype(jnp.bfloat16),
            grad_row,
            (((0,), (0,)), ((), ())),
            preferred_element_type=jnp.float32,
        )
        return (
            grad_query,
            grad_kinds,
            jnp.concatenate([grad_keys, grad_values], axis=-1).astype(jnp.bfloat16),
        )

    grad_query_heads, grad_type_heads, grad_pair_heads = lax.map(
        attend_back,
        (
            query_heads,
            type_heads,
            pair_heads,
            item_segments,
            item_types,
            log_totals,
            grad_mixed_heads,
        ),
    )
    grad_query_tok, grad_type_tok, grad_pair_tok = (
        lax.all_to_all(grad_query_heads, "seq", split_axis=1, concat_axis=0, tiled=True),
        lax.all_to_all(grad_type_heads, "seq", split_axis=1, concat_axis=0, tiled=True),
        lax.all_to_all(grad_pair_heads, "seq", split_axis=1, concat_axis=0, tiled=True),
    )
    grad_query_join = grad_query_tok.astype(jnp.float32).reshape(
        SG, HEAD_COUNT, local_pooled, 2 * HEAD_SIZE
    )
    grad_content = grad_query_join[..., :HEAD_SIZE]
    grad_first_half = grad_query_join[..., HEAD_SIZE : HEAD_SIZE + half_width]
    grad_second_half = grad_query_join[..., HEAD_SIZE + half_width :]
    grad_relative_terms = jnp.concatenate(
        [
            grad_first_half * query_cos + grad_second_half * query_sin,
            grad_first_half * query_sin - grad_second_half * query_cos,
        ],
        axis=-1,
    )
    grad_shifted = jnp.einsum(
        "shpf,hef->shpe", grad_relative_terms, relative_back, precision=highest
    )
    grad_relative_kernel = jnp.einsum(
        "shpe,shpf->hef", shifted, grad_relative_terms, precision=highest
    )
    grad_type_terms = grad_type_tok.astype(jnp.float32).reshape(SG, HEAD_COUNT, local_pooled, 2)
    grad_typed = jnp.einsum("shpb,hbe->shpe", grad_type_terms, table_back, precision=highest)
    grad_type_embed = jnp.einsum("shpe,shpb->hbe", typed, grad_type_terms, precision=highest)
    query_rows_gradient = (grad_content + grad_shifted + grad_typed).astype(jnp.bfloat16)
    grad_content_bias = jnp.sum(grad_content, axis=(0, 2))
    grad_position_bias = jnp.sum(grad_shifted, axis=(0, 2))
    grad_type_bias = jnp.sum(grad_typed, axis=(0, 2))
    grad_query_weight = jnp.einsum(
        "spd,shpe->dhe", pooled_low, query_rows_gradient, preferred_element_type=jnp.float32
    ).reshape(MODEL_WIDTH, MODEL_WIDTH)
    grad_pooled = grad_first + jnp.einsum(
        "shpe,dhe->spd",
        query_rows_gradient,
        query_back.reshape(MODEL_WIDTH, HEAD_COUNT, HEAD_SIZE),
        preferred_element_type=jnp.float32,
    )
    grad_pairs = grad_pair_tok.reshape(SG, HEAD_COUNT, local_tokens, 2 * HEAD_SIZE)
    key_rows_gradient = grad_pairs[..., :HEAD_SIZE]
    value_rows_gradient = grad_pairs[..., HEAD_SIZE:]
    grad_key_weight = jnp.einsum(
        "ozb,opzx->bpx", tokens, key_rows_gradient, preferred_element_type=jnp.float32
    ).reshape(MODEL_WIDTH, MODEL_WIDTH)
    grad_value_weight = jnp.einsum(
        "ozb,opzx->bpx", tokens, value_rows_gradient, preferred_element_type=jnp.float32
    ).reshape(MODEL_WIDTH, MODEL_WIDTH)
    grad_value_bias = jnp.sum(value_rows_gradient.astype(jnp.float32), axis=(0, 2)).reshape(
        MODEL_WIDTH
    )
    grad_direct = jnp.einsum(
        "mivt,git->mvg",
        key_rows_gradient,
        key_back.reshape(MODEL_WIDTH, HEAD_COUNT, HEAD_SIZE),
        preferred_element_type=jnp.float32,
    )
    grad_direct = grad_direct + jnp.einsum(
        "mivt,git->mvg",
        value_rows_gradient,
        value_back.reshape(MODEL_WIDTH, HEAD_COUNT, HEAD_SIZE),
        preferred_element_type=jnp.float32,
    )
    pool_first = jnp.where(pair_same, 0.5 * grad_pooled, grad_pooled)
    pool_second = jnp.where(pair_same, 0.5 * grad_pooled, 0.0)
    grad_tokens = (
        grad_direct
        + jnp.stack([pool_first, pool_second], axis=2).reshape(SG, local_tokens, MODEL_WIDTH)
    ).astype(jnp.bfloat16)
    summed = lax.psum(
        (
            grad_query_weight,
            grad_key_weight,
            grad_value_weight,
            grad_output_weight,
            grad_inner_weight,
            grad_outer_weight,
            grad_value_bias,
            grad_output_bias,
            grad_inner_bias,
            grad_outer_bias,
            grad_gain_one,
            grad_shift_one,
            grad_gain_two,
            grad_shift_two,
            grad_content_bias,
            grad_position_bias,
            grad_type_bias,
            grad_relative_kernel,
            grad_type_embed,
        ),
        "seq",
    )
    owned = (
        lax.psum_scatter(
            summed[0].astype(jnp.bfloat16), "dp", scatter_dimension=0, tiled=True
        ).astype(jnp.float32),
        lax.psum_scatter(
            summed[1].astype(jnp.bfloat16), "dp", scatter_dimension=0, tiled=True
        ).astype(jnp.float32),
        lax.psum_scatter(
            summed[2].astype(jnp.bfloat16), "dp", scatter_dimension=0, tiled=True
        ).astype(jnp.float32),
        lax.psum_scatter(
            summed[3].astype(jnp.bfloat16), "dp", scatter_dimension=0, tiled=True
        ).astype(jnp.float32),
        lax.psum_scatter(
            summed[4].astype(jnp.bfloat16), "dp", scatter_dimension=0, tiled=True
        ).astype(jnp.float32),
        lax.psum_scatter(
            summed[5].astype(jnp.bfloat16), "dp", scatter_dimension=0, tiled=True
        ).astype(jnp.float32),
        lax.psum_scatter(
            summed[6].astype(jnp.bfloat16), "dp", scatter_dimension=0, tiled=True
        ).astype(jnp.float32),
        lax.psum_scatter(
            summed[7].astype(jnp.bfloat16), "dp", scatter_dimension=0, tiled=True
        ).astype(jnp.float32),
        lax.psum_scatter(
            summed[8].astype(jnp.bfloat16), "dp", scatter_dimension=0, tiled=True
        ).astype(jnp.float32),
        lax.psum_scatter(
            summed[9].astype(jnp.bfloat16), "dp", scatter_dimension=0, tiled=True
        ).astype(jnp.float32),
        lax.psum_scatter(
            summed[10].astype(jnp.bfloat16), "dp", scatter_dimension=0, tiled=True
        ).astype(jnp.float32),
        lax.psum_scatter(
            summed[11].astype(jnp.bfloat16), "dp", scatter_dimension=0, tiled=True
        ).astype(jnp.float32),
        lax.psum_scatter(
            summed[12].astype(jnp.bfloat16), "dp", scatter_dimension=0, tiled=True
        ).astype(jnp.float32),
        lax.psum_scatter(
            summed[13].astype(jnp.bfloat16), "dp", scatter_dimension=0, tiled=True
        ).astype(jnp.float32),
        lax.psum_scatter(
            summed[14].astype(jnp.bfloat16), "dp", scatter_dimension=0, tiled=True
        ).astype(jnp.float32),
        lax.psum_scatter(
            summed[15].astype(jnp.bfloat16), "dp", scatter_dimension=0, tiled=True
        ).astype(jnp.float32),
        lax.psum_scatter(
            summed[16].astype(jnp.bfloat16), "dp", scatter_dimension=0, tiled=True
        ).astype(jnp.float32),
        lax.psum_scatter(
            summed[17].astype(jnp.bfloat16), "dp", scatter_dimension=0, tiled=True
        ).astype(jnp.float32),
        lax.psum_scatter(
            summed[18].astype(jnp.bfloat16), "dp", scatter_dimension=0, tiled=True
        ).astype(jnp.float32),
    )
    return (
        output,
        grad_tokens,
        owned[0],
        owned[1],
        owned[2],
        owned[3],
        owned[4],
        owned[5],
        owned[6],
        owned[7],
        owned[8],
        owned[9],
        owned[10],
        owned[11],
        owned[12],
        owned[13],
        owned[14],
        owned[15],
        owned[16],
        owned[17],
        owned[18],
    )


BF16 = jnp.bfloat16
F32 = jnp.float32
PAIRS = HEAD_COUNT // 2
LANES = 2 * HEAD_SIZE
ROWS = 256
FAR = -(2.0**100)
FF = 3072
NN = (((1,), (0,)), ((), ()))
NT = (((1,), (1,)), ((), ()))
TN = (((0,), (0,)), ((), ()))


def mm(left, right, dims=NN):
    return lax.dot_general(left, right, dims, preferred_element_type=F32)


def split(value):
    high = value.astype(BF16)
    return high, (value - high.astype(F32)).astype(BF16)


def lane_ids(rows):
    return lax.broadcasted_iota(jnp.int32, (rows, LANES), 1)


VECTORS = 16


def pair_maps(relative):
    row = lax.broadcasted_iota(jnp.int32, (HEAD_SIZE, LANES), 0)
    twice = (lane_ids(HEAD_SIZE) % HEAD_SIZE == row).astype(BF16)
    lane = lane_ids(LANES)
    row = lax.broadcasted_iota(jnp.int32, (LANES, LANES), 0)
    crossed = (row < HEAD_SIZE) != (lane < HEAD_SIZE)
    plain = jnp.where(crossed, mm(relative, twice), 0.0).astype(BF16)
    half = HEAD_SIZE // 2
    partner = jnp.where(lane % HEAD_SIZE < half, lane + half, lane - half)
    swapped = mm(plain, (row == partner).astype(BF16)).astype(BF16)
    return plain, swapped


def fold_maps(grads):
    row = lax.broadcasted_iota(jnp.int32, (LANES, 2 * LANES), 0)
    lane = lax.broadcasted_iota(jnp.int32, (LANES, 2 * LANES), 1)
    crossed = (row < HEAD_SIZE) != (lane % LANES < HEAD_SIZE)
    high, low = split(jnp.where(crossed, grads, 0.0))
    row = lax.broadcasted_iota(jnp.int32, (2 * LANES, LANES), 0)
    lane = lax.broadcasted_iota(jnp.int32, (2 * LANES, LANES), 1)
    half = HEAD_SIZE // 2
    at = row % HEAD_SIZE
    partner = jnp.where(at < half, at + half, at - half)
    fold = (jnp.where(row < LANES, at, partner) == lane).astype(BF16)
    return mm(high, fold) + mm(low, fold)


def kind_maps(vectors):
    row = lax.broadcasted_iota(jnp.int32, (VECTORS, 4 * LANES), 0)
    column = lax.broadcasted_iota(jnp.int32, (VECTORS, 4 * LANES), 1)
    lane = column % LANES
    wanted = (lane >= 3) & (lane < 6) & (row == 11 - (column // LANES) % 2)
    both = mm(vectors.astype(BF16), wanted.astype(BF16), TN)
    row = lax.broadcasted_iota(jnp.int32, (LANES, 4 * LANES), 0)
    column = lax.broadcasted_iota(jnp.int32, (LANES, 4 * LANES), 1)
    return jnp.where((row < HEAD_SIZE) == (column < 2 * LANES), both, 0.0).astype(BF16)


MESH = pl.DeviceIdType.MESH
SUM_ROWS = 48
STAGES = ("core", "y", "x", "near", "far", "far_back", "near_back", "x_back")


class Place:
    def __init__(self):
        self.seq, self.dp = lax.axis_index("seq"), lax.axis_index("dp")
        self.core, self.y = self.dp % 2, self.dp // 2
        self.x, self.near, self.far = self.seq % 2, (self.seq // 2) % 2, self.seq // 4
        self.partner = {
            "core": (self.seq, self.dp + 1 - 2 * self.core),
            "y": (self.seq, self.dp + 2 - 4 * self.y),
            "x": (self.seq + 1 - 2 * self.x, self.dp),
            "near": (self.seq + 2 - 4 * self.near, self.dp),
            "far": (self.seq + 4 - 8 * self.far, self.dp),
        }

    def peers(self):
        return [((self.seq + k) % SG, self.dp) for k in range(1, SG)]

    def greet(self):
        barrier = pltpu.get_barrier_semaphore()
        others = [self.partner["core"], self.partner["y"], *self.peers()]
        for device in others:
            pl.semaphore_signal(barrier, inc=1, device_id=device, device_id_type=MESH)
        pl.semaphore_wait(barrier, len(others))


def add_rows(target, addend, rows):
    def step(i, carry):
        at = pl.ds(pl.multiple_of(i * SUM_ROWS, 16), SUM_ROWS)
        left, right = target(at), addend(at)
        left[...] = left[...] + right[...]
        return carry

    lax.fori_loop(0, rows // SUM_ROWS, step, 0)


class Chunk:
    def __init__(self, place, index, source, rows, columns, buffers, send, receive, local):
        self.place, self.source, self.rows, self.columns = place, source, rows, columns
        self.own, self.from_core, self.from_y, self.from_x, self.from_near, self.from_far, self.full = buffers
        self.send_at = lambda stage, k=0: send.at[index, STAGES.index(stage) + (8 if k else 0)]
        self.receive_at = lambda stage, k=0: receive.at[index, STAGES.index(stage) + (8 if k else 0)]
        self.local = lambda k: local.at[index, k]
        half, quarter = rows // 2, rows // 4
        self.my_columns = pl.ds(pl.multiple_of(place.x * (columns // 2), 128), columns // 2)
        self.other_columns = pl.ds(
            pl.multiple_of((1 - place.x) * (columns // 2), 128), columns // 2
        )
        self.my_half = pl.multiple_of(place.near * half, 16)
        self.my_quarter = pl.multiple_of(place.near * half + place.far * quarter, 16)

    def remote(self, stage, source, target, k=0):
        return pltpu.make_async_remote_copy(
            src_ref=source,
            dst_ref=target,
            send_sem=self.send_at(stage, k),
            recv_sem=self.receive_at(stage, k),
            device_id=self.place.partner[stage.split("_")[0]],
            device_id_type=MESH,
        )

    def locals(self):
        if self.own is None:
            return []
        return [
            pltpu.make_async_copy(
                self.source(2 * k + self.place.core), self.own.at[k], self.local(k)
            )
            for k in range(2)
        ]

    def copies(self, stage):
        place, rows = self.place, self.rows
        half, quarter = rows // 2, rows // 4
        if stage == "core":
            return [
                self.remote(
                    stage, self.source(2 * k + 1 - place.core), self.from_core.at[k], k
                )
                for k in range(2)
            ]
        if stage == "y":
            return [self.remote(stage, self.from_core.at[1 - place.y], self.from_y)]
        if stage == "x":
            return [self.remote(stage, self.from_y.at[:, self.other_columns], self.from_x)]
        if stage == "near":
            other = pl.ds(pl.multiple_of((1 - place.near) * half, 16), half)
            return [self.remote(stage, self.from_x.at[other, :], self.from_near)]
        if stage == "far":
            other = pl.ds(pl.multiple_of((1 - place.far) * quarter, 16), quarter)
            return [self.remote(stage, self.from_near.at[other, :], self.from_far)]
        if stage == "far_back":
            mine = self.full.at[pl.ds(self.my_quarter, quarter), self.my_columns]
            return [self.remote(stage, self.from_far, mine)]
        if stage == "near_back":
            mine = self.full.at[pl.ds(self.my_half, half), self.my_columns]
            return [self.remote(stage, mine, mine)]
        mine = self.full.at[:, self.my_columns]
        return [self.remote(stage, mine, mine)]

    def start(self, stage):
        if stage == "core":
            for copy in self.locals():
                copy.start()
        for copy in self.copies(stage):
            copy.start()

    def finish(self, stage):
        place, rows = self.place, self.rows
        half, quarter = rows // 2, rows // 4
        for copy in self.copies(stage):
            copy.wait_recv()
        if stage == "core":
            for copy in self.locals():
                copy.wait()
            for k in range(2):
                kept = (
                    self.source(2 * k + place.core) if self.own is None else self.own.at[k]
                )
                add_rows(
                    lambda at: self.from_core.at[k, at, :], lambda at: kept.at[at, :], rows
                )
        elif stage == "y":
            add_rows(
                lambda at: self.from_y.at[at, :],
                lambda at: self.from_core.at[place.y, at, :],
                rows,
            )
        elif stage == "x":
            add_rows(
                lambda at: self.from_x.at[at, :],
                lambda at: self.from_y.at[at, self.my_columns],
                rows,
            )
        elif stage == "near":
            add_rows(
                lambda at: self.from_near.at[at, :],
                lambda at: self.from_x.at[
                    pl.ds(pl.multiple_of(at.start + self.my_half, 16), SUM_ROWS), :
                ],
                half,
            )
        elif stage == "far":
            begin = place.far * quarter
            add_rows(
                lambda at: self.from_far.at[at, :],
                lambda at: self.from_near.at[
                    pl.ds(pl.multiple_of(at.start + begin, 16), SUM_ROWS), :
                ],
                quarter,
            )

    def place_piece(self):
        def step(i, carry):
            at = pl.ds(pl.multiple_of(i * SUM_ROWS, 16), SUM_ROWS)
            to = pl.ds(pl.multiple_of(i * SUM_ROWS + self.my_quarter, 16), SUM_ROWS)
            self.full[to, self.my_columns] = self.from_far[at, :]
            return carry

        lax.fori_loop(0, self.rows // 4 // SUM_ROWS, step, 0)

    def step(self, stage):
        at = STAGES.index(stage)
        if at > 0:
            self.finish(STAGES[at - 1])
        if stage == "far_back":
            self.place_piece()
        self.start(stage)

    def close(self, stages):
        for stage in stages:
            for copy in self.copies(stage):
                copy.wait_send()


DOWN, UP = STAGES[:5], STAGES[5:]
WHOLE = 3


def down_buffers(rows, columns, own):
    buffer = lambda *shape: pltpu.VMEM(shape, BF16)
    return [
        *([buffer(2, rows, columns)] if own else []),
        buffer(2, rows, columns),
        buffer(rows, columns),
        buffer(rows, columns // 2),
        buffer(rows // 2, columns // 2),
        buffer(rows // 4, columns // 2),
    ]


def grad_chunks():
    quarter = MODEL_WIDTH // 4
    half = MODEL_WIDTH // 2
    early = [
        (0, MODEL_WIDTH, 0, 0, half, MODEL_WIDTH),
        (0, MODEL_WIDTH, half, 0, half, MODEL_WIDTH),
        (1, quarter, 0, 0, quarter, FF // 2),
        (1, quarter, 0, FF // 2, quarter, FF // 2),
        (2, quarter, 0, 0, quarter, MODEL_WIDTH),
    ]
    late = [(j, quarter, 0, 0, quarter, MODEL_WIDTH) for j in (3, 4, 5)]
    late.insert(0, (6, quarter, 0, 0, quarter, 2 * LANES))
    return early, late


def chunk_source(grad, chunk):
    _, owner_rows, row, column, rows, columns = chunk

    def source(owner):
        begin = pl.multiple_of(owner * owner_rows + row, 16)
        return grad.at[pl.ds(begin, rows), pl.ds(column, columns)]

    return source


SEND_ORDER = (4, 3, 5, 2, 6, 1, 7, 0)


def finish_kernel(
    grad_query_ref,
    grad_key_ref,
    grad_value_ref,
    tokens_ref,
    pooled_ref,
    grad_first_ref,
    pool_ref,
    weights_ref,
    small_ref,
    *refs,
):
    early, late = grad_chunks()
    early = early[WHOLE:]
    pieces, refs = refs[: len(early)], refs[len(early) :]
    tokens_out, refs = refs[0], refs[1:]
    count = len(early) + len(late)
    outs, refs = refs[:count], refs[count:]
    fulls, refs = refs[:count], refs[count:]
    buffers, refs = refs[: 5 * len(late)], refs[5 * len(late) :]
    (
        tokens_stage,
        late_grads,
        send,
        receive,
        token_send,
        token_receive,
        token_local,
    ) = refs
    place = Place()
    place.greet()
    first = []
    for i, chunk in enumerate(early):
        kept = [None, None, None, None, None, pieces[i], fulls[i]]
        first.append(Chunk(place, i, None, *chunk[4:], kept, send, receive, None))
    second = []
    for j, chunk in enumerate(late):
        i = len(early) + j
        kept = [None, *buffers[5 * j : 5 * j + 5], fulls[i]]
        source = chunk_source(late_grads.at[j - 1] if j else small_ref, chunk)
        second.append(Chunk(place, i, source, *chunk[4:], kept, send, receive, None))
    for item in first:
        item.place_piece()
        item.start("far_back")
    second[0].start("core")

    moved = []

    def send_tokens(k):
        to = (place.seq + k) % SG
        block = LEN // SG
        rows = pl.ds(pl.multiple_of(to * block, block), block)
        pooled_rows = pl.ds(pl.multiple_of(to * (block // 2), block // 2), block // 2)
        weight = lambda j: weights_ref[:, j * MODEL_WIDTH : (j + 1) * MODEL_WIDTH]
        grad_pooled = grad_first_ref[pooled_rows, :] + mm(
            grad_query_ref[pooled_rows, :], weight(0), NT
        )
        high, low = split(grad_pooled)
        total = mm(grad_key_ref[rows, :], weight(1), NT)
        total += mm(grad_value_ref[rows, :], weight(2), NT)
        total += mm(pool_ref[to], high, TN) + mm(pool_ref[to], low, TN)
        tokens_stage[to] = total.astype(BF16)
        if k == 0:
            copy = pltpu.make_async_copy(
                tokens_stage.at[to], tokens_out.at[place.seq], token_local
            )
        else:
            copy = pltpu.make_async_remote_copy(
                src_ref=tokens_stage.at[to],
                dst_ref=tokens_out.at[place.seq],
                send_sem=token_send.at[k - 1],
                recv_sem=token_receive.at[k - 1],
                device_id=(to, place.dp),
                device_id_type=MESH,
            )
        copy.start()
        moved.append(copy)

    for k in SEND_ORDER[:3]:
        send_tokens(k)
    for item in first:
        item.step("near_back")
    for k in SEND_ORDER[3:6]:
        send_tokens(k)
    for item in first:
        item.step("x_back")
    for k in SEND_ORDER[6:]:
        send_tokens(k)

    operands = [
        (pooled_ref, grad_query_ref),
        (tokens_ref, grad_key_ref),
        (tokens_ref, grad_value_ref),
    ]
    for j, (left, right) in enumerate(operands):
        for r in range(0, MODEL_WIDTH, 256):
            late_grads[j, r : r + 256, :] = mm(left[:, r : r + 256], right[...], TN).astype(BF16)
        second[j + 1].start("core")
        second[j].step("y")
    second[len(late) - 1].step("y")
    for stage in STAGES[2:]:
        for item in second:
            item.step(stage)

    for item, out in zip(first, outs):
        item.finish(STAGES[-1])
        out[...] = item.full[...]
        item.close(UP)
    for item, out in zip(second, outs[len(first) :]):
        item.finish(STAGES[-1])
        out[...] = item.full[...]
        item.close(STAGES)
    for copy in moved:
        copy.wait()


def finish(
    grad_query, grad_key, grad_value, tokens, pooled, grad_first, pool, weights, small, pieces
):
    anywhere = pl.BlockSpec(memory_space=pl.ANY)
    early, late = grad_chunks()
    early = early[WHOLE:]
    chunks = early + late
    count = len(chunks)
    inside = pl.BlockSpec(memory_space=pltpu.VMEM)
    out_tokens = (SG, LEN // SG, MODEL_WIDTH)
    return pl.pallas_call(
        finish_kernel,
        in_specs=[inside] * (9 + len(early)),
        out_specs=[anywhere, *[inside] * count],
        out_shape=[
            jax.ShapeDtypeStruct(out_tokens, BF16),
            *[jax.ShapeDtypeStruct(chunk[4:], BF16) for chunk in chunks],
        ],
        scratch_shapes=[
            *[pltpu.VMEM(chunk[4:], BF16) for chunk in chunks],
            *[buffer for chunk in late for buffer in down_buffers(*chunk[4:], False)],
            pltpu.VMEM(out_tokens, BF16),
            pltpu.VMEM((3, MODEL_WIDTH, MODEL_WIDTH), BF16),
            pltpu.SemaphoreType.DMA((count, 16)),
            pltpu.SemaphoreType.DMA((count, 16)),
            pltpu.SemaphoreType.DMA((SG - 1,)),
            pltpu.SemaphoreType.DMA((SG - 1,)),
            pltpu.SemaphoreType.DMA,
        ],
        compiler_params=pltpu.CompilerParams(
            collective_id=3, has_side_effects=True, vmem_limit_bytes=58 * 2**20
        ),
        name="finish",
    )(
        grad_query,
        grad_key,
        grad_value,
        tokens,
        pooled,
        grad_first,
        pool,
        weights,
        small,
        *pieces,
    )


def attend_kernel(
    query_ref,
    key_ref,
    value_ref,
    relative_ref,
    vectors_ref,
    query_side_ref,
    key_side_ref,
    phase_ref,
    cos_ref,
    sin_ref,
    cotangent_ref,
    mixture_ref,
    join_ref,
    upstream_ref,
    key_join,
    value_join,
    send,
    receive,
    local,
):
    place = Place()

    def upstream_copies():
        copies = [
            pltpu.make_async_copy(
                cotangent_ref.at[place.seq], upstream_ref.at[place.seq], local
            )
        ]
        for k in range(1, SG):
            to = (place.seq + k) % SG
            copies.append(
                pltpu.make_async_remote_copy(
                    src_ref=cotangent_ref.at[to],
                    dst_ref=upstream_ref.at[place.seq],
                    send_sem=send.at[k - 1],
                    recv_sem=receive.at[k - 1],
                    device_id=(to, place.dp),
                    device_id_type=MESH,
                )
            )
        return copies

    @pl.when(pl.program_id(0) == 0)
    def _():
        place.greet()
        for copy in upstream_copies():
            copy.start()

    query = query_ref[...]
    high, low = split(query)
    plain, swapped = pair_maps(relative_ref[...])
    kinds = kind_maps(vectors_ref[...])
    maps = jnp.concatenate([plain, swapped, kinds], axis=1)
    position_add, type_add = vectors_ref[8:9, :].astype(BF16), vectors_ref[9:10, :].astype(BF16)
    map_add = jnp.concatenate(
        [mm(position_add, plain), mm(position_add, swapped), mm(type_add, kinds)], axis=1
    )
    terms = mm(jnp.concatenate([high, low], axis=1), jnp.concatenate([maps, maps], axis=0))
    terms = terms + map_add
    lane = lane_ids(PQ)
    left = lane < HEAD_SIZE
    content = query + vectors_ref[7:8, :]
    position = terms[:, :LANES] * cos_ref[...] + terms[:, LANES : 2 * LANES] * sin_ref[...]
    side = query_side_ref[...]
    typed = (lane >= 3) & (lane < 6)
    scale = HEAD_SIZE ** (-0.5)
    for h in range(2):
        first, second = (content, position) if h == 0 else (position, content)
        join_ref[h, :, :LANES] = (jnp.where(left, first, second) * scale).astype(BF16)
        base = 2 * LANES * (h + 1)
        same = terms[:, base : base + LANES]
        other = terms[:, base + LANES : base + 2 * LANES]
        kind = jnp.where(side > 0.5, same, other) * scale
        join_ref[h, :, LANES:] = jnp.where(typed, kind, side).astype(BF16)
    key_left = lane_ids(LEN) < HEAD_SIZE
    key_join[:, LANES:] = key_side_ref[...]
    value_join[:, :LANES] = value_ref[...]
    value_join[:, LANES:] = key_side_ref[...]
    tile_lane = lane_ids(ROWS)
    for h in range(2):
        pieces = (key_ref[...], phase_ref[...]) if h == 0 else (phase_ref[...], key_ref[...])
        key_join[:, :LANES] = jnp.where(key_left, *pieces)
        for i in range(PQ // ROWS):
            rows = slice(i * ROWS, (i + 1) * ROWS)
            scores = mm(join_ref[h, rows, :], key_join[...], NT)
            top = jnp.max(scores, axis=1, keepdims=True)
            weights = jnp.exp(scores - top).astype(BF16)
            mixed = mm(weights, value_join[...])
            total = mixed[:, LANES + 6 : LANES + 7]
            result = (mixed[:, :LANES] / total).astype(BF16)
            if h == 0:
                mixture_ref[rows, :] = result
            else:
                mixture_ref[rows, :] = jnp.where(
                    tile_lane < HEAD_SIZE, mixture_ref[rows, :], result
                )
            shift = -(top + jnp.log(total))
            one = shift.astype(BF16).astype(F32)
            two = (shift - one).astype(BF16).astype(F32)
            three = shift - one - two
            extra = jnp.where(tile_lane == 6, one, jnp.where(tile_lane == 7, two, three))
            kept = join_ref[h, rows, LANES:].astype(F32)
            inside = (tile_lane >= 6) & (tile_lane < 9)
            join_ref[h, rows, LANES:] = jnp.where(inside, extra, kept).astype(BF16)

    @pl.when(pl.program_id(0) == PAIRS - 1)
    def _():
        for copy in upstream_copies():
            copy.wait()


def attend_forward(
    query, pairs, relative, vectors, query_side, key_side, phase, cosm, sinm, cotangent
):
    whole = lambda shape: pl.BlockSpec(shape, lambda i: (0, 0))
    return pl.pallas_call(
        attend_kernel,
        grid=(PAIRS,),
        in_specs=[
            pl.BlockSpec((PQ, LANES), lambda i: (0, i)),
            pl.BlockSpec((LEN, LANES), lambda i: (0, i)),
            pl.BlockSpec((LEN, LANES), lambda i: (0, i + PAIRS)),
            pl.BlockSpec((LANES, HEAD_SIZE), lambda i: (i, 0)),
            pl.BlockSpec((VECTORS, LANES), lambda i: (0, i)),
            whole((PQ, LANES)),
            whole((LEN, LANES)),
            whole((LEN, LANES)),
            whole((PQ, LANES)),
            whole((PQ, LANES)),
            pl.BlockSpec(memory_space=pl.ANY),
        ],
        out_specs=[
            pl.BlockSpec((PQ, LANES), lambda i: (0, i)),
            pl.BlockSpec((2, PQ, 2 * LANES), lambda i: (i, 0, 0)),
            pl.BlockSpec(memory_space=pl.ANY),
        ],
        out_shape=[
            jax.ShapeDtypeStruct((PQ, MODEL_WIDTH), BF16),
            jax.ShapeDtypeStruct((HEAD_COUNT, PQ, 2 * LANES), BF16),
            jax.ShapeDtypeStruct(cotangent.shape, BF16),
        ],
        scratch_shapes=[
            pltpu.VMEM((LEN, 2 * LANES), BF16),
            pltpu.VMEM((LEN, 2 * LANES), BF16),
            pltpu.SemaphoreType.DMA((SG - 1,)),
            pltpu.SemaphoreType.DMA((SG - 1,)),
            pltpu.SemaphoreType.DMA,
        ],
        cost_estimate=pl.CostEstimate(
            flops=4 * HEAD_COUNT * PQ * LEN * 256,
            bytes_accessed=20_000_000,
            transcendentals=HEAD_COUNT * PQ * LEN,
        ),
        compiler_params=pltpu.CompilerParams(
            collective_id=5, has_side_effects=True, vmem_limit_bytes=56 * 2**20
        ),
        name="attend_forward",
    )(query, pairs, pairs, relative, vectors, query_side, key_side, phase, cosm, sinm, cotangent)


FF_STEP = 768
FF_TILES = FF // FF_STEP
ROW_TILES = PQ // ROWS


def row_norm(value):
    centred = value - jnp.mean(value, axis=1, keepdims=True)
    inverse = lax.rsqrt(jnp.mean(centred * centred, axis=1, keepdims=True) + norm_eps)
    return centred * inverse, inverse


def row_norm_back(scaled, normed, inverse):
    along = jnp.mean(scaled * normed, axis=1, keepdims=True)
    return inverse * (scaled - jnp.mean(scaled, axis=1, keepdims=True) - normed * along)


def gelu_pieces(value):
    rate = math.sqrt(2.0 / math.pi)
    square = value * value
    bend = jnp.tanh(rate * value * (1.0 + 0.044715 * square))
    half = 0.5 * (1.0 + bend)
    slope = half + (0.5 * rate) * value * (1.0 - bend * bend) * (1.0 + 0.134145 * square)
    return value * half, slope


def mlp_kernel(
    mixture_ref,
    pooled_ref,
    upstream_ref,
    output_weight_ref,
    inner_weight_ref,
    outer_weight_ref,
    vectors_ref,
    inner_add_ref,
    output_ref,
    grad_mixture_ref,
    grad_first_ref,
    grad_outer_ref,
    grad_inner_ref,
    grad_output_ref,
    sums_ref,
    inner_sums_ref,
    active,
    slopes,
    grad_expanded,
    hidden_low,
    grad_branch,
    grad_attention,
    output_stage,
    mixture_stage,
    first_stage,
    send,
    receive,
    local,
):
    step = pl.program_id(0)
    place = Place()
    block = PQ // SG
    tile = (step + place.seq // 2 + 1) % ROW_TILES
    begin = pl.multiple_of(tile * ROWS, ROWS)

    def output_copy(to):
        return pltpu.make_async_remote_copy(
            src_ref=output_stage.at[to],
            dst_ref=output_ref.at[place.seq],
            send_sem=send.at[to],
            recv_sem=receive.at[place.seq],
            device_id=(to, place.dp),
            device_id_type=MESH,
        )

    def kept_copy():
        return pltpu.make_async_copy(
            output_stage.at[place.seq], output_ref.at[place.seq], local.at[0]
        )

    def row_copies():
        rows = pl.ds(begin, ROWS)
        return [
            pltpu.make_async_copy(
                mixture_stage.at[rows, :], grad_mixture_ref.at[rows, :], local.at[1 + 2 * tile]
            ),
            pltpu.make_async_copy(
                first_stage.at[rows, :], grad_first_ref.at[rows, :], local.at[2 + 2 * tile]
            ),
        ]

    @pl.when(step == 0)
    def _():
        place.greet()

    @pl.when(step < ROW_TILES)
    def _():
        rows = pl.ds(begin, ROWS)
        vector = lambda j: vectors_ref[j : j + 1, :]
        output_add, outer_add, gain_one, shift_one, gain_two, shift_two = map(vector, range(1, 7))
        attention = mm(mixture_ref[rows, :], output_weight_ref[...]) + output_add
        normed_one, inverse_one = row_norm(pooled_ref[rows, :] + attention)
        hidden = normed_one * gain_one + shift_one
        low_hidden = hidden.astype(BF16)
        hidden_low[rows, :] = low_hidden
        branch = jnp.zeros((ROWS, MODEL_WIDTH), F32)
        for j in range(FF_TILES):
            part = slice(j * FF_STEP, (j + 1) * FF_STEP)
            expanded = mm(low_hidden, inner_weight_ref[:, part]) + inner_add_ref[:, part]
            value, slope = gelu_pieces(expanded)
            low_value = value.astype(BF16)
            active[rows, part] = low_value
            slopes[:, part] = slope
            branch += mm(low_value, outer_weight_ref[part, :])
        normed_two, inverse_two = row_norm(hidden + (branch + outer_add))
        result = (normed_two * gain_two + shift_two).astype(BF16)
        for k in range(ROWS // block):
            to = tile * (ROWS // block) + k
            output_stage[to] = result[k * block : (k + 1) * block]

            @pl.when(to == place.seq)
            def _():
                kept_copy().start()

            @pl.when(to != place.seq)
            def _():
                output_copy(to).start()

        upstream = upstream_ref[rows, :].astype(F32)
        grad_second = row_norm_back(upstream * gain_two, normed_two, inverse_two)
        low_branch = grad_second.astype(BF16)
        grad_branch[rows, :] = low_branch
        grad_hidden = grad_second
        inner_sums = []
        for j in range(FF_TILES):
            part = slice(j * FF_STEP, (j + 1) * FF_STEP)
            grad_active = mm(low_branch, outer_weight_ref[part, :], NT)
            low_grad = (slopes[:, part] * grad_active).astype(BF16)
            grad_expanded[rows, part] = low_grad
            inner_sums.append(jnp.sum(low_grad.astype(F32), axis=0, keepdims=True))
            grad_hidden += mm(low_grad, inner_weight_ref[:, part], NT)
        grad_first = row_norm_back(grad_hidden * gain_one, normed_one, inverse_one)
        first_stage[rows, :] = grad_first
        low_attention = grad_first.astype(BF16)
        grad_attention[rows, :] = low_attention
        mixture_stage[rows, :] = mm(low_attention, output_weight_ref[...], NT).astype(BF16)
        for copy in row_copies():
            copy.start()
        row = lambda v: jnp.sum(v, axis=0, keepdims=True)
        sums = jnp.concatenate(
            [
                row(low_attention.astype(F32)),
                row(low_branch.astype(F32)),
                row(grad_hidden * normed_one),
                row(grad_hidden),
                row(upstream * normed_two),
                row(upstream),
                jnp.zeros((2, MODEL_WIDTH), F32),
            ],
            axis=0,
        )
        inner_sum = jnp.concatenate(inner_sums, axis=1)

        @pl.when(step == 0)
        def _():
            sums_ref[...] = sums
            inner_sums_ref[...] = inner_sum

        @pl.when(step > 0)
        def _():
            sums_ref[...] += sums
            inner_sums_ref[...] += inner_sum

    for j in range(FF_TILES):

        @pl.when(step == ROW_TILES + j)
        def _():
            part = slice(j * FF_STEP, (j + 1) * FF_STEP)
            grad_outer_ref[...] = mm(active[:, part], grad_branch[...], TN).astype(BF16)
            grad_inner_ref[...] = mm(hidden_low[...], grad_expanded[:, part], TN).astype(BF16)
            if j == 0:
                grad_output_ref[...] = mm(mixture_ref[...], grad_attention[...], TN).astype(BF16)

    @pl.when(step == ROW_TILES + FF_TILES - 1)
    def _():
        for t in range(ROW_TILES):
            rows = pl.ds(t * ROWS, ROWS)
            pltpu.make_async_copy(
                mixture_stage.at[rows, :], grad_mixture_ref.at[rows, :], local.at[1 + 2 * t]
            ).wait()
            pltpu.make_async_copy(
                first_stage.at[rows, :], grad_first_ref.at[rows, :], local.at[2 + 2 * t]
            ).wait()
        kept_copy().wait()
        for k in range(1, SG):
            other = (place.seq + k) % SG
            output_copy(other).wait_send()
            pltpu.make_async_remote_copy(
                src_ref=output_stage.at[other],
                dst_ref=output_ref.at[other],
                send_sem=send.at[other],
                recv_sem=receive.at[other],
                device_id=(other, place.dp),
                device_id_type=MESH,
            ).wait_recv()


def mlp(mixture, pooled, upstream, output_weight, inner_weight, outer_weight, vectors, inner_add):
    fixed = lambda shape: pl.BlockSpec(shape, lambda i: (0, 0), pipeline_mode=pl.Buffered(1))
    still = lambda shape: pl.BlockSpec(shape, lambda i: (0, 0))
    anywhere = pl.BlockSpec(memory_space=pl.ANY)
    out_shape = (SG, PQ // SG, MODEL_WIDTH)
    late = lambda i: jnp.maximum(i - ROW_TILES, 0)
    whole = (PQ, MODEL_WIDTH)
    square = (MODEL_WIDTH, MODEL_WIDTH)
    return pl.pallas_call(
        mlp_kernel,
        grid=(ROW_TILES + FF_TILES,),
        in_specs=[
            fixed(whole),
            fixed(whole),
            fixed(whole),
            fixed(square),
            fixed((MODEL_WIDTH, FF)),
            fixed((FF, MODEL_WIDTH)),
            fixed((VECTORS, MODEL_WIDTH)),
            fixed((1, FF)),
        ],
        out_specs=[
            anywhere,
            anywhere,
            anywhere,
            pl.BlockSpec((FF_STEP, MODEL_WIDTH), lambda i: (late(i), 0)),
            pl.BlockSpec((MODEL_WIDTH, FF_STEP), lambda i: (0, late(i))),
            still(square),
            still((8, MODEL_WIDTH)),
            still((1, FF)),
        ],
        out_shape=[
            jax.ShapeDtypeStruct(out_shape, BF16),
            jax.ShapeDtypeStruct(whole, BF16),
            jax.ShapeDtypeStruct(whole, F32),
            jax.ShapeDtypeStruct((FF, MODEL_WIDTH), BF16),
            jax.ShapeDtypeStruct((MODEL_WIDTH, FF), BF16),
            jax.ShapeDtypeStruct(square, BF16),
            jax.ShapeDtypeStruct((8, MODEL_WIDTH), F32),
            jax.ShapeDtypeStruct((1, FF), F32),
        ],
        scratch_shapes=[
            pltpu.VMEM((PQ, FF), BF16),
            pltpu.VMEM((ROWS, FF), F32),
            pltpu.VMEM((PQ, FF), BF16),
            pltpu.VMEM(whole, BF16),
            pltpu.VMEM(whole, BF16),
            pltpu.VMEM(whole, BF16),
            pltpu.VMEM(out_shape, BF16),
            pltpu.VMEM(whole, BF16),
            pltpu.VMEM(whole, F32),
            pltpu.SemaphoreType.DMA((SG,)),
            pltpu.SemaphoreType.DMA((SG,)),
            pltpu.SemaphoreType.DMA((1 + 2 * ROW_TILES,)),
        ],
        cost_estimate=pl.CostEstimate(
            flops=2 * PQ * MODEL_WIDTH * (3 * MODEL_WIDTH + 6 * FF),
            bytes_accessed=40_000_000,
            transcendentals=PQ * FF,
        ),
        compiler_params=pltpu.CompilerParams(
            collective_id=1, has_side_effects=True, vmem_limit_bytes=60 * 2**20
        ),
        name="mlp",
    )(mixture, pooled, upstream, output_weight, inner_weight, outer_weight, vectors, inner_add)


SLOTS = 2 * (PQ // ROWS)
EARLY_SLOTS = {}
for _i, _steps in enumerate(
    (
        (3, 12, 17, 20, 23, 26, 29, 34),
        (6, 20, 25, 28, 31, 34, 37, 42),
        (9, 28, 33, 36, 39, 42, 45, 48),
        (12, 36, 41, 44, 48),
        (14, 41, 45, 47, 48),
    )
):
    for _stage, _slot in zip((*STAGES[1 : len(_steps)], None), _steps):
        EARLY_SLOTS.setdefault(_slot, []).append((_i, _stage))


def attend_back_kernel(
    join_ref,
    key_ref,
    value_ref,
    query_ref,
    mixture_ref,
    grad_ref,
    relative_ref,
    vectors_ref,
    query_side_ref,
    key_side_ref,
    phase_ref,
    cos_ref,
    sin_ref,
    mlp_sums_ref,
    grad_outer_ref,
    grad_inner_ref,
    grad_output_ref,
    grad_query_ref,
    grad_key_ref,
    grad_value_ref,
    small_ref,
    *refs,
):
    early, _ = grad_chunks()
    sent, refs = refs[: len(early)], refs[len(early) :]
    key_join, value_join, key_total, value_total, join_grads, *refs = refs
    fulls, refs = refs[:WHOLE], refs[WHOLE:]
    buffers, (send, receive, local) = refs[: 6 * len(early)], refs[6 * len(early) :]
    pair = pl.program_id(0)
    place = Place()
    grads = (grad_outer_ref, grad_inner_ref, grad_output_ref)
    work = []
    for i, chunk in enumerate(early):
        kept = [*buffers[6 * i : 6 * i + 6], fulls[i] if i < WHOLE else None]
        source = chunk_source(grads[chunk[0]], chunk)
        work.append(Chunk(place, i, source, *chunk[4:], kept, send, receive, local))

    def exchange(slot):
        for i, stage in EARLY_SLOTS.get(slot, ()):
            if stage is not None:
                work[i].step(stage)
            elif i < WHOLE:
                work[i].finish(STAGES[-1])
                sent[i][...] = work[i].full[...]
                work[i].close(STAGES)
            else:
                work[i].finish(DOWN[-1])
                sent[i][...] = work[i].from_far[...]
                work[i].close(DOWN)

    @pl.when(pair == 0)
    def _():
        place.greet()
        for item in work:
            item.start("core")

    scale = HEAD_SIZE ** (-0.5)
    key_left = lane_ids(LEN) < HEAD_SIZE
    tile_lane = lane_ids(ROWS)
    key_join[:, LANES:] = key_side_ref[...]
    value_join[:, :LANES] = value_ref[...]
    value_join[:, LANES:] = key_side_ref[...]
    for h in range(2):
        pieces = (key_ref[...], phase_ref[...]) if h == 0 else (phase_ref[...], key_ref[...])
        key_join[:, :LANES] = jnp.where(key_left, *pieces)
        mine = (tile_lane < HEAD_SIZE) if h == 0 else (tile_lane >= HEAD_SIZE)
        part = slice(h * HEAD_SIZE, (h + 1) * HEAD_SIZE)
        for i in range(PQ // ROWS):
            rows = slice(i * ROWS, (i + 1) * ROWS)
            for slot in EARLY_SLOTS:
                if slot % SLOTS == h * (PQ // ROWS) + i:

                    @pl.when(pair == slot // SLOTS)
                    def _():
                        exchange(slot)

            join = join_ref[h, rows, :]
            grad = jnp.where(mine, grad_ref[rows, :].astype(F32), 0.0)
            dot = -jnp.sum(grad * mixture_ref[rows, :].astype(F32), axis=1, keepdims=True)
            one = dot.astype(BF16).astype(F32)
            two = (dot - one).astype(BF16).astype(F32)
            three = dot - one - two
            extra = jnp.where(tile_lane == 6, one, jnp.where(tile_lane == 7, two, three))
            inside = (tile_lane >= 6) & (tile_lane < 9)
            extra = jnp.where(inside, extra, 0.0)
            grad_low = grad.astype(BF16)
            weights = jnp.exp(mm(join, key_join[...], NT))
            slope = mm(
                jnp.concatenate([grad_low, extra.astype(BF16)], axis=1), value_join[...], NT
            )
            low_slope = (weights * slope).astype(BF16)
            low_weights = weights.astype(BF16)
            join_grads[h, rows, :] = mm(low_slope, key_join[...])
            to_key = mm(join_ref[h, rows, part], low_slope, TN)
            to_value = mm(grad_ref[rows, part], low_weights, TN)
            if i == 0:
                key_total[part, :] = to_key
                value_total[part, :] = to_value
            else:
                key_total[part, :] += to_key
                value_total[part, :] += to_value
    grad_key_ref[...] = key_total[...].T.astype(BF16)
    grad_value_ref[...] = value_total[...].T.astype(BF16)
    lane = lane_ids(PQ)
    left = lane < HEAD_SIZE
    typed = (lane >= 3) & (lane < 6)
    rounded = [(join_grads[h, :, :LANES] * scale).astype(BF16).astype(F32) for h in range(2)]
    content = jnp.where(left, rounded[0], rounded[1])
    position = jnp.where(left, rounded[1], rounded[0])
    turned = jnp.concatenate([position * cos_ref[...], position * sin_ref[...]], axis=1)
    turned_high, turned_low = split(turned)
    plain, swapped = pair_maps(relative_ref[...])
    maps = jnp.concatenate([plain, swapped], axis=1)
    shifted_grad = mm(turned_high, maps, NT) + mm(turned_low, maps, NT)
    side = query_side_ref[...]
    sames, others = [], []
    for h in range(2):
        kinds = jnp.where(typed, join_grads[h, :, LANES:], 0.0)
        same = jnp.sum(jnp.where(side > 0.5, kinds, 0.0), axis=1, keepdims=True)
        other = jnp.sum(jnp.where(side > 0.5, 0.0, kinds), axis=1, keepdims=True)
        sames.append((same * scale).astype(BF16).astype(F32))
        others.append((other * scale).astype(BF16).astype(F32))
    same = jnp.where(left, sames[0], sames[1])
    other = jnp.where(left, others[0], others[1])
    position_add = vectors_ref[8:9, :]
    type_add = vectors_ref[9:10, :]
    type_other = vectors_ref[10:11, :]
    type_same = vectors_ref[11:12, :]
    typed_grad = same * type_same + other * type_other
    grad_query_ref[...] = (content + shifted_grad + typed_grad).astype(BF16)
    query = query_ref[...]
    shifted_high, shifted_low = split(query + position_add)
    grad_map = (
        mm(shifted_high, turned_high, TN)
        + mm(shifted_low, turned_high, TN)
        + mm(shifted_high, turned_low, TN)
    )
    kinds = query + type_add
    row = lambda v: jnp.sum(v, axis=0, keepdims=True)
    below = mlp_sums_ref[...]
    columns = jnp.concatenate(
        [
            jnp.zeros((HEAD_SIZE, LANES), F32),
            row(grad_value_ref[...].astype(F32)),
            row(content),
            row(shifted_grad),
            row(typed_grad),
            row(kinds * other),
            row(kinds * same),
            jnp.zeros((2, LANES), F32),
            below,
            jnp.zeros((LANES - HEAD_SIZE - 24, LANES), F32),
        ],
        axis=0,
    )
    small_ref[:, :LANES] = (fold_maps(grad_map) + columns.T).astype(BF16)
    small_ref[:, LANES:] = jnp.zeros((LANES, LANES), BF16)

    @pl.when(pair == PAIRS - 1)
    def _():
        exchange(PAIRS * SLOTS)


def attend_backward(
    join,
    pairs,
    query,
    mixture,
    grad,
    relative,
    vectors,
    query_side,
    key_side,
    phase,
    cosm,
    sinm,
    mlp_sums,
    grads,
):
    early, _ = grad_chunks()
    anywhere = pl.BlockSpec(memory_space=pl.ANY)
    shapes = [
        chunk[4:] if i < WHOLE else (chunk[4] // 4, chunk[5] // 2)
        for i, chunk in enumerate(early)
    ]
    whole = lambda shape: pl.BlockSpec(shape, lambda i: (0, 0))
    return pl.pallas_call(
        attend_back_kernel,
        grid=(PAIRS,),
        in_specs=[
            pl.BlockSpec((2, PQ, 2 * LANES), lambda i: (i, 0, 0)),
            pl.BlockSpec((LEN, LANES), lambda i: (0, i)),
            pl.BlockSpec((LEN, LANES), lambda i: (0, i + PAIRS)),
            pl.BlockSpec((PQ, LANES), lambda i: (0, i)),
            pl.BlockSpec((PQ, LANES), lambda i: (0, i)),
            pl.BlockSpec((PQ, LANES), lambda i: (0, i)),
            pl.BlockSpec((LANES, HEAD_SIZE), lambda i: (i, 0)),
            pl.BlockSpec((VECTORS, LANES), lambda i: (0, i)),
            whole((PQ, LANES)),
            whole((LEN, LANES)),
            whole((LEN, LANES)),
            whole((PQ, LANES)),
            whole((PQ, LANES)),
            pl.BlockSpec((16, LANES), lambda i: (0, i)),
            *[anywhere] * 3,
        ],
        out_specs=[
            pl.BlockSpec((PQ, LANES), lambda i: (0, i)),
            pl.BlockSpec((LEN, LANES), lambda i: (0, i)),
            pl.BlockSpec((LEN, LANES), lambda i: (0, i)),
            pl.BlockSpec((LANES, 2 * LANES), lambda i: (i, 0)),
            *[whole(shape) for shape in shapes],
        ],
        out_shape=[
            jax.ShapeDtypeStruct((PQ, MODEL_WIDTH), BF16),
            jax.ShapeDtypeStruct((LEN, MODEL_WIDTH), BF16),
            jax.ShapeDtypeStruct((LEN, MODEL_WIDTH), BF16),
            jax.ShapeDtypeStruct((MODEL_WIDTH, 2 * LANES), BF16),
            *[jax.ShapeDtypeStruct(shape, BF16) for shape in shapes],
        ],
        scratch_shapes=[
            pltpu.VMEM((LEN, 2 * LANES), BF16),
            pltpu.VMEM((LEN, 2 * LANES), BF16),
            pltpu.VMEM((LANES, LEN), F32),
            pltpu.VMEM((LANES, LEN), F32),
            pltpu.VMEM((2, PQ, 2 * LANES), F32),
            *[pltpu.VMEM(chunk[4:], BF16) for chunk in early[:WHOLE]],
            *[buffer for chunk in early for buffer in down_buffers(*chunk[4:], True)],
            pltpu.SemaphoreType.DMA((len(early), 16)),
            pltpu.SemaphoreType.DMA((len(early), 16)),
            pltpu.SemaphoreType.DMA((len(early), 2)),
        ],
        cost_estimate=pl.CostEstimate(
            flops=10 * HEAD_COUNT * PQ * LEN * 256,
            bytes_accessed=32_000_000,
            transcendentals=HEAD_COUNT * PQ * LEN,
        ),
        compiler_params=pltpu.CompilerParams(
            collective_id=2, has_side_effects=True, vmem_limit_bytes=58 * 2**20
        ),
        name="attend_backward",
    )(
        join,
        pairs,
        pairs,
        query,
        mixture,
        grad,
        relative,
        vectors,
        query_side,
        key_side,
        phase,
        cosm,
        sinm,
        mlp_sums,
        *grads,
    )


def labels_kernel(
    labels_ref,
    query_ref,
    key_ref,
    value_ref,
    output_ref,
    inner_ref,
    outer_ref,
    out_ref,
    first_low,
    output_low,
    inner_low,
    outer_low,
    stage,
    send,
    receive,
    local,
    *full,
):
    place = Place()
    refs = (query_ref, key_ref, value_ref, output_ref, inner_ref, outer_ref)
    loads = [
        pltpu.make_async_copy(ref, buffer, local.at[j])
        for j, (ref, buffer) in enumerate(zip(refs, full))
    ]
    for load in loads:
        load.start()
    place.greet()
    copies = []
    for k in range(1, SG):
        to = (place.seq + k) % SG
        copy = pltpu.make_async_remote_copy(
            src_ref=labels_ref.at[to],
            dst_ref=stage.at[place.seq],
            send_sem=send.at[k - 1],
            recv_sem=receive.at[k - 1],
            device_id=(to, place.dp),
            device_id_type=MESH,
        )
        copy.start()
        copies.append(copy)
    stage[place.seq] = labels_ref[place.seq]
    for j, load in enumerate(loads):
        load.wait()
        if j < 3:
            first_low[:, j * MODEL_WIDTH : (j + 1) * MODEL_WIDTH] = full[j][...].astype(BF16)
        else:
            (output_low, inner_low, outer_low)[j - 3][...] = full[j][...].astype(BF16)
    for copy in copies:
        copy.wait()
    out_ref[...] = stage[...]


def move_labels(labels, weights):
    inside = pl.BlockSpec(memory_space=pltpu.VMEM)
    part = weights[0].shape[0]
    shapes = [(part, 3 * MODEL_WIDTH), *[weight.shape for weight in weights[3:]]]
    return pl.pallas_call(
        labels_kernel,
        in_specs=[inside, *[pl.BlockSpec(memory_space=pl.ANY)] * 6],
        out_specs=[inside] * 5,
        out_shape=[
            jax.ShapeDtypeStruct(labels.shape, jnp.int32),
            *[jax.ShapeDtypeStruct(shape, BF16) for shape in shapes],
        ],
        scratch_shapes=[
            pltpu.VMEM(labels.shape, jnp.int32),
            pltpu.SemaphoreType.DMA((SG - 1,)),
            pltpu.SemaphoreType.DMA((SG - 1,)),
            pltpu.SemaphoreType.DMA((len(weights),)),
            *[pltpu.VMEM(weight.shape, F32) for weight in weights],
        ],
        compiler_params=pltpu.CompilerParams(
            collective_id=4, has_side_effects=True, vmem_limit_bytes=58 * 2**20
        ),
        name="labels",
    )(labels, *weights)


def angle_tables():
    half = HEAD_SIZE // 2
    rate = np.float32(-math.log(10000.0) / half)
    frequency = np.exp(np.arange(half, dtype=np.float32) * rate)
    angle = np.arange(LEN, dtype=np.float32)[:, None] * frequency[None, :]
    cos, sin = np.cos(angle), np.sin(angle)
    phase = np.concatenate([cos, sin, cos, sin], axis=1)
    cos, sin = cos[0::2], sin[0::2]
    return (
        jnp.asarray(phase).astype(BF16),
        np.concatenate([cos, -cos, cos, -cos], axis=1),
        np.concatenate([sin, sin, sin, sin], axis=1),
    )


def sequence_body(
    tokens,
    segments,
    token_types,
    cotangent,
    query_weight,
    key_weight,
    value_weight,
    output_weight,
    inner_weight,
    outer_weight,
    value_bias,
    output_bias,
    inner_bias,
    outer_bias,
    attention_norm_gain,
    first_shift,
    second_gain,
    second_shift,
    content_bias,
    position_bias,
    type_bias,
    relative_kernel,
    type_embed,
):
    owners = lax.axis_size("dp")
    part = MODEL_WIDTH // owners
    low = lambda value: value.astype(BF16)
    half = segments.shape[1] // 2
    labels = jnp.stack(
        [segments[:, :half], segments[:, half:], token_types[:, :half], token_types[:, half:]],
        axis=1,
    )
    labels, first, output_low, inner_low, outer_low = move_labels(
        labels,
        (query_weight, key_weight, value_weight, output_weight, inner_weight, outer_weight),
    )
    tokens, labels = lax.optimization_barrier((tokens, labels))
    rows = lax.all_to_all(tokens, "seq", split_axis=0, concat_axis=0, tiled=True)
    flat = lambda value: low(value).reshape(1, part)
    vectors = [
        flat(value)
        for value in (
            value_bias,
            output_bias,
            outer_bias,
            attention_norm_gain,
            first_shift,
            second_gain,
            second_shift,
            content_bias,
            position_bias,
            type_bias,
            type_embed[:, 0],
            type_embed[:, 1],
        )
    ]
    vectors.append(jnp.zeros((VECTORS - len(vectors), part), BF16))
    vectors = lax.all_gather(jnp.concatenate(vectors, axis=0), "dp", axis=1, tiled=True)
    vectors = vectors.astype(F32)
    inner_add = lax.all_gather(low(inner_bias).reshape(1, -1), "dp", axis=1, tiled=True)
    inner_add = inner_add.astype(F32)
    relative = low(relative_kernel).reshape(part, HEAD_SIZE)
    relative = lax.all_gather(relative, "dp", axis=0, tiled=True)
    first = lax.all_gather(first, "dp", axis=0, tiled=True)
    inner_low = lax.all_gather(inner_low, "dp", axis=0, tiled=True)
    output_low = lax.all_gather(output_low, "dp", axis=0, tiled=True)
    outer_low = lax.all_gather(outer_low, "dp", axis=0, tiled=True)


    segment_row = labels[:, 0:2].reshape(LEN)
    type_row = labels[:, 2:4].reshape(LEN)
    segment_pairs = segment_row.reshape(PQ, 2)
    query_segments = segment_pairs[:, 0]
    query_types = type_row.reshape(PQ, 2)[:, 0]
    pair_same = (segment_pairs[:, 0] == segment_pairs[:, 1]).reshape(SG, PQ // SG)

    first_doc, last_doc = segment_row[0], segment_row[LEN - 1]
    first_type = type_row[0]
    last_type = jnp.max(jnp.where(type_row == first_type, -1, type_row))

    def classes(values, start, end):
        return jnp.where(values == start, 0, jnp.where(values == end, 2, 1))[:, None]

    columns = jnp.arange(LANES, dtype=jnp.int32)[None, :]
    key_side = (
        (columns == classes(segment_row, first_doc, last_doc))
        | (columns == 3 + classes(type_row, first_type, last_type))
        | ((columns >= 6) & (columns < 9))
    ).astype(BF16)
    query_docs = classes(query_segments, first_doc, last_doc)
    query_side = jnp.where(
        columns < 3,
        jnp.where(columns == query_docs, 0.0, FAR),
        (columns == 3 + classes(query_types, first_type, last_type)).astype(F32),
    )
    phase, cosm, sinm = angle_tables()

    block = rows.shape[1]
    pooled_block = block // 2
    at = jnp.arange(block, dtype=jnp.int32)[None, None, :]
    want = 2 * jnp.arange(pooled_block, dtype=jnp.int32)[None, :, None]
    half = jnp.where(pair_same, 0.5, 1.0)[:, :, None]
    other_half = jnp.where(pair_same, 0.5, 0.0)[:, :, None]
    pool = jnp.where(at == want, half, jnp.where(at == want + 1, other_half, 0.0)).astype(BF16)

    pooled = jnp.einsum("cpt,ctd->cpd", pool, rows, preferred_element_type=F32)
    pooled = pooled.reshape(PQ, MODEL_WIDTH)
    pooled_low = low(pooled)
    token_rows = rows.reshape(LEN, MODEL_WIDTH)
    query = mm(pooled_low, first[:, :MODEL_WIDTH])
    value_add = vectors[0:1]
    pair_add = jnp.concatenate([jnp.zeros_like(value_add), value_add], axis=1)
    pairs = low(mm(token_rows, first[:, MODEL_WIDTH:]) + pair_add)
    mixture, join, upstream = attend_forward(
        query, pairs, relative, vectors, query_side, key_side, phase, cosm, sinm, cotangent
    )
    upstream = upstream.reshape(PQ, MODEL_WIDTH)

    (
        output,
        grad_mixture,
        grad_first,
        grad_outer_weight,
        grad_inner_weight,
        grad_output_weight,
        row_sums,
        grad_inner_bias,
    ) = mlp(
        mixture, pooled, upstream, output_low, inner_low, outer_low, vectors, inner_add
    )
    inner_rows = grad_inner_bias.reshape(owners, owners, part).transpose(1, 0, 2)
    mlp_sums = jnp.concatenate(
        [row_sums, inner_rows.reshape(owners, MODEL_WIDTH), jnp.zeros((4, MODEL_WIDTH), F32)],
        axis=0,
    )

    grad_query, grad_key, grad_value, small_grads, *pieces = attend_backward(
        join,
        pairs,
        query,
        mixture,
        grad_mixture,
        relative,
        vectors,
        query_side,
        key_side,
        phase,
        cosm,
        sinm,
        mlp_sums,
        (grad_outer_weight, grad_inner_weight, grad_output_weight),
    )
    grad_tokens, *owned = finish(
        grad_query,
        grad_key,
        grad_value,
        token_rows,
        pooled_low,
        grad_first,
        pool,
        first,
        small_grads,
        pieces[WHOLE:],
    )
    owned = [*pieces[:WHOLE], *owned]
    owned_outer = jnp.concatenate(owned[0:2], axis=0).astype(F32)
    owned_inner = jnp.concatenate(owned[2:4], axis=1).astype(F32)
    owned_output, small_owned, *squares = [value.astype(F32) for value in owned[4:]]
    squares.append(owned_output)
    columns = small_owned[:, HEAD_SIZE : HEAD_SIZE + 24].T
    vector = lambda j: columns[j]
    heads = HEAD_COUNT // owners
    return (
        output,
        grad_tokens,
        squares[0],
        squares[1],
        squares[2],
        squares[3],
        owned_inner,
        owned_outer,
        vector(0),
        vector(8),
        columns[16:20].reshape(FF // owners),
        vector(9),
        vector(10),
        vector(11),
        vector(12),
        vector(13),
        vector(1).reshape(heads, HEAD_SIZE),
        vector(2).reshape(heads, HEAD_SIZE),
        vector(3).reshape(heads, HEAD_SIZE),
        small_owned[:, :HEAD_SIZE].reshape(heads, HEAD_SIZE, HEAD_SIZE),
        columns[4:6].reshape(2, heads, HEAD_SIZE).transpose(1, 0, 2),
    )


def solution(mesh):
    whole = mesh.shape["seq"] == SG and mesh.shape["dp"] == 4
    return jax.shard_map(
        sequence_body if whole else body,
        mesh=mesh,
        in_specs=(
            P("dp", "seq", None),
            P("dp", "seq"),
            P("dp", "seq"),
            P("dp", "seq", None),
            P("dp", None),
            P("dp", None),
            P("dp", None),
            P("dp", None),
            P("dp", None),
            P("dp", None),
            P("dp"),
            P("dp"),
            P("dp"),
            P("dp"),
            P("dp"),
            P("dp"),
            P("dp"),
            P("dp"),
            P("dp", None),
            P("dp", None),
            P("dp", None),
            P("dp", None, None),
            P("dp", None, None),
        ),
        out_specs=(
            P("dp", "seq", None),
            P("dp", "seq", None),
            P("dp", None),
            P("dp", None),
            P("dp", None),
            P("dp", None),
            P("dp", None),
            P("dp", None),
            P("dp"),
            P("dp"),
            P("dp"),
            P("dp"),
            P("dp"),
            P("dp"),
            P("dp"),
            P("dp"),
            P("dp", None),
            P("dp", None),
            P("dp", None),
            P("dp", None, None),
            P("dp", None, None),
        ),
        check_vma=False,
    )
```

```python
from functools import partial
import math

import jax
import jax.numpy as jnp
import numpy as np
from jax import lax
from jax.experimental import pallas as pl
from jax.experimental.pallas import tpu as pltpu
from jax.sharding import PartitionSpec as P

MODEL_WIDTH = 768
HEAD_COUNT = 12
HEAD_SIZE = 64
LEN = 2048
SG = 8
PQ = 1024


highest = lax.Precision.HIGHEST
norm_eps = 1e-05
masked_score = -1e30


def frequencies():
    half_width = HEAD_SIZE // 2
    return jnp.exp(jnp.arange(half_width, dtype=jnp.float32) * (-math.log(10000.0) / half_width))


def norm_forward(inputs, gains, shifts):
    row_mean = jnp.mean(inputs, axis=-1, keepdims=True)
    centred = inputs - row_mean
    inverse = lax.rsqrt(jnp.mean(centred * centred, axis=-1, keepdims=True) + norm_eps)
    normed = centred * inverse
    return (normed * gains + shifts, normed, inverse)


def norm_backward(upstream, normed, inverse, gains):
    scaled = upstream * gains
    along = jnp.mean(scaled * normed, axis=-1, keepdims=True)
    centre = jnp.mean(scaled, axis=-1, keepdims=True)
    return inverse * (scaled - centre - normed * along)


def doc_masks(segment_row, type_row):
    same_document = segment_row[0::2][:, None] == segment_row[None, :]
    same_type = type_row[0::2][:, None] == type_row[None, :]
    return (same_document, same_type)


def score_block(query_row, type_row_terms, pair_row, key_phase, same_document, same_type):
    key_join = jnp.concatenate([pair_row[:, :HEAD_SIZE], key_phase], axis=-1)
    raw_score = lax.dot_general(
        query_row, key_join, (((1,), (1,)), ((), ())), preferred_element_type=jnp.float32
    )
    type_float = type_row_terms.astype(jnp.float32)
    raw_score = raw_score + jnp.where(same_type, type_float[:, 1:2], type_float[:, 0:1])
    return (jnp.where(same_document, raw_score * HEAD_SIZE ** (-0.5), masked_score), key_join)


def body(
    tokens,
    segments,
    token_types,
    cotangent,
    query_weight,
    key_weight,
    value_weight,
    output_weight,
    inner_weight,
    outer_weight,
    value_bias,
    output_bias,
    inner_bias,
    outer_bias,
    attention_norm_gain,
    first_shift,
    second_gain,
    second_shift,
    content_bias,
    position_bias,
    type_bias,
    relative_kernel,
    type_embed,
):
    local_tokens = tokens.shape[1]
    local_pooled = local_tokens // 2
    group_size = lax.axis_size("seq")
    shard_rank = lax.axis_index("seq")
    item_count = SG * HEAD_COUNT // group_size
    half_width = HEAD_SIZE // 2
    score_scale = HEAD_SIZE ** (-0.5)
    frequency = frequencies()
    duplicate_params = (
        lax.all_gather(query_weight.astype(jnp.bfloat16), "dp", axis=0, tiled=True),
        lax.all_gather(key_weight.astype(jnp.bfloat16), "dp", axis=0, tiled=True),
        lax.all_gather(value_weight.astype(jnp.bfloat16), "dp", axis=0, tiled=True),
        lax.all_gather(output_weight.astype(jnp.bfloat16), "dp", axis=0, tiled=True),
        lax.all_gather(inner_weight.astype(jnp.bfloat16), "dp", axis=0, tiled=True),
        lax.all_gather(outer_weight.astype(jnp.bfloat16), "dp", axis=0, tiled=True),
        lax.all_gather(value_bias.astype(jnp.bfloat16), "dp", axis=0, tiled=True),
        lax.all_gather(output_bias.astype(jnp.bfloat16), "dp", axis=0, tiled=True),
        lax.all_gather(inner_bias.astype(jnp.bfloat16), "dp", axis=0, tiled=True),
        lax.all_gather(outer_bias.astype(jnp.bfloat16), "dp", axis=0, tiled=True),
        lax.all_gather(attention_norm_gain.astype(jnp.bfloat16), "dp", axis=0, tiled=True),
        lax.all_gather(first_shift.astype(jnp.bfloat16), "dp", axis=0, tiled=True),
        lax.all_gather(second_gain.astype(jnp.bfloat16), "dp", axis=0, tiled=True),
        lax.all_gather(second_shift.astype(jnp.bfloat16), "dp", axis=0, tiled=True),
        lax.all_gather(content_bias.astype(jnp.bfloat16), "dp", axis=0, tiled=True),
        lax.all_gather(position_bias.astype(jnp.bfloat16), "dp", axis=0, tiled=True),
        lax.all_gather(type_bias.astype(jnp.bfloat16), "dp", axis=0, tiled=True),
        lax.all_gather(relative_kernel.astype(jnp.bfloat16), "dp", axis=0, tiled=True),
        lax.all_gather(type_embed.astype(jnp.bfloat16), "dp", axis=0, tiled=True),
    )
    value_add = duplicate_params[6].astype(jnp.float32)
    output_add = duplicate_params[7].astype(jnp.float32)
    inner_add = duplicate_params[8].astype(jnp.float32)
    outer_add = duplicate_params[9].astype(jnp.float32)
    gain_one = duplicate_params[10].astype(jnp.float32)
    shift_one = duplicate_params[11].astype(jnp.float32)
    gain_two = duplicate_params[12].astype(jnp.float32)
    shift_two = duplicate_params[13].astype(jnp.float32)
    content_add = duplicate_params[14].astype(jnp.float32)[None, :, None, :]
    position_add = duplicate_params[15].astype(jnp.float32)[None, :, None, :]
    type_add = duplicate_params[16].astype(jnp.float32)[None, :, None, :]
    relative = duplicate_params[17].astype(jnp.float32)
    type_table = duplicate_params[18].astype(jnp.float32)
    whole_segments, whole_types = (
        lax.all_gather(segments, "seq", axis=1, tiled=True),
        lax.all_gather(token_types, "seq", axis=1, tiled=True),
    )
    first_rows = tokens[:, 0::2].astype(jnp.float32)
    second = tokens[:, 1::2].astype(jnp.float32)
    pair_same = (segments[:, 0::2] == segments[:, 1::2])[..., None]
    pooled = jnp.where(pair_same, (first_rows + second) * 0.5, first_rows)
    pooled_low = pooled.astype(jnp.bfloat16)
    queries = jnp.einsum(
        "spd,dhe->shpe",
        pooled_low,
        duplicate_params[0].reshape(MODEL_WIDTH, HEAD_COUNT, HEAD_SIZE),
        preferred_element_type=jnp.float32,
    )
    key_rows = jnp.einsum(
        "ukf,fra->urka",
        tokens,
        duplicate_params[1].reshape(MODEL_WIDTH, HEAD_COUNT, HEAD_SIZE),
        preferred_element_type=jnp.float32,
    )
    value_rows = (
        jnp.einsum(
            "ukf,fra->urka",
            tokens,
            duplicate_params[2].reshape(MODEL_WIDTH, HEAD_COUNT, HEAD_SIZE),
            preferred_element_type=jnp.float32,
        )
        + value_add.reshape(HEAD_COUNT, HEAD_SIZE)[None, :, None, :]
    )
    pair_rows = (
        jnp.concatenate([key_rows, value_rows], axis=-1)
        .astype(jnp.bfloat16)
        .reshape(SG * HEAD_COUNT, local_tokens, 2 * HEAD_SIZE)
    )
    shifted = queries + position_add
    relative_terms = jnp.einsum("shpe,hef->shpf", shifted, relative, precision=highest)
    pooled_place = 2.0 * (
        shard_rank * local_pooled + jnp.arange(local_pooled, dtype=jnp.int32)
    ).astype(jnp.float32)
    query_angle = pooled_place[:, None] * frequency[None, :]
    query_cos = jnp.cos(query_angle)
    query_sin = jnp.sin(query_angle)
    relative_cos = relative_terms[..., :half_width]
    relative_sin = relative_terms[..., half_width:]
    position = jnp.concatenate(
        [
            relative_cos * query_cos + relative_sin * query_sin,
            relative_cos * query_sin - relative_sin * query_cos,
        ],
        axis=-1,
    )
    query_join = (
        jnp.concatenate([queries + content_add, position], axis=-1)
        .astype(jnp.bfloat16)
        .reshape(SG * HEAD_COUNT, local_pooled, 2 * HEAD_SIZE)
    )
    typed = queries + type_add
    type_terms = (
        jnp.einsum("shpe,hbe->shpb", typed, type_table, precision=highest)
        .astype(jnp.bfloat16)
        .reshape(SG * HEAD_COUNT, local_pooled, 2)
    )
    query_heads, type_heads, pair_heads = (
        lax.all_to_all(query_join, "seq", split_axis=0, concat_axis=1, tiled=True),
        lax.all_to_all(type_terms, "seq", split_axis=0, concat_axis=1, tiled=True),
        lax.all_to_all(pair_rows, "seq", split_axis=0, concat_axis=1, tiled=True),
    )
    item_rows = (shard_rank * item_count + jnp.arange(item_count, dtype=jnp.int32)) // HEAD_COUNT
    item_segments = whole_segments[item_rows]
    item_types = whole_types[item_rows]
    key_angle = jnp.arange(LEN, dtype=jnp.float32)[:, None] * frequency[None, :]
    key_phase = jnp.concatenate([jnp.cos(key_angle), jnp.sin(key_angle)], axis=-1).astype(
        jnp.bfloat16
    )

    def attend(packed):
        query_row, type_row_terms, pair_row, segment_row, type_row = packed
        same_document, same_type = doc_masks(segment_row, type_row)
        scores, key_join = score_block(
            query_row, type_row_terms, pair_row, key_phase, same_document, same_type
        )
        row_max = jnp.max(scores, axis=1, keepdims=True)
        exponent = jnp.exp(scores - row_max)
        row_total = jnp.sum(exponent, axis=1, keepdims=True)
        weights = exponent / row_total
        mixture = jnp.dot(
            weights.astype(jnp.bfloat16),
            pair_row[:, HEAD_SIZE:],
            preferred_element_type=jnp.float32,
        )
        return (mixture.astype(jnp.bfloat16), row_max + jnp.log(row_total))

    mixed_heads, log_totals = lax.map(
        attend, (query_heads, type_heads, pair_heads, item_segments, item_types)
    )
    mixed_tokens = lax.all_to_all(
        mixed_heads.reshape(item_count, PQ // 2, 2 * HEAD_SIZE),
        "seq",
        split_axis=1,
        concat_axis=0,
        tiled=True,
    ).reshape(SG, HEAD_COUNT, local_pooled, HEAD_SIZE)
    attention = (
        jnp.einsum(
            "shpe,hed->spd",
            mixed_tokens,
            duplicate_params[3].reshape(HEAD_COUNT, HEAD_SIZE, MODEL_WIDTH),
            preferred_element_type=jnp.float32,
        )
        + output_add
    )
    hidden, normed_one, inverse_one = norm_forward(pooled + attention, gain_one, shift_one)
    hidden_low = hidden.astype(jnp.bfloat16)
    expanded = (
        jnp.einsum(
            "spd,df->spf", hidden_low, duplicate_params[4], preferred_element_type=jnp.float32
        )
        + inner_add
    )
    active = jax.nn.gelu(expanded, approximate=True).astype(jnp.bfloat16)
    branch = (
        jnp.einsum("spf,fd->spd", active, duplicate_params[5], preferred_element_type=jnp.float32)
        + outer_add
    )
    result, normed_two, inverse_two = norm_forward(hidden + branch, gain_two, shift_two)
    output = result.astype(jnp.bfloat16)
    again = (
        lax.all_gather(query_weight.astype(jnp.bfloat16), "dp", axis=0, tiled=True),
        lax.all_gather(key_weight.astype(jnp.bfloat16), "dp", axis=0, tiled=True),
        lax.all_gather(value_weight.astype(jnp.bfloat16), "dp", axis=0, tiled=True),
        lax.all_gather(output_weight.astype(jnp.bfloat16), "dp", axis=0, tiled=True),
        lax.all_gather(inner_weight.astype(jnp.bfloat16), "dp", axis=0, tiled=True),
        lax.all_gather(outer_weight.astype(jnp.bfloat16), "dp", axis=0, tiled=True),
        lax.all_gather(attention_norm_gain.astype(jnp.bfloat16), "dp", axis=0, tiled=True),
        lax.all_gather(second_gain.astype(jnp.bfloat16), "dp", axis=0, tiled=True),
        lax.all_gather(relative_kernel.astype(jnp.bfloat16), "dp", axis=0, tiled=True),
        lax.all_gather(type_embed.astype(jnp.bfloat16), "dp", axis=0, tiled=True),
    )
    query_back = again[0]
    key_back = again[1]
    value_back = again[2]
    output_back = again[3]
    inner_back = again[4]
    outer_back = again[5]
    gain_one_back = again[6].astype(jnp.float32)
    gain_two_back = again[7].astype(jnp.float32)
    relative_back = again[8].astype(jnp.float32)
    table_back = again[9].astype(jnp.float32)
    grad_result = cotangent.astype(jnp.float32)
    grad_gain_two = jnp.sum(grad_result * normed_two, axis=(0, 1))
    grad_shift_two = jnp.sum(grad_result, axis=(0, 1))
    grad_second = norm_backward(grad_result, normed_two, inverse_two, gain_two_back)
    grad_branch = grad_second.astype(jnp.bfloat16)
    grad_outer_weight = jnp.einsum(
        "spf,spd->fd", active, grad_branch, preferred_element_type=jnp.float32
    )
    grad_outer_bias = jnp.sum(grad_branch.astype(jnp.float32), axis=(0, 1))
    grad_active = jnp.einsum(
        "spd,fd->spf", grad_branch, outer_back, preferred_element_type=jnp.float32
    )
    gelu_value, gelu_pull = jax.vjp(partial(jax.nn.gelu, approximate=True), expanded)
    grad_expanded = gelu_pull(grad_active)[0].astype(jnp.bfloat16)
    grad_inner_weight = jnp.einsum(
        "spd,spf->df", hidden_low, grad_expanded, preferred_element_type=jnp.float32
    )
    grad_inner_bias = jnp.sum(grad_expanded.astype(jnp.float32), axis=(0, 1))
    grad_hidden = grad_second + jnp.einsum(
        "spf,df->spd", grad_expanded, inner_back, preferred_element_type=jnp.float32
    )
    grad_gain_one = jnp.sum(grad_hidden * normed_one, axis=(0, 1))
    grad_shift_one = jnp.sum(grad_hidden, axis=(0, 1))
    grad_first = norm_backward(grad_hidden, normed_one, inverse_one, gain_one_back)
    grad_attention = grad_first.astype(jnp.bfloat16)
    grad_output_weight = jnp.einsum(
        "shpe,spd->hed", mixed_tokens, grad_attention, preferred_element_type=jnp.float32
    ).reshape(MODEL_WIDTH, MODEL_WIDTH)
    grad_output_bias = jnp.sum(grad_attention.astype(jnp.float32), axis=(0, 1))
    grad_mixture = jnp.einsum(
        "spd,hed->shpe",
        grad_attention,
        output_back.reshape(HEAD_COUNT, HEAD_SIZE, MODEL_WIDTH),
        preferred_element_type=jnp.float32,
    ).astype(jnp.bfloat16)
    grad_mixed_heads = lax.all_to_all(
        grad_mixture.reshape(SG * HEAD_COUNT, local_pooled // 2, 2 * HEAD_SIZE),
        "seq",
        split_axis=0,
        concat_axis=1,
        tiled=True,
    ).reshape(item_count, PQ, HEAD_SIZE)

    def attend_back(packed):
        query_row, type_row_terms, pair_row, segment_row, type_row, log_row, grad_row = packed
        same_document, same_type = doc_masks(segment_row, type_row)
        scores, key_join = score_block(
            query_row, type_row_terms, pair_row, key_phase, same_document, same_type
        )
        weights = jnp.exp(scores - log_row)
        grad_weights = lax.dot_general(
            grad_row,
            pair_row[:, HEAD_SIZE:],
            (((1,), (1,)), ((), ())),
            preferred_element_type=jnp.float32,
        )
        row_dot = jnp.sum(grad_weights * weights, axis=1, keepdims=True)
        grad_scores = (weights * (grad_weights - row_dot)).astype(jnp.bfloat16)
        grad_query = (
            jnp.dot(grad_scores, key_join, preferred_element_type=jnp.float32) * score_scale
        ).astype(jnp.bfloat16)
        grad_float = grad_scores.astype(jnp.float32) * score_scale
        grad_same = jnp.sum(jnp.where(same_type, grad_float, 0.0), axis=1)
        grad_other = jnp.sum(jnp.where(same_type, 0.0, grad_float), axis=1)
        grad_kinds = jnp.stack([grad_other, grad_same], axis=-1).astype(jnp.bfloat16)
        grad_keys = (
            lax.dot_general(
                grad_scores,
                query_row[:, :HEAD_SIZE],
                (((0,), (0,)), ((), ())),
                preferred_element_type=jnp.float32,
            )
            * score_scale
        )
        grad_values = lax.dot_general(
            weights.astype(jnp.bfloat16),
            grad_row,
            (((0,), (0,)), ((), ())),
            preferred_element_type=jnp.float32,
        )
        return (
            grad_query,
            grad_kinds,
            jnp.concatenate([grad_keys, grad_values], axis=-1).astype(jnp.bfloat16),
        )

    grad_query_heads, grad_type_heads, grad_pair_heads = lax.map(
        attend_back,
        (
            query_heads,
            type_heads,
            pair_heads,
            item_segments,
            item_types,
            log_totals,
            grad_mixed_heads,
        ),
    )
    grad_query_tok, grad_type_tok, grad_pair_tok = (
        lax.all_to_all(grad_query_heads, "seq", split_axis=1, concat_axis=0, tiled=True),
        lax.all_to_all(grad_type_heads, "seq", split_axis=1, concat_axis=0, tiled=True),
        lax.all_to_all(grad_pair_heads, "seq", split_axis=1, concat_axis=0, tiled=True),
    )
    grad_query_join = grad_query_tok.astype(jnp.float32).reshape(
        SG, HEAD_COUNT, local_pooled, 2 * HEAD_SIZE
    )
    grad_content = grad_query_join[..., :HEAD_SIZE]
    grad_first_half = grad_query_join[..., HEAD_SIZE : HEAD_SIZE + half_width]
    grad_second_half = grad_query_join[..., HEAD_SIZE + half_width :]
    grad_relative_terms = jnp.concatenate(
        [
            grad_first_half * query_cos + grad_second_half * query_sin,
            grad_first_half * query_sin - grad_second_half * query_cos,
        ],
        axis=-1,
    )
    grad_shifted = jnp.einsum(
        "shpf,hef->shpe", grad_relative_terms, relative_back, precision=highest
    )
    grad_relative_kernel = jnp.einsum(
        "shpe,shpf->hef", shifted, grad_relative_terms, precision=highest
    )
    grad_type_terms = grad_type_tok.astype(jnp.float32).reshape(SG, HEAD_COUNT, local_pooled, 2)
    grad_typed = jnp.einsum("shpb,hbe->shpe", grad_type_terms, table_back, precision=highest)
    grad_type_embed = jnp.einsum("shpe,shpb->hbe", typed, grad_type_terms, precision=highest)
    query_rows_gradient = (grad_content + grad_shifted + grad_typed).astype(jnp.bfloat16)
    grad_content_bias = jnp.sum(grad_content, axis=(0, 2))
    grad_position_bias = jnp.sum(grad_shifted, axis=(0, 2))
    grad_type_bias = jnp.sum(grad_typed, axis=(0, 2))
    grad_query_weight = jnp.einsum(
        "spd,shpe->dhe", pooled_low, query_rows_gradient, preferred_element_type=jnp.float32
    ).reshape(MODEL_WIDTH, MODEL_WIDTH)
    grad_pooled = grad_first + jnp.einsum(
        "shpe,dhe->spd",
        query_rows_gradient,
        query_back.reshape(MODEL_WIDTH, HEAD_COUNT, HEAD_SIZE),
        preferred_element_type=jnp.float32,
    )
    grad_pairs = grad_pair_tok.reshape(SG, HEAD_COUNT, local_tokens, 2 * HEAD_SIZE)
    key_rows_gradient = grad_pairs[..., :HEAD_SIZE]
    value_rows_gradient = grad_pairs[..., HEAD_SIZE:]
    grad_key_weight = jnp.einsum(
        "ozb,opzx->bpx", tokens, key_rows_gradient, preferred_element_type=jnp.float32
    ).reshape(MODEL_WIDTH, MODEL_WIDTH)
    grad_value_weight = jnp.einsum(
        "ozb,opzx->bpx", tokens, value_rows_gradient, preferred_element_type=jnp.float32
    ).reshape(MODEL_WIDTH, MODEL_WIDTH)
    grad_value_bias = jnp.sum(value_rows_gradient.astype(jnp.float32), axis=(0, 2)).reshape(
        MODEL_WIDTH
    )
    grad_direct = jnp.einsum(
        "mivt,git->mvg",
        key_rows_gradient,
        key_back.reshape(MODEL_WIDTH, HEAD_COUNT, HEAD_SIZE),
        preferred_element_type=jnp.float32,
    )
    grad_direct = grad_direct + jnp.einsum(
        "mivt,git->mvg",
        value_rows_gradient,
        value_back.reshape(MODEL_WIDTH, HEAD_COUNT, HEAD_SIZE),
        preferred_element_type=jnp.float32,
    )
    pool_first = jnp.where(pair_same, 0.5 * grad_pooled, grad_pooled)
    pool_second = jnp.where(pair_same, 0.5 * grad_pooled, 0.0)
    grad_tokens = (
        grad_direct
        + jnp.stack([pool_first, pool_second], axis=2).reshape(SG, local_tokens, MODEL_WIDTH)
    ).astype(jnp.bfloat16)
    summed = lax.psum(
        (
            grad_query_weight,
            grad_key_weight,
            grad_value_weight,
            grad_output_weight,
            grad_inner_weight,
            grad_outer_weight,
            grad_value_bias,
            grad_output_bias,
            grad_inner_bias,
            grad_outer_bias,
            grad_gain_one,
            grad_shift_one,
            grad_gain_two,
            grad_shift_two,
            grad_content_bias,
            grad_position_bias,
            grad_type_bias,
            grad_relative_kernel,
            grad_type_embed,
        ),
        "seq",
    )
    owned = (
        lax.psum_scatter(
            summed[0].astype(jnp.bfloat16), "dp", scatter_dimension=0, tiled=True
        ).astype(jnp.float32),
        lax.psum_scatter(
            summed[1].astype(jnp.bfloat16), "dp", scatter_dimension=0, tiled=True
        ).astype(jnp.float32),
        lax.psum_scatter(
            summed[2].astype(jnp.bfloat16), "dp", scatter_dimension=0, tiled=True
        ).astype(jnp.float32),
        lax.psum_scatter(
            summed[3].astype(jnp.bfloat16), "dp", scatter_dimension=0, tiled=True
        ).astype(jnp.float32),
        lax.psum_scatter(
            summed[4].astype(jnp.bfloat16), "dp", scatter_dimension=0, tiled=True
        ).astype(jnp.float32),
        lax.psum_scatter(
            summed[5].astype(jnp.bfloat16), "dp", scatter_dimension=0, tiled=True
        ).astype(jnp.float32),
        lax.psum_scatter(
            summed[6].astype(jnp.bfloat16), "dp", scatter_dimension=0, tiled=True
        ).astype(jnp.float32),
        lax.psum_scatter(
            summed[7].astype(jnp.bfloat16), "dp", scatter_dimension=0, tiled=True
        ).astype(jnp.float32),
        lax.psum_scatter(
            summed[8].astype(jnp.bfloat16), "dp", scatter_dimension=0, tiled=True
        ).astype(jnp.float32),
        lax.psum_scatter(
            summed[9].astype(jnp.bfloat16), "dp", scatter_dimension=0, tiled=True
        ).astype(jnp.float32),
        lax.psum_scatter(
            summed[10].astype(jnp.bfloat16), "dp", scatter_dimension=0, tiled=True
        ).astype(jnp.float32),
        lax.psum_scatter(
            summed[11].astype(jnp.bfloat16), "dp", scatter_dimension=0, tiled=True
        ).astype(jnp.float32),
        lax.psum_scatter(
            summed[12].astype(jnp.bfloat16), "dp", scatter_dimension=0, tiled=True
        ).astype(jnp.float32),
        lax.psum_scatter(
            summed[13].astype(jnp.bfloat16), "dp", scatter_dimension=0, tiled=True
        ).astype(jnp.float32),
        lax.psum_scatter(
            summed[14].astype(jnp.bfloat16), "dp", scatter_dimension=0, tiled=True
        ).astype(jnp.float32),
        lax.psum_scatter(
            summed[15].astype(jnp.bfloat16), "dp", scatter_dimension=0, tiled=True
        ).astype(jnp.float32),
        lax.psum_scatter(
            summed[16].astype(jnp.bfloat16), "dp", scatter_dimension=0, tiled=True
        ).astype(jnp.float32),
        lax.psum_scatter(
            summed[17].astype(jnp.bfloat16), "dp", scatter_dimension=0, tiled=True
        ).astype(jnp.float32),
        lax.psum_scatter(
            summed[18].astype(jnp.bfloat16), "dp", scatter_dimension=0, tiled=True
        ).astype(jnp.float32),
    )
    return (
        output,
        grad_tokens,
        owned[0],
        owned[1],
        owned[2],
        owned[3],
        owned[4],
        owned[5],
        owned[6],
        owned[7],
        owned[8],
        owned[9],
        owned[10],
        owned[11],
        owned[12],
        owned[13],
        owned[14],
        owned[15],
        owned[16],
        owned[17],
        owned[18],
    )


BF16 = jnp.bfloat16
F32 = jnp.float32
PAIRS = HEAD_COUNT // 2
LANES = 2 * HEAD_SIZE
ROWS = 256
FAR = -(2.0**100)
FF = 3072
NN = (((1,), (0,)), ((), ()))
NT = (((1,), (1,)), ((), ()))
TN = (((0,), (0,)), ((), ()))


def mm(left, right, dims=NN):
    return lax.dot_general(left, right, dims, preferred_element_type=F32)


def split(value):
    high = value.astype(BF16)
    return high, (value - high.astype(F32)).astype(BF16)


def lane_ids(rows):
    return lax.broadcasted_iota(jnp.int32, (rows, LANES), 1)


VECTORS = 16


def pair_maps(relative):
    row = lax.broadcasted_iota(jnp.int32, (HEAD_SIZE, LANES), 0)
    twice = (lane_ids(HEAD_SIZE) % HEAD_SIZE == row).astype(BF16)
    lane = lane_ids(LANES)
    row = lax.broadcasted_iota(jnp.int32, (LANES, LANES), 0)
    crossed = (row < HEAD_SIZE) != (lane < HEAD_SIZE)
    plain = jnp.where(crossed, mm(relative, twice), 0.0).astype(BF16)
    half = HEAD_SIZE // 2
    partner = jnp.where(lane % HEAD_SIZE < half, lane + half, lane - half)
    swapped = mm(plain, (row == partner).astype(BF16)).astype(BF16)
    return plain, swapped


def fold_maps(grads):
    row = lax.broadcasted_iota(jnp.int32, (LANES, 2 * LANES), 0)
    lane = lax.broadcasted_iota(jnp.int32, (LANES, 2 * LANES), 1)
    crossed = (row < HEAD_SIZE) != (lane % LANES < HEAD_SIZE)
    high, low = split(jnp.where(crossed, grads, 0.0))
    row = lax.broadcasted_iota(jnp.int32, (2 * LANES, LANES), 0)
    lane = lax.broadcasted_iota(jnp.int32, (2 * LANES, LANES), 1)
    half = HEAD_SIZE // 2
    at = row % HEAD_SIZE
    partner = jnp.where(at < half, at + half, at - half)
    fold = (jnp.where(row < LANES, at, partner) == lane).astype(BF16)
    return mm(high, fold) + mm(low, fold)


def kind_maps(vectors):
    row = lax.broadcasted_iota(jnp.int32, (VECTORS, 4 * LANES), 0)
    column = lax.broadcasted_iota(jnp.int32, (VECTORS, 4 * LANES), 1)
    lane = column % LANES
    wanted = (lane >= 3) & (lane < 6) & (row == 11 - (column // LANES) % 2)
    both = mm(vectors.astype(BF16), wanted.astype(BF16), TN)
    row = lax.broadcasted_iota(jnp.int32, (LANES, 4 * LANES), 0)
    column = lax.broadcasted_iota(jnp.int32, (LANES, 4 * LANES), 1)
    return jnp.where((row < HEAD_SIZE) == (column < 2 * LANES), both, 0.0).astype(BF16)


MESH = pl.DeviceIdType.MESH
SUM_ROWS = 48
STAGES = ("core", "y", "x", "near", "far", "far_back", "near_back", "x_back")


class Place:
    def __init__(self):
        self.seq, self.dp = lax.axis_index("seq"), lax.axis_index("dp")
        self.core, self.y = self.dp % 2, self.dp // 2
        self.x, self.near, self.far = self.seq % 2, (self.seq // 2) % 2, self.seq // 4
        self.partner = {
            "core": (self.seq, self.dp + 1 - 2 * self.core),
            "y": (self.seq, self.dp + 2 - 4 * self.y),
            "x": (self.seq + 1 - 2 * self.x, self.dp),
            "near": (self.seq + 2 - 4 * self.near, self.dp),
            "far": (self.seq + 4 - 8 * self.far, self.dp),
        }

    def peers(self):
        return [((self.seq + k) % SG, self.dp) for k in range(1, SG)]

    def greet(self):
        barrier = pltpu.get_barrier_semaphore()
        others = [self.partner["core"], self.partner["y"], *self.peers()]
        for device in others:
            pl.semaphore_signal(barrier, inc=1, device_id=device, device_id_type=MESH)
        pl.semaphore_wait(barrier, len(others))


def add_rows(target, addend, rows):
    def step(i, carry):
        at = pl.ds(pl.multiple_of(i * SUM_ROWS, 16), SUM_ROWS)
        left, right = target(at), addend(at)
        left[...] = left[...] + right[...]
        return carry

    lax.fori_loop(0, rows // SUM_ROWS, step, 0)


class Chunk:
    def __init__(self, place, index, source, rows, columns, buffers, send, receive, local):
        self.place, self.source, self.rows, self.columns = place, source, rows, columns
        self.own, self.from_core, self.from_y, self.from_x, self.from_near, self.from_far, self.full = buffers
        self.send_at = lambda stage, k=0: send.at[index, STAGES.index(stage) + (8 if k else 0)]
        self.receive_at = lambda stage, k=0: receive.at[index, STAGES.index(stage) + (8 if k else 0)]
        self.local = lambda k: local.at[index, k]
        half, quarter = rows // 2, rows // 4
        self.my_columns = pl.ds(pl.multiple_of(place.x * (columns // 2), 128), columns // 2)
        self.other_columns = pl.ds(
            pl.multiple_of((1 - place.x) * (columns // 2), 128), columns // 2
        )
        self.my_half = pl.multiple_of(place.near * half, 16)
        self.my_quarter = pl.multiple_of(place.near * half + place.far * quarter, 16)

    def remote(self, stage, source, target, k=0):
        return pltpu.make_async_remote_copy(
            src_ref=source,
            dst_ref=target,
            send_sem=self.send_at(stage, k),
            recv_sem=self.receive_at(stage, k),
            device_id=self.place.partner[stage.split("_")[0]],
            device_id_type=MESH,
        )

    def locals(self):
        if self.own is None:
            return []
        return [
            pltpu.make_async_copy(
                self.source(2 * k + self.place.core), self.own.at[k], self.local(k)
            )
            for k in range(2)
        ]

    def copies(self, stage):
        place, rows = self.place, self.rows
        half, quarter = rows // 2, rows // 4
        if stage == "core":
            return [
                self.remote(
                    stage, self.source(2 * k + 1 - place.core), self.from_core.at[k], k
                )
                for k in range(2)
            ]
        if stage == "y":
            return [self.remote(stage, self.from_core.at[1 - place.y], self.from_y)]
        if stage == "x":
            return [self.remote(stage, self.from_y.at[:, self.other_columns], self.from_x)]
        if stage == "near":
            other = pl.ds(pl.multiple_of((1 - place.near) * half, 16), half)
            return [self.remote(stage, self.from_x.at[other, :], self.from_near)]
        if stage == "far":
            other = pl.ds(pl.multiple_of((1 - place.far) * quarter, 16), quarter)
            return [self.remote(stage, self.from_near.at[other, :], self.from_far)]
        if stage == "far_back":
            mine = self.full.at[pl.ds(self.my_quarter, quarter), self.my_columns]
            return [self.remote(stage, self.from_far, mine)]
        if stage == "near_back":
            mine = self.full.at[pl.ds(self.my_half, half), self.my_columns]
            return [self.remote(stage, mine, mine)]
        mine = self.full.at[:, self.my_columns]
        return [self.remote(stage, mine, mine)]

    def start(self, stage):
        if stage == "core":
            for copy in self.locals():
                copy.start()
        for copy in self.copies(stage):
            copy.start()

    def finish(self, stage):
        place, rows = self.place, self.rows
        half, quarter = rows // 2, rows // 4
        for copy in self.copies(stage):
            copy.wait_recv()
        if stage == "core":
            for copy in self.locals():
                copy.wait()
            for k in range(2):
                kept = (
                    self.source(2 * k + place.core) if self.own is None else self.own.at[k]
                )
                add_rows(
                    lambda at: self.from_core.at[k, at, :], lambda at: kept.at[at, :], rows
                )
        elif stage == "y":
            add_rows(
                lambda at: self.from_y.at[at, :],
                lambda at: self.from_core.at[place.y, at, :],
                rows,
            )
        elif stage == "x":
            add_rows(
                lambda at: self.from_x.at[at, :],
                lambda at: self.from_y.at[at, self.my_columns],
                rows,
            )
        elif stage == "near":
            add_rows(
                lambda at: self.from_near.at[at, :],
                lambda at: self.from_x.at[
                    pl.ds(pl.multiple_of(at.start + self.my_half, 16), SUM_ROWS), :
                ],
                half,
            )
        elif stage == "far":
            begin = place.far * quarter
            add_rows(
                lambda at: self.from_far.at[at, :],
                lambda at: self.from_near.at[
                    pl.ds(pl.multiple_of(at.start + begin, 16), SUM_ROWS), :
                ],
                quarter,
            )

    def place_piece(self):
        def step(i, carry):
            at = pl.ds(pl.multiple_of(i * SUM_ROWS, 16), SUM_ROWS)
            to = pl.ds(pl.multiple_of(i * SUM_ROWS + self.my_quarter, 16), SUM_ROWS)
            self.full[to, self.my_columns] = self.from_far[at, :]
            return carry

        lax.fori_loop(0, self.rows // 4 // SUM_ROWS, step, 0)

    def step(self, stage):
        at = STAGES.index(stage)
        if at > 0:
            self.finish(STAGES[at - 1])
        if stage == "far_back":
            self.place_piece()
        self.start(stage)

    def close(self, stages):
        for stage in stages:
            for copy in self.copies(stage):
                copy.wait_send()


DOWN, UP = STAGES[:5], STAGES[5:]
WHOLE = 3


def down_buffers(rows, columns, own):
    buffer = lambda *shape: pltpu.VMEM(shape, BF16)
    return [
        *([buffer(2, rows, columns)] if own else []),
        buffer(2, rows, columns),
        buffer(rows, columns),
        buffer(rows, columns // 2),
        buffer(rows // 2, columns // 2),
        buffer(rows // 4, columns // 2),
    ]


def grad_chunks():
    quarter = MODEL_WIDTH // 4
    half = MODEL_WIDTH // 2
    early = [
        (0, MODEL_WIDTH, 0, 0, half, MODEL_WIDTH),
        (0, MODEL_WIDTH, half, 0, half, MODEL_WIDTH),
        (1, quarter, 0, 0, quarter, FF // 2),
        (1, quarter, 0, FF // 2, quarter, FF // 2),
        (2, quarter, 0, 0, quarter, MODEL_WIDTH),
    ]
    late = [(j, quarter, 0, 0, quarter, MODEL_WIDTH) for j in (3, 4, 5)]
    late.insert(0, (6, quarter, 0, 0, quarter, 2 * LANES))
    return early, late


def chunk_source(grad, chunk):
    _, owner_rows, row, column, rows, columns = chunk

    def source(owner):
        begin = pl.multiple_of(owner * owner_rows + row, 16)
        return grad.at[pl.ds(begin, rows), pl.ds(column, columns)]

    return source


SEND_ORDER = (4, 3, 5, 2, 6, 1, 7, 0)


def finish_kernel(
    grad_query_ref,
    grad_key_ref,
    grad_value_ref,
    tokens_ref,
    pooled_ref,
    grad_first_ref,
    pool_ref,
    weights_ref,
    small_ref,
    *refs,
):
    early, late = grad_chunks()
    early = early[WHOLE:]
    pieces, refs = refs[: len(early)], refs[len(early) :]
    tokens_out, refs = refs[0], refs[1:]
    count = len(early) + len(late)
    outs, refs = refs[:count], refs[count:]
    fulls, refs = refs[:count], refs[count:]
    buffers, refs = refs[: 5 * len(late)], refs[5 * len(late) :]
    (
        tokens_stage,
        late_grads,
        send,
        receive,
        token_send,
        token_receive,
        token_local,
    ) = refs
    place = Place()
    place.greet()
    first = []
    for i, chunk in enumerate(early):
        kept = [None, None, None, None, None, pieces[i], fulls[i]]
        first.append(Chunk(place, i, None, *chunk[4:], kept, send, receive, None))
    second = []
    for j, chunk in enumerate(late):
        i = len(early) + j
        kept = [None, *buffers[5 * j : 5 * j + 5], fulls[i]]
        source = chunk_source(late_grads.at[j - 1] if j else small_ref, chunk)
        second.append(Chunk(place, i, source, *chunk[4:], kept, send, receive, None))
    for item in first:
        item.place_piece()
        item.start("far_back")
    second[0].start("core")

    moved = []

    def send_tokens(k):
        to = (place.seq + k) % SG
        block = LEN // SG
        rows = pl.ds(pl.multiple_of(to * block, block), block)
        pooled_rows = pl.ds(pl.multiple_of(to * (block // 2), block // 2), block // 2)
        weight = lambda j: weights_ref[:, j * MODEL_WIDTH : (j + 1) * MODEL_WIDTH]
        grad_pooled = grad_first_ref[pooled_rows, :] + mm(
            grad_query_ref[pooled_rows, :], weight(0), NT
        )
        high, low = split(grad_pooled)
        total = mm(grad_key_ref[rows, :], weight(1), NT)
        total += mm(grad_value_ref[rows, :], weight(2), NT)
        total += mm(pool_ref[to], high, TN) + mm(pool_ref[to], low, TN)
        tokens_stage[to] = total.astype(BF16)
        if k == 0:
            copy = pltpu.make_async_copy(
                tokens_stage.at[to], tokens_out.at[place.seq], token_local
            )
        else:
            copy = pltpu.make_async_remote_copy(
                src_ref=tokens_stage.at[to],
                dst_ref=tokens_out.at[place.seq],
                send_sem=token_send.at[k - 1],
                recv_sem=token_receive.at[k - 1],
                device_id=(to, place.dp),
                device_id_type=MESH,
            )
        copy.start()
        moved.append(copy)

    for k in SEND_ORDER[:3]:
        send_tokens(k)
    for item in first:
        item.step("near_back")
    for k in SEND_ORDER[3:6]:
        send_tokens(k)
    for item in first:
        item.step("x_back")
    for k in SEND_ORDER[6:]:
        send_tokens(k)

    operands = [
        (pooled_ref, grad_query_ref),
        (tokens_ref, grad_key_ref),
        (tokens_ref, grad_value_ref),
    ]
    for j, (left, right) in enumerate(operands):
        for r in range(0, MODEL_WIDTH, 256):
            late_grads[j, r : r + 256, :] = mm(left[:, r : r + 256], right[...], TN).astype(BF16)
        second[j + 1].start("core")
        second[j].step("y")
    second[len(late) - 1].step("y")
    for stage in STAGES[2:]:
        for item in second:
            item.step(stage)

    for item, out in zip(first, outs):
        item.finish(STAGES[-1])
        out[...] = item.full[...]
        item.close(UP)
    for item, out in zip(second, outs[len(first) :]):
        item.finish(STAGES[-1])
        out[...] = item.full[...]
        item.close(STAGES)
    for copy in moved:
        copy.wait()


def finish(
    grad_query, grad_key, grad_value, tokens, pooled, grad_first, pool, weights, small, pieces
):
    anywhere = pl.BlockSpec(memory_space=pl.ANY)
    early, late = grad_chunks()
    early = early[WHOLE:]
    chunks = early + late
    count = len(chunks)
    inside = pl.BlockSpec(memory_space=pltpu.VMEM)
    out_tokens = (SG, LEN // SG, MODEL_WIDTH)
    return pl.pallas_call(
        finish_kernel,
        in_specs=[inside] * (9 + len(early)),
        out_specs=[anywhere, *[inside] * count],
        out_shape=[
            jax.ShapeDtypeStruct(out_tokens, BF16),
            *[jax.ShapeDtypeStruct(chunk[4:], BF16) for chunk in chunks],
        ],
        scratch_shapes=[
            *[pltpu.VMEM(chunk[4:], BF16) for chunk in chunks],
            *[buffer for chunk in late for buffer in down_buffers(*chunk[4:], False)],
            pltpu.VMEM(out_tokens, BF16),
            pltpu.VMEM((3, MODEL_WIDTH, MODEL_WIDTH), BF16),
            pltpu.SemaphoreType.DMA((count, 16)),
            pltpu.SemaphoreType.DMA((count, 16)),
            pltpu.SemaphoreType.DMA((SG - 1,)),
            pltpu.SemaphoreType.DMA((SG - 1,)),
            pltpu.SemaphoreType.DMA,
        ],
        compiler_params=pltpu.CompilerParams(
            collective_id=3, has_side_effects=True, vmem_limit_bytes=58 * 2**20
        ),
        name="finish",
    )(
        grad_query,
        grad_key,
        grad_value,
        tokens,
        pooled,
        grad_first,
        pool,
        weights,
        small,
        *pieces,
    )


def attend_kernel(
    query_ref,
    key_ref,
    value_ref,
    relative_ref,
    vectors_ref,
    query_side_ref,
    key_side_ref,
    phase_ref,
    cos_ref,
    sin_ref,
    cotangent_ref,
    mixture_ref,
    join_ref,
    upstream_ref,
    key_join,
    value_join,
    send,
    receive,
    local,
):
    place = Place()

    def upstream_copies():
        copies = [
            pltpu.make_async_copy(
                cotangent_ref.at[place.seq], upstream_ref.at[place.seq], local
            )
        ]
        for k in range(1, SG):
            to = (place.seq + k) % SG
            copies.append(
                pltpu.make_async_remote_copy(
                    src_ref=cotangent_ref.at[to],
                    dst_ref=upstream_ref.at[place.seq],
                    send_sem=send.at[k - 1],
                    recv_sem=receive.at[k - 1],
                    device_id=(to, place.dp),
                    device_id_type=MESH,
                )
            )
        return copies

    @pl.when(pl.program_id(0) == 0)
    def _():
        place.greet()
        for copy in upstream_copies():
            copy.start()

    query = query_ref[...]
    high, low = split(query)
    plain, swapped = pair_maps(relative_ref[...])
    kinds = kind_maps(vectors_ref[...])
    maps = jnp.concatenate([plain, swapped, kinds], axis=1)
    position_add, type_add = vectors_ref[8:9, :].astype(BF16), vectors_ref[9:10, :].astype(BF16)
    map_add = jnp.concatenate(
        [mm(position_add, plain), mm(position_add, swapped), mm(type_add, kinds)], axis=1
    )
    terms = mm(jnp.concatenate([high, low], axis=1), jnp.concatenate([maps, maps], axis=0))
    terms = terms + map_add
    lane = lane_ids(PQ)
    left = lane < HEAD_SIZE
    content = query + vectors_ref[7:8, :]
    position = terms[:, :LANES] * cos_ref[...] + terms[:, LANES : 2 * LANES] * sin_ref[...]
    side = query_side_ref[...]
    typed = (lane >= 3) & (lane < 6)
    scale = HEAD_SIZE ** (-0.5)
    for h in range(2):
        first, second = (content, position) if h == 0 else (position, content)
        join_ref[h, :, :LANES] = (jnp.where(left, first, second) * scale).astype(BF16)
        base = 2 * LANES * (h + 1)
        same = terms[:, base : base + LANES]
        other = terms[:, base + LANES : base + 2 * LANES]
        kind = jnp.where(side > 0.5, same, other) * scale
        join_ref[h, :, LANES:] = jnp.where(typed, kind, side).astype(BF16)
    key_left = lane_ids(LEN) < HEAD_SIZE
    key_join[:, LANES:] = key_side_ref[...]
    value_join[:, :LANES] = value_ref[...]
    value_join[:, LANES:] = key_side_ref[...]
    tile_lane = lane_ids(ROWS)
    for h in range(2):
        pieces = (key_ref[...], phase_ref[...]) if h == 0 else (phase_ref[...], key_ref[...])
        key_join[:, :LANES] = jnp.where(key_left, *pieces)
        for i in range(PQ // ROWS):
            rows = slice(i * ROWS, (i + 1) * ROWS)
            scores = mm(join_ref[h, rows, :], key_join[...], NT)
            top = jnp.max(scores, axis=1, keepdims=True)
            weights = jnp.exp(scores - top).astype(BF16)
            mixed = mm(weights, value_join[...])
            total = mixed[:, LANES + 6 : LANES + 7]
            result = (mixed[:, :LANES] / total).astype(BF16)
            if h == 0:
                mixture_ref[rows, :] = result
            else:
                mixture_ref[rows, :] = jnp.where(
                    tile_lane < HEAD_SIZE, mixture_ref[rows, :], result
                )
            shift = -(top + jnp.log(total))
            one = shift.astype(BF16).astype(F32)
            two = (shift - one).astype(BF16).astype(F32)
            three = shift - one - two
            extra = jnp.where(tile_lane == 6, one, jnp.where(tile_lane == 7, two, three))
            kept = join_ref[h, rows, LANES:].astype(F32)
            inside = (tile_lane >= 6) & (tile_lane < 9)
            join_ref[h, rows, LANES:] = jnp.where(inside, extra, kept).astype(BF16)

    @pl.when(pl.program_id(0) == PAIRS - 1)
    def _():
        for copy in upstream_copies():
            copy.wait()


def attend_forward(
    query, pairs, relative, vectors, query_side, key_side, phase, cosm, sinm, cotangent
):
    whole = lambda shape: pl.BlockSpec(shape, lambda i: (0, 0))
    return pl.pallas_call(
        attend_kernel,
        grid=(PAIRS,),
        in_specs=[
            pl.BlockSpec((PQ, LANES), lambda i: (0, i)),
            pl.BlockSpec((LEN, LANES), lambda i: (0, i)),
            pl.BlockSpec((LEN, LANES), lambda i: (0, i + PAIRS)),
            pl.BlockSpec((LANES, HEAD_SIZE), lambda i: (i, 0)),
            pl.BlockSpec((VECTORS, LANES), lambda i: (0, i)),
            whole((PQ, LANES)),
            whole((LEN, LANES)),
            whole((LEN, LANES)),
            whole((PQ, LANES)),
            whole((PQ, LANES)),
            pl.BlockSpec(memory_space=pl.ANY),
        ],
        out_specs=[
            pl.BlockSpec((PQ, LANES), lambda i: (0, i)),
            pl.BlockSpec((2, PQ, 2 * LANES), lambda i: (i, 0, 0)),
            pl.BlockSpec(memory_space=pl.ANY),
        ],
        out_shape=[
            jax.ShapeDtypeStruct((PQ, MODEL_WIDTH), BF16),
            jax.ShapeDtypeStruct((HEAD_COUNT, PQ, 2 * LANES), BF16),
            jax.ShapeDtypeStruct(cotangent.shape, BF16),
        ],
        scratch_shapes=[
            pltpu.VMEM((LEN, 2 * LANES), BF16),
            pltpu.VMEM((LEN, 2 * LANES), BF16),
            pltpu.SemaphoreType.DMA((SG - 1,)),
            pltpu.SemaphoreType.DMA((SG - 1,)),
            pltpu.SemaphoreType.DMA,
        ],
        cost_estimate=pl.CostEstimate(
            flops=4 * HEAD_COUNT * PQ * LEN * 256,
            bytes_accessed=20_000_000,
            transcendentals=HEAD_COUNT * PQ * LEN,
        ),
        compiler_params=pltpu.CompilerParams(
            collective_id=5, has_side_effects=True, vmem_limit_bytes=56 * 2**20
        ),
        name="attend_forward",
    )(query, pairs, pairs, relative, vectors, query_side, key_side, phase, cosm, sinm, cotangent)


FF_STEP = 1024
FF_TILES = FF // FF_STEP
ROW_TILES = PQ // ROWS


def row_norm(value):
    centred = value - jnp.mean(value, axis=1, keepdims=True)
    inverse = lax.rsqrt(jnp.mean(centred * centred, axis=1, keepdims=True) + norm_eps)
    return centred * inverse, inverse


def row_norm_back(scaled, normed, inverse):
    along = jnp.mean(scaled * normed, axis=1, keepdims=True)
    return inverse * (scaled - jnp.mean(scaled, axis=1, keepdims=True) - normed * along)


def gelu_pieces(value):
    rate = math.sqrt(2.0 / math.pi)
    square = value * value
    bend = jnp.tanh(rate * value * (1.0 + 0.044715 * square))
    half = 0.5 * (1.0 + bend)
    slope = half + (0.5 * rate) * value * (1.0 - bend * bend) * (1.0 + 0.134145 * square)
    return value * half, slope


def mlp_kernel(
    mixture_ref,
    pooled_ref,
    upstream_ref,
    output_weight_ref,
    inner_weight_ref,
    outer_weight_ref,
    vectors_ref,
    inner_add_ref,
    output_ref,
    grad_mixture_ref,
    grad_first_ref,
    grad_outer_ref,
    grad_inner_ref,
    grad_output_ref,
    sums_ref,
    inner_sums_ref,
    active,
    slopes,
    grad_expanded,
    hidden_low,
    grad_branch,
    grad_attention,
    output_stage,
    mixture_stage,
    first_stage,
    send,
    receive,
    local,
):
    step = pl.program_id(0)
    place = Place()
    block = PQ // SG
    tile = (step + place.seq // 2 + 1) % ROW_TILES
    begin = pl.multiple_of(tile * ROWS, ROWS)

    def output_copy(to):
        return pltpu.make_async_remote_copy(
            src_ref=output_stage.at[to],
            dst_ref=output_ref.at[place.seq],
            send_sem=send.at[to],
            recv_sem=receive.at[place.seq],
            device_id=(to, place.dp),
            device_id_type=MESH,
        )

    def kept_copy():
        return pltpu.make_async_copy(
            output_stage.at[place.seq], output_ref.at[place.seq], local.at[0]
        )

    def row_copies():
        rows = pl.ds(begin, ROWS)
        return [
            pltpu.make_async_copy(
                mixture_stage.at[rows, :], grad_mixture_ref.at[rows, :], local.at[1 + 2 * tile]
            ),
            pltpu.make_async_copy(
                first_stage.at[rows, :], grad_first_ref.at[rows, :], local.at[2 + 2 * tile]
            ),
        ]

    @pl.when(step == 0)
    def _():
        place.greet()

    @pl.when(step < ROW_TILES)
    def _():
        rows = pl.ds(begin, ROWS)
        vector = lambda j: vectors_ref[j : j + 1, :]
        output_add, outer_add, gain_one, shift_one, gain_two, shift_two = map(vector, range(1, 7))
        attention = mm(mixture_ref[rows, :], output_weight_ref[...]) + output_add
        normed_one, inverse_one = row_norm(pooled_ref[rows, :] + attention)
        hidden = normed_one * gain_one + shift_one
        low_hidden = hidden.astype(BF16)
        hidden_low[rows, :] = low_hidden
        branch = jnp.zeros((ROWS, MODEL_WIDTH), F32)
        for j in range(FF_TILES):
            part = slice(j * FF_STEP, (j + 1) * FF_STEP)
            expanded = mm(low_hidden, inner_weight_ref[:, part]) + inner_add_ref[:, part]
            value, slope = gelu_pieces(expanded)
            low_value = value.astype(BF16)
            active[rows, part] = low_value
            slopes[:, part] = slope
            branch += mm(low_value, outer_weight_ref[part, :])
        normed_two, inverse_two = row_norm(hidden + (branch + outer_add))
        result = (normed_two * gain_two + shift_two).astype(BF16)
        for k in range(ROWS // block):
            to = tile * (ROWS // block) + k
            output_stage[to] = result[k * block : (k + 1) * block]

            @pl.when(to == place.seq)
            def _():
                kept_copy().start()

            @pl.when(to != place.seq)
            def _():
                output_copy(to).start()

        upstream = upstream_ref[rows, :].astype(F32)
        grad_second = row_norm_back(upstream * gain_two, normed_two, inverse_two)
        low_branch = grad_second.astype(BF16)
        grad_branch[rows, :] = low_branch
        grad_hidden = grad_second
        inner_sums = []
        for j in range(FF_TILES):
            part = slice(j * FF_STEP, (j + 1) * FF_STEP)
            grad_active = mm(low_branch, outer_weight_ref[part, :], NT)
            low_grad = (slopes[:, part] * grad_active).astype(BF16)
            grad_expanded[rows, part] = low_grad
            inner_sums.append(jnp.sum(low_grad.astype(F32), axis=0, keepdims=True))
            grad_hidden += mm(low_grad, inner_weight_ref[:, part], NT)
        grad_first = row_norm_back(grad_hidden * gain_one, normed_one, inverse_one)
        first_stage[rows, :] = grad_first
        low_attention = grad_first.astype(BF16)
        grad_attention[rows, :] = low_attention
        mixture_stage[rows, :] = mm(low_attention, output_weight_ref[...], NT).astype(BF16)
        for copy in row_copies():
            copy.start()
        row = lambda v: jnp.sum(v, axis=0, keepdims=True)
        sums = jnp.concatenate(
            [
                row(low_attention.astype(F32)),
                row(low_branch.astype(F32)),
                row(grad_hidden * normed_one),
                row(grad_hidden),
                row(upstream * normed_two),
                row(upstream),
                jnp.zeros((2, MODEL_WIDTH), F32),
            ],
            axis=0,
        )
        inner_sum = jnp.concatenate(inner_sums, axis=1)

        @pl.when(step == 0)
        def _():
            sums_ref[...] = sums
            inner_sums_ref[...] = inner_sum

        @pl.when(step > 0)
        def _():
            sums_ref[...] += sums
            inner_sums_ref[...] += inner_sum

    for j in range(FF_TILES):

        @pl.when(step == ROW_TILES + j)
        def _():
            part = slice(j * FF_STEP, (j + 1) * FF_STEP)
            grad_outer_ref[...] = mm(active[:, part], grad_branch[...], TN).astype(BF16)
            grad_inner_ref[...] = mm(hidden_low[...], grad_expanded[:, part], TN).astype(BF16)
            if j == 0:
                grad_output_ref[...] = mm(mixture_ref[...], grad_attention[...], TN).astype(BF16)

    @pl.when(step == ROW_TILES + FF_TILES - 1)
    def _():
        for t in range(ROW_TILES):
            rows = pl.ds(t * ROWS, ROWS)
            pltpu.make_async_copy(
                mixture_stage.at[rows, :], grad_mixture_ref.at[rows, :], local.at[1 + 2 * t]
            ).wait()
            pltpu.make_async_copy(
                first_stage.at[rows, :], grad_first_ref.at[rows, :], local.at[2 + 2 * t]
            ).wait()
        kept_copy().wait()
        for k in range(1, SG):
            other = (place.seq + k) % SG
            output_copy(other).wait_send()
            pltpu.make_async_remote_copy(
                src_ref=output_stage.at[other],
                dst_ref=output_ref.at[other],
                send_sem=send.at[other],
                recv_sem=receive.at[other],
                device_id=(other, place.dp),
                device_id_type=MESH,
            ).wait_recv()


def mlp(mixture, pooled, upstream, output_weight, inner_weight, outer_weight, vectors, inner_add):
    fixed = lambda shape: pl.BlockSpec(shape, lambda i: (0, 0), pipeline_mode=pl.Buffered(1))
    still = lambda shape: pl.BlockSpec(shape, lambda i: (0, 0))
    anywhere = pl.BlockSpec(memory_space=pl.ANY)
    out_shape = (SG, PQ // SG, MODEL_WIDTH)
    late = lambda i: jnp.maximum(i - ROW_TILES, 0)
    whole = (PQ, MODEL_WIDTH)
    square = (MODEL_WIDTH, MODEL_WIDTH)
    return pl.pallas_call(
        mlp_kernel,
        grid=(ROW_TILES + FF_TILES,),
        in_specs=[
            fixed(whole),
            fixed(whole),
            fixed(whole),
            fixed(square),
            fixed((MODEL_WIDTH, FF)),
            fixed((FF, MODEL_WIDTH)),
            fixed((VECTORS, MODEL_WIDTH)),
            fixed((1, FF)),
        ],
        out_specs=[
            anywhere,
            anywhere,
            anywhere,
            pl.BlockSpec((FF_STEP, MODEL_WIDTH), lambda i: (late(i), 0)),
            pl.BlockSpec((MODEL_WIDTH, FF_STEP), lambda i: (0, late(i))),
            still(square),
            still((8, MODEL_WIDTH)),
            still((1, FF)),
        ],
        out_shape=[
            jax.ShapeDtypeStruct(out_shape, BF16),
            jax.ShapeDtypeStruct(whole, BF16),
            jax.ShapeDtypeStruct(whole, F32),
            jax.ShapeDtypeStruct((FF, MODEL_WIDTH), BF16),
            jax.ShapeDtypeStruct((MODEL_WIDTH, FF), BF16),
            jax.ShapeDtypeStruct(square, BF16),
            jax.ShapeDtypeStruct((8, MODEL_WIDTH), F32),
            jax.ShapeDtypeStruct((1, FF), F32),
        ],
        scratch_shapes=[
            pltpu.VMEM((PQ, FF), BF16),
            pltpu.VMEM((ROWS, FF), F32),
            pltpu.VMEM((PQ, FF), BF16),
            pltpu.VMEM(whole, BF16),
            pltpu.VMEM(whole, BF16),
            pltpu.VMEM(whole, BF16),
            pltpu.VMEM(out_shape, BF16),
            pltpu.VMEM(whole, BF16),
            pltpu.VMEM(whole, F32),
            pltpu.SemaphoreType.DMA((SG,)),
            pltpu.SemaphoreType.DMA((SG,)),
            pltpu.SemaphoreType.DMA((1 + 2 * ROW_TILES,)),
        ],
        cost_estimate=pl.CostEstimate(
            flops=2 * PQ * MODEL_WIDTH * (3 * MODEL_WIDTH + 6 * FF),
            bytes_accessed=40_000_000,
            transcendentals=PQ * FF,
        ),
        compiler_params=pltpu.CompilerParams(
            collective_id=1, has_side_effects=True, vmem_limit_bytes=60 * 2**20
        ),
        name="mlp",
    )(mixture, pooled, upstream, output_weight, inner_weight, outer_weight, vectors, inner_add)


SLOTS = 2 * (PQ // ROWS)
EARLY_SLOTS = {}
for _i, _steps in enumerate(
    (
        (3, 12, 17, 20, 23, 26, 29, 34),
        (6, 20, 25, 28, 31, 34, 37, 42),
        (9, 28, 33, 36, 39, 42, 45, 48),
        (12, 36, 41, 44, 48),
        (14, 41, 45, 47, 48),
    )
):
    for _stage, _slot in zip((*STAGES[1 : len(_steps)], None), _steps):
        EARLY_SLOTS.setdefault(_slot, []).append((_i, _stage))


def attend_back_kernel(
    join_ref,
    key_ref,
    value_ref,
    query_ref,
    mixture_ref,
    grad_ref,
    relative_ref,
    vectors_ref,
    query_side_ref,
    key_side_ref,
    phase_ref,
    cos_ref,
    sin_ref,
    mlp_sums_ref,
    grad_outer_ref,
    grad_inner_ref,
    grad_output_ref,
    grad_query_ref,
    grad_key_ref,
    grad_value_ref,
    small_ref,
    *refs,
):
    early, _ = grad_chunks()
    sent, refs = refs[: len(early)], refs[len(early) :]
    key_join, value_join, key_total, value_total, join_grads, *refs = refs
    fulls, refs = refs[:WHOLE], refs[WHOLE:]
    buffers, (send, receive, local) = refs[: 6 * len(early)], refs[6 * len(early) :]
    pair = pl.program_id(0)
    place = Place()
    grads = (grad_outer_ref, grad_inner_ref, grad_output_ref)
    work = []
    for i, chunk in enumerate(early):
        kept = [*buffers[6 * i : 6 * i + 6], fulls[i] if i < WHOLE else None]
        source = chunk_source(grads[chunk[0]], chunk)
        work.append(Chunk(place, i, source, *chunk[4:], kept, send, receive, local))

    def exchange(slot):
        for i, stage in EARLY_SLOTS.get(slot, ()):
            if stage is not None:
                work[i].step(stage)
            elif i < WHOLE:
                work[i].finish(STAGES[-1])
                sent[i][...] = work[i].full[...]
                work[i].close(STAGES)
            else:
                work[i].finish(DOWN[-1])
                sent[i][...] = work[i].from_far[...]
                work[i].close(DOWN)

    @pl.when(pair == 0)
    def _():
        place.greet()
        for item in work:
            item.start("core")

    scale = HEAD_SIZE ** (-0.5)
    key_left = lane_ids(LEN) < HEAD_SIZE
    tile_lane = lane_ids(ROWS)
    key_join[:, LANES:] = key_side_ref[...]
    value_join[:, :LANES] = value_ref[...]
    value_join[:, LANES:] = key_side_ref[...]
    for h in range(2):
        pieces = (key_ref[...], phase_ref[...]) if h == 0 else (phase_ref[...], key_ref[...])
        key_join[:, :LANES] = jnp.where(key_left, *pieces)
        mine = (tile_lane < HEAD_SIZE) if h == 0 else (tile_lane >= HEAD_SIZE)
        part = slice(h * HEAD_SIZE, (h + 1) * HEAD_SIZE)
        for i in range(PQ // ROWS):
            rows = slice(i * ROWS, (i + 1) * ROWS)
            for slot in EARLY_SLOTS:
                if slot % SLOTS == h * (PQ // ROWS) + i:

                    @pl.when(pair == slot // SLOTS)
                    def _():
                        exchange(slot)

            join = join_ref[h, rows, :]
            grad = jnp.where(mine, grad_ref[rows, :].astype(F32), 0.0)
            dot = -jnp.sum(grad * mixture_ref[rows, :].astype(F32), axis=1, keepdims=True)
            one = dot.astype(BF16).astype(F32)
            two = (dot - one).astype(BF16).astype(F32)
            three = dot - one - two
            extra = jnp.where(tile_lane == 6, one, jnp.where(tile_lane == 7, two, three))
            inside = (tile_lane >= 6) & (tile_lane < 9)
            extra = jnp.where(inside, extra, 0.0)
            grad_low = grad.astype(BF16)
            weights = jnp.exp(mm(join, key_join[...], NT))
            slope = mm(
                jnp.concatenate([grad_low, extra.astype(BF16)], axis=1), value_join[...], NT
            )
            low_slope = (weights * slope).astype(BF16)
            low_weights = weights.astype(BF16)
            join_grads[h, rows, :] = mm(low_slope, key_join[...])
            to_key = mm(join_ref[h, rows, part], low_slope, TN)
            to_value = mm(grad_ref[rows, part], low_weights, TN)
            if i == 0:
                key_total[part, :] = to_key
                value_total[part, :] = to_value
            else:
                key_total[part, :] += to_key
                value_total[part, :] += to_value
    grad_key_ref[...] = key_total[...].T.astype(BF16)
    grad_value_ref[...] = value_total[...].T.astype(BF16)
    lane = lane_ids(PQ)
    left = lane < HEAD_SIZE
    typed = (lane >= 3) & (lane < 6)
    rounded = [(join_grads[h, :, :LANES] * scale).astype(BF16).astype(F32) for h in range(2)]
    content = jnp.where(left, rounded[0], rounded[1])
    position = jnp.where(left, rounded[1], rounded[0])
    turned = jnp.concatenate([position * cos_ref[...], position * sin_ref[...]], axis=1)
    turned_high, turned_low = split(turned)
    plain, swapped = pair_maps(relative_ref[...])
    maps = jnp.concatenate([plain, swapped], axis=1)
    shifted_grad = mm(turned_high, maps, NT) + mm(turned_low, maps, NT)
    side = query_side_ref[...]
    sames, others = [], []
    for h in range(2):
        kinds = jnp.where(typed, join_grads[h, :, LANES:], 0.0)
        same = jnp.sum(jnp.where(side > 0.5, kinds, 0.0), axis=1, keepdims=True)
        other = jnp.sum(jnp.where(side > 0.5, 0.0, kinds), axis=1, keepdims=True)
        sames.append((same * scale).astype(BF16).astype(F32))
        others.append((other * scale).astype(BF16).astype(F32))
    same = jnp.where(left, sames[0], sames[1])
    other = jnp.where(left, others[0], others[1])
    position_add = vectors_ref[8:9, :]
    type_add = vectors_ref[9:10, :]
    type_other = vectors_ref[10:11, :]
    type_same = vectors_ref[11:12, :]
    typed_grad = same * type_same + other * type_other
    grad_query_ref[...] = (content + shifted_grad + typed_grad).astype(BF16)
    query = query_ref[...]
    shifted_high, shifted_low = split(query + position_add)
    grad_map = (
        mm(shifted_high, turned_high, TN)
        + mm(shifted_low, turned_high, TN)
        + mm(shifted_high, turned_low, TN)
    )
    kinds = query + type_add
    row = lambda v: jnp.sum(v, axis=0, keepdims=True)
    below = mlp_sums_ref[...]
    columns = jnp.concatenate(
        [
            jnp.zeros((HEAD_SIZE, LANES), F32),
            row(grad_value_ref[...].astype(F32)),
            row(content),
            row(shifted_grad),
            row(typed_grad),
            row(kinds * other),
            row(kinds * same),
            jnp.zeros((2, LANES), F32),
            below,
            jnp.zeros((LANES - HEAD_SIZE - 24, LANES), F32),
        ],
        axis=0,
    )
    small_ref[:, :LANES] = (fold_maps(grad_map) + columns.T).astype(BF16)
    small_ref[:, LANES:] = jnp.zeros((LANES, LANES), BF16)

    @pl.when(pair == PAIRS - 1)
    def _():
        exchange(PAIRS * SLOTS)


def attend_backward(
    join,
    pairs,
    query,
    mixture,
    grad,
    relative,
    vectors,
    query_side,
    key_side,
    phase,
    cosm,
    sinm,
    mlp_sums,
    grads,
):
    early, _ = grad_chunks()
    anywhere = pl.BlockSpec(memory_space=pl.ANY)
    shapes = [
        chunk[4:] if i < WHOLE else (chunk[4] // 4, chunk[5] // 2)
        for i, chunk in enumerate(early)
    ]
    whole = lambda shape: pl.BlockSpec(shape, lambda i: (0, 0))
    return pl.pallas_call(
        attend_back_kernel,
        grid=(PAIRS,),
        in_specs=[
            pl.BlockSpec((2, PQ, 2 * LANES), lambda i: (i, 0, 0)),
            pl.BlockSpec((LEN, LANES), lambda i: (0, i)),
            pl.BlockSpec((LEN, LANES), lambda i: (0, i + PAIRS)),
            pl.BlockSpec((PQ, LANES), lambda i: (0, i)),
            pl.BlockSpec((PQ, LANES), lambda i: (0, i)),
            pl.BlockSpec((PQ, LANES), lambda i: (0, i)),
            pl.BlockSpec((LANES, HEAD_SIZE), lambda i: (i, 0)),
            pl.BlockSpec((VECTORS, LANES), lambda i: (0, i)),
            whole((PQ, LANES)),
            whole((LEN, LANES)),
            whole((LEN, LANES)),
            whole((PQ, LANES)),
            whole((PQ, LANES)),
            pl.BlockSpec((16, LANES), lambda i: (0, i)),
            *[anywhere] * 3,
        ],
        out_specs=[
            pl.BlockSpec((PQ, LANES), lambda i: (0, i)),
            pl.BlockSpec((LEN, LANES), lambda i: (0, i)),
            pl.BlockSpec((LEN, LANES), lambda i: (0, i)),
            pl.BlockSpec((LANES, 2 * LANES), lambda i: (i, 0)),
            *[whole(shape) for shape in shapes],
        ],
        out_shape=[
            jax.ShapeDtypeStruct((PQ, MODEL_WIDTH), BF16),
            jax.ShapeDtypeStruct((LEN, MODEL_WIDTH), BF16),
            jax.ShapeDtypeStruct((LEN, MODEL_WIDTH), BF16),
            jax.ShapeDtypeStruct((MODEL_WIDTH, 2 * LANES), BF16),
            *[jax.ShapeDtypeStruct(shape, BF16) for shape in shapes],
        ],
        scratch_shapes=[
            pltpu.VMEM((LEN, 2 * LANES), BF16),
            pltpu.VMEM((LEN, 2 * LANES), BF16),
            pltpu.VMEM((LANES, LEN), F32),
            pltpu.VMEM((LANES, LEN), F32),
            pltpu.VMEM((2, PQ, 2 * LANES), F32),
            *[pltpu.VMEM(chunk[4:], BF16) for chunk in early[:WHOLE]],
            *[buffer for chunk in early for buffer in down_buffers(*chunk[4:], True)],
            pltpu.SemaphoreType.DMA((len(early), 16)),
            pltpu.SemaphoreType.DMA((len(early), 16)),
            pltpu.SemaphoreType.DMA((len(early), 2)),
        ],
        cost_estimate=pl.CostEstimate(
            flops=10 * HEAD_COUNT * PQ * LEN * 256,
            bytes_accessed=32_000_000,
            transcendentals=HEAD_COUNT * PQ * LEN,
        ),
        compiler_params=pltpu.CompilerParams(
            collective_id=2, has_side_effects=True, vmem_limit_bytes=58 * 2**20
        ),
        name="attend_backward",
    )(
        join,
        pairs,
        pairs,
        query,
        mixture,
        grad,
        relative,
        vectors,
        query_side,
        key_side,
        phase,
        cosm,
        sinm,
        mlp_sums,
        *grads,
    )


def labels_kernel(
    labels_ref,
    query_ref,
    key_ref,
    value_ref,
    output_ref,
    inner_ref,
    outer_ref,
    out_ref,
    first_low,
    output_low,
    inner_low,
    outer_low,
    stage,
    send,
    receive,
    local,
    *full,
):
    place = Place()
    refs = (query_ref, key_ref, value_ref, output_ref, inner_ref, outer_ref)
    loads = [
        pltpu.make_async_copy(ref, buffer, local.at[j])
        for j, (ref, buffer) in enumerate(zip(refs, full))
    ]
    for load in loads:
        load.start()
    place.greet()
    copies = []
    for k in range(1, SG):
        to = (place.seq + k) % SG
        copy = pltpu.make_async_remote_copy(
            src_ref=labels_ref.at[to],
            dst_ref=stage.at[place.seq],
            send_sem=send.at[k - 1],
            recv_sem=receive.at[k - 1],
            device_id=(to, place.dp),
            device_id_type=MESH,
        )
        copy.start()
        copies.append(copy)
    stage[place.seq] = labels_ref[place.seq]
    for j, load in enumerate(loads):
        load.wait()
        if j < 3:
            first_low[:, j * MODEL_WIDTH : (j + 1) * MODEL_WIDTH] = full[j][...].astype(BF16)
        else:
            (output_low, inner_low, outer_low)[j - 3][...] = full[j][...].astype(BF16)
    for copy in copies:
        copy.wait()
    out_ref[...] = stage[...]


def move_labels(labels, weights):
    inside = pl.BlockSpec(memory_space=pltpu.VMEM)
    part = weights[0].shape[0]
    shapes = [(part, 3 * MODEL_WIDTH), *[weight.shape for weight in weights[3:]]]
    return pl.pallas_call(
        labels_kernel,
        in_specs=[inside, *[pl.BlockSpec(memory_space=pl.ANY)] * 6],
        out_specs=[inside] * 5,
        out_shape=[
            jax.ShapeDtypeStruct(labels.shape, jnp.int32),
            *[jax.ShapeDtypeStruct(shape, BF16) for shape in shapes],
        ],
        scratch_shapes=[
            pltpu.VMEM(labels.shape, jnp.int32),
            pltpu.SemaphoreType.DMA((SG - 1,)),
            pltpu.SemaphoreType.DMA((SG - 1,)),
            pltpu.SemaphoreType.DMA((len(weights),)),
            *[pltpu.VMEM(weight.shape, F32) for weight in weights],
        ],
        compiler_params=pltpu.CompilerParams(
            collective_id=4, has_side_effects=True, vmem_limit_bytes=58 * 2**20
        ),
        name="labels",
    )(labels, *weights)


def angle_tables():
    half = HEAD_SIZE // 2
    rate = np.float32(-math.log(10000.0) / half)
    frequency = np.exp(np.arange(half, dtype=np.float32) * rate)
    angle = np.arange(LEN, dtype=np.float32)[:, None] * frequency[None, :]
    cos, sin = np.cos(angle), np.sin(angle)
    phase = np.concatenate([cos, sin, cos, sin], axis=1)
    cos, sin = cos[0::2], sin[0::2]
    return (
        jnp.asarray(phase).astype(BF16),
        np.concatenate([cos, -cos, cos, -cos], axis=1),
        np.concatenate([sin, sin, sin, sin], axis=1),
    )


def sequence_body(
    tokens,
    segments,
    token_types,
    cotangent,
    query_weight,
    key_weight,
    value_weight,
    output_weight,
    inner_weight,
    outer_weight,
    value_bias,
    output_bias,
    inner_bias,
    outer_bias,
    attention_norm_gain,
    first_shift,
    second_gain,
    second_shift,
    content_bias,
    position_bias,
    type_bias,
    relative_kernel,
    type_embed,
):
    owners = lax.axis_size("dp")
    part = MODEL_WIDTH // owners
    low = lambda value: value.astype(BF16)
    half = segments.shape[1] // 2
    labels = jnp.stack(
        [segments[:, :half], segments[:, half:], token_types[:, :half], token_types[:, half:]],
        axis=1,
    )
    labels, first, output_low, inner_low, outer_low = move_labels(
        labels,
        (query_weight, key_weight, value_weight, output_weight, inner_weight, outer_weight),
    )
    tokens, labels = lax.optimization_barrier((tokens, labels))
    rows = lax.all_to_all(tokens, "seq", split_axis=0, concat_axis=0, tiled=True)
    flat = lambda value: low(value).reshape(1, part)
    vectors = [
        flat(value)
        for value in (
            value_bias,
            output_bias,
            outer_bias,
            attention_norm_gain,
            first_shift,
            second_gain,
            second_shift,
            content_bias,
            position_bias,
            type_bias,
            type_embed[:, 0],
            type_embed[:, 1],
        )
    ]
    vectors.append(jnp.zeros((VECTORS - len(vectors), part), BF16))
    vectors = lax.all_gather(jnp.concatenate(vectors, axis=0), "dp", axis=1, tiled=True)
    vectors = vectors.astype(F32)
    inner_add = lax.all_gather(low(inner_bias).reshape(1, -1), "dp", axis=1, tiled=True)
    inner_add = inner_add.astype(F32)
    relative = low(relative_kernel).reshape(part, HEAD_SIZE)
    relative = lax.all_gather(relative, "dp", axis=0, tiled=True)
    first = lax.all_gather(first, "dp", axis=0, tiled=True)
    inner_low = lax.all_gather(inner_low, "dp", axis=0, tiled=True)
    output_low = lax.all_gather(output_low, "dp", axis=0, tiled=True)
    outer_low = lax.all_gather(outer_low, "dp", axis=0, tiled=True)


    segment_row = labels[:, 0:2].reshape(LEN)
    type_row = labels[:, 2:4].reshape(LEN)
    segment_pairs = segment_row.reshape(PQ, 2)
    query_segments = segment_pairs[:, 0]
    query_types = type_row.reshape(PQ, 2)[:, 0]
    pair_same = (segment_pairs[:, 0] == segment_pairs[:, 1]).reshape(SG, PQ // SG)

    first_doc, last_doc = segment_row[0], segment_row[LEN - 1]
    first_type = type_row[0]
    last_type = jnp.max(jnp.where(type_row == first_type, -1, type_row))

    def classes(values, start, end):
        return jnp.where(values == start, 0, jnp.where(values == end, 2, 1))[:, None]

    columns = jnp.arange(LANES, dtype=jnp.int32)[None, :]
    key_side = (
        (columns == classes(segment_row, first_doc, last_doc))
        | (columns == 3 + classes(type_row, first_type, last_type))
        | ((columns >= 6) & (columns < 9))
    ).astype(BF16)
    query_docs = classes(query_segments, first_doc, last_doc)
    query_side = jnp.where(
        columns < 3,
        jnp.where(columns == query_docs, 0.0, FAR),
        (columns == 3 + classes(query_types, first_type, last_type)).astype(F32),
    )
    phase, cosm, sinm = angle_tables()

    block = rows.shape[1]
    pooled_block = block // 2
    at = jnp.arange(block, dtype=jnp.int32)[None, None, :]
    want = 2 * jnp.arange(pooled_block, dtype=jnp.int32)[None, :, None]
    half = jnp.where(pair_same, 0.5, 1.0)[:, :, None]
    other_half = jnp.where(pair_same, 0.5, 0.0)[:, :, None]
    pool = jnp.where(at == want, half, jnp.where(at == want + 1, other_half, 0.0)).astype(BF16)

    pooled = jnp.einsum("cpt,ctd->cpd", pool, rows, preferred_element_type=F32)
    pooled = pooled.reshape(PQ, MODEL_WIDTH)
    pooled_low = low(pooled)
    token_rows = rows.reshape(LEN, MODEL_WIDTH)
    query = mm(pooled_low, first[:, :MODEL_WIDTH])
    value_add = vectors[0:1]
    pair_add = jnp.concatenate([jnp.zeros_like(value_add), value_add], axis=1)
    pairs = low(mm(token_rows, first[:, MODEL_WIDTH:]) + pair_add)
    mixture, join, upstream = attend_forward(
        query, pairs, relative, vectors, query_side, key_side, phase, cosm, sinm, cotangent
    )
    upstream = upstream.reshape(PQ, MODEL_WIDTH)

    (
        output,
        grad_mixture,
        grad_first,
        grad_outer_weight,
        grad_inner_weight,
        grad_output_weight,
        row_sums,
        grad_inner_bias,
    ) = mlp(
        mixture, pooled, upstream, output_low, inner_low, outer_low, vectors, inner_add
    )
    inner_rows = grad_inner_bias.reshape(owners, owners, part).transpose(1, 0, 2)
    mlp_sums = jnp.concatenate(
        [row_sums, inner_rows.reshape(owners, MODEL_WIDTH), jnp.zeros((4, MODEL_WIDTH), F32)],
        axis=0,
    )

    grad_query, grad_key, grad_value, small_grads, *pieces = attend_backward(
        join,
        pairs,
        query,
        mixture,
        grad_mixture,
        relative,
        vectors,
        query_side,
        key_side,
        phase,
        cosm,
        sinm,
        mlp_sums,
        (grad_outer_weight, grad_inner_weight, grad_output_weight),
    )
    grad_tokens, *owned = finish(
        grad_query,
        grad_key,
        grad_value,
        token_rows,
        pooled_low,
        grad_first,
        pool,
        first,
        small_grads,
        pieces[WHOLE:],
    )
    owned = [*pieces[:WHOLE], *owned]
    owned_outer = jnp.concatenate(owned[0:2], axis=0).astype(F32)
    owned_inner = jnp.concatenate(owned[2:4], axis=1).astype(F32)
    owned_output, small_owned, *squares = [value.astype(F32) for value in owned[4:]]
    squares.append(owned_output)
    columns = small_owned[:, HEAD_SIZE : HEAD_SIZE + 24].T
    vector = lambda j: columns[j]
    heads = HEAD_COUNT // owners
    return (
        output,
        grad_tokens,
        squares[0],
        squares[1],
        squares[2],
        squares[3],
        owned_inner,
        owned_outer,
        vector(0),
        vector(8),
        columns[16:20].reshape(FF // owners),
        vector(9),
        vector(10),
        vector(11),
        vector(12),
        vector(13),
        vector(1).reshape(heads, HEAD_SIZE),
        vector(2).reshape(heads, HEAD_SIZE),
        vector(3).reshape(heads, HEAD_SIZE),
        small_owned[:, :HEAD_SIZE].reshape(heads, HEAD_SIZE, HEAD_SIZE),
        columns[4:6].reshape(2, heads, HEAD_SIZE).transpose(1, 0, 2),
    )


def solution(mesh):
    whole = mesh.shape["seq"] == SG and mesh.shape["dp"] == 4
    return jax.shard_map(
        sequence_body if whole else body,
        mesh=mesh,
        in_specs=(
            P("dp", "seq", None),
            P("dp", "seq"),
            P("dp", "seq"),
            P("dp", "seq", None),
            P("dp", None),
            P("dp", None),
            P("dp", None),
            P("dp", None),
            P("dp", None),
            P("dp", None),
            P("dp"),
            P("dp"),
            P("dp"),
            P("dp"),
            P("dp"),
            P("dp"),
            P("dp"),
            P("dp"),
            P("dp", None),
            P("dp", None),
            P("dp", None),
            P("dp", None, None),
            P("dp", None, None),
        ),
        out_specs=(
            P("dp", "seq", None),
            P("dp", "seq", None),
            P("dp", None),
            P("dp", None),
            P("dp", None),
            P("dp", None),
            P("dp", None),
            P("dp", None),
            P("dp"),
            P("dp"),
            P("dp"),
            P("dp"),
            P("dp"),
            P("dp"),
            P("dp"),
            P("dp"),
            P("dp", None),
            P("dp", None),
            P("dp", None),
            P("dp", None, None),
            P("dp", None, None),
        ),
        check_vma=False,
    )
```
